32 devices in a mesh: fsdp: 4 (over z), ctx: 4 (over y, x), tp: 2 (over core).
Axes of the slice: x: 2, y: 2, z: 4, core: 2. Of those that a mesh axis runs over, the one named last changes fastest.
Arguments:
- layer_input: bfloat16 [4096, 1536], P(('fsdp', 'ctx')), may hold values from -6 to 6
- segments: int32 [4, 1024], P('fsdp'), may hold values from 0 to 7, as said below
- routes: int32 [4096, 8], P(('fsdp', 'ctx')), may hold values from 0 to 15, all different within a row; in each aligned block of 256 rows (0 to 255, 256 to 511, ...) at most 192 rows name the same one
- norm_gain: bfloat16 [1536], P(('fsdp', 'ctx')), may hold values from 0.5 to 1.5
- query_weight: bfloat16 [1536, 1536], P(('fsdp', 'ctx'), 'tp'), may hold values from -0.3125 to 0.3125
- key_weight: bfloat16 [1536, 512], P(('fsdp', 'ctx'), 'tp'), may hold values from -0.15625 to 0.15625
- value_weight: bfloat16 [1536, 512], P(('fsdp', 'ctx'), 'tp'), may hold values from -0.15625 to 0.15625
- output_weight: bfloat16 [1536, 1536], P('tp', ('fsdp', 'ctx')), may hold values from -0.625 to 0.625
- ffn_gain: bfloat16 [1536], P(('fsdp', 'ctx')), may hold values from 0.5 to 1.5
- router_weight: bfloat16 [1536, 16], P(('fsdp', 'ctx')), may hold values from -0.078125 to 0.078125
- gate_weight: bfloat16 [16, 1536, 512], P(None, ('fsdp', 'ctx'), 'tp'), may hold values from -0.15625 to 0.15625
- up_weight: bfloat16 [16, 1536, 512], P(None, ('fsdp', 'ctx'), 'tp'), may hold values from -0.15625 to 0.15625
- down_weight: bfloat16 [16, 512, 1536], P(None, 'tp', ('fsdp', 'ctx')), may hold values from -0.5 to 0.5
- cotangent: bfloat16 [4096, 1536], P(('fsdp', 'ctx')), may hold values from -6 to 6
Outputs:
- layer_output: bfloat16 [4096, 1536], P(('fsdp', 'ctx'))
- input_grad: float32 [4096, 1536], P(('fsdp', 'ctx'))
- norm_gain_grad: float32 [1536], P(('fsdp', 'ctx'))
- query_grad: float32 [1536, 1536], P(('fsdp', 'ctx'), 'tp')
- key_grad: float32 [1536, 512], P(('fsdp', 'ctx'), 'tp')
- value_grad: float32 [1536, 512], P(('fsdp', 'ctx'), 'tp')
- output_grad: float32 [1536, 1536], P('tp', ('fsdp', 'ctx'))
- ffn_gain_grad: float32 [1536], P(('fsdp', 'ctx'))
- router_grad: float32 [1536, 16], P(('fsdp', 'ctx'))
- gate_grad: float32 [16, 1536, 512], P(None, ('fsdp', 'ctx'), 'tp')
- up_grad: float32 [16, 1536, 512], P(None, ('fsdp', 'ctx'), 'tp')
- down_grad: float32 [16, 512, 1536], P(None, 'tp', ('fsdp', 'ctx'))
The draws below stay inside these ranges and needn't reach their ends.
Inputs may be any that keep to these rules, and one draw needn't show every extreme that they name: Each row of segments never falls and numbers its documents from 0 in order. One row, drawn from the seed, holds three documents: the first and the last have 256/8 to 127 tokens, the middle one the rest. Every other row holds eight documents, cut at seven distinct places drawn from the seed. `routes`: each row names 8 different experts. Among the 256 rows of one device no expert is named by more than 192 rows.
All inputs are finite; a program needn't handle non-finite values.
Results may differ from the reference program's by a relative error of at most 0.025.
Values may be sent and summed in bfloat16 or wider, within the bound.
A program may use at most 256 MiB of HBM per device.

```python
import math
import jax
import jax.numpy as jnp
import numpy as np
from jax import lax

D = 1536
HQ = 24
KV = 8
HD = 64
FF = 512
TOP = 8
EXPERTS = 16
TOK_DEV = 256
SEQS = 4
LEN = 1024
TOKENS = 4096
CAP = 192


def draw_cut_places(sub_key):
    return jax.random.permutation(sub_key, LEN - 1)[:7] + 1


def draw_segments(key, part):
    key = jax.random.fold_in(key, 7)
    head_key, tail_key, cut_key, pick_key = jax.random.split(key, 4)
    cut_keys = jax.random.split(cut_key, SEQS)
    cut_places = jax.vmap(draw_cut_places)(cut_keys).astype(jnp.int32)
    order = jnp.arange(LEN, dtype=jnp.int32)
    packed = jnp.sum((order[None, :, None] >= cut_places[:, None, :]).astype(jnp.int32), -1)
    heading = jax.random.randint(head_key, (SEQS, 1), TOK_DEV // 8, TOK_DEV // 2)
    trailing = jax.random.randint(tail_key, (SEQS, 1), TOK_DEV // 8, TOK_DEV // 2)
    spanning = (order[None, :] >= heading).astype(jnp.int32) + (order[None, :] >= LEN - trailing).astype(jnp.int32)
    chosen_row = jax.random.randint(pick_key, (), 0, SEQS)
    rows = jnp.arange(SEQS, dtype=jnp.int32)[:, None] == chosen_row
    return jnp.where(rows, spanning, packed).astype(jnp.int32)


def block_scale(rng, dims, shards, smallest, top_value):
    level, own = 1.0, jax.random.fold_in(rng, 6)
    for dim, parts in shards:
        draws = jnp.exp(jax.random.uniform(jax.random.fold_in(own, dim), (parts,), jnp.float32, smallest / len(shards), top_value / len(shards)))
        level = level * jnp.repeat(draws, dims[dim] // parts).reshape([-1 if axis == dim else 1 for axis in range(len(dims))])
    return level


def shared_out(rng, own, number, rows, number_of, top, reach, skew):
    sequence = jax.random.permutation(rng, number_of)
    heavy_load, common = portions_of(number_of, rows * top, reach, skew, True), portions_of(number_of, rows * top, reach, skew, False)
    places = jnp.arange(number_of)

    def named(sizes, rotation):
        used = int((sizes > 0).sum())
        fixed = max(1, used // 4)
        shifted = fixed + (places - fixed + rotation * (used - fixed)) % max(1, number_of - fixed)
        return jnp.zeros((number_of,), jnp.int32).at[sequence[jnp.where(places < fixed, places, shifted)]].set(jnp.asarray(sizes, jnp.int32))

    sizes = jnp.where(number % 4 == 0, named(heavy_load, number // 4), named(common, number - number // 4 - 1))
    mixed = jax.random.permutation(jax.random.fold_in(own, 3), number_of)
    donor, sink = mixed[0:number_of // 2 * 2:2], mixed[1:number_of // 2 * 2:2]
    margin = jnp.minimum(sizes[donor] - 1, reach - sizes[sink]) // 2
    margin = jnp.where((donor == sequence[0]) | (sink == sequence[0]) | (sizes[sink] == 0), 0, jnp.maximum(margin, 0))
    shifted = jax.random.randint(jax.random.fold_in(own, 4), (number_of // 2,), 0, 1 << 20) % (margin + 1)
    sizes = sizes.at[donor].add(-shifted).at[sink].add(shifted)
    labels = jnp.searchsorted(jnp.cumsum(sizes), jnp.arange(rows * top), side="right").astype(jnp.int32)
    grid = labels.reshape(top, rows).T
    grid = grid[jax.random.permutation(jax.random.fold_in(own, 1), rows)]
    rotation = jax.random.randint(jax.random.fold_in(own, 2), (rows, 1), 0, top)
    return jnp.take_along_axis(grid, (jnp.arange(top)[None, :] + rotation) % top, axis=1)


def portions_of(amount, total, most, lean, full):
    loads = [(1 << 20) // math.isqrt(standing ** lean) + 1 for standing in range(1, amount + 1)]
    largest = most if full else min(most, max(-(-total // amount), total * loads[0] // sum(loads)))
    least = 1 if total - largest >= amount - 1 else 0
    holding, rest = [largest] + [least] * (amount - 1), total - largest - least * (amount - 1)
    while rest > 0:
        free = [i for i in range(1, amount) if holding[i] < largest] or [i for i in range(1, amount) if holding[i] < most]
        whole, remaining = sum([loads[i] for i in free]), rest
        for i in free:
            more = min(most - holding[i], max(1, remaining * loads[i] // whole), rest)
            holding[i] = holding[i] + more
            rest = rest - more
    return np.array(holding)


def scatter_about(own_key, shape, spread, bound, pieces=(), held_as=jnp.bfloat16):
    entries = jax.random.normal(own_key, shape, jnp.float32) * spread
    if len(pieces) > 0:
        entries = block_scale(own_key, shape, pieces, -0.22, 0.18) * entries
    return jnp.clip(entries, min=-bound, max=bound).astype(held_as)


def setup_inputs(seed: int = 0) -> dict:
    keys = jax.random.split(jax.random.key(seed), 15)
    layer_input = scatter_about(keys[0], (TOKENS, D), 1.0, 6.0, ((0, 16),))
    segments = draw_segments(jax.random.fold_in(keys[14], 71), 0)
    routes_keys = jax.random.split(jax.random.fold_in(keys[2], 1), TOKENS // TOK_DEV)
    routes_turns = jax.random.permutation(jax.random.fold_in(keys[2], 3), TOKENS // TOK_DEV)
    routes = jax.vmap(lambda own, number: shared_out(jax.random.fold_in(keys[2], 2), own, number, TOK_DEV, EXPERTS, TOP, CAP, 2))(routes_keys, routes_turns).reshape((TOKENS, TOP))
    norm_gain = jnp.clip(1.0 + 0.1 * jax.random.normal(keys[3], (D,), jnp.float32), 0.5, 1.5).astype(jnp.bfloat16)
    query_weight = scatter_about(keys[4], (D, HQ * HD), (D // 4) ** -0.5, 0.3125, ((0, 16), (1, 2)))
    key_weight = scatter_about(keys[5], (D, KV * HD), D ** -0.5, 0.15625, ((0, 16), (1, 2)))
    value_weight = scatter_about(keys[6], (D, KV * HD), D ** -0.5, 0.15625, ((0, 16), (1, 2)))
    output_weight = scatter_about(keys[7], (HQ * HD, D), (HQ * HD // 16) ** -0.5, 0.625, ((0, 2), (1, 16)))
    ffn_gain = jnp.clip(1.0 + 0.1 * jax.random.normal(keys[8], (D,), jnp.float32), 0.5, 1.5).astype(jnp.bfloat16)
    router_weight = scatter_about(keys[9], (D, EXPERTS), (4 * D) ** -0.5, 0.078125, ((0, 16),))
    gate_weight = scatter_about(keys[10], (EXPERTS, D, FF), D ** -0.5, 0.15625, ((1, 16), (2, 2)))
    up_weight = scatter_about(keys[11], (EXPERTS, D, FF), D ** -0.5, 0.15625, ((1, 16), (2, 2)))
    down_weight = scatter_about(keys[12], (EXPERTS, FF, D), (FF // 4) ** -0.5, 0.5, ((1, 2), (2, 16)))
    cotangent = scatter_about(keys[13], (TOKENS, D), 1.0, 6.0, ((0, 16),))
    return {"layer_input": layer_input, "segments": segments, "routes": routes, "norm_gain": norm_gain, "query_weight": query_weight, "key_weight": key_weight, "value_weight": value_weight, "output_weight": output_weight, "ffn_gain": ffn_gain, "router_weight": router_weight, "gate_weight": gate_weight, "up_weight": up_weight, "down_weight": down_weight, "cotangent": cotangent}


EPSILON = 1e-05
MASKED_SCORE = -1e+30

@jax.custom_vjp
def low(v):
    return lax.optimization_barrier(v.astype(jnp.bfloat16)).astype(jnp.float32)

@jax.custom_vjp
def low_back(v):
    return v

def low_keep(v):
    return (low(v), None)

def low_pass(kept, grad):
    return (grad,)

def back_keep(v):
    return (v, None)

def back_low(kept, grad):
    return (low(grad),)
low.defvjp(low_keep, low_pass)
low_back.defvjp(back_keep, back_low)

def rotate(values, place, sign):
    rows = values.shape[0]
    shaped = values.reshape(rows, -1, HD)
    half = HD // 2
    freq = 10000.0 ** (-2.0 * jnp.arange(half, dtype=jnp.float32) / HD)
    angle = place.astype(jnp.float32)[:, None] * freq[None, :]
    cosine = jnp.cos(angle)[:, None, :]
    sine = sign * jnp.sin(angle)[:, None, :]
    former = shaped[..., :half]
    latter = shaped[..., half:]
    turned = jnp.concatenate([former * cosine - latter * sine, latter * cosine + former * sine], -1)
    return turned.reshape(rows, -1)

def normalize(values, gain):
    inverse = lax.rsqrt(lax.optimization_barrier(jnp.mean(values * values, -1, keepdims=True)) + EPSILON)
    return values * inverse * gain

def document_place(segment_row):
    length = segment_row.shape[0]
    order = jnp.arange(length, dtype=jnp.int32)
    fresh = jnp.concatenate([jnp.ones((1,), jnp.bool_), segment_row[1:] != segment_row[:-1]])
    starts = lax.cummax(jnp.where(fresh, order, 0), axis=0)
    return order - starts

def attend_sequence(query, key, value, segment_row):
    exact = lax.Precision.HIGHEST
    groups = HQ // KV
    block = 512 if LEN % 512 == 0 else LEN
    order = jnp.arange(LEN, dtype=jnp.int32)
    key_heads = key.reshape(LEN, KV, HD)
    value_heads = value.reshape(LEN, KV, HD)

    def one_block(begin):
        rows = lax.dynamic_slice_in_dim(query, begin, block, 0).reshape(block, KV, groups, HD)
        query_order = begin + jnp.arange(block, dtype=jnp.int32)
        query_doc = lax.dynamic_slice_in_dim(segment_row, begin, block, 0)
        seen = (segment_row[None, :] == query_doc[:, None]) & (order[None, :] <= query_order[:, None])
        scores = low_back(jnp.einsum('qkgd,nkd->qkgn', rows, key_heads, precision=exact) * HD ** (-0.5))
        scores = jnp.where(seen[:, None, None, :], scores, MASKED_SCORE)
        probs = low(jax.nn.softmax(scores, axis=-1))
        mixed = jnp.einsum('qkgn,nkd->qkgd', probs, value_heads, precision=exact)
        return low(low_back(mixed)).reshape(block, HQ * HD)
    begins = jnp.arange(LEN // block, dtype=jnp.int32) * block
    return lax.map(jax.checkpoint(one_block), begins).reshape(LEN, HQ * HD)

def forward(layer_input, norm_gain, query_weight, key_weight, value_weight, output_weight, ffn_gain, router_weight, gate_weight, up_weight, down_weight, place, segments, routes):
    exact = lax.Precision.HIGHEST
    normed1 = low(normalize(layer_input, norm_gain))
    query = low(rotate(low_back(jnp.dot(normed1, query_weight, precision=exact)), place, 1.0))
    key = low(rotate(low_back(jnp.dot(normed1, key_weight, precision=exact)), place, 1.0))
    value = low(low_back(jnp.dot(normed1, value_weight, precision=exact)))
    mixed = lax.map(lambda item: attend_sequence(item[0], item[1], item[2], item[3]), (query.reshape(SEQS, LEN, -1), key.reshape(SEQS, LEN, -1), value.reshape(SEQS, LEN, -1), segments))
    attention = low_back(jnp.dot(mixed.reshape(TOKENS, -1), output_weight, precision=exact))
    middle = layer_input + attention
    normed2 = low(normalize(middle, ffn_gain))
    logits = low_back(jnp.dot(normed2, router_weight, precision=exact))
    picks = (routes[:, :, None] == jnp.arange(EXPERTS, dtype=jnp.int32)[None, None, :]).astype(jnp.float32)
    chosen = jnp.take_along_axis(logits, routes, 1)
    gates = jax.nn.softmax(chosen, axis=-1)
    gate_table = lax.optimization_barrier(jnp.sum(gates[:, :, None] * picks, 1))

    def expert(summed, item):
        gate_e, up_e, down_e, weight_e = item
        former = low_back(jnp.dot(normed2, gate_e, precision=exact))
        latter = low_back(jnp.dot(normed2, up_e, precision=exact))
        hidden = low(jax.nn.silu(former) * latter)
        result = low_back(jnp.dot(hidden, down_e, precision=exact))
        return (summed + weight_e[:, None] * result, None)
    mixture, _ = lax.scan(jax.checkpoint(expert), jnp.zeros((TOKENS, D), jnp.float32), (gate_weight, up_weight, down_weight, gate_table.T))
    return middle + mixture

def reference(layer_input, segments, routes, norm_gain, query_weight, key_weight, value_weight, output_weight, ffn_gain, router_weight, gate_weight, up_weight, down_weight, cotangent):
    place = jax.vmap(document_place)(segments).reshape(TOKENS)
    floats = [item.astype(jnp.float32) for item in (layer_input, norm_gain, query_weight, key_weight, value_weight, output_weight, ffn_gain, router_weight, gate_weight, up_weight, down_weight)]

    def run(*values):
        return forward(*values, place, segments, routes)
    result, pullback = jax.vjp(run, *floats)
    grads = pullback(cotangent.astype(jnp.float32))
    return (result.astype(jnp.bfloat16), grads[0], grads[1], grads[2], grads[3], grads[4], grads[5], grads[6], grads[7], grads[8], grads[9], grads[10])
```

```python
import jax
import jax.numpy as jnp
from jax import lax
from jax.experimental import pallas as pl
from jax.experimental.pallas import tpu as pltpu
from jax.sharding import PartitionSpec as P

MESH = pl.DeviceIdType.MESH

D = 1536
HD = 64
EXPERTS = 16


EPSILON = 1e-05
MASKED_SCORE = -1e30


def rotate(values, place, sign):
    rows = values.shape[0]
    shaped = values.reshape(rows, -1, HD)
    half = HD // 2
    freq = 10000.0 ** (-2.0 * jnp.arange(half, dtype=jnp.float32) / HD)
    angle = place.astype(jnp.float32)[:, None] * freq[None, :]
    cosine = jnp.cos(angle)[:, None, :]
    sine = sign * jnp.sin(angle)[:, None, :]
    former = shaped[..., :half]
    latter = shaped[..., half:]
    turned = jnp.concatenate([former * cosine - latter * sine, latter * cosine + former * sine], -1)
    return turned.reshape(rows, -1)


def normalize(values, gain):
    inverse = lax.rsqrt(jnp.mean(values * values, -1, keepdims=True) + EPSILON)
    return (values * inverse * gain.astype(jnp.float32), inverse)


def norm_back(grad, values, inverse, gain):
    scaled = grad * gain.astype(jnp.float32)
    gain_grad = jnp.sum(grad * values * inverse, 0)
    mean_term = jnp.mean(scaled * values, -1, keepdims=True)
    return (inverse * scaled - values * inverse**3 * mean_term, gain_grad)


def document_place(segment_row):
    length = segment_row.shape[0]
    order = jnp.arange(length, dtype=jnp.int32)
    fresh = jnp.concatenate([jnp.ones((1,), jnp.bool_), segment_row[1:] != segment_row[:-1]])
    starts = lax.cummax(jnp.where(fresh, order, 0), axis=0)
    return order - starts


def contract_rows(left, right):
    return lax.dot_general(
        left, right, (((0,), (0,)), ((), ())), preferred_element_type=jnp.float32
    )


def times_transpose(left, right):
    return lax.dot_general(
        left, right, (((1,), (1,)), ((), ())), preferred_element_type=jnp.float32
    )


def spread_experts(packed):
    ep = lax.axis_size("fsdp")
    local = packed.shape[0] // ep
    rows = packed.shape[1]
    swapped = lax.all_to_all(packed, "fsdp", 0, 0, tiled=True)
    swapped = swapped.reshape(ep, local, rows, -1).transpose(0, 2, 1, 3)
    swapped = swapped.reshape(ep, rows, -1)
    whole = lax.all_gather(swapped, "ctx", axis=1)
    return whole.reshape(ep * lax.axis_size("ctx") * rows, -1)


def collect_experts(sums, rows):
    ep, ring = lax.axis_size("fsdp"), lax.axis_size("ctx")
    turned = sums.reshape(ep, ring, rows, -1).transpose(1, 0, 2, 3).reshape(sums.shape)
    mine = lax.psum_scatter(turned, "ctx", scatter_dimension=0, tiled=True)
    return lax.all_to_all(mine, "fsdp", 0, 0, tiled=True)


def at_device(fsdp, ctx, tp):
    return {"fsdp": fsdp, "ctx": ctx, "tp": tp}


def greet(partners):
    barrier = pltpu.get_barrier_semaphore()
    for device in partners:
        pl.semaphore_signal(barrier, inc=1, device_id=device, device_id_type=MESH)
    pl.semaphore_wait(barrier, len(partners))


def remote(source, target, send, recv, device):
    return pltpu.make_async_remote_copy(
        src_ref=source, dst_ref=target, send_sem=send, recv_sem=recv, device_id=device, device_id_type=MESH
    )


def gather_kernel(
    attn_ref, gate_ref, up_ref, down_ref, outer_ref,
    attn_out, expert_out, outer_out,
    local_sem, z_send, z_recv, plane_send, plane_recv, relay_send, relay_recv, core_send, core_recv,
):
    ep = z_send.shape[1] + 1
    f, c, t = lax.axis_index("fsdp"), lax.axis_index("ctx"), lax.axis_index("tp")
    rows = attn_ref.shape[0]
    local = gate_ref.shape[0] // ep
    hidden = gate_ref.shape[2]
    tokens = outer_ref.shape[0]
    half = tokens // 2
    outs = (attn_out, expert_out)
    cuts = [(out.shape[1] // 256) * 128 for out in outs]

    def peer(distance):
        return lax.rem(f + distance, ep)

    def shard_rows(fsdp, ctx):
        return pl.ds(pl.multiple_of((fsdp * 4 + ctx) * rows, 16), rows)

    def columns(kind, side):
        cut, width = cuts[kind], outs[kind].shape[1]
        return pl.ds(0, cut) if side == 0 else pl.ds(cut, width - cut)

    x_device = at_device(f, c ^ 1, t)
    y_device = at_device(f, c ^ 2, t)
    core = at_device(f, c, 1 - t)
    greet([at_device(peer(d), c, t) for d in range(1, ep)] + [x_device, y_device, core])

    mine = shard_rows(f, c)
    sent = []
    for d in range(1, ep):
        device = at_device(peer(d), c, t)
        copy = remote(attn_ref, attn_out.at[mine], z_send.at[0, d - 1], z_recv.at[0, d - 1], device)
        copy.start()
        sent.append(copy)
    copies = [pltpu.make_async_copy(attn_ref, attn_out.at[mine], local_sem.at[0])]
    copies[0].start()
    for d in range(ep):
        for kind, ref in enumerate((gate_ref, up_ref, down_ref)):
            for e in range(local):
                target = expert_out.at[mine, pl.ds((kind * local + e) * hidden, hidden)]
                source = ref.at[peer(d) * local + e]
                if d == 0:
                    pltpu.make_async_copy(source, target, local_sem.at[1]).start()
                else:
                    remote(
                        source, target, z_send.at[1, d - 1], z_recv.at[1, d - 1], at_device(peer(d), c, t)
                    ).start()
    here = pl.ds(pl.multiple_of(f * tokens + t * half, 16), half)
    my_half = outer_ref.at[pl.ds(pl.multiple_of(t * half, 16), half)]
    for d in range(1, ep):
        copy = remote(
            my_half, outer_out.at[here], z_send.at[2, d - 1], z_recv.at[2, d - 1], at_device(peer(d), c, t)
        )
        copy.start()
        sent.append(copy)
    copies.append(
        pltpu.make_async_copy(
            outer_ref, outer_out.at[pl.ds(pl.multiple_of(f * tokens, 16), tokens)], local_sem.at[2]
        )
    )
    copies[1].start()

    def z_arrival(kind, d):
        back = lax.rem(f + ep - d, ep)
        place = shard_rows(back, c)
        remote(
            outs[kind].at[place], outs[kind].at[place], z_send.at[kind, d - 1], z_recv.at[kind, d - 1], x_device
        ).wait_recv()

    def spread(kind, d):
        place = shard_rows(lax.rem(f + ep - d, ep), c)
        for step in range(2):
            for way, device in enumerate((x_device, y_device)):
                side = step ^ way
                block = outs[kind].at[place, columns(kind, side)]
                copy = remote(
                    block, block, plane_send.at[kind, d, way, side], plane_recv.at[kind, d, way, side], device
                )
                copy.start()
                sent.append(copy)

    def pass_on(kind, d):
        for way, device in enumerate((y_device, x_device)):
            origin = c ^ (1 if way == 0 else 2)
            place = shard_rows(lax.rem(f + ep - d, ep), origin)
            block = outs[kind].at[place, columns(kind, way)]
            remote(
                block, block, plane_send.at[kind, d, way, way], plane_recv.at[kind, d, way, way], device
            ).wait_recv()
            copy = remote(block, block, relay_send.at[kind, d, way], relay_recv.at[kind, d, way], device)
            copy.start()
            sent.append(copy)

    copies[0].wait()
    spread(0, 0)
    pltpu.make_async_copy(expert_out.at[mine], expert_out.at[mine], local_sem.at[1]).wait()
    spread(1, 0)
    for d in range(1, ep):
        z_arrival(0, d)
        spread(0, d)
        pass_on(0, d - 1)
    pass_on(1, 0)
    pass_on(0, ep - 1)
    for d in range(1, ep):
        z_arrival(1, d)
        spread(1, d)
        if d > 1:
            pass_on(1, d - 1)
    pass_on(1, ep - 1)
    for d in range(1, ep):
        back = lax.rem(f + ep - d, ep)
        place = pl.ds(pl.multiple_of(back * tokens + t * half, 16), half)
        remote(
            outer_out.at[place], outer_out.at[place], z_send.at[2, d - 1], z_recv.at[2, d - 1], core
        ).wait_recv()
        copy = remote(
            outer_out.at[place], outer_out.at[place], core_send.at[d - 1], core_recv.at[d - 1], core
        )
        copy.start()
        sent.append(copy)
    copies[1].wait()
    for kind in range(2):
        for d in range(ep):
            back = lax.rem(f + ep - d, ep)
            for way, device in enumerate((x_device, y_device)):
                side = 1 - way
                block = outs[kind].at[shard_rows(back, c ^ (1 << way)), columns(kind, side)]
                remote(
                    block, block, plane_send.at[kind, d, way, side], plane_recv.at[kind, d, way, side], device
                ).wait_recv()
                block = outs[kind].at[shard_rows(back, c ^ 3), columns(kind, way)]
                remote(
                    block, block, relay_send.at[kind, d, way], relay_recv.at[kind, d, way], device
                ).wait_recv()
    for d in range(1, ep):
        back = lax.rem(f + ep - d, ep)
        place = pl.ds(pl.multiple_of(back * tokens + (1 - t) * half, 16), half)
        remote(
            outer_out.at[place], outer_out.at[place], core_send.at[d - 1], core_recv.at[d - 1], core
        ).wait_recv()
        remote(
            expert_out.at[mine], expert_out.at[mine], z_send.at[1, d - 1], z_recv.at[1, d - 1], core
        ).wait_send()
    for copy in sent:
        copy.wait_send()


def gather_all(attn, gate, up, down, outer):
    ep = lax.axis_size("fsdp")
    rows = attn.shape[0]
    total = rows * ep * lax.axis_size("ctx")
    local = gate.shape[0] // ep
    low = jnp.bfloat16
    dma = pltpu.SemaphoreType.DMA
    anywhere = pl.BlockSpec(memory_space=pl.ANY)
    return pl.pallas_call(
        gather_kernel,
        out_shape=(
            jax.ShapeDtypeStruct((total, attn.shape[1]), low),
            jax.ShapeDtypeStruct((total, 3 * local * gate.shape[2]), low),
            jax.ShapeDtypeStruct((ep * outer.shape[0], outer.shape[1]), low),
        ),
        in_specs=[anywhere] * 5,
        out_specs=(anywhere,) * 3,
        scratch_shapes=[
            dma((3,)),
            dma((3, ep - 1)),
            dma((3, ep - 1)),
            dma((2, ep, 2, 2)),
            dma((2, ep, 2, 2)),
            dma((2, ep, 2)),
            dma((2, ep, 2)),
            dma((ep - 1,)),
            dma((ep - 1,)),
        ],
        compiler_params=pltpu.CompilerParams(collective_id=1, has_side_effects=True),
        name="gather_all",
    )(attn, gate, up, down, outer)


def along_z_kernel(mine_ref, all_ref, local_sem, z_send, z_recv, core_send, core_recv):
    ep = z_send.shape[0] + 1
    f, c, t = lax.axis_index("fsdp"), lax.axis_index("ctx"), lax.axis_index("tp")
    tokens = mine_ref.shape[0]
    half = tokens // 2

    def peer(distance):
        return lax.rem(f + distance, ep)

    def place(fsdp, part):
        return pl.ds(pl.multiple_of(fsdp * tokens + part * half, 16), half)

    core = at_device(f, c, 1 - t)
    greet([at_device(peer(d), c, t) for d in range(1, ep)] + [core])
    sent = []
    source = mine_ref.at[pl.ds(pl.multiple_of(t * half, 16), half)]
    for d in range(1, ep):
        copy = remote(
            source, all_ref.at[place(f, t)], z_send.at[d - 1], z_recv.at[d - 1], at_device(peer(d), c, t)
        )
        copy.start()
        sent.append(copy)
    own = pltpu.make_async_copy(
        mine_ref, all_ref.at[pl.ds(pl.multiple_of(f * tokens, 16), tokens)], local_sem
    )
    own.start()
    for d in range(1, ep):
        block = all_ref.at[place(peer(ep - d), t)]
        remote(block, block, z_send.at[d - 1], z_recv.at[d - 1], core).wait_recv()
        copy = remote(block, block, core_send.at[d - 1], core_recv.at[d - 1], core)
        copy.start()
        sent.append(copy)
    for d in range(1, ep):
        block = all_ref.at[place(peer(ep - d), 1 - t)]
        remote(block, block, core_send.at[d - 1], core_recv.at[d - 1], core).wait_recv()
    own.wait()
    for copy in sent:
        copy.wait_send()


def along_z(mine):
    ep = lax.axis_size("fsdp")
    dma = pltpu.SemaphoreType.DMA
    anywhere = pl.BlockSpec(memory_space=pl.ANY)
    return pl.pallas_call(
        along_z_kernel,
        out_shape=jax.ShapeDtypeStruct((ep * mine.shape[0], mine.shape[1]), mine.dtype),
        in_specs=[anywhere],
        out_specs=anywhere,
        scratch_shapes=[dma, dma((ep - 1,)), dma((ep - 1,)), dma((ep - 1,)), dma((ep - 1,))],
        compiler_params=pltpu.CompilerParams(collective_id=2, has_side_effects=True),
        name="along_z",
    )(mine)


def sum_z_kernel(
    part_ref, sum_ref, core_in, z_out, z_in, core_send, core_recv, z_send, z_recv, back_send, back_recv
):
    ep = z_send.shape[0] + 1
    f, c, t = lax.axis_index("fsdp"), lax.axis_index("ctx"), lax.axis_index("tp")
    tokens = sum_ref.shape[0]
    half = tokens // 2

    def peer(distance):
        return lax.rem(f + distance, ep)

    def place(fsdp, part):
        return pl.ds(pl.multiple_of(fsdp * tokens + part * half, 16), half)

    core = at_device(f, c, 1 - t)
    greet([at_device(peer(d), c, t) for d in range(1, ep)] + [core])
    sent = []
    order = list(range(1, ep)) + [0]
    for d in order:
        copy = remote(
            part_ref.at[place(peer(d), 1 - t)], core_in.at[d], core_send.at[d], core_recv.at[d], core
        )
        copy.start()
        sent.append(copy)
    for d in order:
        remote(core_in.at[d], core_in.at[d], core_send.at[d], core_recv.at[d], core).wait_recv()
        added = part_ref[place(peer(d), t), :].astype(jnp.float32) + core_in[d].astype(jnp.float32)
        if d == 0:
            total = added
            continue
        z_out[d - 1] = added.astype(z_out.dtype)
        copy = remote(
            z_out.at[d - 1], z_in.at[d - 1], z_send.at[d - 1], z_recv.at[d - 1], at_device(peer(d), c, t)
        )
        copy.start()
        sent.append(copy)
    for d in range(1, ep):
        remote(z_in.at[d - 1], z_in.at[d - 1], z_send.at[d - 1], z_recv.at[d - 1], core).wait_recv()
        total = total + z_in[d - 1].astype(jnp.float32)
    rows = pl.ds(pl.multiple_of(t * half, 16), half)
    sum_ref[rows, :] = total
    copy = remote(sum_ref.at[rows], sum_ref.at[rows], back_send, back_recv, core)
    copy.start()
    other = sum_ref.at[pl.ds(pl.multiple_of((1 - t) * half, 16), half)]
    remote(other, other, back_send, back_recv, core).wait_recv()
    sent.append(copy)
    for copy in sent:
        copy.wait_send()


def sum_z(part, collective_id):
    ep = lax.axis_size("fsdp")
    tokens = part.shape[0] // ep
    width = part.shape[1]
    dma = pltpu.SemaphoreType.DMA
    vmem = pl.BlockSpec(memory_space=pltpu.VMEM)
    return pl.pallas_call(
        sum_z_kernel,
        out_shape=jax.ShapeDtypeStruct((tokens, width), jnp.float32),
        in_specs=[vmem],
        out_specs=vmem,
        scratch_shapes=[
            pltpu.VMEM((ep, tokens // 2, width), part.dtype),
            pltpu.VMEM((ep - 1, tokens // 2, width), part.dtype),
            pltpu.VMEM((ep - 1, tokens // 2, width), part.dtype),
            dma((ep,)),
            dma((ep,)),
            dma((ep - 1,)),
            dma((ep - 1,)),
            dma,
            dma,
        ],
        compiler_params=pltpu.CompilerParams(
            collective_id=collective_id, has_side_effects=True, vmem_limit_bytes=40 * 1024 * 1024
        ),
        name="sum_z",
    )(part)


def pair_kernel(part_ref, sum_ref, other, send, recv):
    f, c, t = lax.axis_index("fsdp"), lax.axis_index("ctx"), lax.axis_index("tp")
    core = at_device(f, c, 1 - t)
    greet([core])
    copy = remote(part_ref, other, send, recv, core)
    copy.start()
    copy.wait()
    sum_ref[...] = part_ref[...].astype(jnp.float32) + other[...].astype(jnp.float32)


def add_pair(part, collective_id):
    dma = pltpu.SemaphoreType.DMA
    vmem = pl.BlockSpec(memory_space=pltpu.VMEM)
    return pl.pallas_call(
        pair_kernel,
        out_shape=jax.ShapeDtypeStruct(part.shape, jnp.float32),
        in_specs=[vmem],
        out_specs=vmem,
        scratch_shapes=[pltpu.VMEM(part.shape, part.dtype), dma, dma],
        compiler_params=pltpu.CompilerParams(
            collective_id=collective_id, has_side_effects=True, vmem_limit_bytes=32 * 1024 * 1024
        ),
        name="add_pair",
    )(part)


def scatter_kernel(
    part_ref, sum_ref, first_in_x, first_in_y, second_out_x, second_out_y, second_in_x, second_in_y, z_out, z_in,
    first_send, first_recv, second_send, second_recv, z_send, z_recv,
):
    ep = z_send.shape[0] + 1
    f, c, t = lax.axis_index("fsdp"), lax.axis_index("ctx"), lax.axis_index("tp")
    rows, width = sum_ref.shape
    first_in, second_out, second_in = (first_in_x, first_in_y), (second_out_x, second_out_y), (second_in_x, second_in_y)
    cut = first_in_x.shape[-1]
    columns = (pl.ds(0, cut), pl.ds(cut, width - cut))
    low = part_ref.dtype

    def peer(distance):
        return lax.rem(f + distance, ep)

    def block(distance, ctx, way):
        start = pl.multiple_of((peer(distance) * 4 + ctx) * rows, 16)
        return pl.ds(start, rows), columns[way]

    neighbours = (at_device(f, c ^ 1, t), at_device(f, c ^ 2, t))
    greet([at_device(peer(d), c, t) for d in range(1, ep)] + list(neighbours))
    sent = []
    order = list(range(1, ep)) + [0]
    for d in order:
        for number in range(2):
            for way in range(2):
                target = c ^ 3 if number == 0 else c ^ (1 << way)
                copy = remote(
                    part_ref.at[block(d, target, way)], first_in[way].at[d, number],
                    first_send.at[way, d, number], first_recv.at[way, d, number], neighbours[way],
                )
                copy.start()
                sent.append(copy)
    for d in order:
        for way in range(2):
            for number in range(2):
                landing = first_in[way].at[d, number]
                remote(
                    landing, landing, first_send.at[way, d, number], first_recv.at[way, d, number], neighbours[way]
                ).wait_recv()
                if number == 0:
                    own = part_ref[block(d, c ^ (2 >> way), way)]
                    second_out[way][d] = (
                        own.astype(jnp.float32) + first_in[way][d, 0].astype(jnp.float32)
                    ).astype(low)
                    copy = remote(
                        second_out[way].at[d], second_in[way].at[d],
                        second_send.at[way, d], second_recv.at[way, d], neighbours[1 - way],
                    )
                    copy.start()
                    sent.append(copy)
    for d in order:
        for way in range(2):
            landing = second_in[way].at[d]
            remote(
                landing, landing, second_send.at[way, d], second_recv.at[way, d], neighbours[1 - way]
            ).wait_recv()
            total = (
                part_ref[block(d, c, way)].astype(jnp.float32)
                + first_in[way][d, 1].astype(jnp.float32)
                + second_in[way][d].astype(jnp.float32)
            )
            if d == 0:
                sum_ref[:, columns[way]] = total
            else:
                z_out[d - 1, :, columns[way]] = total.astype(low)
        if d > 0:
            copy = remote(
                z_out.at[d - 1], z_in.at[d - 1], z_send.at[d - 1], z_recv.at[d - 1], at_device(peer(d), c, t)
            )
            copy.start()
            sent.append(copy)
    for d in range(1, ep):
        remote(z_in.at[d - 1], z_in.at[d - 1], z_send.at[d - 1], z_recv.at[d - 1], neighbours[0]).wait_recv()
        sum_ref[...] += z_in[d - 1].astype(jnp.float32)
    for copy in sent:
        copy.wait_send()


def scatter_sums(part, collective_id):
    ep = lax.axis_size("fsdp")
    rows = part.shape[0] // (ep * lax.axis_size("ctx"))
    width = part.shape[1]
    low = part.dtype
    cut = -(-width // 256) * 128
    dma = pltpu.SemaphoreType.DMA
    vmem = pl.BlockSpec(memory_space=pltpu.VMEM)
    return pl.pallas_call(
        scatter_kernel,
        out_shape=jax.ShapeDtypeStruct((rows, width), jnp.float32),
        in_specs=[vmem],
        out_specs=vmem,
        scratch_shapes=[
            pltpu.VMEM((ep, 2, rows, cut), low),
            pltpu.VMEM((ep, 2, rows, width - cut), low),
            pltpu.VMEM((ep, rows, cut), low),
            pltpu.VMEM((ep, rows, width - cut), low),
            pltpu.VMEM((ep, rows, cut), low),
            pltpu.VMEM((ep, rows, width - cut), low),
            pltpu.VMEM((ep - 1, rows, width), low),
            pltpu.VMEM((ep - 1, rows, width), low),
            dma((2, ep, 2)),
            dma((2, ep, 2)),
            dma((2, ep)),
            dma((2, ep)),
            dma((ep - 1,)),
            dma((ep - 1,)),
        ],
        compiler_params=pltpu.CompilerParams(
            collective_id=collective_id, has_side_effects=True, vmem_limit_bytes=48 * 1024 * 1024
        ),
        name="scatter_sums",
    )(part)


def shards(
    layer_input,
    segments,
    routes,
    norm_gain,
    query_weight,
    key_weight,
    value_weight,
    output_weight,
    ffn_gain,
    router_weight,
    gate_weight,
    up_weight,
    down_weight,
    cotangent,
):
    low = jnp.bfloat16
    both = ("fsdp", "ctx")
    ep = lax.axis_size("fsdp")
    tokens = layer_input.shape[0]
    seq_len = segments.shape[1]
    rows = query_weight.shape[0]
    width = query_weight.shape[1]
    kv_width = key_weight.shape[1]
    hidden_width = gate_weight.shape[2]
    local = EXPERTS // ep
    span = local * hidden_width

    qkv_width = width + 2 * kv_width
    extra = jnp.concatenate([router_weight, norm_gain[:, None], ffn_gain[:, None]], 1)
    extra = jnp.pad(extra, ((0, 0), (0, 128 - extra.shape[1])))
    attn_shard = jnp.concatenate([query_weight, key_weight, value_weight, extra, output_weight.T], 1)
    down_shard = down_weight.transpose(0, 2, 1)
    routes_all = lax.all_gather(routes, "fsdp", axis=0, tiled=True)
    if lax.axis_size("ctx") == 4:
        attn_full, expert_full, outer_all = gather_all(
            attn_shard, gate_weight, up_weight, down_shard, cotangent
        )
    else:
        attn_full = lax.all_gather(attn_shard, both, axis=0, tiled=True)
        packed = jnp.concatenate([gate_weight, up_weight, down_shard], -1)
        expert_full = spread_experts(packed)
        expert_full = expert_full.reshape(D, local, 3, hidden_width).transpose(0, 2, 1, 3)
        expert_full = expert_full.reshape(D, 3 * span)
        outer_all = lax.all_gather(cotangent, "fsdp", axis=0, tiled=True)
    qkv_full = attn_full[:, :qkv_width]
    router_full = attn_full[:, qkv_width : qkv_width + EXPERTS]
    gain_one = attn_full[:, qkv_width + EXPERTS]
    gain_two = attn_full[:, qkv_width + EXPERTS + 1]
    output_turned = attn_full[:, qkv_width + 128 :]
    gate_up = expert_full[:, : 2 * span]
    down_turned = expert_full[:, 2 * span :]

    begin = lax.axis_index("ctx") * tokens
    segment_row = segments[0]
    place = lax.dynamic_slice_in_dim(document_place(segment_row), begin, tokens)
    query_doc = lax.dynamic_slice_in_dim(segment_row, begin, tokens)
    query_order = begin + jnp.arange(tokens, dtype=jnp.int32)
    scale = HD ** (-0.5)
    inputs = layer_input.astype(jnp.float32)
    first_norm, first_inverse = normalize(inputs, gain_one)
    normed1 = first_norm.astype(low)
    projected = jnp.dot(normed1, qkv_full, preferred_element_type=jnp.float32)
    query = rotate(projected[:, :width], place, 1.0).astype(low)
    key = rotate(projected[:, width : width + kv_width], place, 1.0).astype(low)
    value = projected[:, width + kv_width :].astype(low)
    key_groups = kv_width // HD
    groups = width // kv_width
    grouped = query.reshape(tokens, key_groups, groups, HD)
    pair_all = lax.all_gather(jnp.concatenate([key, value], 1), "ctx", axis=0, tiled=True)
    key_all = pair_all[:, :kv_width]
    value_all = pair_all[:, kv_width:]

    def block_scores(key_piece, offset):
        count = key_piece.shape[0]
        key_heads = key_piece.reshape(count, key_groups, HD)
        scores = (
            jnp.einsum("qkgd,nkd->qkgn", grouped, key_heads, preferred_element_type=jnp.float32)
            * scale
        )
        key_doc = lax.dynamic_slice_in_dim(segment_row, offset, count)
        key_order = offset + jnp.arange(count, dtype=jnp.int32)
        seen = (key_doc[None, :] == query_doc[:, None]) & (
            key_order[None, :] <= query_order[:, None]
        )
        return (scores, seen[:, None, None, :], key_heads)

    def masked_away(offset, count):
        last_doc = lax.dynamic_index_in_dim(segment_row, offset + count - 1, keepdims=False)
        return (offset > query_order[tokens - 1]) | (last_doc < query_doc[0])

    scores, seen, key_heads = block_scores(key_all, jnp.int32(0))
    scores = jnp.where(seen, scores, MASKED_SCORE)
    running = jnp.max(scores, -1)
    weights = jnp.where(seen, jnp.exp(scores - running[..., None]), 0.0)
    summed = jnp.einsum(
        "qkgn,nkd->qkgd",
        weights.astype(low),
        value_all.reshape(seq_len, key_groups, HD),
        preferred_element_type=jnp.float32,
    )
    totals = jnp.sum(weights, -1)
    mixed = summed / totals[..., None]
    log_total = running + jnp.log(totals)
    mixed_low = mixed.reshape(tokens, -1).astype(low)
    attention = add_pair(times_transpose(mixed_low, output_turned).astype(low), 3)
    middle = inputs + attention
    second_norm, second_inverse = normalize(middle, gain_two)
    normed2 = second_norm.astype(low)

    normed2_all = along_z(normed2)
    logits_all = jnp.dot(normed2_all, router_full, preferred_element_type=jnp.float32)
    expert_ids = jnp.arange(EXPERTS, dtype=jnp.int32)
    chosen_all = jnp.any(routes_all[:, :, None] == expert_ids[None, None, :], 1)
    masked_logits = jnp.where(chosen_all, logits_all, MASKED_SCORE)
    top = jnp.max(masked_logits, -1, keepdims=True)
    lifted = jnp.where(chosen_all, jnp.exp(masked_logits - top), 0.0)
    gates_all = lifted / jnp.sum(lifted, -1, keepdims=True)
    place_z = lax.axis_index("fsdp")
    gates_here = lax.dynamic_slice_in_dim(gates_all, place_z * local, local, 1)
    chosen_here = lax.dynamic_slice_in_dim(chosen_all, place_z * local, local, 1)
    chosen = lax.dynamic_slice_in_dim(chosen_all, place_z * tokens, tokens, 0)
    gates = lax.dynamic_slice_in_dim(gates_all, place_z * tokens, tokens, 0)

    reach = normed2_all.shape[0]
    both_sides = jnp.dot(normed2_all, gate_up, preferred_element_type=jnp.float32)
    former = both_sides[:, :span]
    latter = both_sides[:, span:]
    hidden_grad = jnp.dot(outer_all, down_turned, preferred_element_type=jnp.float32)
    gate_wide = jnp.broadcast_to(gates_here[:, :, None], (reach, local, hidden_width)).reshape(reach, span)
    logistic = jax.nn.sigmoid(former)
    active = former * logistic
    hidden = (active * latter).astype(low).astype(jnp.float32)
    gated = (hidden * gate_wide).astype(low)
    dgates = jnp.sum((hidden * hidden_grad).reshape(reach, local, hidden_width), -1)
    scaled_grad = hidden_grad * gate_wide
    former_grad = (scaled_grad * latter * logistic * (1.0 + former * (1.0 - logistic))).astype(low)
    latter_grad = (scaled_grad * active).astype(low)
    side_grads = jnp.concatenate([former_grad, latter_grad], 1)
    mixture_part = times_transpose(gated, down_turned)
    input_part = times_transpose(side_grads, gate_up)
    side_sums = contract_rows(normed2_all, side_grads)
    down_sums = contract_rows(outer_all, gated)
    dgates = jnp.where(chosen_here, dgates, 0.0)
    dgates_wide = lax.dynamic_update_slice_in_dim(
        jnp.zeros((reach, EXPERTS), jnp.float32), dgates, place_z * local, 1
    )
    dgates_high = dgates_wide.astype(low)
    dgates_rest = (dgates_wide - dgates_high.astype(jnp.float32)).astype(low)
    dgates_sent = jnp.concatenate([dgates_high, dgates_rest], 1)
    dgates_sent = jnp.pad(dgates_sent, ((0, 0), (0, 128 - 2 * EXPERTS)))
    returned = sum_z(jnp.concatenate([input_part.astype(low), dgates_sent], 1), 4)
    mixture = lax.psum_scatter(
        lax.psum(mixture_part.astype(low), "tp"), "fsdp", scatter_dimension=0, tiled=True
    ).astype(jnp.float32)
    layer_output = (middle + mixture).astype(low)
    side_out = collect_experts(side_sums.astype(low), rows).reshape(ep, rows, 2, local, hidden_width)
    side_out = side_out.transpose(2, 0, 3, 1, 4).reshape(2, EXPERTS, rows, hidden_width).astype(jnp.float32)
    down_out = collect_experts(down_sums.astype(low), rows).reshape(ep, rows, local, hidden_width)
    down_out = down_out.transpose(0, 2, 3, 1).reshape(EXPERTS, hidden_width, rows).astype(jnp.float32)

    outer_grad = cotangent.astype(jnp.float32)
    input_grad_part = returned[:, :D]
    picked = returned[:, D : D + EXPERTS] + returned[:, D + EXPERTS : D + 2 * EXPERTS]
    logit_grad = (gates * (picked - jnp.sum(gates * picked, -1, keepdims=True))).astype(low)
    router_sums = contract_rows(normed2, logit_grad)
    second_grad = input_grad_part + times_transpose(logit_grad, router_full)
    middle_back, gain_two_sums = norm_back(second_grad, middle, second_inverse, gain_two)
    middle_grad = outer_grad + middle_back
    attention_grad = middle_grad.astype(low)
    output_sums = contract_rows(attention_grad, mixed_low)
    mixed_grad = jnp.dot(attention_grad, output_turned, preferred_element_type=jnp.float32).astype(low)
    mixed_heads = mixed_grad.reshape(tokens, key_groups, groups, HD)
    delta = jnp.sum(mixed_heads.astype(jnp.float32) * mixed, -1)

    def back_two(number, state):
        offset = number * tokens
        key_piece = lax.dynamic_slice_in_dim(key_all, offset, tokens, 0)
        value_piece = lax.dynamic_slice_in_dim(value_all, offset, tokens, 0)

        def back_compute(inner):
            query_sum, pair_sum = inner
            scores, seen, key_heads = block_scores(key_piece, offset)
            probs = jnp.where(seen, jnp.exp(scores - log_total[..., None]), 0.0)
            value_heads = value_piece.reshape(tokens, key_groups, HD)
            prob_grad = jnp.einsum(
                "qkgd,nkd->qkgn", mixed_heads, value_heads, preferred_element_type=jnp.float32
            )
            score_grad = (probs * (prob_grad - delta[..., None])).astype(low)
            query_sum = (
                query_sum
                + jnp.einsum(
                    "qkgn,nkd->qkgd", score_grad, key_heads, preferred_element_type=jnp.float32
                )
                * scale
            )
            key_block = (
                jnp.einsum(
                    "qkgn,qkgd->nkd", score_grad, grouped, preferred_element_type=jnp.float32
                )
                * scale
            )
            value_block = jnp.einsum(
                "qkgn,qkgd->nkd", probs.astype(low), mixed_heads, preferred_element_type=jnp.float32
            )
            pair = jnp.concatenate([key_block.reshape(tokens, -1), value_block.reshape(tokens, -1)], 1)
            return (query_sum, lax.dynamic_update_slice_in_dim(pair_sum, pair, offset, 0))

        return lax.cond(masked_away(offset, tokens), lambda inner: inner, back_compute, state)

    back_state = (
        jnp.zeros((tokens, key_groups, groups, HD), jnp.float32),
        jnp.zeros((seq_len, 2 * kv_width), jnp.float32),
    )
    query_sum, pair_sum = lax.fori_loop(0, seq_len // tokens, back_two, back_state)
    pair_local = lax.psum_scatter(
        pair_sum.astype(low), "ctx", scatter_dimension=0, tiled=True
    ).astype(jnp.float32)
    query_back = rotate(query_sum.reshape(tokens, -1), place, -1.0)
    key_back = rotate(pair_local[:, :kv_width], place, -1.0)
    qkv_back = jnp.concatenate([query_back, key_back, pair_local[:, kv_width:]], 1).astype(low)
    qkv_sums = contract_rows(normed1, qkv_back)
    first_part = times_transpose(qkv_back, qkv_full)
    first_grad = add_pair(first_part.astype(low), 5)
    input_back, gain_one_sums = norm_back(first_grad, inputs, first_inverse, gain_one)
    input_grad = middle_grad + input_back
    small_sums = jnp.concatenate([router_sums, gain_one_sums[:, None], gain_two_sums[:, None]], 1)
    small_sums = jnp.pad(small_sums, ((0, 0), (0, 128 - small_sums.shape[1])))
    attn_sums = jnp.concatenate([qkv_sums.astype(low), small_sums.astype(low), output_sums.astype(low)], 1)
    if lax.axis_size("ctx") == 4:
        attn_out = scatter_sums(attn_sums, 6)
    else:
        attn_out = lax.psum_scatter(attn_sums, both, scatter_dimension=0, tiled=True).astype(jnp.float32)
    small_out = attn_out[:, qkv_width : qkv_width + 128]
    return (
        layer_output,
        input_grad,
        small_out[:, EXPERTS],
        attn_out[:, :width],
        attn_out[:, width : width + kv_width],
        attn_out[:, width + kv_width : qkv_width],
        attn_out[:, qkv_width + 128 :].T,
        small_out[:, EXPERTS + 1],
        small_out[:, :EXPERTS],
        side_out[0],
        side_out[1],
        down_out,
    )


def solution(mesh):
    in_specs = (
        P(("fsdp", "ctx"), None),
        P("fsdp", None),
        P(("fsdp", "ctx"), None),
        P(("fsdp", "ctx")),
        P(("fsdp", "ctx"), "tp"),
        P(("fsdp", "ctx"), "tp"),
        P(("fsdp", "ctx"), "tp"),
        P("tp", ("fsdp", "ctx")),
        P(("fsdp", "ctx")),
        P(("fsdp", "ctx"), None),
        P(None, ("fsdp", "ctx"), "tp"),
        P(None, ("fsdp", "ctx"), "tp"),
        P(None, "tp", ("fsdp", "ctx")),
        P(("fsdp", "ctx"), None),
    )
    out_specs = (
        P(("fsdp", "ctx"), None),
        P(("fsdp", "ctx"), None),
        P(("fsdp", "ctx")),
        P(("fsdp", "ctx"), "tp"),
        P(("fsdp", "ctx"), "tp"),
        P(("fsdp", "ctx"), "tp"),
        P("tp", ("fsdp", "ctx")),
        P(("fsdp", "ctx")),
        P(("fsdp", "ctx"), None),
        P(None, ("fsdp", "ctx"), "tp"),
        P(None, ("fsdp", "ctx"), "tp"),
        P(None, "tp", ("fsdp", "ctx")),
    )
    return jax.shard_map(shards, mesh=mesh, in_specs=in_specs, out_specs=out_specs, check_vma=False)
```

```python
import jax
import jax.numpy as jnp
from jax import lax
from jax.experimental import pallas as pl
from jax.experimental.pallas import tpu as pltpu
from jax.sharding import PartitionSpec as P

MESH = pl.DeviceIdType.MESH

D = 1536
HD = 64
EXPERTS = 16


EPSILON = 1e-05
MASKED_SCORE = -1e30


def rotate(values, cosine, sine):
    rows = values.shape[0]
    shaped = values.reshape(rows, -1, HD)
    half = HD // 2
    cosine, sine = cosine[:, None, :], sine[:, None, :]
    former = shaped[..., :half]
    latter = shaped[..., half:]
    turned = jnp.concatenate([former * cosine - latter * sine, latter * cosine + former * sine], -1)
    return turned.reshape(rows, -1)


def normalize(values, gain):
    inverse = lax.rsqrt(jnp.mean(values * values, -1, keepdims=True) + EPSILON)
    return (values * inverse * gain.astype(jnp.float32), inverse)


def norm_back(grad, values, inverse, gain):
    scaled = grad * gain.astype(jnp.float32)
    gain_grad = jnp.sum(grad * values * inverse, 0)
    mean_term = jnp.mean(scaled * values, -1, keepdims=True)
    return (inverse * scaled - values * inverse**3 * mean_term, gain_grad)


def document_place(segment_row):
    length = segment_row.shape[0]
    order = jnp.arange(length, dtype=jnp.int32)
    fresh = jnp.concatenate([jnp.ones((1,), jnp.bool_), segment_row[1:] != segment_row[:-1]])
    starts = lax.cummax(jnp.where(fresh, order, 0), axis=0)
    return order - starts


def contract_rows(left, right):
    return lax.dot_general(
        left, right, (((0,), (0,)), ((), ())), preferred_element_type=jnp.float32
    )


def times_transpose(left, right):
    return lax.dot_general(
        left, right, (((1,), (1,)), ((), ())), preferred_element_type=jnp.float32
    )


def spread_experts(packed):
    ep = lax.axis_size("fsdp")
    local = packed.shape[0] // ep
    rows = packed.shape[1]
    swapped = lax.all_to_all(packed, "fsdp", 0, 0, tiled=True)
    swapped = swapped.reshape(ep, local, rows, -1).transpose(0, 2, 1, 3)
    swapped = swapped.reshape(ep, rows, -1)
    whole = lax.all_gather(swapped, "ctx", axis=1)
    return whole.reshape(ep * lax.axis_size("ctx") * rows, -1)


def collect_experts(sums, rows):
    ep, ring = lax.axis_size("fsdp"), lax.axis_size("ctx")
    turned = sums.reshape(ep, ring, rows, -1).transpose(1, 0, 2, 3).reshape(sums.shape)
    mine = lax.psum_scatter(turned, "ctx", scatter_dimension=0, tiled=True)
    return lax.all_to_all(mine, "fsdp", 0, 0, tiled=True)


def at_device(fsdp, ctx, tp):
    return {"fsdp": fsdp, "ctx": ctx, "tp": tp}


def greet(partners):
    barrier = pltpu.get_barrier_semaphore()
    for device in partners:
        pl.semaphore_signal(barrier, inc=1, device_id=device, device_id_type=MESH)
    pl.semaphore_wait(barrier, len(partners))


def remote(source, target, send, recv, device):
    return pltpu.make_async_remote_copy(
        src_ref=source, dst_ref=target, send_sem=send, recv_sem=recv, device_id=device, device_id_type=MESH
    )


def lasting(us):
    return pl.CostEstimate(flops=0, bytes_accessed=us * 3690000, transcendentals=0)


def front_kernel(
    attn_ref, gate_ref, up_ref, down_ref, outer_ref, routes_ref, input_ref, segment_ref, freq_ref,
    expert_out, outer_out, routes_out, normed2_out,
    attn_out, normed1_out, query_out, pair_out, mixed_out, log_out, middle_out, cos_out, sin_out,
    query_s, key_s, value_s, mixed_s, bias_s, part_s, other_s, normed2_s,
    local_sem, z_send, z_recv, plane_send, plane_recv, relay_send, relay_recv, core_send, core_recv,
    key_send, key_recv, pair_send, pair_recv,
):
    ep = z_send.shape[1] + 1
    f, c, t = lax.axis_index("fsdp"), lax.axis_index("ctx"), lax.axis_index("tp")
    low = jnp.bfloat16
    rows = attn_ref.shape[0]
    local = gate_ref.shape[0] // ep
    hidden = gate_ref.shape[2]
    tokens = outer_ref.shape[0]
    half = tokens // 2
    heads = query_s.shape[0]
    key_heads = key_s.shape[0]
    width, kv_width = heads * HD, key_heads * HD
    qkv_width = width + 2 * kv_width
    outs = (attn_out, expert_out)
    cuts = [(out.shape[1] // 256) * 128 for out in outs]

    def peer(distance):
        return lax.rem(f + distance, ep)

    def shard_rows(fsdp, ctx):
        return pl.ds(pl.multiple_of((fsdp * 4 + ctx) * rows, 16), rows)

    def columns(kind, side):
        cut, full = cuts[kind], outs[kind].shape[1]
        return pl.ds(0, cut) if side == 0 else pl.ds(cut, full - cut)

    line = [at_device(peer(d), c, t) for d in range(1, ep)]
    plane = [at_device(f, c ^ k, t) for k in range(1, 4)]
    x_device, y_device = plane[0], plane[1]
    core = at_device(f, c, 1 - t)
    greet(line + plane + [core])

    mine = shard_rows(f, c)
    sent = []

    def send(copy):
        copy.start()
        sent.append(copy)

    def z_arrival(kind, d):
        place = shard_rows(peer(ep - d), c)
        remote(
            outs[kind].at[place], outs[kind].at[place], z_send.at[kind, d - 1], z_recv.at[kind, d - 1], x_device
        ).wait_recv()

    def spread(kind, d):
        place = shard_rows(peer(ep - d), c)
        for step in range(2):
            for way, device in enumerate((x_device, y_device)):
                side = step ^ way
                block = outs[kind].at[place, columns(kind, side)]
                send(
                    remote(
                        block, block, plane_send.at[kind, d, way, side], plane_recv.at[kind, d, way, side], device
                    )
                )

    def pass_on(kind, d):
        for way, device in enumerate((y_device, x_device)):
            place = shard_rows(peer(ep - d), c ^ (1 << way))
            block = outs[kind].at[place, columns(kind, way)]
            remote(
                block, block, plane_send.at[kind, d, way, way], plane_recv.at[kind, d, way, way], device
            ).wait_recv()
            send(remote(block, block, relay_send.at[kind, d, way], relay_recv.at[kind, d, way], device))

    def settle(kind):
        for d in range(ep):
            back = peer(ep - d)
            for way, device in enumerate((x_device, y_device)):
                side = 1 - way
                block = outs[kind].at[shard_rows(back, c ^ (1 << way)), columns(kind, side)]
                remote(
                    block, block, plane_send.at[kind, d, way, side], plane_recv.at[kind, d, way, side], device
                ).wait_recv()
                block = outs[kind].at[shard_rows(back, c ^ 3), columns(kind, way)]
                remote(
                    block, block, relay_send.at[kind, d, way], relay_recv.at[kind, d, way], device
                ).wait_recv()

    def line_place(fsdp, part):
        return pl.ds(pl.multiple_of(fsdp * tokens + part * half, 16), half)

    own_tokens = pl.ds(pl.multiple_of(f * tokens, 16), tokens)
    my_half = pl.ds(pl.multiple_of(t * half, 16), half)

    def line_send(kind, source, target):
        for d in range(1, ep):
            send(
                remote(
                    source, target.at[line_place(f, t)], z_send.at[kind, d - 1], z_recv.at[kind, d - 1], line[d - 1]
                )
            )

    def line_forward(kind, target):
        for d in range(1, ep):
            block = target.at[line_place(peer(ep - d), t)]
            remote(block, block, z_send.at[kind, d - 1], z_recv.at[kind, d - 1], core).wait_recv()
            send(remote(block, block, core_send.at[kind - 2, d - 1], core_recv.at[kind - 2, d - 1], core))

    def line_settle(kind, target):
        for d in range(1, ep):
            block = target.at[line_place(peer(ep - d), 1 - t)]
            remote(block, block, core_send.at[kind - 2, d - 1], core_recv.at[kind - 2, d - 1], core).wait_recv()

    for d in range(1, ep):
        send(remote(attn_ref, attn_out.at[mine], z_send.at[0, d - 1], z_recv.at[0, d - 1], line[d - 1]))
    own_attn = pltpu.make_async_copy(attn_ref, attn_out.at[mine], local_sem.at[0])
    own_attn.start()
    own_outer = pltpu.make_async_copy(outer_ref, outer_out.at[own_tokens], local_sem.at[2])
    own_outer.start()
    own_routes = pltpu.make_async_copy(routes_ref, routes_out.at[own_tokens], local_sem.at[3])
    own_routes.start()
    for d in range(1, ep):
        send(
            remote(
                routes_ref, routes_out.at[own_tokens], z_send.at[4, d - 1], z_recv.at[4, d - 1], line[d - 1]
            )
        )
    for kind, ref in enumerate((gate_ref, up_ref, down_ref)):
        for e in range(local):
            target = expert_out.at[mine, pl.ds((kind * local + e) * hidden, hidden)]
            pltpu.make_async_copy(ref.at[f * local + e], target, local_sem.at[1]).start()
    own_attn.wait()
    spread(0, 0)

    length = segment_ref.shape[1]
    seg_keys = segment_ref[...].astype(jnp.float32)
    seg_here = segment_ref[:, pl.ds(pl.multiple_of(c * tokens, 128), tokens)].astype(jnp.float32)
    seg_queries = jnp.broadcast_to(seg_here, (128, tokens)).T[:, :1]
    key_order = lax.broadcasted_iota(jnp.int32, (tokens, length), 1)
    query_order = lax.broadcasted_iota(jnp.int32, (tokens, length), 0) + c * tokens
    same = seg_keys == seg_queries
    seen = same & (key_order <= query_order)
    bias_s[...] = jnp.where(seen, 0.0, MASKED_SCORE)
    place = jnp.sum(jnp.where(same & (key_order < query_order), 1.0, 0.0), -1, keepdims=True)
    angle = place * freq_ref[...]
    lane = lax.broadcasted_iota(jnp.int32, (tokens, 128), 1)
    first_half = lax.rem(lane, HD) < HD // 2
    cosine = jnp.cos(angle)
    sine = jnp.where(first_half, -jnp.sin(angle), jnp.sin(angle))
    cos_out[...] = cosine
    sin_out[...] = sine
    inputs = input_ref[...].astype(jnp.float32)
    inverse = lax.rsqrt(jnp.mean(inputs * inputs, -1, keepdims=True) + EPSILON)

    for d in range(1, ep):
        z_arrival(0, d)
        spread(0, d)
        pass_on(0, d - 1)
    for d in range(1, ep):
        for kind, ref in enumerate((gate_ref, up_ref, down_ref)):
            for e in range(local):
                target = expert_out.at[mine, pl.ds((kind * local + e) * hidden, hidden)]
                remote(
                    ref.at[peer(d) * local + e], target, z_send.at[1, d - 1], z_recv.at[1, d - 1], line[d - 1]
                ).start()
    pass_on(0, ep - 1)
    settle(0)

    gains = attn_out[:, qkv_width : qkv_width + 128].astype(jnp.float32).T
    normed1_out[...] = (inputs * inverse * gains[EXPERTS : EXPERTS + 1, :]).astype(low)

    def project(start):
        return jnp.dot(
            normed1_out[...], attn_out[:, start : start + 256], preferred_element_type=jnp.float32
        )

    def turned(tile):
        swapped = jnp.where(first_half, pltpu.roll(tile, 128 - HD // 2, 1), pltpu.roll(tile, HD // 2, 1))
        return tile * cos_out[...] + swapped * sin_out[...]

    here = pl.ds(pl.multiple_of(c * tokens, 16), tokens)
    for start in range(0, kv_width, 256):
        tile = project(width + start)
        for side in (0, 128):
            pair_out[here, start + side : start + side + 128] = turned(tile[:, side : side + 128]).astype(low)
    for start in range(0, kv_width, 256):
        pair_out[here, kv_width + start : kv_width + start + 256] = project(width + kv_width + start).astype(low)
    for k in (3, 1, 2):
        send(remote(pair_out.at[here], pair_out.at[here], key_send.at[k - 1], key_recv.at[k - 1], plane[k - 1]))
    for start in range(0, width, 256):
        tile = project(start)
        for side in (0, 128):
            query_out[:, start + side : start + side + 128] = turned(tile[:, side : side + 128]).astype(low)
    for h in range(heads):
        query_s[h] = query_out[:, h * HD : (h + 1) * HD]
    pltpu.make_async_copy(expert_out.at[mine], expert_out.at[mine], local_sem.at[1]).wait()
    for k in range(1, 4):
        block = pair_out.at[pl.ds(pl.multiple_of((c ^ k) * tokens, 16), tokens)]
        remote(block, block, key_send.at[k - 1], key_recv.at[k - 1], plane[k - 1]).wait_recv()
    spread(1, 0)
    for g in range(key_heads):
        key_s[g] = pair_out[:, g * HD : (g + 1) * HD]
        value_s[g] = pair_out[:, kv_width + g * HD : kv_width + (g + 1) * HD]
    pass_on(1, 0)

    def attend(h, carry):
        g = lax.div(h, heads // key_heads)
        query = query_s[h] * jnp.asarray(HD**-0.5, low)
        scores = lax.dot_general(
            query, key_s[g], (((1,), (1,)), ((), ())), preferred_element_type=jnp.float32
        ) + bias_s[...]
        top = jnp.max(scores, -1, keepdims=True)
        weights = jnp.exp(scores - top)
        total = jnp.sum(weights, -1, keepdims=True)
        summed = jnp.dot(weights.astype(low), value_s[g], preferred_element_type=jnp.float32)
        mixed_s[h] = (summed / total).astype(low)
        log_out[h] = top + jnp.log(total)
        return carry

    lax.fori_loop(0, heads, attend, 0)
    for h in range(heads):
        mixed_out[:, h * HD : (h + 1) * HD] = mixed_s[h]
    z_arrival(1, 1)
    spread(1, 1)
    line_send(2, outer_ref.at[my_half], outer_out)

    model = input_ref.shape[1]
    for start in range(0, model, 256):
        part_s[:, start : start + 256] = lax.dot_general(
            mixed_out[...], attn_out[start : start + 256, qkv_width + 128 :],
            (((1,), (1,)), ((), ())), preferred_element_type=jnp.float32,
        ).astype(low)
    exchange = remote(part_s, other_s, pair_send, pair_recv, core)
    send(exchange)
    for d in range(2, ep):
        z_arrival(1, d)
        spread(1, d)
        pass_on(1, d - 1)
    exchange.wait_recv()
    middle = input_ref[...].astype(jnp.float32) + (
        part_s[...].astype(jnp.float32) + other_s[...].astype(jnp.float32)
    )
    middle_out[...] = middle
    inverse = lax.rsqrt(jnp.mean(middle * middle, -1, keepdims=True) + EPSILON)
    gains = attn_out[:, qkv_width : qkv_width + 128].astype(jnp.float32).T
    normed2_s[...] = (middle * inverse * gains[EXPERTS + 1 : EXPERTS + 2, :]).astype(low)
    line_send(3, normed2_s.at[my_half], normed2_out)
    own_normed2 = pltpu.make_async_copy(normed2_s, normed2_out.at[own_tokens], local_sem.at[4])
    own_normed2.start()
    pass_on(1, ep - 1)
    line_forward(2, outer_out)
    line_forward(3, normed2_out)
    settle(1)
    line_settle(2, outer_out)
    line_settle(3, normed2_out)
    for d in range(1, ep):
        place = pl.ds(pl.multiple_of(peer(ep - d) * tokens, 16), tokens)
        remote(
            routes_out.at[place], routes_out.at[place], z_send.at[4, d - 1], z_recv.at[4, d - 1], core
        ).wait_recv()
        remote(
            expert_out.at[mine], expert_out.at[mine], z_send.at[1, d - 1], z_recv.at[1, d - 1], core
        ).wait_send()
    own_outer.wait()
    own_routes.wait()
    own_normed2.wait()
    for copy in sent:
        copy.wait_send()


def front(attn, gate, up, down, outer, routes, inputs, segments, freq, heads, key_heads):
    ep = lax.axis_size("fsdp")
    rows = attn.shape[0]
    total = rows * ep * lax.axis_size("ctx")
    local = gate.shape[0] // ep
    tokens, model = inputs.shape
    length = segments.shape[1]
    low = jnp.bfloat16
    dma = pltpu.SemaphoreType.DMA
    anywhere = pl.BlockSpec(memory_space=pl.ANY)
    vmem = pl.BlockSpec(memory_space=pltpu.VMEM)
    shape = jax.ShapeDtypeStruct
    return pl.pallas_call(
        front_kernel,
        out_shape=(
            shape((total, 3 * local * gate.shape[2]), low),
            shape((ep * tokens, model), low),
            shape((ep * tokens, routes.shape[1]), routes.dtype),
            shape((ep * tokens, model), low),
            shape((total, attn.shape[1]), low),
            shape((tokens, model), low),
            shape((tokens, heads * HD), low),
            shape((length, 2 * key_heads * HD), low),
            shape((tokens, heads * HD), low),
            shape((heads, tokens, 1), jnp.float32),
            shape((tokens, model), jnp.float32),
            shape((tokens, 128), jnp.float32),
            shape((tokens, 128), jnp.float32),
        ),
        in_specs=[anywhere] * 6 + [vmem] * 3,
        out_specs=(anywhere,) * 4 + (vmem,) * 9,
        scratch_shapes=[
            pltpu.VMEM((heads, tokens, HD), low),
            pltpu.VMEM((key_heads, length, HD), low),
            pltpu.VMEM((key_heads, length, HD), low),
            pltpu.VMEM((heads, tokens, HD), low),
            pltpu.VMEM((tokens, length), jnp.float32),
            pltpu.VMEM((tokens, model), low),
            pltpu.VMEM((tokens, model), low),
            pltpu.VMEM((tokens, model), low),
            dma((5,)),
            dma((5, ep - 1)),
            dma((5, ep - 1)),
            dma((2, ep, 2, 2)),
            dma((2, ep, 2, 2)),
            dma((2, ep, 2)),
            dma((2, ep, 2)),
            dma((2, ep - 1)),
            dma((2, ep - 1)),
            dma((3,)),
            dma((3,)),
            dma,
            dma,
        ],
        compiler_params=pltpu.CompilerParams(
            collective_id=1, has_side_effects=True, vmem_limit_bytes=56 * 1024 * 1024
        ),
        cost_estimate=lasting(180),
        name="front",
    )(attn, gate, up, down, outer, routes, inputs, segments, freq)


def z_sum_scratch(ep, tokens, width, low):
    dma = pltpu.SemaphoreType.DMA
    return [
        pltpu.VMEM((ep, tokens // 2, width), low),
        pltpu.VMEM((ep - 1, tokens // 2, width), low),
        pltpu.VMEM((ep - 1, tokens // 2, width), low),
        dma((ep,)),
        dma((ep,)),
        dma((ep - 1,)),
        dma((ep - 1,)),
        dma,
        dma,
    ]


class ZSum:
    size = 9

    def __init__(self, part, out, scratch, sent):
        self.part, self.out, self.sent = part, out, sent
        (
            self.core_in, self.z_out, self.z_in, self.core_send, self.core_recv,
            self.z_send, self.z_recv, self.back_send, self.back_recv,
        ) = scratch
        self.ep = self.core_in.shape[0]
        self.f, self.c, self.t = lax.axis_index("fsdp"), lax.axis_index("ctx"), lax.axis_index("tp")
        self.half = out.shape[0] // 2
        self.core = at_device(self.f, self.c, 1 - self.t)

    def peer(self, distance):
        return lax.rem(self.f + distance, self.ep)

    def place(self, fsdp, part):
        return pl.ds(pl.multiple_of(fsdp * 2 * self.half + part * self.half, 16), self.half)

    def send(self, copy):
        copy.start()
        self.sent.append(copy)

    def to_core(self):
        for d in list(range(1, self.ep)) + [0]:
            self.send(
                remote(
                    self.part.at[self.place(self.peer(d), 1 - self.t)], self.core_in.at[d],
                    self.core_send.at[d], self.core_recv.at[d], self.core,
                )
            )

    def added(self, d):
        landing = self.core_in.at[d]
        remote(landing, landing, self.core_send.at[d], self.core_recv.at[d], self.core).wait_recv()
        mine = self.part[self.place(self.peer(d), self.t), :]
        return mine.astype(jnp.float32) + self.core_in[d].astype(jnp.float32)

    def to_z(self):
        for d in range(1, self.ep):
            self.z_out[d - 1] = self.added(d).astype(self.z_out.dtype)
            self.send(
                remote(
                    self.z_out.at[d - 1], self.z_in.at[d - 1], self.z_send.at[d - 1], self.z_recv.at[d - 1],
                    at_device(self.peer(d), self.c, self.t),
                )
            )

    def from_z(self):
        rows = pl.ds(pl.multiple_of(self.t * self.half, 16), self.half)
        self.out[rows, :] = self.added(0)
        for d in range(1, self.ep):
            landing = self.z_in.at[d - 1]
            remote(landing, landing, self.z_send.at[d - 1], self.z_recv.at[d - 1], self.core).wait_recv()
            self.out[rows, :] += self.z_in[d - 1].astype(jnp.float32)
        mine = self.out.at[rows]
        self.send(remote(mine, mine, self.back_send, self.back_recv, self.core))

    def finish(self):
        other = self.out.at[pl.ds(pl.multiple_of((1 - self.t) * self.half, 16), self.half)]
        remote(other, other, self.back_send, self.back_recv, self.core).wait_recv()


def plane_sum_scratch(ep, rows, width, low):
    cut = -(-width // 256) * 128
    dma = pltpu.SemaphoreType.DMA
    return [
        pltpu.VMEM((ep, 2, rows, cut), low),
        pltpu.VMEM((ep, 2, rows, width - cut), low),
        pltpu.VMEM((ep, rows, cut), low),
        pltpu.VMEM((ep, rows, width - cut), low),
        pltpu.VMEM((ep, rows, cut), low),
        pltpu.VMEM((ep, rows, width - cut), low),
        dma((2, ep, 2)),
        dma((2, ep, 2)),
        dma((2, ep)),
        dma((2, ep)),
    ]


class PlaneSum:
    size = 10

    def __init__(self, part, rows, scratch, sent):
        self.part, self.rows, self.sent = part, rows, sent
        self.first_in, self.second_out, self.second_in = scratch[0:2], scratch[2:4], scratch[4:6]
        self.first_send, self.first_recv, self.second_send, self.second_recv = scratch[6:10]
        self.ep = self.first_in[0].shape[0]
        self.f, self.c, self.t = lax.axis_index("fsdp"), lax.axis_index("ctx"), lax.axis_index("tp")
        cut = self.first_in[0].shape[-1]
        self.columns = (pl.ds(0, cut), pl.ds(cut, part.shape[1] - cut))
        self.neighbours = (at_device(self.f, self.c ^ 1, self.t), at_device(self.f, self.c ^ 2, self.t))
        self.order = list(range(1, self.ep)) + [0]

    def block(self, distance, ctx, way):
        start = (lax.rem(self.f + distance, self.ep) * 4 + ctx) * self.rows
        return pl.ds(pl.multiple_of(start, 16), self.rows), self.columns[way]

    def send(self, copy):
        copy.start()
        self.sent.append(copy)

    def first(self):
        for d in self.order:
            for number in range(2):
                for way in range(2):
                    target = self.c ^ 3 if number == 0 else self.c ^ (1 << way)
                    self.send(
                        remote(
                            self.part.at[self.block(d, target, way)], self.first_in[way].at[d, number],
                            self.first_send.at[way, d, number], self.first_recv.at[way, d, number],
                            self.neighbours[way],
                        )
                    )

    def second(self):
        for d in self.order:
            for way in range(2):
                for number in range(2):
                    landing = self.first_in[way].at[d, number]
                    remote(
                        landing, landing, self.first_send.at[way, d, number],
                        self.first_recv.at[way, d, number], self.neighbours[way],
                    ).wait_recv()
                own = self.part[self.block(d, self.c ^ (2 >> way), way)]
                added = own.astype(jnp.float32) + self.first_in[way][d, 0].astype(jnp.float32)
                self.second_out[way][d] = added.astype(self.part.dtype)
                self.send(
                    remote(
                        self.second_out[way].at[d], self.second_in[way].at[d],
                        self.second_send.at[way, d], self.second_recv.at[way, d], self.neighbours[1 - way],
                    )
                )

    def total(self, d, way):
        landing = self.second_in[way].at[d]
        remote(
            landing, landing, self.second_send.at[way, d], self.second_recv.at[way, d], self.neighbours[1 - way]
        ).wait_recv()
        return (
            self.part[self.block(d, self.c, way)].astype(jnp.float32)
            + self.first_in[way][d, 1].astype(jnp.float32)
            + self.second_in[way][d].astype(jnp.float32)
        )


def all_partners(ep):
    f, c, t = lax.axis_index("fsdp"), lax.axis_index("ctx"), lax.axis_index("tp")
    line = [at_device(lax.rem(f + d, ep), c, t) for d in range(1, ep)]
    return line + [at_device(f, c ^ 1, t), at_device(f, c ^ 2, t), at_device(f, c, 1 - t)]


def back_kernel(part_ref, down_ref, sum_ref, down_out, *scratch):
    ep, rows = down_out.shape[0], down_out.shape[1]
    sent = []
    tokens = ZSum(part_ref, sum_ref, scratch[: ZSum.size], sent)
    plane = PlaneSum(down_ref, rows, scratch[ZSum.size :], sent)
    greet(all_partners(ep))
    tokens.to_core()
    plane.first()
    tokens.to_z()
    plane.second()
    tokens.from_z()
    for d in plane.order:
        for way in range(2):
            down_out[plane_row(d, ep), :, plane.columns[way]] = plane.total(d, way).astype(down_out.dtype)
    tokens.finish()
    for copy in sent:
        copy.wait_send()


def plane_row(distance, ep):
    return lax.rem(lax.axis_index("fsdp") + distance, ep)


def sum_back(part, down, collective_id):
    ep = lax.axis_size("fsdp")
    rows = down.shape[0] // (4 * ep)
    tokens, width = part.shape[0] // ep, part.shape[1]
    vmem = pl.BlockSpec(memory_space=pltpu.VMEM)
    return pl.pallas_call(
        back_kernel,
        out_shape=(
            jax.ShapeDtypeStruct((tokens, width), jnp.float32),
            jax.ShapeDtypeStruct((ep, rows, down.shape[1]), down.dtype),
        ),
        in_specs=[vmem] * 2,
        out_specs=(vmem,) * 2,
        scratch_shapes=z_sum_scratch(ep, tokens, width, part.dtype)
        + plane_sum_scratch(ep, rows, down.shape[1], down.dtype),
        compiler_params=pltpu.CompilerParams(
            collective_id=collective_id, has_side_effects=True, vmem_limit_bytes=48 * 1024 * 1024
        ),
        cost_estimate=lasting(45),
        name="sum_back",
    )(part, down)


def keys_kernel(part_ref, down_ref, sum_ref, down_out, landing, send, recv, z_send, z_recv):
    ep = down_ref.shape[0]
    f, c, t = lax.axis_index("fsdp"), lax.axis_index("ctx"), lax.axis_index("tp")
    tokens = sum_ref.shape[0]

    def peer(distance):
        return lax.rem(f + distance, ep)

    plane = [at_device(f, c ^ k, t) for k in range(1, 4)]
    greet([at_device(peer(d), c, t) for d in range(1, ep)] + plane)
    sent = []
    for k in (3, 1, 2):
        place = pl.ds(pl.multiple_of((c ^ k) * tokens, 16), tokens)
        copy = remote(part_ref.at[place], landing.at[k - 1], send.at[k - 1], recv.at[k - 1], plane[k - 1])
        copy.start()
        sent.append(copy)
    for d in range(1, ep):
        copy = remote(
            down_ref.at[peer(d)], down_out.at[f], z_send.at[d - 1], z_recv.at[d - 1], at_device(peer(d), c, t)
        )
        copy.start()
        sent.append(copy)
    down_out[f] = down_ref[f]
    sum_ref[...] = part_ref[pl.ds(pl.multiple_of(c * tokens, 16), tokens), :].astype(jnp.float32)
    for k in (1, 2, 3):
        block = landing.at[k - 1]
        remote(block, block, send.at[k - 1], recv.at[k - 1], plane[k - 1]).wait_recv()
        sum_ref[...] += landing[k - 1].astype(jnp.float32)
    for d in range(1, ep):
        block = down_out.at[peer(ep - d)]
        remote(block, block, z_send.at[d - 1], z_recv.at[d - 1], plane[0]).wait_recv()
    for copy in sent:
        copy.wait_send()


def sum_keys(part, down, collective_id):
    ep = lax.axis_size("fsdp")
    tokens, width = part.shape[0] // 4, part.shape[1]
    dma = pltpu.SemaphoreType.DMA
    vmem = pl.BlockSpec(memory_space=pltpu.VMEM)
    return pl.pallas_call(
        keys_kernel,
        out_shape=(
            jax.ShapeDtypeStruct((tokens, width), jnp.float32),
            jax.ShapeDtypeStruct(down.shape, down.dtype),
        ),
        in_specs=[vmem] * 2,
        out_specs=(vmem,) * 2,
        scratch_shapes=[
            pltpu.VMEM((3, tokens, width), part.dtype), dma((3,)), dma((3,)), dma((ep - 1,)), dma((ep - 1,))
        ],
        compiler_params=pltpu.CompilerParams(
            collective_id=collective_id, has_side_effects=True, vmem_limit_bytes=32 * 1024 * 1024
        ),
        cost_estimate=lasting(20),
        name="sum_keys",
    )(part, down)


def pair_kernel(part_ref, sum_ref, other, send, recv):
    f, c, t = lax.axis_index("fsdp"), lax.axis_index("ctx"), lax.axis_index("tp")
    core = at_device(f, c, 1 - t)
    greet([core])
    copy = remote(part_ref, other, send, recv, core)
    copy.start()
    copy.wait()
    sum_ref[...] = part_ref[...].astype(jnp.float32) + other[...].astype(jnp.float32)


def add_pair(part, collective_id):
    dma = pltpu.SemaphoreType.DMA
    vmem = pl.BlockSpec(memory_space=pltpu.VMEM)
    return pl.pallas_call(
        pair_kernel,
        out_shape=jax.ShapeDtypeStruct(part.shape, jnp.float32),
        in_specs=[vmem],
        out_specs=vmem,
        scratch_shapes=[pltpu.VMEM(part.shape, part.dtype), dma, dma],
        compiler_params=pltpu.CompilerParams(
            collective_id=collective_id, has_side_effects=True, vmem_limit_bytes=32 * 1024 * 1024
        ),
        cost_estimate=lasting(5),
        name="add_pair",
    )(part)


def last_kernel(part_ref, mixture_ref, sum_ref, mixed_ref, *scratch):
    ep = lax.axis_size("fsdp")
    rows = sum_ref.shape[0]
    sent = []
    tokens = ZSum(mixture_ref, mixed_ref, scratch[: ZSum.size], sent)
    plane = PlaneSum(part_ref, rows, scratch[ZSum.size : ZSum.size + PlaneSum.size], sent)
    z_out, z_in, z_send, z_recv = scratch[ZSum.size + PlaneSum.size :]
    partners = all_partners(ep)
    greet(partners)
    plane.first()
    tokens.to_core()
    tokens.to_z()
    plane.second()
    for d in plane.order:
        for way in range(2):
            total = plane.total(d, way)
            if d == 0:
                sum_ref[:, plane.columns[way]] = total
            else:
                z_out[d - 1, :, plane.columns[way]] = total.astype(z_out.dtype)
        if d > 0:
            copy = remote(z_out.at[d - 1], z_in.at[d - 1], z_send.at[d - 1], z_recv.at[d - 1], partners[d - 1])
            copy.start()
            sent.append(copy)
    tokens.from_z()
    for d in range(1, ep):
        landing = z_in.at[d - 1]
        remote(landing, landing, z_send.at[d - 1], z_recv.at[d - 1], partners[d - 1]).wait_recv()
        sum_ref[...] += z_in[d - 1].astype(jnp.float32)
    tokens.finish()
    for copy in sent:
        copy.wait_send()


def sum_last(part, mixture, collective_id):
    ep = lax.axis_size("fsdp")
    rows = part.shape[0] // (4 * ep)
    width, low = part.shape[1], part.dtype
    tokens = mixture.shape[0] // ep
    dma = pltpu.SemaphoreType.DMA
    vmem = pl.BlockSpec(memory_space=pltpu.VMEM)
    return pl.pallas_call(
        last_kernel,
        out_shape=(
            jax.ShapeDtypeStruct((rows, width), jnp.float32),
            jax.ShapeDtypeStruct((tokens, mixture.shape[1]), jnp.float32),
        ),
        in_specs=[vmem] * 2,
        out_specs=(vmem,) * 2,
        scratch_shapes=z_sum_scratch(ep, tokens, mixture.shape[1], low)
        + plane_sum_scratch(ep, rows, width, low)
        + [
            pltpu.VMEM((ep - 1, rows, width), low),
            pltpu.VMEM((ep - 1, rows, width), low),
            dma((ep - 1,)),
            dma((ep - 1,)),
        ],
        compiler_params=pltpu.CompilerParams(
            collective_id=collective_id, has_side_effects=True, vmem_limit_bytes=48 * 1024 * 1024
        ),
        cost_estimate=lasting(75),
        name="sum_last",
    )(part, mixture)


def shards(
    layer_input,
    segments,
    routes,
    norm_gain,
    query_weight,
    key_weight,
    value_weight,
    output_weight,
    ffn_gain,
    router_weight,
    gate_weight,
    up_weight,
    down_weight,
    cotangent,
):
    low = jnp.bfloat16
    both = ("fsdp", "ctx")
    ep = lax.axis_size("fsdp")
    tokens = layer_input.shape[0]
    seq_len = segments.shape[1]
    rows = query_weight.shape[0]
    width = query_weight.shape[1]
    kv_width = key_weight.shape[1]
    hidden_width = gate_weight.shape[2]
    local = EXPERTS // ep
    span = local * hidden_width

    qkv_width = width + 2 * kv_width
    extra = jnp.concatenate([router_weight, norm_gain[:, None], ffn_gain[:, None]], 1)
    extra = jnp.pad(extra, ((0, 0), (0, 128 - extra.shape[1])))
    attn_shard = jnp.concatenate([query_weight, key_weight, value_weight, extra, output_weight.T], 1)
    down_shard = down_weight.transpose(0, 2, 1)
    begin = lax.axis_index("ctx") * tokens
    segment_row = segments[0]
    query_doc = lax.dynamic_slice_in_dim(segment_row, begin, tokens)
    query_order = begin + jnp.arange(tokens, dtype=jnp.int32)
    scale = HD ** (-0.5)
    inputs = layer_input.astype(jnp.float32)
    key_groups = kv_width // HD
    groups = width // kv_width
    freq = 10000.0 ** (-2.0 * jnp.arange(HD // 2, dtype=jnp.float32) / HD)

    def unpack(attn_full):
        return (
            attn_full[:, :qkv_width],
            attn_full[:, qkv_width : qkv_width + EXPERTS],
            attn_full[:, qkv_width + EXPERTS],
            attn_full[:, qkv_width + EXPERTS + 1],
            attn_full[:, qkv_width + 128 :],
        )

    if lax.axis_size("ctx") == 4:
        (
            expert_full, outer_all, routes_all, normed2_all,
            attn_full, normed1, query, pair_all, mixed_low, log_total, middle, cosine, sine,
        ) = front(
            attn_shard, gate_weight, up_weight, down_shard, cotangent, routes, layer_input, segments,
            jnp.tile(freq, 4)[None, :], width // HD, key_groups,
        )
        qkv_full, router_full, gain_one, gain_two, output_turned = unpack(attn_full)
        log_total = log_total[:, :, 0].T.reshape(tokens, key_groups, groups)
        cosine, sine = cosine[:, : HD // 2], sine[:, HD // 2 : HD]
        first_inverse = lax.rsqrt(jnp.mean(inputs * inputs, -1, keepdims=True) + EPSILON)
        second_inverse = lax.rsqrt(jnp.mean(middle * middle, -1, keepdims=True) + EPSILON)
        normed2 = lax.dynamic_slice_in_dim(normed2_all, lax.axis_index("fsdp") * tokens, tokens)
    else:
        attn_full = lax.all_gather(attn_shard, both, axis=0, tiled=True)
        qkv_full, router_full, gain_one, gain_two, output_turned = unpack(attn_full)
        packed = jnp.concatenate([gate_weight, up_weight, down_shard], -1)
        expert_full = spread_experts(packed)
        expert_full = expert_full.reshape(D, local, 3, hidden_width).transpose(0, 2, 1, 3)
        expert_full = expert_full.reshape(D, 3 * span)
        outer_all = lax.all_gather(cotangent, "fsdp", axis=0, tiled=True)
        routes_all = lax.all_gather(routes, "fsdp", axis=0, tiled=True)
        place = lax.dynamic_slice_in_dim(document_place(segment_row), begin, tokens)
        angle = place.astype(jnp.float32)[:, None] * freq[None, :]
        cosine, sine = jnp.cos(angle), jnp.sin(angle)
        first_norm, first_inverse = normalize(inputs, gain_one)
        normed1 = first_norm.astype(low)
        projected = jnp.dot(normed1, qkv_full, preferred_element_type=jnp.float32)
        query = rotate(projected[:, :width], cosine, sine).astype(low)
        key = rotate(projected[:, width : width + kv_width], cosine, sine).astype(low)
        value = projected[:, width + kv_width :].astype(low)
        pair_all = lax.all_gather(jnp.concatenate([key, value], 1), "ctx", axis=0, tiled=True)
        heads = query.reshape(tokens, key_groups, groups, HD)
        key_heads = pair_all[:, :kv_width].reshape(seq_len, key_groups, HD)
        value_heads = pair_all[:, kv_width:].reshape(seq_len, key_groups, HD)
        scores = jnp.einsum("qkgd,nkd->qkgn", heads, key_heads, preferred_element_type=jnp.float32) * scale
        seen = (segment_row[None, :] == query_doc[:, None]) & (
            jnp.arange(seq_len, dtype=jnp.int32)[None, :] <= query_order[:, None]
        )
        scores = jnp.where(seen[:, None, None, :], scores, MASKED_SCORE)
        running = jnp.max(scores, -1)
        weights = jnp.exp(scores - running[..., None])
        summed = jnp.einsum(
            "qkgn,nkd->qkgd", weights.astype(low), value_heads, preferred_element_type=jnp.float32
        )
        totals = jnp.sum(weights, -1)
        log_total = running + jnp.log(totals)
        mixed_low = (summed / totals[..., None]).reshape(tokens, -1).astype(low)
        attention = add_pair(times_transpose(mixed_low, output_turned).astype(low), 3)
        middle = inputs + attention
        second_norm, second_inverse = normalize(middle, gain_two)
        normed2 = second_norm.astype(low)
        normed2_all = lax.all_gather(normed2, "fsdp", axis=0, tiled=True)
    gate_up = expert_full[:, : 2 * span]
    down_turned = expert_full[:, 2 * span :]
    key_all = pair_all[:, :kv_width]
    value_all = pair_all[:, kv_width:]
    grouped = query.reshape(tokens, key_groups, groups, HD)

    def block_scores(key_piece, offset):
        count = key_piece.shape[0]
        key_heads = key_piece.reshape(count, key_groups, HD)
        scores = (
            jnp.einsum("qkgd,nkd->qkgn", grouped, key_heads, preferred_element_type=jnp.float32)
            * scale
        )
        key_doc = lax.dynamic_slice_in_dim(segment_row, offset, count)
        key_order = offset + jnp.arange(count, dtype=jnp.int32)
        seen = (key_doc[None, :] == query_doc[:, None]) & (
            key_order[None, :] <= query_order[:, None]
        )
        return (scores, seen[:, None, None, :], key_heads)

    def masked_away(offset, count):
        last_doc = lax.dynamic_index_in_dim(segment_row, offset + count - 1, keepdims=False)
        return (offset > query_order[tokens - 1]) | (last_doc < query_doc[0])

    logits_all = jnp.dot(normed2_all, router_full, preferred_element_type=jnp.float32)
    expert_ids = jnp.arange(EXPERTS, dtype=jnp.int32)
    chosen_all = jnp.any(routes_all[:, :, None] == expert_ids[None, None, :], 1)
    masked_logits = jnp.where(chosen_all, logits_all, MASKED_SCORE)
    top = jnp.max(masked_logits, -1, keepdims=True)
    lifted = jnp.where(chosen_all, jnp.exp(masked_logits - top), 0.0)
    gates_all = lifted / jnp.sum(lifted, -1, keepdims=True)
    place_z = lax.axis_index("fsdp")
    gates_here = lax.dynamic_slice_in_dim(gates_all, place_z * local, local, 1)
    chosen_here = lax.dynamic_slice_in_dim(chosen_all, place_z * local, local, 1)
    chosen = lax.dynamic_slice_in_dim(chosen_all, place_z * tokens, tokens, 0)
    gates = lax.dynamic_slice_in_dim(gates_all, place_z * tokens, tokens, 0)

    reach = normed2_all.shape[0]
    both_sides = jnp.dot(normed2_all, gate_up, preferred_element_type=jnp.float32)
    former = both_sides[:, :span]
    latter = both_sides[:, span:]
    hidden_grad = jnp.dot(outer_all, down_turned, preferred_element_type=jnp.float32)
    gate_wide = jnp.concatenate(
        [jnp.broadcast_to(gates_here[:, e : e + 1], (reach, hidden_width)) for e in range(local)], 1
    )
    logistic = jax.nn.sigmoid(former)
    active = former * logistic
    hidden = (active * latter).astype(low).astype(jnp.float32)
    gated = (hidden * gate_wide).astype(low)
    parts = [slice(e * hidden_width, (e + 1) * hidden_width) for e in range(local)]
    dgates = jnp.stack([jnp.sum(hidden[:, part] * hidden_grad[:, part], -1) for part in parts], 1)
    scaled_grad = hidden_grad * gate_wide
    former_grad = (scaled_grad * latter * logistic * (1.0 + former * (1.0 - logistic))).astype(low)
    latter_grad = (scaled_grad * active).astype(low)
    side_grads = jnp.concatenate([former_grad, latter_grad], 1)
    mixture_part = times_transpose(gated, down_turned)
    input_part = times_transpose(side_grads, gate_up)
    side_sums = contract_rows(normed2_all, side_grads)
    down_sums = contract_rows(outer_all, gated)
    dgates = jnp.where(chosen_here, dgates, 0.0)
    dgates_wide = lax.dynamic_update_slice_in_dim(
        jnp.zeros((reach, EXPERTS), jnp.float32), dgates, place_z * local, 1
    )
    dgates_high = dgates_wide.astype(low)
    dgates_rest = (dgates_wide - dgates_high.astype(jnp.float32)).astype(low)
    dgates_sent = jnp.concatenate([dgates_high, dgates_rest], 1)
    dgates_sent = jnp.pad(dgates_sent, ((0, 0), (0, 128 - 2 * EXPERTS)))
    back_part = jnp.concatenate([input_part.astype(low), dgates_sent], 1)
    if lax.axis_size("ctx") == 4:
        returned, down_mine = sum_back(back_part, down_sums.astype(low), 4)
    else:
        returned = lax.psum_scatter(
            lax.psum(back_part, "tp"), "fsdp", scatter_dimension=0, tiled=True
        ).astype(jnp.float32)
    side_out = collect_experts(side_sums.astype(low), rows).reshape(ep, rows, 2, local, hidden_width)
    side_out = side_out.transpose(2, 0, 3, 1, 4).reshape(2, EXPERTS, rows, hidden_width).astype(jnp.float32)

    outer_grad = cotangent.astype(jnp.float32)
    input_grad_part = returned[:, :D]
    picked = returned[:, D : D + EXPERTS] + returned[:, D + EXPERTS : D + 2 * EXPERTS]
    logit_grad = (gates * (picked - jnp.sum(gates * picked, -1, keepdims=True))).astype(low)
    router_sums = contract_rows(normed2, logit_grad)
    second_grad = input_grad_part + times_transpose(logit_grad, router_full)
    middle_back, gain_two_sums = norm_back(second_grad, middle, second_inverse, gain_two)
    middle_grad = outer_grad + middle_back
    attention_grad = middle_grad.astype(low)
    output_sums = contract_rows(attention_grad, mixed_low)
    mixed_grad = jnp.dot(attention_grad, output_turned, preferred_element_type=jnp.float32).astype(low)
    mixed_heads = mixed_grad.reshape(tokens, key_groups, groups, HD)
    delta = jnp.sum(mixed_heads.astype(jnp.float32) * mixed_low.reshape(mixed_heads.shape), -1)

    def back_two(number, state):
        offset = number * tokens
        key_piece = lax.dynamic_slice_in_dim(key_all, offset, tokens, 0)
        value_piece = lax.dynamic_slice_in_dim(value_all, offset, tokens, 0)

        def back_compute(inner):
            query_sum, pair_sum = inner
            scores, seen, key_heads = block_scores(key_piece, offset)
            probs = jnp.where(seen, jnp.exp(scores - log_total[..., None]), 0.0)
            value_heads = value_piece.reshape(tokens, key_groups, HD)
            prob_grad = jnp.einsum(
                "qkgd,nkd->qkgn", mixed_heads, value_heads, preferred_element_type=jnp.float32
            )
            score_grad = (probs * (prob_grad - delta[..., None])).astype(low)
            query_sum = (
                query_sum
                + jnp.einsum(
                    "qkgn,nkd->qkgd", score_grad, key_heads, preferred_element_type=jnp.float32
                )
                * scale
            )
            key_block = (
                jnp.einsum(
                    "qkgn,qkgd->nkd", score_grad, grouped, preferred_element_type=jnp.float32
                )
                * scale
            )
            value_block = jnp.einsum(
                "qkgn,qkgd->nkd", probs.astype(low), mixed_heads, preferred_element_type=jnp.float32
            )
            pair = jnp.concatenate([key_block.reshape(tokens, -1), value_block.reshape(tokens, -1)], 1)
            return (query_sum, lax.dynamic_update_slice_in_dim(pair_sum, pair, offset, 0))

        return lax.cond(masked_away(offset, tokens), lambda inner: inner, back_compute, state)

    back_state = (
        jnp.zeros((tokens, key_groups, groups, HD), jnp.float32),
        jnp.zeros((seq_len, 2 * kv_width), jnp.float32),
    )
    query_sum, pair_sum = lax.fori_loop(0, seq_len // tokens, back_two, back_state)
    if lax.axis_size("ctx") == 4:
        pair_local, down_out = sum_keys(pair_sum.astype(low), down_mine, 7)
    else:
        pair_local = lax.psum_scatter(
            pair_sum.astype(low), "ctx", scatter_dimension=0, tiled=True
        ).astype(jnp.float32)
        down_out = collect_experts(down_sums.astype(low), rows)
    down_out = down_out.reshape(ep, rows, local, hidden_width)
    down_out = down_out.transpose(0, 2, 3, 1).reshape(EXPERTS, hidden_width, rows).astype(jnp.float32)
    query_back = rotate(query_sum.reshape(tokens, -1), cosine, -sine)
    key_back = rotate(pair_local[:, :kv_width], cosine, -sine)
    qkv_back = jnp.concatenate([query_back, key_back, pair_local[:, kv_width:]], 1).astype(low)
    qkv_sums = contract_rows(normed1, qkv_back)
    first_part = times_transpose(qkv_back, qkv_full)
    first_grad = add_pair(first_part.astype(low), 5)
    input_back, gain_one_sums = norm_back(first_grad, inputs, first_inverse, gain_one)
    input_grad = middle_grad + input_back
    small_sums = jnp.concatenate([router_sums, gain_one_sums[:, None], gain_two_sums[:, None]], 1)
    small_sums = jnp.pad(small_sums, ((0, 0), (0, 128 - small_sums.shape[1])))
    attn_sums = jnp.concatenate([qkv_sums.astype(low), small_sums.astype(low), output_sums.astype(low)], 1)
    mixture_low = mixture_part.astype(low)
    if lax.axis_size("ctx") == 4:
        attn_out, mixture = sum_last(attn_sums, mixture_low, 6)
    else:
        attn_out = lax.psum_scatter(attn_sums, both, scatter_dimension=0, tiled=True).astype(jnp.float32)
        mixture = lax.psum_scatter(
            lax.psum(mixture_low, "tp"), "fsdp", scatter_dimension=0, tiled=True
        ).astype(jnp.float32)
    layer_output = (middle + mixture).astype(low)
    small_out = attn_out[:, qkv_width : qkv_width + 128]
    return (
        layer_output,
        input_grad,
        small_out[:, EXPERTS],
        attn_out[:, :width],
        attn_out[:, width : width + kv_width],
        attn_out[:, width + kv_width : qkv_width],
        attn_out[:, qkv_width + 128 :].T,
        small_out[:, EXPERTS + 1],
        small_out[:, :EXPERTS],
        side_out[0],
        side_out[1],
        down_out,
    )


def solution(mesh):
    in_specs = (
        P(("fsdp", "ctx"), None),
        P("fsdp", None),
        P(("fsdp", "ctx"), None),
        P(("fsdp", "ctx")),
        P(("fsdp", "ctx"), "tp"),
        P(("fsdp", "ctx"), "tp"),
        P(("fsdp", "ctx"), "tp"),
        P("tp", ("fsdp", "ctx")),
        P(("fsdp", "ctx")),
        P(("fsdp", "ctx"), None),
        P(None, ("fsdp", "ctx"), "tp"),
        P(None, ("fsdp", "ctx"), "tp"),
        P(None, "tp", ("fsdp", "ctx")),
        P(("fsdp", "ctx"), None),
    )
    out_specs = (
        P(("fsdp", "ctx"), None),
        P(("fsdp", "ctx"), None),
        P(("fsdp", "ctx")),
        P(("fsdp", "ctx"), "tp"),
        P(("fsdp", "ctx"), "tp"),
        P(("fsdp", "ctx"), "tp"),
        P("tp", ("fsdp", "ctx")),
        P(("fsdp", "ctx")),
        P(("fsdp", "ctx"), None),
        P(None, ("fsdp", "ctx"), "tp"),
        P(None, ("fsdp", "ctx"), "tp"),
        P(None, "tp", ("fsdp", "ctx")),
    )
    return jax.shard_map(shards, mesh=mesh, in_specs=in_specs, out_specs=out_specs, check_vma=False)
```

```python
import jax
import jax.numpy as jnp
from jax import lax
from jax.experimental import pallas as pl
from jax.experimental.pallas import tpu as pltpu
from jax.sharding import PartitionSpec as P

MESH = pl.DeviceIdType.MESH

D = 1536
HD = 64
EXPERTS = 16


EPSILON = 1e-05
MASKED_SCORE = -1e30


def rotate(values, cosine, sine):
    rows = values.shape[0]
    shaped = values.reshape(rows, -1, HD)
    half = HD // 2
    cosine, sine = cosine[:, None, :], sine[:, None, :]
    former = shaped[..., :half]
    latter = shaped[..., half:]
    turned = jnp.concatenate([former * cosine - latter * sine, latter * cosine + former * sine], -1)
    return turned.reshape(rows, -1)


def normalize(values, gain):
    inverse = lax.rsqrt(jnp.mean(values * values, -1, keepdims=True) + EPSILON)
    return (values * inverse * gain.astype(jnp.float32), inverse)


def norm_back(grad, values, inverse, gain):
    scaled = grad * gain.astype(jnp.float32)
    gain_grad = jnp.sum(grad * values * inverse, 0)
    mean_term = jnp.mean(scaled * values, -1, keepdims=True)
    return (inverse * scaled - values * inverse**3 * mean_term, gain_grad)


def document_place(segment_row):
    length = segment_row.shape[0]
    order = jnp.arange(length, dtype=jnp.int32)
    fresh = jnp.concatenate([jnp.ones((1,), jnp.bool_), segment_row[1:] != segment_row[:-1]])
    starts = lax.cummax(jnp.where(fresh, order, 0), axis=0)
    return order - starts


def contract_rows(left, right):
    return lax.dot_general(
        left, right, (((0,), (0,)), ((), ())), preferred_element_type=jnp.float32
    )


def times_transpose(left, right):
    return lax.dot_general(
        left, right, (((1,), (1,)), ((), ())), preferred_element_type=jnp.float32
    )


def spread_experts(packed):
    ep = lax.axis_size("fsdp")
    local = packed.shape[0] // ep
    rows = packed.shape[1]
    swapped = lax.all_to_all(packed, "fsdp", 0, 0, tiled=True)
    swapped = swapped.reshape(ep, local, rows, -1).transpose(0, 2, 1, 3)
    swapped = swapped.reshape(ep, rows, -1)
    whole = lax.all_gather(swapped, "ctx", axis=1)
    return whole.reshape(ep * lax.axis_size("ctx") * rows, -1)


def collect_experts(sums, rows):
    ep, ring = lax.axis_size("fsdp"), lax.axis_size("ctx")
    turned = sums.reshape(ep, ring, rows, -1).transpose(1, 0, 2, 3).reshape(sums.shape)
    mine = lax.psum_scatter(turned, "ctx", scatter_dimension=0, tiled=True)
    return lax.all_to_all(mine, "fsdp", 0, 0, tiled=True)


def at_device(fsdp, ctx, tp):
    return {"fsdp": fsdp, "ctx": ctx, "tp": tp}


def greet(partners):
    barrier = pltpu.get_barrier_semaphore()
    for device in partners:
        pl.semaphore_signal(barrier, inc=1, device_id=device, device_id_type=MESH)
    pl.semaphore_wait(barrier, len(partners))


def remote(source, target, send, recv, device):
    return pltpu.make_async_remote_copy(
        src_ref=source, dst_ref=target, send_sem=send, recv_sem=recv, device_id=device, device_id_type=MESH
    )


def lasting(us):
    return pl.CostEstimate(flops=0, bytes_accessed=us * 3690000, transcendentals=0)


def front_kernel(
    attn_ref, gate_ref, up_ref, down_ref, outer_ref, routes_ref, input_ref, segment_ref, freq_ref,
    expert_out, outer_out, routes_out, normed2_out,
    attn_out, normed1_out, query_out, pair_out, mixed_out, log_out, middle_out, cos_out, sin_out, extra_out,
    query_s, key_s, value_s, mixed_s, bias_s, part_s, other_s, normed2_s,
    local_sem, z_send, z_recv, plane_send, plane_recv, relay_send, relay_recv, core_send, core_recv,
    key_send, key_recv, pair_send, pair_recv,
):
    ep = z_send.shape[1] + 1
    f, c, t = lax.axis_index("fsdp"), lax.axis_index("ctx"), lax.axis_index("tp")
    low = jnp.bfloat16
    rows = attn_ref.shape[0]
    local = gate_ref.shape[0] // ep
    hidden = gate_ref.shape[2]
    tokens = outer_ref.shape[0]
    half = tokens // 2
    heads = query_s.shape[0]
    key_heads = key_s.shape[0]
    width, kv_width = heads * HD, key_heads * HD
    qkv_width = width + 2 * kv_width
    outs = (attn_out, expert_out)
    cuts = [(out.shape[1] // 256) * 128 for out in outs]

    def peer(distance):
        return lax.rem(f + distance, ep)

    def shard_rows(fsdp, ctx):
        return pl.ds(pl.multiple_of((fsdp * 4 + ctx) * rows, 16), rows)

    def columns(kind, side):
        cut, full = cuts[kind], outs[kind].shape[1]
        return pl.ds(0, cut) if side == 0 else pl.ds(cut, full - cut)

    line = [at_device(peer(d), c, t) for d in range(1, ep)]
    plane = [at_device(f, c ^ k, t) for k in range(1, 4)]
    x_device, y_device = plane[0], plane[1]
    core = at_device(f, c, 1 - t)
    greet(line + plane + [core])

    mine = shard_rows(f, c)
    sent = []

    def send(copy):
        copy.start()
        sent.append(copy)

    def z_arrival(kind, d):
        place = shard_rows(peer(ep - d), c)
        remote(
            outs[kind].at[place], outs[kind].at[place], z_send.at[kind, d - 1], z_recv.at[kind, d - 1], x_device
        ).wait_recv()

    def spread(kind, d):
        place = shard_rows(peer(ep - d), c)
        for step in range(2):
            for way, device in enumerate((x_device, y_device)):
                side = step ^ way
                block = outs[kind].at[place, columns(kind, side)]
                send(
                    remote(
                        block, block, plane_send.at[kind, d, way, side], plane_recv.at[kind, d, way, side], device
                    )
                )

    def pass_on(kind, d):
        for way, device in enumerate((y_device, x_device)):
            place = shard_rows(peer(ep - d), c ^ (1 << way))
            block = outs[kind].at[place, columns(kind, way)]
            remote(
                block, block, plane_send.at[kind, d, way, way], plane_recv.at[kind, d, way, way], device
            ).wait_recv()
            send(remote(block, block, relay_send.at[kind, d, way], relay_recv.at[kind, d, way], device))

    def settle(kind):
        for d in range(ep):
            back = peer(ep - d)
            for way, device in enumerate((x_device, y_device)):
                side = 1 - way
                block = outs[kind].at[shard_rows(back, c ^ (1 << way)), columns(kind, side)]
                remote(
                    block, block, plane_send.at[kind, d, way, side], plane_recv.at[kind, d, way, side], device
                ).wait_recv()
                block = outs[kind].at[shard_rows(back, c ^ 3), columns(kind, way)]
                remote(
                    block, block, relay_send.at[kind, d, way], relay_recv.at[kind, d, way], device
                ).wait_recv()

    def line_place(fsdp, part):
        return pl.ds(pl.multiple_of(fsdp * tokens + part * half, 16), half)

    own_tokens = pl.ds(pl.multiple_of(f * tokens, 16), tokens)
    my_half = pl.ds(pl.multiple_of(t * half, 16), half)

    def line_send(kind, source, target):
        for d in range(1, ep):
            send(
                remote(
                    source, target.at[line_place(f, t)], z_send.at[kind, d - 1], z_recv.at[kind, d - 1], line[d - 1]
                )
            )

    def line_forward(kind, target):
        for d in range(1, ep):
            block = target.at[line_place(peer(ep - d), t)]
            remote(block, block, z_send.at[kind, d - 1], z_recv.at[kind, d - 1], core).wait_recv()
            send(remote(block, block, core_send.at[kind - 2, d - 1], core_recv.at[kind - 2, d - 1], core))

    def line_settle(kind, target):
        for d in range(1, ep):
            block = target.at[line_place(peer(ep - d), 1 - t)]
            remote(block, block, core_send.at[kind - 2, d - 1], core_recv.at[kind - 2, d - 1], core).wait_recv()

    for d in range(1, ep):
        send(remote(attn_ref, attn_out.at[mine], z_send.at[0, d - 1], z_recv.at[0, d - 1], line[d - 1]))
    own_attn = pltpu.make_async_copy(attn_ref, attn_out.at[mine], local_sem.at[0])
    own_attn.start()
    own_outer = pltpu.make_async_copy(outer_ref, outer_out.at[own_tokens], local_sem.at[2])
    own_outer.start()
    own_routes = pltpu.make_async_copy(routes_ref, routes_out.at[own_tokens], local_sem.at[3])
    own_routes.start()
    for d in range(1, ep):
        send(
            remote(
                routes_ref, routes_out.at[own_tokens], z_send.at[4, d - 1], z_recv.at[4, d - 1], line[d - 1]
            )
        )
    for kind, ref in enumerate((gate_ref, up_ref, down_ref)):
        for e in range(local):
            target = expert_out.at[mine, pl.ds((kind * local + e) * hidden, hidden)]
            pltpu.make_async_copy(ref.at[f * local + e], target, local_sem.at[1]).start()
    own_attn.wait()
    spread(0, 0)

    length = segment_ref.shape[1]
    seg_keys = segment_ref[...].astype(jnp.float32)
    seg_here = segment_ref[:, pl.ds(pl.multiple_of(c * tokens, 128), tokens)].astype(jnp.float32)
    seg_queries = jnp.broadcast_to(seg_here, (128, tokens)).T[:, :1]
    key_order = lax.broadcasted_iota(jnp.int32, (tokens, length), 1)
    query_order = lax.broadcasted_iota(jnp.int32, (tokens, length), 0) + c * tokens
    same = seg_keys == seg_queries
    seen = same & (key_order <= query_order)
    bias_s[...] = jnp.where(seen, 0.0, MASKED_SCORE)
    place = jnp.sum(jnp.where(same & (key_order < query_order), 1.0, 0.0), -1, keepdims=True)
    angle = place * freq_ref[...]
    lane = lax.broadcasted_iota(jnp.int32, (tokens, 128), 1)
    first_half = lax.rem(lane, HD) < HD // 2
    cosine = jnp.cos(angle)
    sine = jnp.where(first_half, -jnp.sin(angle), jnp.sin(angle))
    cos_out[...] = cosine
    sin_out[...] = sine
    inputs = input_ref[...].astype(jnp.float32)
    inverse = lax.rsqrt(jnp.mean(inputs * inputs, -1, keepdims=True) + EPSILON)

    for d in range(1, ep):
        z_arrival(0, d)
        spread(0, d)
        pass_on(0, d - 1)
    for d in range(1, ep):
        for kind, ref in enumerate((gate_ref, up_ref, down_ref)):
            for e in range(local):
                target = expert_out.at[mine, pl.ds((kind * local + e) * hidden, hidden)]
                remote(
                    ref.at[peer(d) * local + e], target, z_send.at[1, d - 1], z_recv.at[1, d - 1], line[d - 1]
                ).start()
    pass_on(0, ep - 1)
    settle(0)

    gains = attn_out[:, qkv_width : qkv_width + 128].astype(jnp.float32).T
    normed1_out[...] = (inputs * inverse * gains[EXPERTS : EXPERTS + 1, :]).astype(low)

    def project(start):
        return jnp.dot(
            normed1_out[...], attn_out[:, start : start + 256], preferred_element_type=jnp.float32
        )

    def turned(tile):
        swapped = jnp.where(first_half, pltpu.roll(tile, 128 - HD // 2, 1), pltpu.roll(tile, HD // 2, 1))
        return tile * cos_out[...] + swapped * sin_out[...]

    here = pl.ds(pl.multiple_of(c * tokens, 16), tokens)
    for start in range(0, kv_width, 256):
        tile = project(width + start)
        for side in (0, 128):
            pair_out[here, start + side : start + side + 128] = turned(tile[:, side : side + 128]).astype(low)
    for start in range(0, kv_width, 256):
        pair_out[here, kv_width + start : kv_width + start + 256] = project(width + kv_width + start).astype(low)
    for k in (3, 1, 2):
        send(remote(pair_out.at[here], pair_out.at[here], key_send.at[k - 1], key_recv.at[k - 1], plane[k - 1]))
    for start in range(0, width, 256):
        tile = project(start)
        for side in (0, 128):
            query_out[:, start + side : start + side + 128] = turned(tile[:, side : side + 128]).astype(low)
    for h in range(heads):
        query_s[h] = query_out[:, h * HD : (h + 1) * HD]
    pltpu.make_async_copy(expert_out.at[mine], expert_out.at[mine], local_sem.at[1]).wait()
    for k in range(1, 4):
        block = pair_out.at[pl.ds(pl.multiple_of((c ^ k) * tokens, 16), tokens)]
        remote(block, block, key_send.at[k - 1], key_recv.at[k - 1], plane[k - 1]).wait_recv()
    spread(1, 0)
    for g in range(key_heads):
        key_s[g] = pair_out[:, g * HD : (g + 1) * HD]
        value_s[g] = pair_out[:, kv_width + g * HD : kv_width + (g + 1) * HD]
    pass_on(1, 0)

    def attend(h, carry):
        g = lax.div(h, heads // key_heads)
        query = query_s[h] * jnp.asarray(HD**-0.5, low)
        scores = lax.dot_general(
            query, key_s[g], (((1,), (1,)), ((), ())), preferred_element_type=jnp.float32
        ) + bias_s[...]
        top = jnp.max(scores, -1, keepdims=True)
        weights = jnp.exp(scores - top)
        total = jnp.sum(weights, -1, keepdims=True)
        summed = jnp.dot(weights.astype(low), value_s[g], preferred_element_type=jnp.float32)
        mixed_s[h] = (summed / total).astype(low)
        log_out[h] = jnp.broadcast_to(top + jnp.log(total), (tokens, 128)).T[:1, :]
        return carry

    lax.fori_loop(0, heads, attend, 0)
    for h in range(heads):
        mixed_out[:, h * HD : (h + 1) * HD] = mixed_s[h]
    z_arrival(1, 1)
    spread(1, 1)
    line_send(2, outer_ref.at[my_half], outer_out)

    model = input_ref.shape[1]
    for start in range(0, model, 256):
        part_s[:, start : start + 256] = lax.dot_general(
            mixed_out[...], attn_out[start : start + 256, qkv_width + 128 :],
            (((1,), (1,)), ((), ())), preferred_element_type=jnp.float32,
        ).astype(low)
    exchange = remote(part_s, other_s, pair_send, pair_recv, core)
    send(exchange)
    for d in range(2, ep):
        z_arrival(1, d)
        spread(1, d)
        pass_on(1, d - 1)
    exchange.wait_recv()
    middle = input_ref[...].astype(jnp.float32) + (
        part_s[...].astype(jnp.float32) + other_s[...].astype(jnp.float32)
    )
    middle_out[...] = middle
    inverse = lax.rsqrt(jnp.mean(middle * middle, -1, keepdims=True) + EPSILON)
    gains = attn_out[:, qkv_width : qkv_width + 128].astype(jnp.float32).T
    normed2_s[...] = (middle * inverse * gains[EXPERTS + 1 : EXPERTS + 2, :]).astype(low)
    line_send(3, normed2_s.at[my_half], normed2_out)
    own_normed2 = pltpu.make_async_copy(normed2_s, normed2_out.at[own_tokens], local_sem.at[4])
    own_normed2.start()
    pass_on(1, ep - 1)
    line_forward(2, outer_out)
    line_forward(3, normed2_out)
    settle(1)
    line_settle(2, outer_out)
    line_settle(3, normed2_out)
    for d in range(1, ep):
        place = pl.ds(pl.multiple_of(peer(ep - d) * tokens, 16), tokens)
        remote(
            routes_out.at[place], routes_out.at[place], z_send.at[4, d - 1], z_recv.at[4, d - 1], core
        ).wait_recv()
        remote(
            expert_out.at[mine], expert_out.at[mine], z_send.at[1, d - 1], z_recv.at[1, d - 1], core
        ).wait_send()
    extra_out[...] = attn_out[:, qkv_width : qkv_width + 128]
    own_outer.wait()
    own_routes.wait()
    own_normed2.wait()
    for copy in sent:
        copy.wait_send()


def front(attn, gate, up, down, outer, routes, inputs, segments, freq, heads, key_heads):
    ep = lax.axis_size("fsdp")
    rows = attn.shape[0]
    total = rows * ep * lax.axis_size("ctx")
    local = gate.shape[0] // ep
    tokens, model = inputs.shape
    length = segments.shape[1]
    low = jnp.bfloat16
    dma = pltpu.SemaphoreType.DMA
    anywhere = pl.BlockSpec(memory_space=pl.ANY)
    vmem = pl.BlockSpec(memory_space=pltpu.VMEM)
    shape = jax.ShapeDtypeStruct
    return pl.pallas_call(
        front_kernel,
        out_shape=(
            shape((total, 3 * local * gate.shape[2]), low),
            shape((ep * tokens, model), low),
            shape((ep * tokens, routes.shape[1]), routes.dtype),
            shape((ep * tokens, model), low),
            shape((total, attn.shape[1]), low),
            shape((tokens, model), low),
            shape((tokens, heads * HD), low),
            shape((length, 2 * key_heads * HD), low),
            shape((tokens, heads * HD), low),
            shape((heads, 1, tokens), jnp.float32),
            shape((tokens, model), jnp.float32),
            shape((tokens, 128), jnp.float32),
            shape((tokens, 128), jnp.float32),
            shape((total, 128), low),
        ),
        in_specs=[anywhere] * 6 + [vmem] * 3,
        out_specs=(anywhere,) * 4 + (vmem,) * 10,
        scratch_shapes=[
            pltpu.VMEM((heads, tokens, HD), low),
            pltpu.VMEM((key_heads, length, HD), low),
            pltpu.VMEM((key_heads, length, HD), low),
            pltpu.VMEM((heads, tokens, HD), low),
            pltpu.VMEM((tokens, length), jnp.float32),
            pltpu.VMEM((tokens, model), low),
            pltpu.VMEM((tokens, model), low),
            pltpu.VMEM((tokens, model), low),
            dma((5,)),
            dma((5, ep - 1)),
            dma((5, ep - 1)),
            dma((2, ep, 2, 2)),
            dma((2, ep, 2, 2)),
            dma((2, ep, 2)),
            dma((2, ep, 2)),
            dma((2, ep - 1)),
            dma((2, ep - 1)),
            dma((3,)),
            dma((3,)),
            dma,
            dma,
        ],
        compiler_params=pltpu.CompilerParams(
            collective_id=1, has_side_effects=True, vmem_limit_bytes=56 * 1024 * 1024
        ),
        cost_estimate=lasting(180),
        name="front",
    )(attn, gate, up, down, outer, routes, inputs, segments, freq)


def z_sum_scratch(ep, tokens, width, low):
    dma = pltpu.SemaphoreType.DMA
    return [
        pltpu.VMEM((ep, tokens // 2, width), low),
        pltpu.VMEM((ep - 1, tokens // 2, width), low),
        pltpu.VMEM((ep - 1, tokens // 2, width), low),
        dma((ep,)),
        dma((ep,)),
        dma((ep - 1,)),
        dma((ep - 1,)),
        dma,
        dma,
    ]


class ZSum:
    size = 9

    def __init__(self, part, scratch, sent, own=None):
        self.part, self.own, self.sent = part, own, sent
        (
            self.core_in, self.z_out, self.z_in, self.core_send, self.core_recv,
            self.z_send, self.z_recv, self.back_send, self.back_recv,
        ) = scratch
        self.ep, self.half = self.core_in.shape[0], self.core_in.shape[1]
        self.f, self.c, self.t = lax.axis_index("fsdp"), lax.axis_index("ctx"), lax.axis_index("tp")
        self.core = at_device(self.f, self.c, 1 - self.t)

    def peer(self, distance):
        return lax.rem(self.f + distance, self.ep)

    def place(self, fsdp, part):
        return pl.ds(pl.multiple_of(fsdp * 2 * self.half + part * self.half, 16), self.half)

    def rows(self, part):
        return pl.ds(pl.multiple_of(part * self.half, 16), self.half)

    def send(self, copy):
        copy.start()
        self.sent.append(copy)

    def to_core(self, d):
        self.send(
            remote(
                self.part.at[self.place(self.peer(d), 1 - self.t)], self.core_in.at[d],
                self.core_send.at[d], self.core_recv.at[d], self.core,
            )
        )

    def added(self, d):
        landing = self.core_in.at[d]
        remote(landing, landing, self.core_send.at[d], self.core_recv.at[d], self.core).wait_recv()
        mine = self.part[self.place(self.peer(d), self.t), :] if self.own is None else self.own[d]
        return mine.astype(jnp.float32) + self.core_in[d].astype(jnp.float32)

    def to_z(self, d):
        self.z_out[d - 1] = self.added(d).astype(self.z_out.dtype)
        self.send(
            remote(
                self.z_out.at[d - 1], self.z_in.at[d - 1], self.z_send.at[d - 1], self.z_recv.at[d - 1],
                at_device(self.peer(d), self.c, self.t),
            )
        )

    def collect(self):
        total = self.added(0)
        for d in range(1, self.ep):
            landing = self.z_in.at[d - 1]
            remote(landing, landing, self.z_send.at[d - 1], self.z_recv.at[d - 1], self.core).wait_recv()
            total = total + self.z_in[d - 1].astype(jnp.float32)
        return total

    def share(self, out):
        mine = out.at[self.rows(self.t)]
        self.send(remote(mine, mine, self.back_send, self.back_recv, self.core))

    def finish(self, out):
        other = out.at[self.rows(1 - self.t)]
        remote(other, other, self.back_send, self.back_recv, self.core).wait_recv()


def shard_sum_scratch(ep, rows, width, low, along_z=True):
    cut = first_columns(width)
    widths = [cut] if cut == width else [cut, width - cut]
    dma = pltpu.SemaphoreType.DMA
    scratch = []
    for part in widths:
        scratch += [pltpu.VMEM((ep, 2, rows, part), low), pltpu.VMEM((ep, rows, part), low)]
        if along_z:
            scratch.append(pltpu.VMEM((ep - 1, rows, part), low))
    return scratch + [
        dma((2, ep, 2)), dma((2, ep, 2)), dma((2, ep)), dma((2, ep)), dma((2, ep)), dma((2, ep))
    ]


def first_columns(width):
    return width if width == 128 else -(-width // 256) * 128


class ShardSum:
    def __init__(self, part, rows, width, scratch, sent, own=None, relay=None):
        self.part, self.rows, self.sent, self.own, self.relay = part, rows, sent, own, relay
        cut = first_columns(width)
        self.columns = [pl.ds(0, cut)] + ([] if cut == width else [pl.ds(cut, width - cut)])
        self.ways = range(len(self.columns))
        (
            self.first_send, self.first_recv, self.second_send, self.second_recv, self.z_send, self.z_recv
        ) = scratch[-6:]
        each = (len(scratch) - 6) // len(self.columns)
        self.first_in = [scratch[each * way] for way in self.ways]
        self.second_in = [scratch[each * way + 1] for way in self.ways]
        self.z_in = [scratch[each * way + 2] for way in self.ways] if each == 3 else None
        self.ep = self.first_in[0].shape[0]
        self.f, self.c, self.t = lax.axis_index("fsdp"), lax.axis_index("ctx"), lax.axis_index("tp")
        self.neighbours = (at_device(self.f, self.c ^ 1, self.t), at_device(self.f, self.c ^ 2, self.t))
        self.order = list(range(1, self.ep)) + [0]

    def peer(self, distance):
        return lax.rem(self.f + distance, self.ep)

    def block(self, distance, ctx, way):
        start = (self.peer(distance) * 4 + ctx) * self.rows
        return pl.ds(pl.multiple_of(start, 16), self.rows), self.columns[way]

    def send(self, copy):
        copy.start()
        self.sent.append(copy)

    def load(self, sem):
        for d in range(self.ep):
            for way in self.ways:
                for target, ctx in ((self.own, self.c), (self.relay, self.c ^ (2 >> way))):
                    pltpu.make_async_copy(
                        self.part.at[self.block(d, ctx, way)], target.at[d, :, self.columns[way]], sem
                    ).start()

    def loaded(self, sem):
        for target in (self.own, self.relay):
            pltpu.make_async_copy(target, target, sem).wait()

    def first(self):
        for d in self.order:
            for number in range(2):
                for way in self.ways:
                    target = self.c ^ 3 if number == 0 else self.c ^ (1 << way)
                    self.send(
                        remote(
                            self.part.at[self.block(d, target, way)], self.first_in[way].at[d, number],
                            self.first_send.at[way, d, number], self.first_recv.at[way, d, number],
                            self.neighbours[way],
                        )
                    )

    def second(self, d):
        for way in self.ways:
            for number in range(2):
                landing = self.first_in[way].at[d, number]
                remote(
                    landing, landing, self.first_send.at[way, d, number],
                    self.first_recv.at[way, d, number], self.neighbours[way],
                ).wait_recv()
            if self.relay is None:
                term = self.part[self.block(d, self.c ^ (2 >> way), way)]
            else:
                term = self.relay[d, :, self.columns[way]]
            added = term.astype(jnp.float32) + self.first_in[way][d, 0].astype(jnp.float32)
            self.first_in[way][d, 0] = added.astype(self.part.dtype)
            self.send(
                remote(
                    self.first_in[way].at[d, 0], self.second_in[way].at[d],
                    self.second_send.at[way, d], self.second_recv.at[way, d], self.neighbours[1 - way],
                )
            )

    def total(self, d, way):
        landing = self.second_in[way].at[d]
        remote(
            landing, landing, self.second_send.at[way, d], self.second_recv.at[way, d], self.neighbours[1 - way]
        ).wait_recv()
        term = self.part[self.block(d, self.c, way)] if self.own is None else self.own[d, :, self.columns[way]]
        return (
            term.astype(jnp.float32)
            + self.first_in[way][d, 1].astype(jnp.float32)
            + self.second_in[way][d].astype(jnp.float32)
        )

    def to_z(self, d, out):
        for way in self.ways:
            total = self.total(d, way)
            if d == 0:
                out[:, self.columns[way]] = total
                continue
            self.first_in[way][d, 1] = total.astype(self.part.dtype)
            self.send(
                remote(
                    self.first_in[way].at[d, 1], self.z_in[way].at[d - 1],
                    self.z_send.at[way, d], self.z_recv.at[way, d], at_device(self.peer(d), self.c, self.t),
                )
            )

    def from_z(self, out):
        for way in self.ways:
            for d in range(1, self.ep):
                landing = self.z_in[way].at[d - 1]
                remote(
                    landing, landing, self.z_send.at[way, d], self.z_recv.at[way, d], self.neighbours[0]
                ).wait_recv()
                out[:, self.columns[way]] += self.z_in[way][d - 1].astype(jnp.float32)

    def swap_z(self, d, out):
        for way in self.ways:
            self.first_in[way][d, 1] = self.total(d, way).astype(self.part.dtype)
            source, target = self.first_in[way].at[d, 1], out.at[self.f, :, self.columns[way]]
            if d == 0:
                pltpu.make_async_copy(source, target, self.z_send.at[way, 0]).start()
            else:
                self.send(
                    remote(
                        source, target, self.z_send.at[way, d], self.z_recv.at[way, d],
                        at_device(self.peer(d), self.c, self.t),
                    )
                )

    def swapped_z(self, out):
        for way in self.ways:
            target = out.at[self.f, :, self.columns[way]]
            pltpu.make_async_copy(self.first_in[way].at[0, 1], target, self.z_send.at[way, 0]).wait()
            for d in range(1, self.ep):
                landing = out.at[self.peer(self.ep - d), :, self.columns[way]]
                remote(
                    landing, landing, self.z_send.at[way, d], self.z_recv.at[way, d], self.neighbours[0]
                ).wait_recv()


def all_partners(ep):
    f, c, t = lax.axis_index("fsdp"), lax.axis_index("ctx"), lax.axis_index("tp")
    line = [at_device(lax.rem(f + d, ep), c, t) for d in range(1, ep)]
    return line + [at_device(f, c ^ 1, t), at_device(f, c ^ 2, t), at_device(f, c, 1 - t)]


def experts_kernel(
    tokens_ref, outer_ref, routes_ref, extra_ref, weight_ref,
    returned_ref, mixture_out, sums_out, gates_out,
    gates_s, gated_s, side_s, part_s, *scratch,
):
    ep = lax.axis_size("fsdp")
    f = lax.axis_index("fsdp")
    low = jnp.bfloat16
    reach, model = tokens_ref.shape
    span = weight_ref.shape[1] // 3
    tokens = reach // ep
    local = EXPERTS // ep
    hidden = span // local
    sent = []
    back = ZSum(part_s, scratch, sent)
    partners = all_partners(ep)
    greet(partners[: ep - 1] + partners[-1:])

    lane = lax.broadcasted_iota(jnp.int32, (reach, 128), 1)
    chosen = routes_ref[:, 0:1] == lane
    for k in range(1, routes_ref.shape[1]):
        chosen = chosen | (routes_ref[:, k : k + 1] == lane)
    logits = jnp.dot(tokens_ref[...], extra_ref[...], preferred_element_type=jnp.float32)
    logits = jnp.where(chosen, logits, MASKED_SCORE)
    lifted = jnp.where(chosen, jnp.exp(logits - jnp.max(logits, -1, keepdims=True)), 0.0)
    gates_s[...] = lifted / jnp.sum(lifted, -1, keepdims=True)
    own = pl.ds(pl.multiple_of(f * tokens, 16), tokens)
    gates_out[...] = gates_s[own, :]
    small_lane = lax.broadcasted_iota(jnp.int32, (tokens, 128), 1)

    def block(d):
        here = pl.ds(pl.multiple_of(back.peer(d) * tokens, 16), tokens)
        gates = gates_s[here, :]
        dgates = jnp.zeros((tokens, 128), jnp.float32)
        for e in range(local):
            at = slice(e * hidden, (e + 1) * hidden)
            mine = small_lane == f * local + e
            gate = jnp.sum(jnp.where(mine, gates, 0.0), -1, keepdims=True)
            former = jnp.dot(tokens_ref[here, :], weight_ref[:, at], preferred_element_type=jnp.float32)
            at_up = slice(span + e * hidden, span + (e + 1) * hidden)
            latter = jnp.dot(tokens_ref[here, :], weight_ref[:, at_up], preferred_element_type=jnp.float32)
            at_down = slice(2 * span + e * hidden, 2 * span + (e + 1) * hidden)
            grad = jnp.dot(outer_ref[here, :], weight_ref[:, at_down], preferred_element_type=jnp.float32)
            logistic = 1.0 / (1.0 + jnp.exp(-former))
            active = former * logistic
            value = (active * latter).astype(low).astype(jnp.float32)
            gated_s[here, at] = (value * gate).astype(low)
            picked = jnp.sum(value * grad, -1, keepdims=True)
            dgates = jnp.where(mine & (gate > 0.0), picked, dgates)
            grad = grad * gate
            side_s[here, at] = (grad * latter * logistic * (1.0 + former * (1.0 - logistic))).astype(low)
            side_s[here, at_up] = (grad * active).astype(low)
        high = dgates.astype(low).astype(jnp.float32)
        part_s[here, model:] = (high + pltpu.roll(dgates - high, EXPERTS, 1)).astype(low)

        def tile(n, carry):
            at = pl.ds(pl.multiple_of(n * 256, 256), 256)
            part_s[here, at] = lax.dot_general(
                side_s[here, :], weight_ref[at, : 2 * span], (((1,), (1,)), ((), ())),
                preferred_element_type=jnp.float32,
            ).astype(low)
            mixture_out[here, at] = lax.dot_general(
                gated_s[here, :], weight_ref[at, 2 * span :], (((1,), (1,)), ((), ())),
                preferred_element_type=jnp.float32,
            ).astype(low)
            return carry

        lax.fori_loop(0, model // 256, tile, 0)

    order = list(range(1, ep)) + [0]
    for step, d in enumerate(order):
        block(d)
        back.to_core(d)
        if step > 0:
            back.to_z(order[step - 1])

    def sums(n, carry):
        at = pl.ds(pl.multiple_of(n * 256, 256), 256)
        over = (((0,), (0,)), ((), ()))
        sums_out[at, : 2 * span] = lax.dot_general(
            tokens_ref[:, at], side_s[...], over, preferred_element_type=jnp.float32
        ).astype(low)
        sums_out[at, 2 * span :] = lax.dot_general(
            outer_ref[:, at], gated_s[...], over, preferred_element_type=jnp.float32
        ).astype(low)
        return carry

    lax.fori_loop(0, model // 256, sums, 0)
    returned_ref[back.rows(back.t), :] = back.collect()
    back.share(returned_ref)
    back.finish(returned_ref)
    for copy in sent:
        copy.wait_send()


def run_experts(tokens_all, outer_all, routes_all, extra, weights, collective_id):
    ep = lax.axis_size("fsdp")
    reach, model = tokens_all.shape
    tokens, low = reach // ep, tokens_all.dtype
    span = weights.shape[1] // 3
    vmem = pl.BlockSpec(memory_space=pltpu.VMEM)
    shape = jax.ShapeDtypeStruct
    return pl.pallas_call(
        experts_kernel,
        out_shape=(
            shape((tokens, model + 128), jnp.float32),
            shape((reach, model), low),
            shape(weights.shape, low),
            shape((tokens, 128), jnp.float32),
        ),
        in_specs=[vmem] * 5,
        out_specs=(vmem,) * 4,
        scratch_shapes=[
            pltpu.VMEM((reach, 128), jnp.float32),
            pltpu.VMEM((reach, span), low),
            pltpu.VMEM((reach, 2 * span), low),
            pltpu.VMEM((reach, model + 128), low),
        ]
        + z_sum_scratch(ep, tokens, model + 128, low),
        compiler_params=pltpu.CompilerParams(
            collective_id=collective_id, has_side_effects=True, vmem_limit_bytes=60 * 1024 * 1024
        ),
        cost_estimate=lasting(70),
        name="experts",
    )(tokens_all, outer_all, routes_all, extra, weights)


def rear_kernel(
    returned_ref, gates_ref, middle_ref, input_ref, outer_ref, normed1_ref, query_ref, pair_ref, mixed_ref,
    log_ref, cos_ref, sin_ref, segment_ref, extra_ref, mixture_ref, sums_ref, attn_ref,
    input_grad, layer_out, qkv_out, wo_out, small_out, expert_out,
    wo_s, qkv_s, small_s, query_s, grad_s, mixed_s, key_s, value_s, bias_s, query_grad_s, key_grad_s, value_grad_s,
    pair_s, landing_s, back_s, attn_grad_s, part_s, other_s, logit_s, gains_s, mixture_s, own_s, relay_s,
    local_sem, key_send, key_recv, pair_send, pair_recv, *scratch,
):
    ep, rows = expert_out.shape[0], expert_out.shape[1]
    f, c, t = lax.axis_index("fsdp"), lax.axis_index("ctx"), lax.axis_index("tp")
    low = jnp.bfloat16
    tokens, model = input_ref.shape
    heads, key_heads = query_s.shape[0], key_s.shape[0]
    groups = heads // key_heads
    width, kv_width = heads * HD, key_heads * HD
    qkv_width = width + 2 * kv_width
    sent = []
    mixture = ZSum(mixture_ref, scratch[: ZSum.size], sent, mixture_s)
    scratch = scratch[ZSum.size :]
    size = len(shard_sum_scratch(ep, rows, 256, low, False))
    experts = ShardSum(sums_ref, rows, sums_ref.shape[1], scratch[:size], sent, own_s, relay_s)
    scratch = scratch[size:]
    size = len(shard_sum_scratch(ep, rows, 256, low))
    wo = ShardSum(wo_s, rows, width, scratch[:size], sent)
    qkv = ShardSum(qkv_s, rows, qkv_width, scratch[size : 2 * size], sent)
    small = ShardSum(small_s, rows, 128, scratch[2 * size :], sent)
    partners = all_partners(ep)
    plane = [at_device(f, c ^ k, t) for k in range(1, 4)]
    core = partners[-1]

    copies = [
        pltpu.make_async_copy(attn_ref.at[:, pl.ds(qkv_width + 128, width)], wo_s, local_sem.at[0]),
        pltpu.make_async_copy(attn_ref.at[:, pl.ds(0, qkv_width)], qkv_s, local_sem.at[1]),
    ]
    for copy in copies:
        copy.start()
    for d in range(ep):
        pltpu.make_async_copy(
            mixture_ref.at[mixture.place(mixture.peer(d), t)], mixture_s.at[d], local_sem.at[2]
        ).start()
    experts.load(local_sem.at[3])
    greet(partners + plane[2:])
    for d in experts.order:
        mixture.to_core(d)
    experts.first()

    small_lane = lax.broadcasted_iota(jnp.int32, (tokens, 128), 1)
    gains = extra_ref[...].astype(jnp.float32).T
    gain_one, gain_two = gains[EXPERTS : EXPERTS + 1, :], gains[EXPERTS + 1 : EXPERTS + 2, :]
    tail = returned_ref[:, model:]
    picked = jnp.where(small_lane < EXPERTS, tail + pltpu.roll(tail, 128 - EXPERTS, 1), 0.0)
    gates = gates_ref[...]
    logit_grad = (gates * (picked - jnp.sum(gates * picked, -1, keepdims=True))).astype(low)
    logit_s[...] = logit_grad
    second_grad = returned_ref[:, :model] + lax.dot_general(
        logit_grad, extra_ref[...], (((1,), (1,)), ((), ())), preferred_element_type=jnp.float32
    )
    middle = middle_ref[...]
    inverse = lax.rsqrt(jnp.mean(middle * middle, -1, keepdims=True) + EPSILON)
    scaled = second_grad * gain_two
    mean_term = jnp.mean(scaled * middle, -1, keepdims=True)
    gains_s[1:2, :] = jnp.sum(second_grad * middle * inverse, 0, keepdims=True)
    middle_grad = outer_ref[...].astype(jnp.float32) + (
        inverse * scaled - middle * (inverse * inverse * inverse) * mean_term
    )
    input_grad[...] = middle_grad
    attn_grad_s[...] = middle_grad.astype(low)

    copies[0].wait()
    for start in range(0, width, 256):
        tile = jnp.dot(
            attn_grad_s[...], wo_s[:, start : start + 256], preferred_element_type=jnp.float32
        ).astype(low)
        for side in range(0, 256, HD):
            grad_s[(start + side) // HD] = tile[:, side : side + HD]

    def wo_sums(n, carry):
        at = pl.ds(pl.multiple_of(n * 256, 256), 256)
        wo_s[at, :] = lax.dot_general(
            attn_grad_s[:, at], mixed_ref[...], (((0,), (0,)), ((), ())), preferred_element_type=jnp.float32
        ).astype(low)
        return carry

    lax.fori_loop(0, model // 256, wo_sums, 0)
    pltpu.make_async_copy(mixture_s, mixture_s, local_sem.at[2]).wait()
    for d in range(1, ep):
        mixture.to_z(d)
    wo.first()

    length = segment_ref.shape[1]
    seg_keys = jnp.broadcast_to(segment_ref[...].astype(jnp.float32), (128, length)).T[:, :1]
    seg_queries = segment_ref[:, pl.ds(pl.multiple_of(c * tokens, 128), tokens)].astype(jnp.float32)
    key_order = lax.broadcasted_iota(jnp.int32, (length, tokens), 0)
    query_order = lax.broadcasted_iota(jnp.int32, (length, tokens), 1) + c * tokens
    bias_s[...] = jnp.where((seg_keys == seg_queries) & (key_order <= query_order), 0.0, MASKED_SCORE)
    for h in range(heads):
        query_s[h] = query_ref[:, h * HD : (h + 1) * HD]
        mixed_s[h] = mixed_ref[:, h * HD : (h + 1) * HD]
    for g in range(key_heads):
        key_s[g] = pair_ref[:, g * HD : (g + 1) * HD]
        value_s[g] = pair_ref[:, kv_width + g * HD : kv_width + (g + 1) * HD]
    across = (((1,), (1,)), ((), ()))

    def attend_back(g, carry):
        key_grad = jnp.zeros((length, HD), jnp.float32)
        value_grad = jnp.zeros((length, HD), jnp.float32)
        for number in range(groups):
            h = g * groups + number
            query = query_s[h] * jnp.asarray(HD**-0.5, low)
            grad = grad_s[h]
            scores = lax.dot_general(key_s[g], query, across, preferred_element_type=jnp.float32) + bias_s[...]
            probs = jnp.exp(scores - log_ref[h])
            value_grad += jnp.dot(probs.astype(low), grad, preferred_element_type=jnp.float32)
            prob_grad = lax.dot_general(value_s[g], grad, across, preferred_element_type=jnp.float32)
            delta = jnp.sum((grad.astype(jnp.float32) * mixed_s[h].astype(jnp.float32)).T, 0, keepdims=True)
            score_grad = (probs * (prob_grad - delta)).astype(low)
            key_grad += jnp.dot(score_grad, query, preferred_element_type=jnp.float32)
            query_grad = lax.dot_general(
                key_s[g], score_grad, (((0,), (0,)), ((), ())), preferred_element_type=jnp.float32
            )
            query_grad_s[h] = query_grad.T * (HD**-0.5)
        key_grad_s[g] = key_grad.astype(low)
        value_grad_s[g] = value_grad.astype(low)
        return carry

    lax.fori_loop(0, key_heads, attend_back, 0)
    for g in range(key_heads):
        pair_s[:, g * HD : (g + 1) * HD] = key_grad_s[g]
        pair_s[:, kv_width + g * HD : kv_width + (g + 1) * HD] = value_grad_s[g]
    for k in (3, 1, 2):
        place = pl.ds(pl.multiple_of((c ^ k) * tokens, 16), tokens)
        copy = remote(pair_s.at[place], landing_s.at[k - 1], key_send.at[k - 1], key_recv.at[k - 1], plane[k - 1])
        copy.start()
        sent.append(copy)
    first_half = lax.rem(small_lane, HD) < HD // 2

    def turned_back(tile):
        swapped = jnp.where(first_half, pltpu.roll(tile, 128 - HD // 2, 1), pltpu.roll(tile, HD // 2, 1))
        return tile * cos_ref[...] - swapped * sin_ref[...]

    for start in range(0, width, 128):
        tile = jnp.concatenate([query_grad_s[start // HD], query_grad_s[start // HD + 1]], 1)
        back_s[:, start : start + 128] = turned_back(tile).astype(low)

    experts.loaded(local_sem.at[3])
    for d in experts.order:
        experts.second(d)
    total = mixture.collect()
    half = mixture.rows(t)
    layer_out[half, :] = (middle_ref[half, :] + total).astype(low)
    mixture.share(layer_out)

    pair = pair_s[pl.ds(pl.multiple_of(c * tokens, 16), tokens), :].astype(jnp.float32)
    for k in (1, 2, 3):
        block = landing_s.at[k - 1]
        remote(block, block, key_send.at[k - 1], key_recv.at[k - 1], plane[k - 1]).wait_recv()
        pair = pair + landing_s[k - 1].astype(jnp.float32)
    for start in range(0, kv_width, 128):
        back_s[:, width + start : width + start + 128] = turned_back(pair[:, start : start + 128]).astype(low)
    back_s[:, width + kv_width :] = pair[:, kv_width:].astype(low)
    copies[1].wait()
    for start in range(0, model, 256):
        part_s[:, start : start + 256] = lax.dot_general(
            back_s[...], qkv_s[start : start + 256, :], across, preferred_element_type=jnp.float32
        ).astype(low)
    exchange = remote(part_s, other_s, pair_send, pair_recv, core)
    exchange.start()
    sent.append(exchange)

    def qkv_sums(n, carry):
        at = pl.ds(pl.multiple_of(n * 256, 256), 256)
        qkv_s[at, :] = lax.dot_general(
            normed1_ref[:, at], back_s[...], (((0,), (0,)), ((), ())), preferred_element_type=jnp.float32
        ).astype(low)
        return carry

    lax.fori_loop(0, model // 256, qkv_sums, 0)
    qkv.first()
    for d in wo.order:
        wo.second(d)
    for d in experts.order:
        experts.swap_z(d, expert_out)

    exchange.wait_recv()
    first_grad = part_s[...].astype(jnp.float32) + other_s[...].astype(jnp.float32)
    inputs = input_ref[...].astype(jnp.float32)
    inverse = lax.rsqrt(jnp.mean(inputs * inputs, -1, keepdims=True) + EPSILON)
    gains_s[0:1, :] = jnp.sum(first_grad * inputs * inverse, 0, keepdims=True)
    scaled = first_grad * gain_one
    mean_term = jnp.mean(scaled * inputs, -1, keepdims=True)
    input_grad[...] += inverse * scaled - inputs * (inverse * inverse * inverse) * mean_term
    middle = middle_ref[...]
    inverse = lax.rsqrt(jnp.mean(middle * middle, -1, keepdims=True) + EPSILON)
    normed2 = (middle * inverse * gain_two).astype(low)
    router_sums = lax.dot_general(
        normed2, logit_s[...], (((0,), (0,)), ((), ())), preferred_element_type=jnp.float32
    )
    line = lax.broadcasted_iota(jnp.int32, (128, model), 0)
    turned = jnp.where(line == EXPERTS, gains_s[0:1, :], jnp.where(line == EXPERTS + 1, gains_s[1:2, :], 0.0)).T
    small_s[...] = (router_sums + turned).astype(low)
    small.first()

    for d in wo.order:
        wo.to_z(d, wo_out)
    for d in qkv.order:
        qkv.second(d)
    for d in small.order:
        small.second(d)
    for d in qkv.order:
        qkv.to_z(d, qkv_out)
    for d in small.order:
        small.to_z(d, small_out)
    mixture.finish(layer_out)
    experts.swapped_z(expert_out)
    wo.from_z(wo_out)
    small.from_z(small_out)
    qkv.from_z(qkv_out)
    for copy in sent:
        copy.wait_send()


def rear(
    returned, gates, middle, inputs, outer, normed1, query, pair, mixed, log_total, cosine, sine, segments, extra,
    mixture, sums, attn, collective_id,
):
    ep = lax.axis_size("fsdp")
    tokens, model = inputs.shape
    rows = sums.shape[0] // (4 * ep)
    heads, key_heads = query.shape[1] // HD, pair.shape[1] // (2 * HD)
    width, kv_width = heads * HD, key_heads * HD
    qkv_width = width + 2 * kv_width
    length = pair.shape[0]
    low = jnp.bfloat16
    dma = pltpu.SemaphoreType.DMA
    anywhere = pl.BlockSpec(memory_space=pl.ANY)
    vmem = pl.BlockSpec(memory_space=pltpu.VMEM)
    shape = jax.ShapeDtypeStruct
    room = pltpu.VMEM
    return pl.pallas_call(
        rear_kernel,
        out_shape=(
            shape((tokens, model), jnp.float32),
            shape((tokens, model), low),
            shape((rows, qkv_width), jnp.float32),
            shape((rows, width), jnp.float32),
            shape((rows, 128), jnp.float32),
            shape((ep, rows, sums.shape[1]), low),
        ),
        in_specs=[vmem] * 14 + [anywhere] * 3,
        out_specs=(vmem,) * 5 + (anywhere,),
        scratch_shapes=[
            room((model, width), low),
            room((model, qkv_width), low),
            room((model, 128), low),
            room((heads, tokens, HD), low),
            room((heads, tokens, HD), low),
            room((heads, tokens, HD), low),
            room((key_heads, length, HD), low),
            room((key_heads, length, HD), low),
            room((length, tokens), jnp.float32),
            room((heads, tokens, HD), jnp.float32),
            room((key_heads, length, HD), low),
            room((key_heads, length, HD), low),
            room((length, 2 * kv_width), low),
            room((3, tokens, 2 * kv_width), low),
            room((tokens, qkv_width), low),
            room((tokens, model), low),
            room((tokens, model), low),
            room((tokens, model), low),
            room((tokens, 128), low),
            room((8, model), jnp.float32),
            room((ep, tokens // 2, model), low),
            room((ep, rows, sums.shape[1]), low),
            room((ep, rows, sums.shape[1]), low),
            dma((4,)),
            dma((3,)),
            dma((3,)),
            dma,
            dma,
        ]
        + z_sum_scratch(ep, tokens, model, low)
        + shard_sum_scratch(ep, rows, sums.shape[1], low, False)
        + shard_sum_scratch(ep, rows, width, low)
        + shard_sum_scratch(ep, rows, qkv_width, low)
        + shard_sum_scratch(ep, rows, 128, low),
        compiler_params=pltpu.CompilerParams(
            collective_id=collective_id, has_side_effects=True, vmem_limit_bytes=63 * 1024 * 1024
        ),
        cost_estimate=lasting(170),
        name="rear",
    )(
        returned, gates, middle, inputs, outer, normed1, query, pair, mixed, log_total, cosine, sine, segments,
        extra, mixture, sums, attn,
    )


def plain_shards(
    layer_input,
    segments,
    routes,
    norm_gain,
    query_weight,
    key_weight,
    value_weight,
    output_weight,
    ffn_gain,
    router_weight,
    gate_weight,
    up_weight,
    down_weight,
    cotangent,
):
    low = jnp.bfloat16
    both = ("fsdp", "ctx")
    ep = lax.axis_size("fsdp")
    tokens = layer_input.shape[0]
    seq_len = segments.shape[1]
    rows = query_weight.shape[0]
    width = query_weight.shape[1]
    kv_width = key_weight.shape[1]
    hidden_width = gate_weight.shape[2]
    local = EXPERTS // ep
    span = local * hidden_width

    qkv_width = width + 2 * kv_width
    extra = jnp.concatenate([router_weight, norm_gain[:, None], ffn_gain[:, None]], 1)
    extra = jnp.pad(extra, ((0, 0), (0, 128 - extra.shape[1])))
    attn_shard = jnp.concatenate([query_weight, key_weight, value_weight, extra, output_weight.T], 1)
    down_shard = down_weight.transpose(0, 2, 1)
    begin = lax.axis_index("ctx") * tokens
    segment_row = segments[0]
    query_doc = lax.dynamic_slice_in_dim(segment_row, begin, tokens)
    query_order = begin + jnp.arange(tokens, dtype=jnp.int32)
    scale = HD ** (-0.5)
    inputs = layer_input.astype(jnp.float32)
    key_groups = kv_width // HD
    groups = width // kv_width
    freq = 10000.0 ** (-2.0 * jnp.arange(HD // 2, dtype=jnp.float32) / HD)

    def unpack(attn_full):
        return (
            attn_full[:, :qkv_width],
            attn_full[:, qkv_width : qkv_width + EXPERTS],
            attn_full[:, qkv_width + EXPERTS],
            attn_full[:, qkv_width + EXPERTS + 1],
            attn_full[:, qkv_width + 128 :],
        )

    attn_full = lax.all_gather(attn_shard, both, axis=0, tiled=True)
    qkv_full, router_full, gain_one, gain_two, output_turned = unpack(attn_full)
    packed = jnp.concatenate([gate_weight, up_weight, down_shard], -1)
    expert_full = spread_experts(packed)
    expert_full = expert_full.reshape(D, local, 3, hidden_width).transpose(0, 2, 1, 3)
    expert_full = expert_full.reshape(D, 3 * span)
    outer_all = lax.all_gather(cotangent, "fsdp", axis=0, tiled=True)
    routes_all = lax.all_gather(routes, "fsdp", axis=0, tiled=True)
    place = lax.dynamic_slice_in_dim(document_place(segment_row), begin, tokens)
    angle = place.astype(jnp.float32)[:, None] * freq[None, :]
    cosine, sine = jnp.cos(angle), jnp.sin(angle)
    first_norm, first_inverse = normalize(inputs, gain_one)
    normed1 = first_norm.astype(low)
    projected = jnp.dot(normed1, qkv_full, preferred_element_type=jnp.float32)
    query = rotate(projected[:, :width], cosine, sine).astype(low)
    key = rotate(projected[:, width : width + kv_width], cosine, sine).astype(low)
    value = projected[:, width + kv_width :].astype(low)
    pair_all = lax.all_gather(jnp.concatenate([key, value], 1), "ctx", axis=0, tiled=True)
    heads = query.reshape(tokens, key_groups, groups, HD)
    key_heads = pair_all[:, :kv_width].reshape(seq_len, key_groups, HD)
    value_heads = pair_all[:, kv_width:].reshape(seq_len, key_groups, HD)
    scores = jnp.einsum("qkgd,nkd->qkgn", heads, key_heads, preferred_element_type=jnp.float32) * scale
    seen = (segment_row[None, :] == query_doc[:, None]) & (
        jnp.arange(seq_len, dtype=jnp.int32)[None, :] <= query_order[:, None]
    )
    scores = jnp.where(seen[:, None, None, :], scores, MASKED_SCORE)
    running = jnp.max(scores, -1)
    weights = jnp.exp(scores - running[..., None])
    summed = jnp.einsum(
        "qkgn,nkd->qkgd", weights.astype(low), value_heads, preferred_element_type=jnp.float32
    )
    totals = jnp.sum(weights, -1)
    log_total = running + jnp.log(totals)
    mixed_low = (summed / totals[..., None]).reshape(tokens, -1).astype(low)
    attention = lax.psum(
        times_transpose(mixed_low, output_turned).astype(low), "tp"
    ).astype(jnp.float32)
    middle = inputs + attention
    second_norm, second_inverse = normalize(middle, gain_two)
    normed2 = second_norm.astype(low)
    normed2_all = lax.all_gather(normed2, "fsdp", axis=0, tiled=True)
    gate_up = expert_full[:, : 2 * span]
    down_turned = expert_full[:, 2 * span :]
    key_all = pair_all[:, :kv_width]
    value_all = pair_all[:, kv_width:]
    grouped = query.reshape(tokens, key_groups, groups, HD)

    def block_scores(key_piece, offset):
        count = key_piece.shape[0]
        key_heads = key_piece.reshape(count, key_groups, HD)
        scores = (
            jnp.einsum("qkgd,nkd->qkgn", grouped, key_heads, preferred_element_type=jnp.float32)
            * scale
        )
        key_doc = lax.dynamic_slice_in_dim(segment_row, offset, count)
        key_order = offset + jnp.arange(count, dtype=jnp.int32)
        seen = (key_doc[None, :] == query_doc[:, None]) & (
            key_order[None, :] <= query_order[:, None]
        )
        return (scores, seen[:, None, None, :], key_heads)

    def masked_away(offset, count):
        last_doc = lax.dynamic_index_in_dim(segment_row, offset + count - 1, keepdims=False)
        return (offset > query_order[tokens - 1]) | (last_doc < query_doc[0])

    place_z = lax.axis_index("fsdp")
    logits_all = jnp.dot(normed2_all, router_full, preferred_element_type=jnp.float32)
    expert_ids = jnp.arange(EXPERTS, dtype=jnp.int32)
    chosen_all = jnp.any(routes_all[:, :, None] == expert_ids[None, None, :], 1)
    masked_logits = jnp.where(chosen_all, logits_all, MASKED_SCORE)
    top = jnp.max(masked_logits, -1, keepdims=True)
    lifted = jnp.where(chosen_all, jnp.exp(masked_logits - top), 0.0)
    gates_all = lifted / jnp.sum(lifted, -1, keepdims=True)
    gates_here = lax.dynamic_slice_in_dim(gates_all, place_z * local, local, 1)
    chosen_here = lax.dynamic_slice_in_dim(chosen_all, place_z * local, local, 1)
    chosen = lax.dynamic_slice_in_dim(chosen_all, place_z * tokens, tokens, 0)
    gates = lax.dynamic_slice_in_dim(gates_all, place_z * tokens, tokens, 0)

    reach = normed2_all.shape[0]
    both_sides = jnp.dot(normed2_all, gate_up, preferred_element_type=jnp.float32)
    former = both_sides[:, :span]
    latter = both_sides[:, span:]
    hidden_grad = jnp.dot(outer_all, down_turned, preferred_element_type=jnp.float32)
    gate_wide = jnp.concatenate(
        [jnp.broadcast_to(gates_here[:, e : e + 1], (reach, hidden_width)) for e in range(local)], 1
    )
    logistic = jax.nn.sigmoid(former)
    active = former * logistic
    hidden = (active * latter).astype(low).astype(jnp.float32)
    gated = (hidden * gate_wide).astype(low)
    parts = [slice(e * hidden_width, (e + 1) * hidden_width) for e in range(local)]
    dgates = jnp.stack([jnp.sum(hidden[:, part] * hidden_grad[:, part], -1) for part in parts], 1)
    scaled_grad = hidden_grad * gate_wide
    former_grad = (scaled_grad * latter * logistic * (1.0 + former * (1.0 - logistic))).astype(low)
    latter_grad = (scaled_grad * active).astype(low)
    side_grads = jnp.concatenate([former_grad, latter_grad], 1)
    mixture_low = times_transpose(gated, down_turned).astype(low)
    input_part = times_transpose(side_grads, gate_up)
    side_sums = contract_rows(normed2_all, side_grads)
    down_sums = contract_rows(outer_all, gated)
    dgates = jnp.where(chosen_here, dgates, 0.0)
    dgates_wide = lax.dynamic_update_slice_in_dim(
        jnp.zeros((reach, EXPERTS), jnp.float32), dgates, place_z * local, 1
    )
    dgates_high = dgates_wide.astype(low)
    dgates_rest = (dgates_wide - dgates_high.astype(jnp.float32)).astype(low)
    dgates_sent = jnp.concatenate([dgates_high, dgates_rest], 1)
    dgates_sent = jnp.pad(dgates_sent, ((0, 0), (0, 128 - 2 * EXPERTS)))
    back_part = jnp.concatenate([input_part.astype(low), dgates_sent], 1)
    returned = lax.psum_scatter(
        lax.psum(back_part, "tp"), "fsdp", scatter_dimension=0, tiled=True
    ).astype(jnp.float32)
    expert_sums = jnp.concatenate([side_sums, down_sums], 1).astype(low)
    expert_out = collect_experts(expert_sums, rows).reshape(ep, rows, 3, local, hidden_width)
    side_out = expert_out[:, :, :2].transpose(2, 0, 3, 1, 4).reshape(2, EXPERTS, rows, hidden_width)
    side_out = side_out.astype(jnp.float32)
    down_out = expert_out[:, :, 2].transpose(0, 2, 3, 1).reshape(EXPERTS, hidden_width, rows).astype(jnp.float32)

    outer_grad = cotangent.astype(jnp.float32)
    input_grad_part = returned[:, :D]
    picked = returned[:, D : D + EXPERTS] + returned[:, D + EXPERTS : D + 2 * EXPERTS]
    logit_grad = (gates * (picked - jnp.sum(gates * picked, -1, keepdims=True))).astype(low)
    router_sums = contract_rows(normed2, logit_grad)
    second_grad = input_grad_part + times_transpose(logit_grad, router_full)
    middle_back, gain_two_sums = norm_back(second_grad, middle, second_inverse, gain_two)
    middle_grad = outer_grad + middle_back
    attention_grad = middle_grad.astype(low)
    output_sums = contract_rows(attention_grad, mixed_low)
    mixed_grad = jnp.dot(attention_grad, output_turned, preferred_element_type=jnp.float32).astype(low)
    mixed_heads = mixed_grad.reshape(tokens, key_groups, groups, HD)
    delta = jnp.sum(mixed_heads.astype(jnp.float32) * mixed_low.reshape(mixed_heads.shape), -1)

    def back_two(number, state):
        offset = number * tokens
        key_piece = lax.dynamic_slice_in_dim(key_all, offset, tokens, 0)
        value_piece = lax.dynamic_slice_in_dim(value_all, offset, tokens, 0)

        def back_compute(inner):
            query_sum, pair_sum = inner
            scores, seen, key_heads = block_scores(key_piece, offset)
            probs = jnp.where(seen, jnp.exp(scores - log_total[..., None]), 0.0)
            value_heads = value_piece.reshape(tokens, key_groups, HD)
            prob_grad = jnp.einsum(
                "qkgd,nkd->qkgn", mixed_heads, value_heads, preferred_element_type=jnp.float32
            )
            score_grad = (probs * (prob_grad - delta[..., None])).astype(low)
            query_sum = (
                query_sum
                + jnp.einsum(
                    "qkgn,nkd->qkgd", score_grad, key_heads, preferred_element_type=jnp.float32
                )
                * scale
            )
            key_block = (
                jnp.einsum(
                    "qkgn,qkgd->nkd", score_grad, grouped, preferred_element_type=jnp.float32
                )
                * scale
            )
            value_block = jnp.einsum(
                "qkgn,qkgd->nkd", probs.astype(low), mixed_heads, preferred_element_type=jnp.float32
            )
            pair = jnp.concatenate([key_block.reshape(tokens, -1), value_block.reshape(tokens, -1)], 1)
            return (query_sum, lax.dynamic_update_slice_in_dim(pair_sum, pair, offset, 0))

        return lax.cond(masked_away(offset, tokens), lambda inner: inner, back_compute, state)

    back_state = (
        jnp.zeros((tokens, key_groups, groups, HD), jnp.float32),
        jnp.zeros((seq_len, 2 * kv_width), jnp.float32),
    )
    query_sum, pair_sum = lax.fori_loop(0, seq_len // tokens, back_two, back_state)
    pair_local = lax.psum_scatter(
        pair_sum.astype(low), "ctx", scatter_dimension=0, tiled=True
    ).astype(jnp.float32)
    query_back = rotate(query_sum.reshape(tokens, -1), cosine, -sine)
    key_back = rotate(pair_local[:, :kv_width], cosine, -sine)
    qkv_back = jnp.concatenate([query_back, key_back, pair_local[:, kv_width:]], 1).astype(low)
    qkv_sums = contract_rows(normed1, qkv_back)
    first_part = times_transpose(qkv_back, qkv_full)
    first_grad = lax.psum(first_part.astype(low), "tp").astype(jnp.float32)
    input_back, gain_one_sums = norm_back(first_grad, inputs, first_inverse, gain_one)
    input_grad = middle_grad + input_back
    small_sums = jnp.concatenate([router_sums, gain_one_sums[:, None], gain_two_sums[:, None]], 1)
    small_sums = jnp.pad(small_sums, ((0, 0), (0, 128 - small_sums.shape[1])))
    attn_sums = jnp.concatenate([qkv_sums.astype(low), small_sums.astype(low), output_sums.astype(low)], 1)
    attn_out = lax.psum_scatter(attn_sums, both, scatter_dimension=0, tiled=True).astype(jnp.float32)
    mixture = lax.psum_scatter(
        lax.psum(mixture_low, "tp"), "fsdp", scatter_dimension=0, tiled=True
    ).astype(jnp.float32)
    layer_output = (middle + mixture).astype(low)
    small_out = attn_out[:, qkv_width : qkv_width + 128]
    return (
        layer_output,
        input_grad,
        small_out[:, EXPERTS],
        attn_out[:, :width],
        attn_out[:, width : width + kv_width],
        attn_out[:, width + kv_width : qkv_width],
        attn_out[:, qkv_width + 128 :].T,
        small_out[:, EXPERTS + 1],
        small_out[:, :EXPERTS],
        side_out[0],
        side_out[1],
        down_out,
    )


def shards(
    layer_input,
    segments,
    routes,
    norm_gain,
    query_weight,
    key_weight,
    value_weight,
    output_weight,
    ffn_gain,
    router_weight,
    gate_weight,
    up_weight,
    down_weight,
    cotangent,
):
    low = jnp.bfloat16
    ep = lax.axis_size("fsdp")
    rows, width = query_weight.shape
    kv_width = key_weight.shape[1]
    hidden_width = gate_weight.shape[2]
    local = EXPERTS // ep
    extra = jnp.concatenate([router_weight, norm_gain[:, None], ffn_gain[:, None]], 1)
    extra = jnp.pad(extra, ((0, 0), (0, 128 - extra.shape[1])))
    attn_shard = jnp.concatenate([query_weight, key_weight, value_weight, extra, output_weight.T], 1)
    freq = 10000.0 ** (-2.0 * jnp.arange(HD // 2, dtype=jnp.float32) / HD)
    (
        expert_full, outer_all, routes_all, normed2_all,
        attn_full, normed1, query, pair_all, mixed, log_total, middle, cosine, sine, extra_all,
    ) = front(
        attn_shard, gate_weight, up_weight, down_weight.transpose(0, 2, 1), cotangent, routes, layer_input,
        segments, jnp.tile(freq, 4)[None, :], width // HD, kv_width // HD,
    )
    returned, mixture, expert_sums, gates = run_experts(
        normed2_all, outer_all, routes_all, extra_all, expert_full, 2
    )
    input_grad, layer_output, qkv_out, wo_out, small_out, expert_out = rear(
        returned, gates, middle, layer_input, cotangent, normed1, query, pair_all, mixed, log_total, cosine, sine,
        segments, extra_all, mixture, expert_sums, attn_full, 3,
    )
    expert_out = expert_out.reshape(ep, rows, 3, local, hidden_width)
    side_out = expert_out[:, :, :2].transpose(2, 0, 3, 1, 4).reshape(2, EXPERTS, rows, hidden_width)
    side_out = side_out.astype(jnp.float32)
    down_out = expert_out[:, :, 2].transpose(0, 2, 3, 1).reshape(EXPERTS, hidden_width, rows).astype(jnp.float32)
    return (
        layer_output,
        input_grad,
        small_out[:, EXPERTS],
        qkv_out[:, :width],
        qkv_out[:, width : width + kv_width],
        qkv_out[:, width + kv_width :],
        wo_out.T,
        small_out[:, EXPERTS + 1],
        small_out[:, :EXPERTS],
        side_out[0],
        side_out[1],
        down_out,
    )


def solution(mesh):
    in_specs = (
        P(("fsdp", "ctx"), None),
        P("fsdp", None),
        P(("fsdp", "ctx"), None),
        P(("fsdp", "ctx")),
        P(("fsdp", "ctx"), "tp"),
        P(("fsdp", "ctx"), "tp"),
        P(("fsdp", "ctx"), "tp"),
        P("tp", ("fsdp", "ctx")),
        P(("fsdp", "ctx")),
        P(("fsdp", "ctx"), None),
        P(None, ("fsdp", "ctx"), "tp"),
        P(None, ("fsdp", "ctx"), "tp"),
        P(None, "tp", ("fsdp", "ctx")),
        P(("fsdp", "ctx"), None),
    )
    out_specs = (
        P(("fsdp", "ctx"), None),
        P(("fsdp", "ctx"), None),
        P(("fsdp", "ctx")),
        P(("fsdp", "ctx"), "tp"),
        P(("fsdp", "ctx"), "tp"),
        P(("fsdp", "ctx"), "tp"),
        P("tp", ("fsdp", "ctx")),
        P(("fsdp", "ctx")),
        P(("fsdp", "ctx"), None),
        P(None, ("fsdp", "ctx"), "tp"),
        P(None, ("fsdp", "ctx"), "tp"),
        P(None, "tp", ("fsdp", "ctx")),
    )
    body = shards if mesh.shape["ctx"] == 4 else plain_shards
    return jax.shard_map(body, mesh=mesh, in_specs=in_specs, out_specs=out_specs, check_vma=False)
```

```python
import jax
import jax.numpy as jnp
from jax import lax
from jax.experimental import pallas as pl
from jax.experimental.pallas import tpu as pltpu
from jax.sharding import PartitionSpec as P

MESH = pl.DeviceIdType.MESH

D = 1536
HD = 64
EXPERTS = 16
EARLY = 768


EPSILON = 1e-05
MASKED_SCORE = -1e30


def rotate(values, cosine, sine):
    rows = values.shape[0]
    shaped = values.reshape(rows, -1, HD)
    half = HD // 2
    cosine, sine = cosine[:, None, :], sine[:, None, :]
    former = shaped[..., :half]
    latter = shaped[..., half:]
    turned = jnp.concatenate([former * cosine - latter * sine, latter * cosine + former * sine], -1)
    return turned.reshape(rows, -1)


def normalize(values, gain):
    inverse = lax.rsqrt(jnp.mean(values * values, -1, keepdims=True) + EPSILON)
    return (values * inverse * gain.astype(jnp.float32), inverse)


def norm_back(grad, values, inverse, gain):
    scaled = grad * gain.astype(jnp.float32)
    gain_grad = jnp.sum(grad * values * inverse, 0)
    mean_term = jnp.mean(scaled * values, -1, keepdims=True)
    return (inverse * scaled - values * inverse**3 * mean_term, gain_grad)


def document_place(segment_row):
    length = segment_row.shape[0]
    order = jnp.arange(length, dtype=jnp.int32)
    fresh = jnp.concatenate([jnp.ones((1,), jnp.bool_), segment_row[1:] != segment_row[:-1]])
    starts = lax.cummax(jnp.where(fresh, order, 0), axis=0)
    return order - starts


def contract_rows(left, right):
    return lax.dot_general(
        left, right, (((0,), (0,)), ((), ())), preferred_element_type=jnp.float32
    )


def times_transpose(left, right):
    return lax.dot_general(
        left, right, (((1,), (1,)), ((), ())), preferred_element_type=jnp.float32
    )


def spread_experts(packed):
    ep = lax.axis_size("fsdp")
    local = packed.shape[0] // ep
    rows = packed.shape[1]
    swapped = lax.all_to_all(packed, "fsdp", 0, 0, tiled=True)
    swapped = swapped.reshape(ep, local, rows, -1).transpose(0, 2, 1, 3)
    swapped = swapped.reshape(ep, rows, -1)
    whole = lax.all_gather(swapped, "ctx", axis=1)
    return whole.reshape(ep * lax.axis_size("ctx") * rows, -1)


def collect_experts(sums, rows):
    ep, ring = lax.axis_size("fsdp"), lax.axis_size("ctx")
    turned = sums.reshape(ep, ring, rows, -1).transpose(1, 0, 2, 3).reshape(sums.shape)
    mine = lax.psum_scatter(turned, "ctx", scatter_dimension=0, tiled=True)
    return lax.all_to_all(mine, "fsdp", 0, 0, tiled=True)


def at_device(fsdp, ctx, tp):
    return {"fsdp": fsdp, "ctx": ctx, "tp": tp}


def greet(partners):
    barrier = pltpu.get_barrier_semaphore()
    for device in partners:
        pl.semaphore_signal(barrier, inc=1, device_id=device, device_id_type=MESH)
    pl.semaphore_wait(barrier, len(partners))


def remote(source, target, send, recv, device):
    return pltpu.make_async_remote_copy(
        src_ref=source, dst_ref=target, send_sem=send, recv_sem=recv, device_id=device, device_id_type=MESH
    )


def lasting(us):
    return pl.CostEstimate(flops=0, bytes_accessed=us * 3690000, transcendentals=0)


def front_kernel(
    attn_ref, gate_ref, up_ref, down_ref, outer_ref, routes_ref, input_ref, segment_ref, freq_ref,
    expert_out, outer_out, routes_out, normed2_out,
    attn_out, normed1_out, query_out, pair_out, mixed_out, log_out, middle_out, cos_out, sin_out, extra_out,
    query_s, key_s, value_s, mixed_s, bias_s, part_s, other_s, normed2_s,
    local_sem, z_send, z_recv, plane_send, plane_recv, relay_send, relay_recv, core_send, core_recv,
    key_send, key_recv, pair_send, pair_recv, chain_send, chain_recv,
):
    ep = z_send.shape[1] + 1
    f, c, t = lax.axis_index("fsdp"), lax.axis_index("ctx"), lax.axis_index("tp")
    low = jnp.bfloat16
    rows = attn_ref.shape[0]
    local = gate_ref.shape[0] // ep
    hidden = gate_ref.shape[2]
    tokens = outer_ref.shape[0]
    half = tokens // 2
    heads = query_s.shape[0]
    key_heads = key_s.shape[0]
    width, kv_width = heads * HD, key_heads * HD
    qkv_width = width + 2 * kv_width
    outs = (attn_out, expert_out)
    cuts = [(out.shape[1] // 256) * 128 for out in outs]

    def peer(distance):
        return lax.rem(f + distance, ep)

    def shard_rows(fsdp, ctx):
        return pl.ds(pl.multiple_of((fsdp * 4 + ctx) * rows, 16), rows)

    def columns(kind, side):
        cut, full = cuts[kind], outs[kind].shape[1]
        return pl.ds(0, cut) if side == 0 else pl.ds(cut, full - cut)

    line = [at_device(peer(d), c, t) for d in range(1, ep)]
    plane = [at_device(f, c ^ k, t) for k in range(1, 4)]
    x_device, y_device = plane[0], plane[1]
    core = at_device(f, c, 1 - t)
    greet(line + plane + [core])

    mine = shard_rows(f, c)
    sent = []

    def send(copy, when=None):
        if when is None:
            copy.start()
        else:
            pl.when(when)(copy.start)
        sent.append((when, copy))

    def await_arrival(copy, when=None):
        if when is None:
            copy.wait_recv()
        else:
            pl.when(when)(copy.wait_recv)

    def z_arrival(kind, d):
        place = shard_rows(peer(ep - d), c)
        remote(
            outs[kind].at[place], outs[kind].at[place], z_send.at[kind, d - 1], z_recv.at[kind, d - 1], x_device
        ).wait_recv()

    def spread(kind, g, when=None):
        place = shard_rows(g, c)
        for step in range(2):
            for way, device in enumerate((x_device, y_device)):
                side = step ^ way
                block = outs[kind].at[place, columns(kind, side)]
                send(
                    remote(
                        block, block, plane_send.at[kind, g, way, side], plane_recv.at[kind, g, way, side], device
                    ),
                    when,
                )

    def pass_on(kind, g, when=None):
        for way, device in enumerate((y_device, x_device)):
            place = shard_rows(g, c ^ (1 << way))
            block = outs[kind].at[place, columns(kind, way)]
            await_arrival(
                remote(
                    block, block, plane_send.at[kind, g, way, way], plane_recv.at[kind, g, way, way], device
                ),
                when,
            )
            send(remote(block, block, relay_send.at[kind, g, way], relay_recv.at[kind, g, way], device), when)

    def settle(kind):
        for g in range(ep):
            for way, device in enumerate((x_device, y_device)):
                side = 1 - way
                block = outs[kind].at[shard_rows(g, c ^ (1 << way)), columns(kind, side)]
                remote(
                    block, block, plane_send.at[kind, g, way, side], plane_recv.at[kind, g, way, side], device
                ).wait_recv()
                block = outs[kind].at[shard_rows(g, c ^ 3), columns(kind, way)]
                remote(
                    block, block, relay_send.at[kind, g, way], relay_recv.at[kind, g, way], device
                ).wait_recv()

    nexts = (at_device(jnp.minimum(f + 1, ep - 1), c, t), at_device(jnp.maximum(f - 1, 0), c, t))
    more = (f < ep - 1, f > 0)

    def chain_origin(way, hop):
        if way == 0:
            return jnp.maximum(f - hop, 0), f >= hop
        return jnp.minimum(f + hop, ep - 1), f + hop < ep

    def chain_begin(kind, source, target):
        for way in range(2):
            send(
                remote(source, target, chain_send.at[kind, way, 0], chain_recv.at[kind, way, 0], nexts[way]),
                more[way],
            )

    def chain_hop(kind, way, hop, block):
        there = chain_origin(way, hop)[1]
        await_arrival(
            remote(
                block, block, chain_send.at[kind, way, hop - 1], chain_recv.at[kind, way, hop - 1], nexts[way]
            ),
            there,
        )
        if hop < ep - 1:
            send(
                remote(block, block, chain_send.at[kind, way, hop], chain_recv.at[kind, way, hop], nexts[way]),
                there & more[way],
            )

    def line_place(fsdp, part):
        return pl.ds(pl.multiple_of(fsdp * tokens + part * half, 16), half)

    own_tokens = pl.ds(pl.multiple_of(f * tokens, 16), tokens)
    my_half = pl.ds(pl.multiple_of(t * half, 16), half)

    def line_send(kind, source, target):
        for d in range(1, ep):
            send(
                remote(
                    source, target.at[line_place(f, t)], z_send.at[kind, d - 1], z_recv.at[kind, d - 1], line[d - 1]
                )
            )

    def line_forward(kind, target):
        for d in range(1, ep):
            block = target.at[line_place(peer(ep - d), t)]
            remote(block, block, z_send.at[kind, d - 1], z_recv.at[kind, d - 1], core).wait_recv()
            send(remote(block, block, core_send.at[kind - 2, d], core_recv.at[kind - 2, d], core))

    def line_settle(kind, target):
        for d in range(1, ep):
            block = target.at[line_place(peer(ep - d), 1 - t)]
            remote(block, block, core_send.at[kind - 2, d], core_recv.at[kind - 2, d], core).wait_recv()

    chain_begin(0, attn_ref, attn_out.at[mine])
    own_attn = pltpu.make_async_copy(attn_ref, attn_out.at[mine], local_sem.at[0])
    own_attn.start()
    own_outer = pltpu.make_async_copy(outer_ref, outer_out.at[own_tokens], local_sem.at[2])
    own_outer.start()
    own_routes = pltpu.make_async_copy(routes_ref, routes_out.at[own_tokens], local_sem.at[3])
    own_routes.start()
    for d in range(1, ep):
        send(
            remote(
                routes_ref, routes_out.at[own_tokens], z_send.at[4, d - 1], z_recv.at[4, d - 1], line[d - 1]
            )
        )
    for kind, ref in enumerate((gate_ref, up_ref, down_ref)):
        for e in range(local):
            target = expert_out.at[mine, pl.ds((kind * local + e) * hidden, hidden)]
            pltpu.make_async_copy(ref.at[f * local + e], target, local_sem.at[1]).start()
    own_attn.wait()
    spread(0, f)

    length = segment_ref.shape[1]
    seg_keys = segment_ref[...].astype(jnp.float32)
    seg_here = segment_ref[:, pl.ds(pl.multiple_of(c * tokens, 128), tokens)].astype(jnp.float32)
    seg_queries = jnp.broadcast_to(seg_here, (128, tokens)).T[:, :1]
    key_order = lax.broadcasted_iota(jnp.int32, (tokens, length), 1)
    query_order = lax.broadcasted_iota(jnp.int32, (tokens, length), 0) + c * tokens
    same = seg_keys == seg_queries
    seen = same & (key_order <= query_order)
    bias_s[...] = jnp.where(seen, 0.0, MASKED_SCORE)
    place = jnp.sum(jnp.where(same & (key_order < query_order), 1.0, 0.0), -1, keepdims=True)
    angle = place * freq_ref[...]
    lane = lax.broadcasted_iota(jnp.int32, (tokens, 128), 1)
    first_half = lax.rem(lane, HD) < HD // 2
    cosine = jnp.cos(angle)
    sine = jnp.where(first_half, -jnp.sin(angle), jnp.sin(angle))
    cos_out[...] = cosine
    sin_out[...] = sine
    inputs = input_ref[...].astype(jnp.float32)
    inverse = lax.rsqrt(jnp.mean(inputs * inputs, -1, keepdims=True) + EPSILON)

    pass_on(0, f)
    for hop in range(1, ep):
        for way in range(2):
            g, there = chain_origin(way, hop)
            chain_hop(0, way, hop, attn_out.at[shard_rows(g, c)])
            spread(0, g, there)
        if hop > 1:
            for way in range(2):
                pass_on(0, *chain_origin(way, hop - 1))
    for way in range(2):
        pass_on(0, *chain_origin(way, ep - 1))
    for d in range(1, ep):
        for kind, ref in enumerate((gate_ref, up_ref, down_ref)):
            for e in range(local):
                target = expert_out.at[mine, pl.ds((kind * local + e) * hidden, hidden)]
                remote(
                    ref.at[peer(d) * local + e], target, z_send.at[1, d - 1], z_recv.at[1, d - 1],
                    line[d - 1],
                ).start()
    pltpu.make_async_copy(expert_out.at[mine], expert_out.at[mine], local_sem.at[1]).wait()
    spread(1, f)
    settle(0)

    gains = attn_out[:, qkv_width : qkv_width + 128].astype(jnp.float32).T
    normed1_out[...] = (inputs * inverse * gains[EXPERTS : EXPERTS + 1, :]).astype(low)

    def project(start):
        return jnp.dot(
            normed1_out[...], attn_out[:, start : start + 256], preferred_element_type=jnp.float32
        )

    def turned(tile):
        swapped = jnp.where(first_half, pltpu.roll(tile, 128 - HD // 2, 1), pltpu.roll(tile, HD // 2, 1))
        return tile * cos_out[...] + swapped * sin_out[...]

    here = pl.ds(pl.multiple_of(c * tokens, 16), tokens)
    for start in range(0, kv_width, 256):
        tile = project(width + start)
        for side in (0, 128):
            pair_out[here, start + side : start + side + 128] = turned(tile[:, side : side + 128]).astype(low)
    for start in range(0, kv_width, 256):
        pair_out[here, kv_width + start : kv_width + start + 256] = project(width + kv_width + start).astype(low)
    for k in (3, 1, 2):
        send(remote(pair_out.at[here], pair_out.at[here], key_send.at[k - 1], key_recv.at[k - 1], plane[k - 1]))
    for start in range(0, width, 256):
        tile = project(start)
        for side in (0, 128):
            query_out[:, start + side : start + side + 128] = turned(tile[:, side : side + 128]).astype(low)
    for h in range(heads):
        query_s[h] = query_out[:, h * HD : (h + 1) * HD]
    for k in range(1, 4):
        block = pair_out.at[pl.ds(pl.multiple_of((c ^ k) * tokens, 16), tokens)]
        remote(block, block, key_send.at[k - 1], key_recv.at[k - 1], plane[k - 1]).wait_recv()
    for g in range(key_heads):
        key_s[g] = pair_out[:, g * HD : (g + 1) * HD]
        value_s[g] = pair_out[:, kv_width + g * HD : kv_width + (g + 1) * HD]
    pass_on(1, f)
    for d in range(1, ep):
        z_arrival(1, d)
        spread(1, peer(ep - d))
    line_send(2, outer_ref.at[my_half], outer_out)

    def attend(h, carry):
        g = lax.div(h, heads // key_heads)
        query = query_s[h] * jnp.asarray(HD**-0.5, low)
        scores = lax.dot_general(
            query, key_s[g], (((1,), (1,)), ((), ())), preferred_element_type=jnp.float32
        ) + bias_s[...]
        top = jnp.max(scores, -1, keepdims=True)
        weights = jnp.exp(scores - top)
        total = jnp.sum(weights, -1, keepdims=True)
        summed = jnp.dot(weights.astype(low), value_s[g], preferred_element_type=jnp.float32)
        mixed_s[h] = (summed / total).astype(low)
        log_out[h] = jnp.broadcast_to(top + jnp.log(total), (tokens, 128)).T[:1, :]
        return carry

    lax.fori_loop(0, heads, attend, 0)
    for h in range(heads):
        mixed_out[:, h * HD : (h + 1) * HD] = mixed_s[h]
    model = input_ref.shape[1]
    for start in range(0, model, 256):
        part_s[:, start : start + 256] = lax.dot_general(
            mixed_out[...], attn_out[start : start + 256, qkv_width + 128 :],
            (((1,), (1,)), ((), ())), preferred_element_type=jnp.float32,
        ).astype(low)
    exchange = remote(part_s, other_s, pair_send, pair_recv, core)
    send(exchange)
    pass_on(1, peer(ep - 1))
    exchange.wait_recv()
    middle = input_ref[...].astype(jnp.float32) + (
        part_s[...].astype(jnp.float32) + other_s[...].astype(jnp.float32)
    )
    middle_out[...] = middle
    inverse = lax.rsqrt(jnp.mean(middle * middle, -1, keepdims=True) + EPSILON)
    gains = attn_out[:, qkv_width : qkv_width + 128].astype(jnp.float32).T
    normed2_s[...] = (middle * inverse * gains[EXPERTS + 1 : EXPERTS + 2, :]).astype(low)
    chain_begin(1, normed2_s.at[my_half], normed2_out.at[line_place(f, t)])
    own_normed2 = pltpu.make_async_copy(normed2_s, normed2_out.at[own_tokens], local_sem.at[4])
    own_normed2.start()
    for d in range(2, ep):
        pass_on(1, peer(ep - d))
    for hop in range(1, ep):
        for way in range(2):
            g, there = chain_origin(way, hop)
            block = normed2_out.at[line_place(g, t)]
            chain_hop(1, way, hop, block)
            send(remote(block, block, core_send.at[1, g], core_recv.at[1, g], core), there)
    line_forward(2, outer_out)
    settle(1)
    line_settle(2, outer_out)
    for g in range(ep):
        block = normed2_out.at[line_place(g, 1 - t)]
        await_arrival(remote(block, block, core_send.at[1, g], core_recv.at[1, g], core), f != g)
    for d in range(1, ep):
        place = pl.ds(pl.multiple_of(peer(ep - d) * tokens, 16), tokens)
        remote(
            routes_out.at[place], routes_out.at[place], z_send.at[4, d - 1], z_recv.at[4, d - 1], core
        ).wait_recv()
        remote(
            expert_out.at[mine], expert_out.at[mine], z_send.at[1, d - 1], z_recv.at[1, d - 1], core
        ).wait_send()
    extra_out[...] = attn_out[:, qkv_width : qkv_width + 128]
    own_outer.wait()
    own_routes.wait()
    own_normed2.wait()
    all_sent(sent)


def front(attn, gate, up, down, outer, routes, inputs, segments, freq, heads, key_heads):
    ep = lax.axis_size("fsdp")
    rows = attn.shape[0]
    total = rows * ep * lax.axis_size("ctx")
    local = gate.shape[0] // ep
    tokens, model = inputs.shape
    length = segments.shape[1]
    low = jnp.bfloat16
    dma = pltpu.SemaphoreType.DMA
    anywhere = pl.BlockSpec(memory_space=pl.ANY)
    vmem = pl.BlockSpec(memory_space=pltpu.VMEM)
    shape = jax.ShapeDtypeStruct
    return pl.pallas_call(
        front_kernel,
        out_shape=(
            shape((total, 3 * local * gate.shape[2]), low),
            shape((ep * tokens, model), low),
            shape((ep * tokens, routes.shape[1]), routes.dtype),
            shape((ep * tokens, model), low),
            shape((total, attn.shape[1]), low),
            shape((tokens, model), low),
            shape((tokens, heads * HD), low),
            shape((length, 2 * key_heads * HD), low),
            shape((tokens, heads * HD), low),
            shape((heads, 1, tokens), jnp.float32),
            shape((tokens, model), jnp.float32),
            shape((tokens, 128), jnp.float32),
            shape((tokens, 128), jnp.float32),
            shape((total, 128), low),
        ),
        in_specs=[anywhere] * 6 + [vmem] * 3,
        out_specs=(anywhere,) * 4 + (vmem,) * 10,
        scratch_shapes=[
            pltpu.VMEM((heads, tokens, HD), low),
            pltpu.VMEM((key_heads, length, HD), low),
            pltpu.VMEM((key_heads, length, HD), low),
            pltpu.VMEM((heads, tokens, HD), low),
            pltpu.VMEM((tokens, length), jnp.float32),
            pltpu.VMEM((tokens, model), low),
            pltpu.VMEM((tokens, model), low),
            pltpu.VMEM((tokens, model), low),
            dma((5,)),
            dma((5, ep - 1)),
            dma((5, ep - 1)),
            dma((2, ep, 2, 2)),
            dma((2, ep, 2, 2)),
            dma((2, ep, 2)),
            dma((2, ep, 2)),
            dma((2, ep)),
            dma((2, ep)),
            dma((3,)),
            dma((3,)),
            dma,
            dma,
            dma((2, 2, ep - 1)),
            dma((2, 2, ep - 1)),
        ],
        compiler_params=pltpu.CompilerParams(
            collective_id=1, has_side_effects=True, vmem_limit_bytes=56 * 1024 * 1024
        ),
        cost_estimate=lasting(180),
        name="front",
    )(attn, gate, up, down, outer, routes, inputs, segments, freq)


def z_sum_scratch(ep, tokens, width, low):
    dma = pltpu.SemaphoreType.DMA
    return [
        pltpu.VMEM((ep, tokens // 2, width), low),
        pltpu.VMEM((ep - 1, tokens // 2, width), low),
        pltpu.VMEM((ep - 1, tokens // 2, width), low),
        dma((ep,)),
        dma((ep,)),
        dma((ep - 1,)),
        dma((ep - 1,)),
        dma,
        dma,
    ]


class ZSum:
    size = 9

    def __init__(self, part, scratch, sent, own=None):
        self.part, self.own, self.sent = part, own, sent
        (
            self.core_in, self.z_out, self.z_in, self.core_send, self.core_recv,
            self.z_send, self.z_recv, self.back_send, self.back_recv,
        ) = scratch
        self.ep, self.half = self.core_in.shape[0], self.core_in.shape[1]
        self.f, self.c, self.t = lax.axis_index("fsdp"), lax.axis_index("ctx"), lax.axis_index("tp")
        self.core = at_device(self.f, self.c, 1 - self.t)

    def peer(self, distance):
        return lax.rem(self.f + distance, self.ep)

    def place(self, fsdp, part):
        return pl.ds(pl.multiple_of(fsdp * 2 * self.half + part * self.half, 16), self.half)

    def rows(self, part):
        return pl.ds(pl.multiple_of(part * self.half, 16), self.half)

    def send(self, copy):
        copy.start()
        self.sent.append((None, copy))

    def to_core(self, d):
        self.send(
            remote(
                self.part.at[self.place(self.peer(d), 1 - self.t), pl.ds(0, self.core_in.shape[2])],
                self.core_in.at[d],
                self.core_send.at[d], self.core_recv.at[d], self.core,
            )
        )

    def added(self, d):
        landing = self.core_in.at[d]
        remote(landing, landing, self.core_send.at[d], self.core_recv.at[d], self.core).wait_recv()
        if self.own is None:
            mine = self.part[self.place(self.peer(d), self.t), : self.core_in.shape[2]]
        else:
            mine = self.own[d]
        return mine.astype(jnp.float32) + self.core_in[d].astype(jnp.float32)

    def to_z(self, d):
        self.z_out[d - 1] = self.added(d).astype(self.z_out.dtype)
        self.send(
            remote(
                self.z_out.at[d - 1], self.z_in.at[d - 1], self.z_send.at[d - 1], self.z_recv.at[d - 1],
                at_device(self.peer(d), self.c, self.t),
            )
        )

    def collect(self):
        total = self.added(0)
        for d in range(1, self.ep):
            landing = self.z_in.at[d - 1]
            remote(landing, landing, self.z_send.at[d - 1], self.z_recv.at[d - 1], self.core).wait_recv()
            total = total + self.z_in[d - 1].astype(jnp.float32)
        return total

    def share(self, out):
        mine = out.at[self.rows(self.t)]
        self.send(remote(mine, mine, self.back_send, self.back_recv, self.core))

    def finish(self, out):
        other = out.at[self.rows(1 - self.t)]
        remote(other, other, self.back_send, self.back_recv, self.core).wait_recv()


def all_sent(sent):
    for when, copy in sent:
        if when is None:
            copy.wait_send()
        else:
            pl.when(when)(copy.wait_send)


def shard_sum_scratch(ep, rows, width, low):
    cut = first_columns(width)
    widths = [cut] if cut == width else [cut, width - cut]
    dma = pltpu.SemaphoreType.DMA
    scratch = []
    for part in widths:
        scratch += [
            pltpu.VMEM((ep, 2, rows, part), low),
            pltpu.VMEM((ep, rows, part), low),
            pltpu.VMEM((ep - 1, rows, part), low),
        ]
    return scratch + [
        dma((2, ep, 2)), dma((2, ep, 2)), dma((2, ep)), dma((2, ep)), dma((2, ep)), dma((2, ep))
    ]


def first_columns(width):
    return width if width == 128 else -(-width // 256) * 128


class ShardSum:
    def __init__(self, part, rows, width, scratch, sent):
        self.part, self.rows, self.sent = part, rows, sent
        cut = first_columns(width)
        self.columns = [pl.ds(0, cut)] + ([] if cut == width else [pl.ds(cut, width - cut)])
        self.ways = range(len(self.columns))
        (
            self.first_send, self.first_recv, self.second_send, self.second_recv, self.z_send, self.z_recv
        ) = scratch[-6:]
        self.first_in = [scratch[3 * way] for way in self.ways]
        self.second_in = [scratch[3 * way + 1] for way in self.ways]
        self.z_in = [scratch[3 * way + 2] for way in self.ways]
        self.ep = self.first_in[0].shape[0]
        self.f, self.c, self.t = lax.axis_index("fsdp"), lax.axis_index("ctx"), lax.axis_index("tp")
        self.neighbours = (at_device(self.f, self.c ^ 1, self.t), at_device(self.f, self.c ^ 2, self.t))
        self.order = list(range(1, self.ep)) + [0]

    def peer(self, distance):
        return lax.rem(self.f + distance, self.ep)

    def block(self, distance, ctx, way):
        start = (self.peer(distance) * 4 + ctx) * self.rows
        return pl.ds(pl.multiple_of(start, 16), self.rows), self.columns[way]

    def send(self, copy):
        copy.start()
        self.sent.append((None, copy))

    def first(self, d):
        for number in range(2):
            for way in self.ways:
                target = self.c ^ 3 if number == 0 else self.c ^ (1 << way)
                self.send(
                    remote(
                        self.part.at[self.block(d, target, way)], self.first_in[way].at[d, number],
                        self.first_send.at[way, d, number], self.first_recv.at[way, d, number],
                        self.neighbours[way],
                    )
                )

    def second(self, d):
        for way in self.ways:
            for number in range(2):
                landing = self.first_in[way].at[d, number]
                remote(
                    landing, landing, self.first_send.at[way, d, number],
                    self.first_recv.at[way, d, number], self.neighbours[way],
                ).wait_recv()
            term = self.part[self.block(d, self.c ^ (2 >> way), way)]
            added = term.astype(jnp.float32) + self.first_in[way][d, 0].astype(jnp.float32)
            self.first_in[way][d, 0] = added.astype(self.part.dtype)
            self.send(
                remote(
                    self.first_in[way].at[d, 0], self.second_in[way].at[d],
                    self.second_send.at[way, d], self.second_recv.at[way, d], self.neighbours[1 - way],
                )
            )

    def total(self, d, way):
        landing = self.second_in[way].at[d]
        remote(
            landing, landing, self.second_send.at[way, d], self.second_recv.at[way, d], self.neighbours[1 - way]
        ).wait_recv()
        term = self.part[self.block(d, self.c, way)]
        return (
            term.astype(jnp.float32)
            + self.first_in[way][d, 1].astype(jnp.float32)
            + self.second_in[way][d].astype(jnp.float32)
        )

    def to_z(self, d, out):
        for way in self.ways:
            total = self.total(d, way)
            if d == 0:
                out[:, self.columns[way]] = total
                continue
            self.first_in[way][d, 1] = total.astype(self.part.dtype)
            self.send(
                remote(
                    self.first_in[way].at[d, 1], self.z_in[way].at[d - 1],
                    self.z_send.at[way, d], self.z_recv.at[way, d], at_device(self.peer(d), self.c, self.t),
                )
            )

    def from_z(self, out):
        for way in self.ways:
            for d in range(1, self.ep):
                landing = self.z_in[way].at[d - 1]
                remote(
                    landing, landing, self.z_send.at[way, d], self.z_recv.at[way, d], self.neighbours[0]
                ).wait_recv()
                out[:, self.columns[way]] += self.z_in[way][d - 1].astype(jnp.float32)


def all_partners(ep):
    f, c, t = lax.axis_index("fsdp"), lax.axis_index("ctx"), lax.axis_index("tp")
    line = [at_device(lax.rem(f + d, ep), c, t) for d in range(1, ep)]
    return line + [at_device(f, c ^ 1, t), at_device(f, c ^ 2, t), at_device(f, c, 1 - t)]


class PlaneHalf:
    def __init__(self, part, rows, landings, send_sem, recv_sem, sent):
        self.part, self.rows, self.landings, self.sent = part, rows, landings, sent
        self.send_sem, self.recv_sem = send_sem, recv_sem
        cut = landings[0].shape[-1]
        self.columns = (pl.ds(0, cut), pl.ds(cut, part.shape[1] - cut))
        self.ep = landings[0].shape[0]
        self.f, self.c, t = lax.axis_index("fsdp"), lax.axis_index("ctx"), lax.axis_index("tp")
        self.neighbours = (at_device(self.f, self.c ^ 1, t), at_device(self.f, self.c ^ 2, t))

    def block(self, distance, ctx, way):
        start = (lax.rem(self.f + distance, self.ep) * 4 + ctx) * self.rows
        return pl.ds(pl.multiple_of(start, 16), self.rows), self.columns[way]

    def start(self, d):
        for number in range(2):
            for way in range(2):
                target = self.c ^ 3 if number == 0 else self.c ^ (1 << way)
                copy = remote(
                    self.part.at[self.block(d, target, way)], self.landings[way].at[d, number],
                    self.send_sem.at[way, d, number], self.recv_sem.at[way, d, number], self.neighbours[way],
                )
                copy.start()
                self.sent.append((None, copy))

    def finish(self, d):
        for way in range(2):
            for number in range(2):
                landing = self.landings[way].at[d, number]
                remote(
                    landing, landing, self.send_sem.at[way, d, number], self.recv_sem.at[way, d, number],
                    self.neighbours[way],
                ).wait_recv()
                ctx = self.c ^ (2 >> way) if number == 0 else self.c
                term = self.part[self.block(d, ctx, way)].astype(jnp.float32)
                added = term + self.landings[way][d, number].astype(jnp.float32)
                self.landings[way][d, number] = added.astype(self.part.dtype)


def experts_kernel(
    tokens_ref, outer_ref, routes_ref, extra_ref, weight_ref,
    returned_ref, mixed_ref, mixture_out, relay_out, own_out, gates_out,
    gates_s, gated_s, side_s, part_s, mixture_s, sums_s, first_x, first_y, plane_send, plane_recv, local_sem, *scratch,
):
    ep = lax.axis_size("fsdp")
    f = lax.axis_index("fsdp")
    low = jnp.bfloat16
    reach, model = tokens_ref.shape
    span = weight_ref.shape[1] // 3
    tokens = reach // ep
    rows = model // (4 * ep)
    local = EXPERTS // ep
    hidden = span // local
    sent = []
    back = ZSum(part_s, scratch[: ZSum.size], sent)
    mixture = ZSum(mixture_s, scratch[ZSum.size :], sent)
    plane = PlaneHalf(sums_s, rows, (first_x, first_y), plane_send, plane_recv, sent)
    greet(all_partners(ep))

    lane = lax.broadcasted_iota(jnp.int32, (reach, 128), 1)
    chosen = routes_ref[:, 0:1] == lane
    for k in range(1, routes_ref.shape[1]):
        chosen = chosen | (routes_ref[:, k : k + 1] == lane)
    logits = jnp.dot(tokens_ref[...], extra_ref[...], preferred_element_type=jnp.float32)
    logits = jnp.where(chosen, logits, MASKED_SCORE)
    lifted = jnp.where(chosen, jnp.exp(logits - jnp.max(logits, -1, keepdims=True)), 0.0)
    gates_s[...] = lifted / jnp.sum(lifted, -1, keepdims=True)
    own = pl.ds(pl.multiple_of(f * tokens, 16), tokens)
    gates_out[...] = gates_s[own, :]

    part_s[:, model:] = jnp.zeros((reach, 128), low)
    for e in range(local):
        at = slice(e * hidden, (e + 1) * hidden)
        at_up = slice(span + e * hidden, span + (e + 1) * hidden)
        at_down = slice(2 * span + e * hidden, 2 * span + (e + 1) * hidden)
        mine = lane == f * local + e
        gate = jnp.sum(jnp.where(mine, gates_s[...], 0.0), -1, keepdims=True)
        former = jnp.dot(tokens_ref[...], weight_ref[:, at], preferred_element_type=jnp.float32)
        latter = jnp.dot(tokens_ref[...], weight_ref[:, at_up], preferred_element_type=jnp.float32)
        grad = jnp.dot(outer_ref[...], weight_ref[:, at_down], preferred_element_type=jnp.float32)
        logistic = 1.0 / (1.0 + jnp.exp(-former))
        active = former * logistic
        value = (active * latter).astype(low).astype(jnp.float32)
        gated_s[:, at] = (value * gate).astype(low)
        picked = jnp.sum(value * grad, -1, keepdims=True)
        dgate = jnp.where(mine & (gate > 0.0), picked, 0.0)
        high = dgate.astype(low).astype(jnp.float32)
        part_s[:, model:] += (high + pltpu.roll(dgate - high, EXPERTS, 1)).astype(low)
        grad = grad * gate
        side_s[:, at] = (grad * latter * logistic * (1.0 + former * (1.0 - logistic))).astype(low)
        side_s[:, at_up] = (grad * active).astype(low)

    order = list(range(1, ep)) + [0]
    over = (((0,), (0,)), ((), ()))
    across = (((1,), (1,)), ((), ()))

    def mixtures(n, carry):
        at = pl.ds(pl.multiple_of(n * 256, 256), 256)
        mixture_s[:, at] = lax.dot_general(
            gated_s[...], weight_ref[at, 2 * span :], across, preferred_element_type=jnp.float32
        ).astype(low)
        return carry

    for step, d in enumerate(order):
        if step == 1:
            lax.fori_loop(0, model // 256, mixtures, 0)
            for g in order:
                mixture.to_core(g)
            later = pltpu.make_async_copy(mixture_s.at[:, pl.ds(EARLY, model - EARLY)], mixture_out, local_sem.at[2])
            later.start()
        if step > 1:
            mixture.to_z(order[step - 2])
        at = pl.ds(pl.multiple_of(back.peer(d) * 4 * rows, 128), 4 * rows)
        sums_s[at, : 2 * span] = lax.dot_general(
            tokens_ref[:, at], side_s[...], over, preferred_element_type=jnp.float32
        ).astype(low)
        sums_s[at, 2 * span :] = lax.dot_general(
            outer_ref[:, at], gated_s[...], over, preferred_element_type=jnp.float32
        ).astype(low)
        plane.start(d)

    mixture.to_z(order[2])
    for step, d in enumerate(order):
        here = pl.ds(pl.multiple_of(back.peer(d) * tokens, 16), tokens)

        def tile(n, carry):
            at = pl.ds(pl.multiple_of(n * 256, 256), 256)
            part_s[here, at] = lax.dot_general(
                side_s[here, :], weight_ref[at, : 2 * span], across, preferred_element_type=jnp.float32
            ).astype(low)
            return carry

        lax.fori_loop(0, model // 256, tile, 0)
        back.to_core(d)
        if step > 0:
            back.to_z(order[step - 1])

    for d in order:
        plane.finish(d)
        for way in range(2):
            for number, out in enumerate((relay_out, own_out)):
                pltpu.make_async_copy(
                    plane.landings[way].at[d, number], out.at[d, :, plane.columns[way]], local_sem.at[number]
                ).start()
    returned_ref[back.rows(back.t), :] = back.collect()
    back.share(returned_ref)
    mixed_ref[...] = mixture.collect()
    later.wait()
    back.finish(returned_ref)
    for number, out in enumerate((relay_out, own_out)):
        pltpu.make_async_copy(out, out, local_sem.at[number]).wait()
    all_sent(sent)


def run_experts(tokens_all, outer_all, routes_all, extra, weights, collective_id):
    ep = lax.axis_size("fsdp")
    reach, model = tokens_all.shape
    tokens, low = reach // ep, tokens_all.dtype
    rows = model // (4 * ep)
    full = weights.shape[1]
    span = full // 3
    dma = pltpu.SemaphoreType.DMA
    anywhere = pl.BlockSpec(memory_space=pl.ANY)
    vmem = pl.BlockSpec(memory_space=pltpu.VMEM)
    shape = jax.ShapeDtypeStruct
    return pl.pallas_call(
        experts_kernel,
        out_shape=(
            shape((tokens, model + 128), jnp.float32),
            shape((tokens // 2, EARLY), jnp.float32),
            shape((reach, model - EARLY), low),
            shape((ep, rows, full), low),
            shape((ep, rows, full), low),
            shape((tokens, 128), jnp.float32),
        ),
        in_specs=[vmem] * 5,
        out_specs=(vmem, vmem, anywhere, anywhere, anywhere, vmem),
        scratch_shapes=[
            pltpu.VMEM((reach, 128), jnp.float32),
            pltpu.VMEM((reach, span), low),
            pltpu.VMEM((reach, 2 * span), low),
            pltpu.VMEM((reach, model + 128), low),
            pltpu.VMEM((reach, model), low),
            pltpu.VMEM(weights.shape, low),
            pltpu.VMEM((ep, 2, rows, full // 2), low),
            pltpu.VMEM((ep, 2, rows, full // 2), low),
            dma((2, ep, 2)),
            dma((2, ep, 2)),
            dma((3,)),
        ]
        + z_sum_scratch(ep, tokens, model + 128, low)
        + z_sum_scratch(ep, tokens, EARLY, low),
        compiler_params=pltpu.CompilerParams(
            collective_id=collective_id, has_side_effects=True, vmem_limit_bytes=63 * 1024 * 1024
        ),
        cost_estimate=lasting(90),
        name="experts",
    )(tokens_all, outer_all, routes_all, extra, weights)


def rear_kernel(
    returned_ref, gates_ref, middle_ref, input_ref, outer_ref, normed1_ref, query_ref, pair_ref, mixed_ref,
    log_ref, cos_ref, sin_ref, segment_ref, extra_ref, mixed_sum_ref, mixture_ref, relay_ref, own_ref, attn_ref,
    input_grad, layer_out, qkv_out, wo_out, expert_out,
    wo_s, qkv_s, query_s, grad_s, mixed_s, key_s, value_s, bias_s, query_grad_s, key_grad_s, value_grad_s,
    pair_s, landing_s, back_s, attn_grad_s, part_s, other_s, router_s, gains_s, mixture_s, own_s, second_s,
    local_sem, key_send, key_recv, pair_send, pair_recv, second_send, second_recv, swap_send, swap_recv, *scratch,
):
    ep, rows = expert_out.shape[0], expert_out.shape[1]
    f, c, t = lax.axis_index("fsdp"), lax.axis_index("ctx"), lax.axis_index("tp")
    low = jnp.bfloat16
    tokens, model = input_ref.shape
    heads, key_heads = query_s.shape[0], key_s.shape[0]
    groups = heads // key_heads
    width, kv_width = heads * HD, key_heads * HD
    qkv_width = width + 2 * kv_width
    sent = []
    mixture = ZSum(mixture_ref, scratch[: ZSum.size], sent, mixture_s)
    scratch = scratch[ZSum.size :]
    size = len(shard_sum_scratch(ep, rows, 256, low))
    wo = ShardSum(wo_s, rows, width, scratch[:size], sent)
    qkv = ShardSum(qkv_s, rows, qkv_width + 128, scratch[size:], sent)
    partners = all_partners(ep)
    plane = [at_device(f, c ^ k, t) for k in range(1, 4)]
    core = partners[-1]

    copies = [
        pltpu.make_async_copy(attn_ref.at[:, pl.ds(qkv_width + 128, width)], wo_s, local_sem.at[0]),
        pltpu.make_async_copy(attn_ref.at[:, pl.ds(0, qkv_width + 128)], qkv_s, local_sem.at[1]),
    ]
    for copy in copies:
        copy.start()
    for d in range(ep):
        pltpu.make_async_copy(
            mixture_ref.at[mixture.place(mixture.peer(d), t)], mixture_s.at[d], local_sem.at[2]
        ).start()
    copies.append(pltpu.make_async_copy(own_ref, own_s, local_sem.at[3]))
    copies[2].start()
    greet(partners + plane[2:])
    order = wo.order
    for d in order:
        mixture.to_core(d)
    full = relay_ref.shape[2]
    seconds = {}

    def second(d):
        for way in range(2):
            block = (d, slice(None), pl.ds(way * (full // 2), full // 2))
            copy = remote(
                relay_ref.at[block], second_s.at[block], second_send.at[way, d], second_recv.at[way, d],
                plane[1 - way],
            )
            copy.start()
            sent.append((None, copy))
            seconds[way, d] = copy

    def swap(d):
        for way in range(2):
            seconds[way, d].wait_recv()
        own_s[d] = (own_s[d].astype(jnp.float32) + second_s[d].astype(jnp.float32)).astype(low)
        if d == 0:
            copy = pltpu.make_async_copy(own_s.at[0], expert_out.at[f], swap_send.at[0])
            copy.start()
            copies.append(copy)
        else:
            copy = remote(own_s.at[d], expert_out.at[f], swap_send.at[d], swap_recv.at[d], partners[d - 1])
            copy.start()
            sent.append((None, copy))

    for d in order:
        second(d)

    small_lane = lax.broadcasted_iota(jnp.int32, (tokens, 128), 1)
    gains = extra_ref[...].astype(jnp.float32).T
    gain_one, gain_two = gains[EXPERTS : EXPERTS + 1, :], gains[EXPERTS + 1 : EXPERTS + 2, :]
    tail = returned_ref[:, model:]
    picked = jnp.where(small_lane < EXPERTS, tail + pltpu.roll(tail, 128 - EXPERTS, 1), 0.0)
    gates = gates_ref[...]
    logit_grad = (gates * (picked - jnp.sum(gates * picked, -1, keepdims=True))).astype(low)
    second_grad = returned_ref[:, :model] + lax.dot_general(
        logit_grad, extra_ref[...], (((1,), (1,)), ((), ())), preferred_element_type=jnp.float32
    )
    middle = middle_ref[...]
    inverse = lax.rsqrt(jnp.mean(middle * middle, -1, keepdims=True) + EPSILON)
    scaled = second_grad * gain_two
    mean_term = jnp.mean(scaled * middle, -1, keepdims=True)
    gains_s[1:2, :] = jnp.sum(second_grad * middle * inverse, 0, keepdims=True)
    middle_grad = outer_ref[...].astype(jnp.float32) + (
        inverse * scaled - middle * (inverse * inverse * inverse) * mean_term
    )
    input_grad[...] = middle_grad
    attn_grad_s[...] = middle_grad.astype(low)

    pltpu.make_async_copy(mixture_s, mixture_s, local_sem.at[2]).wait()
    for d in range(1, ep):
        mixture.to_z(d)
    copies[0].wait()
    for start in range(0, width, 256):
        tile = jnp.dot(
            attn_grad_s[...], wo_s[:, start : start + 256], preferred_element_type=jnp.float32
        ).astype(low)
        for side in range(0, 256, HD):
            grad_s[(start + side) // HD] = tile[:, side : side + HD]

    length = segment_ref.shape[1]
    seg_keys = jnp.broadcast_to(segment_ref[...].astype(jnp.float32), (128, length)).T[:, :1]
    seg_queries = segment_ref[:, pl.ds(pl.multiple_of(c * tokens, 128), tokens)].astype(jnp.float32)
    key_order = lax.broadcasted_iota(jnp.int32, (length, tokens), 0)
    query_order = lax.broadcasted_iota(jnp.int32, (length, tokens), 1) + c * tokens
    bias_s[...] = jnp.where((seg_keys == seg_queries) & (key_order <= query_order), 0.0, MASKED_SCORE)
    for h in range(heads):
        query_s[h] = query_ref[:, h * HD : (h + 1) * HD]
        mixed_s[h] = mixed_ref[:, h * HD : (h + 1) * HD]
    for g in range(key_heads):
        key_s[g] = pair_ref[:, g * HD : (g + 1) * HD]
        value_s[g] = pair_ref[:, kv_width + g * HD : kv_width + (g + 1) * HD]
    across = (((1,), (1,)), ((), ()))

    def attend_back(g, carry):
        key_grad = jnp.zeros((length, HD), jnp.float32)
        value_grad = jnp.zeros((length, HD), jnp.float32)
        for number in range(groups):
            h = g * groups + number
            query = query_s[h] * jnp.asarray(HD**-0.5, low)
            grad = grad_s[h]
            scores = lax.dot_general(key_s[g], query, across, preferred_element_type=jnp.float32) + bias_s[...]
            probs = jnp.exp(scores - log_ref[h])
            value_grad += jnp.dot(probs.astype(low), grad, preferred_element_type=jnp.float32)
            prob_grad = lax.dot_general(value_s[g], grad, across, preferred_element_type=jnp.float32)
            delta = jnp.sum((grad.astype(jnp.float32) * mixed_s[h].astype(jnp.float32)).T, 0, keepdims=True)
            score_grad = (probs * (prob_grad - delta)).astype(low)
            key_grad += jnp.dot(score_grad, query, preferred_element_type=jnp.float32)
            query_grad = lax.dot_general(
                key_s[g], score_grad, (((0,), (0,)), ((), ())), preferred_element_type=jnp.float32
            )
            query_grad_s[h] = query_grad.T * (HD**-0.5)
        key_grad_s[g] = key_grad.astype(low)
        value_grad_s[g] = value_grad.astype(low)
        return carry

    lax.fori_loop(0, key_heads, attend_back, 0)
    for g in range(key_heads):
        pair_s[:, g * HD : (g + 1) * HD] = key_grad_s[g]
        pair_s[:, kv_width + g * HD : kv_width + (g + 1) * HD] = value_grad_s[g]
    for k in (3, 1, 2):
        place = pl.ds(pl.multiple_of((c ^ k) * tokens, 16), tokens)
        copy = remote(pair_s.at[place], landing_s.at[k - 1], key_send.at[k - 1], key_recv.at[k - 1], plane[k - 1])
        copy.start()
        sent.append((None, copy))
    def wo_sums(n, carry):
        at = pl.ds(pl.multiple_of(n * 256, 256), 256)
        wo_s[at, :] = lax.dot_general(
            attn_grad_s[:, at], mixed_ref[...], (((0,), (0,)), ((), ())), preferred_element_type=jnp.float32
        ).astype(low)
        return carry

    lax.fori_loop(0, model // 256, wo_sums, 0)
    router_s[...] = lax.dot_general(
        (middle * inverse * gain_two).astype(low), logit_grad, (((0,), (0,)), ((), ())),
        preferred_element_type=jnp.float32,
    )

    copies[2].wait()
    for d in order:
        wo.first(d)
    for d in order:
        swap(d)
    first_half = lax.rem(small_lane, HD) < HD // 2

    def turned_back(tile):
        swapped = jnp.where(first_half, pltpu.roll(tile, 128 - HD // 2, 1), pltpu.roll(tile, HD // 2, 1))
        return tile * cos_ref[...] - swapped * sin_ref[...]

    for start in range(0, width, 128):
        tile = jnp.concatenate([query_grad_s[start // HD], query_grad_s[start // HD + 1]], 1)
        back_s[:, start : start + 128] = turned_back(tile).astype(low)

    pair = pair_s[pl.ds(pl.multiple_of(c * tokens, 16), tokens), :].astype(jnp.float32)
    for k in (1, 2, 3):
        block = landing_s.at[k - 1]
        remote(block, block, key_send.at[k - 1], key_recv.at[k - 1], plane[k - 1]).wait_recv()
        pair = pair + landing_s[k - 1].astype(jnp.float32)
    for start in range(0, kv_width, 128):
        back_s[:, width + start : width + start + 128] = turned_back(pair[:, start : start + 128]).astype(low)
    back_s[:, width + kv_width :] = pair[:, kv_width:].astype(low)
    copies[1].wait()
    for start in range(0, model, 256):
        part_s[:, start : start + 256] = lax.dot_general(
            back_s[...], qkv_s[start : start + 256, :qkv_width], across, preferred_element_type=jnp.float32
        ).astype(low)
    exchange = remote(part_s, other_s, pair_send, pair_recv, core)
    exchange.start()
    sent.append((None, exchange))

    def qkv_sums(n, carry):
        at = pl.ds(pl.multiple_of(n * 256, 256), 256)
        qkv_s[at, :qkv_width] = lax.dot_general(
            normed1_ref[:, at], back_s[...], (((0,), (0,)), ((), ())), preferred_element_type=jnp.float32
        ).astype(low)
        return carry

    lax.fori_loop(0, model // 256, qkv_sums, 0)
    exchange.wait_recv()
    first_grad = part_s[...].astype(jnp.float32) + other_s[...].astype(jnp.float32)
    inputs = input_ref[...].astype(jnp.float32)
    inverse = lax.rsqrt(jnp.mean(inputs * inputs, -1, keepdims=True) + EPSILON)
    gains_s[0:1, :] = jnp.sum(first_grad * inputs * inverse, 0, keepdims=True)
    line = lax.broadcasted_iota(jnp.int32, (128, model), 0)
    turned = jnp.where(line == EXPERTS, gains_s[0:1, :], jnp.where(line == EXPERTS + 1, gains_s[1:2, :], 0.0)).T
    qkv_s[:, qkv_width:] = (router_s[...] + turned).astype(low)
    qkv.first(1)
    qkv.first(2)
    for d in wo.order:
        wo.second(d)
    scaled = first_grad * gain_one
    mean_term = jnp.mean(scaled * inputs, -1, keepdims=True)
    input_grad[...] += inverse * scaled - inputs * (inverse * inverse * inverse) * mean_term
    qkv.second(1)
    qkv.first(3)
    wo.to_z(1, wo_out)
    qkv.second(2)
    qkv.first(0)
    qkv.to_z(1, qkv_out)
    wo.to_z(2, wo_out)
    qkv.second(3)
    qkv.to_z(2, qkv_out)
    wo.to_z(3, wo_out)
    qkv.second(0)
    qkv.to_z(3, qkv_out)
    wo.to_z(0, wo_out)
    qkv.to_z(0, qkv_out)
    half = mixture.rows(t)
    layer_out[half, :EARLY] = (middle_ref[half, :EARLY] + mixed_sum_ref[...]).astype(low)
    layer_out[half, EARLY:] = (middle_ref[half, EARLY:] + mixture.collect()).astype(low)
    mixture.share(layer_out)
    copies[3].wait()
    for d in range(1, ep):
        landing = expert_out.at[lax.rem(f + ep - d, ep)]
        remote(landing, landing, swap_send.at[d], swap_recv.at[d], core).wait_recv()
    wo.from_z(wo_out)
    mixture.finish(layer_out)
    qkv.from_z(qkv_out)
    all_sent(sent)


def rear(
    returned, gates, middle, inputs, outer, normed1, query, pair, mixed, log_total, cosine, sine, segments, extra,
    mixed_sum, mixture, relay, own, attn, collective_id,
):
    ep = lax.axis_size("fsdp")
    tokens, model = inputs.shape
    rows = own.shape[1]
    heads, key_heads = query.shape[1] // HD, pair.shape[1] // (2 * HD)
    width, kv_width = heads * HD, key_heads * HD
    qkv_width = width + 2 * kv_width
    length = pair.shape[0]
    low = jnp.bfloat16
    dma = pltpu.SemaphoreType.DMA
    anywhere = pl.BlockSpec(memory_space=pl.ANY)
    vmem = pl.BlockSpec(memory_space=pltpu.VMEM)
    shape = jax.ShapeDtypeStruct
    room = pltpu.VMEM
    return pl.pallas_call(
        rear_kernel,
        out_shape=(
            shape((tokens, model), jnp.float32),
            shape((tokens, model), low),
            shape((rows, qkv_width + 128), jnp.float32),
            shape((rows, width), jnp.float32),
            shape(own.shape, low),
        ),
        in_specs=[vmem] * 15 + [anywhere] * 4,
        out_specs=(vmem,) * 4 + (anywhere,),
        scratch_shapes=[
            room((model, width), low),
            room((model, qkv_width + 128), low),
            room((heads, tokens, HD), low),
            room((heads, tokens, HD), low),
            room((heads, tokens, HD), low),
            room((key_heads, length, HD), low),
            room((key_heads, length, HD), low),
            room((length, tokens), jnp.float32),
            room((heads, tokens, HD), jnp.float32),
            room((key_heads, length, HD), low),
            room((key_heads, length, HD), low),
            room((length, 2 * kv_width), low),
            room((3, tokens, 2 * kv_width), low),
            room((tokens, qkv_width), low),
            room((tokens, model), low),
            room((tokens, model), low),
            room((tokens, model), low),
            room((model, 128), jnp.float32),
            room((8, model), jnp.float32),
            room((ep, tokens // 2, model - EARLY), low),
            room(own.shape, low),
            room(own.shape, low),
            dma((4,)),
            dma((3,)),
            dma((3,)),
            dma,
            dma,
            dma((2, ep)),
            dma((2, ep)),
            dma((ep,)),
            dma((ep,)),
        ]
        + z_sum_scratch(ep, tokens, model - EARLY, low)
        + shard_sum_scratch(ep, rows, width, low)
        + shard_sum_scratch(ep, rows, qkv_width + 128, low),
        compiler_params=pltpu.CompilerParams(
            collective_id=collective_id, has_side_effects=True, vmem_limit_bytes=63 * 1024 * 1024
        ),
        cost_estimate=lasting(170),
        name="rear",
    )(
        returned, gates, middle, inputs, outer, normed1, query, pair, mixed, log_total, cosine, sine, segments,
        extra, mixed_sum, mixture, relay, own, attn,
    )


def finish_kernel(
    expert_ref, qkv_ref, wo_ref, query_out, key_out, value_out, output_out, gate_out, up_out, down_out
):
    local, _, hidden = gate_out.shape
    for e in range(local):
        for kind, out in enumerate((gate_out, up_out, down_out)):
            start = (kind * local + e) * hidden
            block = expert_ref[0, :, start : start + hidden].astype(jnp.float32)
            out[e] = block.T if kind == 2 else block

    @pl.when(pl.program_id(0) == 0)
    def _():
        width, kv_width = query_out.shape[1], key_out.shape[1]
        query_out[...] = qkv_ref[:, :width]
        key_out[...] = qkv_ref[:, width : width + kv_width]
        value_out[...] = qkv_ref[:, width + kv_width : width + 2 * kv_width]
        output_out[...] = wo_ref[...].T


def finish(experts, qkv, wo, kv_width, hidden):
    ep, rows, full = experts.shape
    width = wo.shape[1]
    local = full // (3 * hidden)
    shape = jax.ShapeDtypeStruct

    def whole(*dims):
        return pl.BlockSpec(dims, lambda i: (0, 0))

    return pl.pallas_call(
        finish_kernel,
        grid=(ep,),
        out_shape=(
            shape((rows, width), jnp.float32),
            shape((rows, kv_width), jnp.float32),
            shape((rows, kv_width), jnp.float32),
            shape((width, rows), jnp.float32),
            shape((ep * local, rows, hidden), jnp.float32),
            shape((ep * local, rows, hidden), jnp.float32),
            shape((ep * local, hidden, rows), jnp.float32),
        ),
        in_specs=[
            pl.BlockSpec((1, rows, full), lambda i: (i, 0, 0)),
            whole(*qkv.shape),
            whole(*wo.shape),
        ],
        out_specs=(
            whole(rows, width),
            whole(rows, kv_width),
            whole(rows, kv_width),
            whole(width, rows),
            pl.BlockSpec((local, rows, hidden), lambda i: (i, 0, 0)),
            pl.BlockSpec((local, rows, hidden), lambda i: (i, 0, 0)),
            pl.BlockSpec((local, hidden, rows), lambda i: (i, 0, 0)),
        ),
        compiler_params=pltpu.CompilerParams(vmem_limit_bytes=32 * 1024 * 1024),
        cost_estimate=lasting(6),
        name="finish",
    )(experts, qkv, wo)


def plain_shards(
    layer_input,
    segments,
    routes,
    norm_gain,
    query_weight,
    key_weight,
    value_weight,
    output_weight,
    ffn_gain,
    router_weight,
    gate_weight,
    up_weight,
    down_weight,
    cotangent,
):
    low = jnp.bfloat16
    both = ("fsdp", "ctx")
    ep = lax.axis_size("fsdp")
    tokens = layer_input.shape[0]
    seq_len = segments.shape[1]
    rows = query_weight.shape[0]
    width = query_weight.shape[1]
    kv_width = key_weight.shape[1]
    hidden_width = gate_weight.shape[2]
    local = EXPERTS // ep
    span = local * hidden_width

    qkv_width = width + 2 * kv_width
    extra = jnp.concatenate([router_weight, norm_gain[:, None], ffn_gain[:, None]], 1)
    extra = jnp.pad(extra, ((0, 0), (0, 128 - extra.shape[1])))
    attn_shard = jnp.concatenate([query_weight, key_weight, value_weight, extra, output_weight.T], 1)
    down_shard = down_weight.transpose(0, 2, 1)
    begin = lax.axis_index("ctx") * tokens
    segment_row = segments[0]
    query_doc = lax.dynamic_slice_in_dim(segment_row, begin, tokens)
    query_order = begin + jnp.arange(tokens, dtype=jnp.int32)
    scale = HD ** (-0.5)
    inputs = layer_input.astype(jnp.float32)
    key_groups = kv_width // HD
    groups = width // kv_width
    freq = 10000.0 ** (-2.0 * jnp.arange(HD // 2, dtype=jnp.float32) / HD)

    def unpack(attn_full):
        return (
            attn_full[:, :qkv_width],
            attn_full[:, qkv_width : qkv_width + EXPERTS],
            attn_full[:, qkv_width + EXPERTS],
            attn_full[:, qkv_width + EXPERTS + 1],
            attn_full[:, qkv_width + 128 :],
        )

    attn_full = lax.all_gather(attn_shard, both, axis=0, tiled=True)
    qkv_full, router_full, gain_one, gain_two, output_turned = unpack(attn_full)
    packed = jnp.concatenate([gate_weight, up_weight, down_shard], -1)
    expert_full = spread_experts(packed)
    expert_full = expert_full.reshape(D, local, 3, hidden_width).transpose(0, 2, 1, 3)
    expert_full = expert_full.reshape(D, 3 * span)
    outer_all = lax.all_gather(cotangent, "fsdp", axis=0, tiled=True)
    routes_all = lax.all_gather(routes, "fsdp", axis=0, tiled=True)
    place = lax.dynamic_slice_in_dim(document_place(segment_row), begin, tokens)
    angle = place.astype(jnp.float32)[:, None] * freq[None, :]
    cosine, sine = jnp.cos(angle), jnp.sin(angle)
    first_norm, first_inverse = normalize(inputs, gain_one)
    normed1 = first_norm.astype(low)
    projected = jnp.dot(normed1, qkv_full, preferred_element_type=jnp.float32)
    query = rotate(projected[:, :width], cosine, sine).astype(low)
    key = rotate(projected[:, width : width + kv_width], cosine, sine).astype(low)
    value = projected[:, width + kv_width :].astype(low)
    pair_all = lax.all_gather(jnp.concatenate([key, value], 1), "ctx", axis=0, tiled=True)
    heads = query.reshape(tokens, key_groups, groups, HD)
    key_heads = pair_all[:, :kv_width].reshape(seq_len, key_groups, HD)
    value_heads = pair_all[:, kv_width:].reshape(seq_len, key_groups, HD)
    scores = jnp.einsum("qkgd,nkd->qkgn", heads, key_heads, preferred_element_type=jnp.float32) * scale
    seen = (segment_row[None, :] == query_doc[:, None]) & (
        jnp.arange(seq_len, dtype=jnp.int32)[None, :] <= query_order[:, None]
    )
    scores = jnp.where(seen[:, None, None, :], scores, MASKED_SCORE)
    running = jnp.max(scores, -1)
    weights = jnp.exp(scores - running[..., None])
    summed = jnp.einsum(
        "qkgn,nkd->qkgd", weights.astype(low), value_heads, preferred_element_type=jnp.float32
    )
    totals = jnp.sum(weights, -1)
    log_total = running + jnp.log(totals)
    mixed_low = (summed / totals[..., None]).reshape(tokens, -1).astype(low)
    attention = lax.psum(
        times_transpose(mixed_low, output_turned).astype(low), "tp"
    ).astype(jnp.float32)
    middle = inputs + attention
    second_norm, second_inverse = normalize(middle, gain_two)
    normed2 = second_norm.astype(low)
    normed2_all = lax.all_gather(normed2, "fsdp", axis=0, tiled=True)
    gate_up = expert_full[:, : 2 * span]
    down_turned = expert_full[:, 2 * span :]
    key_all = pair_all[:, :kv_width]
    value_all = pair_all[:, kv_width:]
    grouped = query.reshape(tokens, key_groups, groups, HD)

    def block_scores(key_piece, offset):
        count = key_piece.shape[0]
        key_heads = key_piece.reshape(count, key_groups, HD)
        scores = (
            jnp.einsum("qkgd,nkd->qkgn", grouped, key_heads, preferred_element_type=jnp.float32)
            * scale
        )
        key_doc = lax.dynamic_slice_in_dim(segment_row, offset, count)
        key_order = offset + jnp.arange(count, dtype=jnp.int32)
        seen = (key_doc[None, :] == query_doc[:, None]) & (
            key_order[None, :] <= query_order[:, None]
        )
        return (scores, seen[:, None, None, :], key_heads)

    def masked_away(offset, count):
        last_doc = lax.dynamic_index_in_dim(segment_row, offset + count - 1, keepdims=False)
        return (offset > query_order[tokens - 1]) | (last_doc < query_doc[0])

    place_z = lax.axis_index("fsdp")
    logits_all = jnp.dot(normed2_all, router_full, preferred_element_type=jnp.float32)
    expert_ids = jnp.arange(EXPERTS, dtype=jnp.int32)
    chosen_all = jnp.any(routes_all[:, :, None] == expert_ids[None, None, :], 1)
    masked_logits = jnp.where(chosen_all, logits_all, MASKED_SCORE)
    top = jnp.max(masked_logits, -1, keepdims=True)
    lifted = jnp.where(chosen_all, jnp.exp(masked_logits - top), 0.0)
    gates_all = lifted / jnp.sum(lifted, -1, keepdims=True)
    gates_here = lax.dynamic_slice_in_dim(gates_all, place_z * local, local, 1)
    chosen_here = lax.dynamic_slice_in_dim(chosen_all, place_z * local, local, 1)
    chosen = lax.dynamic_slice_in_dim(chosen_all, place_z * tokens, tokens, 0)
    gates = lax.dynamic_slice_in_dim(gates_all, place_z * tokens, tokens, 0)

    reach = normed2_all.shape[0]
    both_sides = jnp.dot(normed2_all, gate_up, preferred_element_type=jnp.float32)
    former = both_sides[:, :span]
    latter = both_sides[:, span:]
    hidden_grad = jnp.dot(outer_all, down_turned, preferred_element_type=jnp.float32)
    gate_wide = jnp.concatenate(
        [jnp.broadcast_to(gates_here[:, e : e + 1], (reach, hidden_width)) for e in range(local)], 1
    )
    logistic = jax.nn.sigmoid(former)
    active = former * logistic
    hidden = (active * latter).astype(low).astype(jnp.float32)
    gated = (hidden * gate_wide).astype(low)
    parts = [slice(e * hidden_width, (e + 1) * hidden_width) for e in range(local)]
    dgates = jnp.stack([jnp.sum(hidden[:, part] * hidden_grad[:, part], -1) for part in parts], 1)
    scaled_grad = hidden_grad * gate_wide
    former_grad = (scaled_grad * latter * logistic * (1.0 + former * (1.0 - logistic))).astype(low)
    latter_grad = (scaled_grad * active).astype(low)
    side_grads = jnp.concatenate([former_grad, latter_grad], 1)
    mixture_low = times_transpose(gated, down_turned).astype(low)
    input_part = times_transpose(side_grads, gate_up)
    side_sums = contract_rows(normed2_all, side_grads)
    down_sums = contract_rows(outer_all, gated)
    dgates = jnp.where(chosen_here, dgates, 0.0)
    dgates_wide = lax.dynamic_update_slice_in_dim(
        jnp.zeros((reach, EXPERTS), jnp.float32), dgates, place_z * local, 1
    )
    dgates_high = dgates_wide.astype(low)
    dgates_rest = (dgates_wide - dgates_high.astype(jnp.float32)).astype(low)
    dgates_sent = jnp.concatenate([dgates_high, dgates_rest], 1)
    dgates_sent = jnp.pad(dgates_sent, ((0, 0), (0, 128 - 2 * EXPERTS)))
    back_part = jnp.concatenate([input_part.astype(low), dgates_sent], 1)
    returned = lax.psum_scatter(
        lax.psum(back_part, "tp"), "fsdp", scatter_dimension=0, tiled=True
    ).astype(jnp.float32)
    expert_sums = jnp.concatenate([side_sums, down_sums], 1).astype(low)
    expert_out = collect_experts(expert_sums, rows).reshape(ep, rows, 3, local, hidden_width)
    side_out = expert_out[:, :, :2].transpose(2, 0, 3, 1, 4).reshape(2, EXPERTS, rows, hidden_width)
    side_out = side_out.astype(jnp.float32)
    down_out = expert_out[:, :, 2].transpose(0, 2, 3, 1).reshape(EXPERTS, hidden_width, rows).astype(jnp.float32)

    outer_grad = cotangent.astype(jnp.float32)
    input_grad_part = returned[:, :D]
    picked = returned[:, D : D + EXPERTS] + returned[:, D + EXPERTS : D + 2 * EXPERTS]
    logit_grad = (gates * (picked - jnp.sum(gates * picked, -1, keepdims=True))).astype(low)
    router_sums = contract_rows(normed2, logit_grad)
    second_grad = input_grad_part + times_transpose(logit_grad, router_full)
    middle_back, gain_two_sums = norm_back(second_grad, middle, second_inverse, gain_two)
    middle_grad = outer_grad + middle_back
    attention_grad = middle_grad.astype(low)
    output_sums = contract_rows(attention_grad, mixed_low)
    mixed_grad = jnp.dot(attention_grad, output_turned, preferred_element_type=jnp.float32).astype(low)
    mixed_heads = mixed_grad.reshape(tokens, key_groups, groups, HD)
    delta = jnp.sum(mixed_heads.astype(jnp.float32) * mixed_low.reshape(mixed_heads.shape), -1)

    def back_two(number, state):
        offset = number * tokens
        key_piece = lax.dynamic_slice_in_dim(key_all, offset, tokens, 0)
        value_piece = lax.dynamic_slice_in_dim(value_all, offset, tokens, 0)

        def back_compute(inner):
            query_sum, pair_sum = inner
            scores, seen, key_heads = block_scores(key_piece, offset)
            probs = jnp.where(seen, jnp.exp(scores - log_total[..., None]), 0.0)
            value_heads = value_piece.reshape(tokens, key_groups, HD)
            prob_grad = jnp.einsum(
                "qkgd,nkd->qkgn", mixed_heads, value_heads, preferred_element_type=jnp.float32
            )
            score_grad = (probs * (prob_grad - delta[..., None])).astype(low)
            query_sum = (
                query_sum
                + jnp.einsum(
                    "qkgn,nkd->qkgd", score_grad, key_heads, preferred_element_type=jnp.float32
                )
                * scale
            )
            key_block = (
                jnp.einsum(
                    "qkgn,qkgd->nkd", score_grad, grouped, preferred_element_type=jnp.float32
                )
                * scale
            )
            value_block = jnp.einsum(
                "qkgn,qkgd->nkd", probs.astype(low), mixed_heads, preferred_element_type=jnp.float32
            )
            pair = jnp.concatenate([key_block.reshape(tokens, -1), value_block.reshape(tokens, -1)], 1)
            return (query_sum, lax.dynamic_update_slice_in_dim(pair_sum, pair, offset, 0))

        return lax.cond(masked_away(offset, tokens), lambda inner: inner, back_compute, state)

    back_state = (
        jnp.zeros((tokens, key_groups, groups, HD), jnp.float32),
        jnp.zeros((seq_len, 2 * kv_width), jnp.float32),
    )
    query_sum, pair_sum = lax.fori_loop(0, seq_len // tokens, back_two, back_state)
    pair_local = lax.psum_scatter(
        pair_sum.astype(low), "ctx", scatter_dimension=0, tiled=True
    ).astype(jnp.float32)
    query_back = rotate(query_sum.reshape(tokens, -1), cosine, -sine)
    key_back = rotate(pair_local[:, :kv_width], cosine, -sine)
    qkv_back = jnp.concatenate([query_back, key_back, pair_local[:, kv_width:]], 1).astype(low)
    qkv_sums = contract_rows(normed1, qkv_back)
    first_part = times_transpose(qkv_back, qkv_full)
    first_grad = lax.psum(first_part.astype(low), "tp").astype(jnp.float32)
    input_back, gain_one_sums = norm_back(first_grad, inputs, first_inverse, gain_one)
    input_grad = middle_grad + input_back
    small_sums = jnp.concatenate([router_sums, gain_one_sums[:, None], gain_two_sums[:, None]], 1)
    small_sums = jnp.pad(small_sums, ((0, 0), (0, 128 - small_sums.shape[1])))
    attn_sums = jnp.concatenate([qkv_sums.astype(low), small_sums.astype(low), output_sums.astype(low)], 1)
    attn_out = lax.psum_scatter(attn_sums, both, scatter_dimension=0, tiled=True).astype(jnp.float32)
    mixture = lax.psum_scatter(
        lax.psum(mixture_low, "tp"), "fsdp", scatter_dimension=0, tiled=True
    ).astype(jnp.float32)
    layer_output = (middle + mixture).astype(low)
    small_out = attn_out[:, qkv_width : qkv_width + 128]
    return (
        layer_output,
        input_grad,
        small_out[:, EXPERTS],
        attn_out[:, :width],
        attn_out[:, width : width + kv_width],
        attn_out[:, width + kv_width : qkv_width],
        attn_out[:, qkv_width + 128 :].T,
        small_out[:, EXPERTS + 1],
        small_out[:, :EXPERTS],
        side_out[0],
        side_out[1],
        down_out,
    )


def shards(
    layer_input,
    segments,
    routes,
    norm_gain,
    query_weight,
    key_weight,
    value_weight,
    output_weight,
    ffn_gain,
    router_weight,
    gate_weight,
    up_weight,
    down_weight,
    cotangent,
):
    low = jnp.bfloat16
    width = query_weight.shape[1]
    kv_width = key_weight.shape[1]
    hidden_width = gate_weight.shape[2]
    extra = jnp.concatenate([router_weight, norm_gain[:, None], ffn_gain[:, None]], 1)
    extra = jnp.pad(extra, ((0, 0), (0, 128 - extra.shape[1])))
    attn_shard = jnp.concatenate([query_weight, key_weight, value_weight, extra, output_weight.T], 1)
    freq = 10000.0 ** (-2.0 * jnp.arange(HD // 2, dtype=jnp.float32) / HD)
    (
        expert_full, outer_all, routes_all, normed2_all,
        attn_full, normed1, query, pair_all, mixed, log_total, middle, cosine, sine, extra_all,
    ) = front(
        attn_shard, gate_weight, up_weight, down_weight.transpose(0, 2, 1), cotangent, routes, layer_input,
        segments, jnp.tile(freq, 4)[None, :], width // HD, kv_width // HD,
    )
    returned, mixed_sum, mixture, relay, own, gates = run_experts(
        normed2_all, outer_all, routes_all, extra_all, expert_full, 2
    )
    input_grad, layer_output, qkv_out, wo_out, expert_out = rear(
        returned, gates, middle, layer_input, cotangent, normed1, query, pair_all, mixed, log_total, cosine, sine,
        segments, extra_all, mixed_sum, mixture, relay, own, attn_full, 3,
    )
    small_out = qkv_out[:, width + 2 * kv_width :]
    query_out, key_out, value_out, output_out, gate_out, up_out, down_out = finish(
        expert_out, qkv_out, wo_out, kv_width, hidden_width
    )
    return (
        layer_output,
        input_grad,
        small_out[:, EXPERTS],
        query_out,
        key_out,
        value_out,
        output_out,
        small_out[:, EXPERTS + 1],
        small_out[:, :EXPERTS],
        gate_out,
        up_out,
        down_out,
    )


def solution(mesh):
    in_specs = (
        P(("fsdp", "ctx"), None),
        P("fsdp", None),
        P(("fsdp", "ctx"), None),
        P(("fsdp", "ctx")),
        P(("fsdp", "ctx"), "tp"),
        P(("fsdp", "ctx"), "tp"),
        P(("fsdp", "ctx"), "tp"),
        P("tp", ("fsdp", "ctx")),
        P(("fsdp", "ctx")),
        P(("fsdp", "ctx"), None),
        P(None, ("fsdp", "ctx"), "tp"),
        P(None, ("fsdp", "ctx"), "tp"),
        P(None, "tp", ("fsdp", "ctx")),
        P(("fsdp", "ctx"), None),
    )
    out_specs = (
        P(("fsdp", "ctx"), None),
        P(("fsdp", "ctx"), None),
        P(("fsdp", "ctx")),
        P(("fsdp", "ctx"), "tp"),
        P(("fsdp", "ctx"), "tp"),
        P(("fsdp", "ctx"), "tp"),
        P("tp", ("fsdp", "ctx")),
        P(("fsdp", "ctx")),
        P(("fsdp", "ctx"), None),
        P(None, ("fsdp", "ctx"), "tp"),
        P(None, ("fsdp", "ctx"), "tp"),
        P(None, "tp", ("fsdp", "ctx")),
    )
    body = shards if mesh.shape["ctx"] == 4 else plain_shards
    return jax.shard_map(body, mesh=mesh, in_specs=in_specs, out_specs=out_specs, check_vma=False)
```

```python
import jax
import jax.numpy as jnp
import numpy as np
from jax import lax
from jax.experimental import pallas as pl
from jax.experimental.pallas import tpu as pltpu
from jax.sharding import PartitionSpec as P

MESH = pl.DeviceIdType.MESH

D = 1536
HD = 64
EXPERTS = 16


EPSILON = 1e-05
MASKED_SCORE = -1e30


def rotate(values, cosine, sine):
    rows = values.shape[0]
    shaped = values.reshape(rows, -1, HD)
    half = HD // 2
    cosine, sine = cosine[:, None, :], sine[:, None, :]
    former = shaped[..., :half]
    latter = shaped[..., half:]
    turned = jnp.concatenate([former * cosine - latter * sine, latter * cosine + former * sine], -1)
    return turned.reshape(rows, -1)


def normalize(values, gain):
    inverse = lax.rsqrt(jnp.mean(values * values, -1, keepdims=True) + EPSILON)
    return (values * inverse * gain.astype(jnp.float32), inverse)


def norm_back(grad, values, inverse, gain):
    scaled = grad * gain.astype(jnp.float32)
    gain_grad = jnp.sum(grad * values * inverse, 0)
    mean_term = jnp.mean(scaled * values, -1, keepdims=True)
    return (inverse * scaled - values * inverse**3 * mean_term, gain_grad)


def document_place(segment_row):
    length = segment_row.shape[0]
    order = jnp.arange(length, dtype=jnp.int32)
    fresh = jnp.concatenate([jnp.ones((1,), jnp.bool_), segment_row[1:] != segment_row[:-1]])
    starts = lax.cummax(jnp.where(fresh, order, 0), axis=0)
    return order - starts


def contract_rows(left, right):
    return lax.dot_general(
        left, right, (((0,), (0,)), ((), ())), preferred_element_type=jnp.float32
    )


def times_transpose(left, right):
    return lax.dot_general(
        left, right, (((1,), (1,)), ((), ())), preferred_element_type=jnp.float32
    )


def spread_experts(packed):
    ep = lax.axis_size("fsdp")
    local = packed.shape[0] // ep
    rows = packed.shape[1]
    swapped = lax.all_to_all(packed, "fsdp", 0, 0, tiled=True)
    swapped = swapped.reshape(ep, local, rows, -1).transpose(0, 2, 1, 3)
    swapped = swapped.reshape(ep, rows, -1)
    whole = lax.all_gather(swapped, "ctx", axis=1)
    return whole.reshape(ep * lax.axis_size("ctx") * rows, -1)


def collect_experts(sums, rows):
    ep, ring = lax.axis_size("fsdp"), lax.axis_size("ctx")
    turned = sums.reshape(ep, ring, rows, -1).transpose(1, 0, 2, 3).reshape(sums.shape)
    mine = lax.psum_scatter(turned, "ctx", scatter_dimension=0, tiled=True)
    return lax.all_to_all(mine, "fsdp", 0, 0, tiled=True)


def at_device(fsdp, ctx, tp):
    return {"fsdp": fsdp, "ctx": ctx, "tp": tp}


def fetch(pairs, sems):
    copies = [pltpu.make_async_copy(source, target, sems.at[i]) for i, (source, target) in enumerate(pairs)]
    for copy in copies:
        copy.start()
    return copies


def greet(partners):
    barrier = pltpu.get_barrier_semaphore()
    for device in partners:
        pl.semaphore_signal(barrier, inc=1, device_id=device, device_id_type=MESH)
    pl.semaphore_wait(barrier, len(partners))


def remote(source, target, send, recv, device):
    return pltpu.make_async_remote_copy(
        src_ref=source, dst_ref=target, send_sem=send, recv_sem=recv, device_id=device, device_id_type=MESH
    )


def lasting(us):
    return pl.CostEstimate(flops=0, bytes_accessed=us * 3690000, transcendentals=0)


def front_kernel(
    query_ref, key_ref, value_ref, extra_ref, wo_ref, gate_ref, up_ref, down_ref, outer_ref, routes_ref,
    input_ref, segment_ref, freq_ref,
    expert_out, outer_out, routes_out, normed2_out,
    attn_hbm, normed1_hbm, query_hbm, pair_hbm, mixed_hbm, middle_hbm, log_out, cos_out, sin_out, extra_out,
    attn_out, normed1_out, query_out, pair_out, mixed_out, middle_out, out_sem,
    query_s, key_s, value_s, mixed_s, bias_s, part_s, other_s, normed2_s,
    local_sem, z_send, z_recv, plane_send, plane_recv, relay_send, relay_recv, core_send, core_recv,
    key_send, key_recv, pair_send, pair_recv, chain_send, chain_recv,
):
    ep = z_send.shape[1] + 1
    f, c, t = lax.axis_index("fsdp"), lax.axis_index("ctx"), lax.axis_index("tp")
    low = jnp.bfloat16
    rows = query_ref.shape[0]
    local = gate_ref.shape[0] // ep
    hidden = gate_ref.shape[2]
    tokens = outer_ref.shape[0]
    half = tokens // 2
    heads = query_s.shape[0]
    key_heads = key_s.shape[0]
    width, kv_width = heads * HD, key_heads * HD
    qkv_width = width + 2 * kv_width
    outs = (attn_out, expert_out)
    cuts = [(out.shape[1] // 256) * 128 for out in outs]

    def peer(distance):
        return lax.rem(f + distance, ep)

    def shard_rows(fsdp, ctx):
        return pl.ds(pl.multiple_of((fsdp * 4 + ctx) * rows, 16), rows)

    def columns(kind, side):
        cut, full = cuts[kind], outs[kind].shape[1]
        return pl.ds(0, cut) if side == 0 else pl.ds(cut, full - cut)

    line = [at_device(peer(d), c, t) for d in range(1, ep)]
    plane = [at_device(f, c ^ k, t) for k in range(1, 4)]
    x_device, y_device = plane[0], plane[1]
    core = at_device(f, c, 1 - t)
    greet(line + plane + [core])

    mine = shard_rows(f, c)
    sent = []

    def send(copy, when=None):
        if when is None:
            copy.start()
        else:
            pl.when(when)(copy.start)
        sent.append((when, copy))

    def await_arrival(copy, when=None):
        if when is None:
            copy.wait_recv()
        else:
            pl.when(when)(copy.wait_recv)

    def z_arrival(kind, d):
        place = shard_rows(peer(ep - d), c)
        remote(
            outs[kind].at[place], outs[kind].at[place], z_send.at[kind, d - 1], z_recv.at[kind, d - 1], x_device
        ).wait_recv()

    def spread(kind, g, when=None):
        place = shard_rows(g, c)
        for step in range(2):
            for way, device in enumerate((x_device, y_device)):
                side = step ^ way
                block = outs[kind].at[place, columns(kind, side)]
                send(
                    remote(
                        block, block, plane_send.at[kind, g, way, side], plane_recv.at[kind, g, way, side], device
                    ),
                    when,
                )

    def pass_on(kind, g, when=None):
        for way, device in enumerate((y_device, x_device)):
            place = shard_rows(g, c ^ (1 << way))
            block = outs[kind].at[place, columns(kind, way)]
            await_arrival(
                remote(
                    block, block, plane_send.at[kind, g, way, way], plane_recv.at[kind, g, way, way], device
                ),
                when,
            )
            send(remote(block, block, relay_send.at[kind, g, way], relay_recv.at[kind, g, way], device), when)

    def settle(kind):
        for g in range(ep):
            for way, device in enumerate((x_device, y_device)):
                side = 1 - way
                block = outs[kind].at[shard_rows(g, c ^ (1 << way)), columns(kind, side)]
                remote(
                    block, block, plane_send.at[kind, g, way, side], plane_recv.at[kind, g, way, side], device
                ).wait_recv()
                block = outs[kind].at[shard_rows(g, c ^ 3), columns(kind, way)]
                remote(
                    block, block, relay_send.at[kind, g, way], relay_recv.at[kind, g, way], device
                ).wait_recv()

    nexts = (at_device(jnp.minimum(f + 1, ep - 1), c, t), at_device(jnp.maximum(f - 1, 0), c, t))
    more = (f < ep - 1, f > 0)

    def chain_origin(way, hop):
        if way == 0:
            return jnp.maximum(f - hop, 0), f >= hop
        return jnp.minimum(f + hop, ep - 1), f + hop < ep

    def chain_begin(kind, source, target):
        for way in range(2):
            send(
                remote(source, target, chain_send.at[kind, way, 0], chain_recv.at[kind, way, 0], nexts[way]),
                more[way],
            )

    def chain_hop(kind, way, hop, block):
        there = chain_origin(way, hop)[1]
        await_arrival(
            remote(
                block, block, chain_send.at[kind, way, hop - 1], chain_recv.at[kind, way, hop - 1], nexts[way]
            ),
            there,
        )
        if hop < ep - 1:
            send(
                remote(block, block, chain_send.at[kind, way, hop], chain_recv.at[kind, way, hop], nexts[way]),
                there & more[way],
            )

    def line_place(fsdp, part):
        return pl.ds(pl.multiple_of(fsdp * tokens + part * half, 16), half)

    own_tokens = pl.ds(pl.multiple_of(f * tokens, 16), tokens)
    my_half = pl.ds(pl.multiple_of(t * half, 16), half)

    def line_hop(kind, hop, target):
        for way in range(2):
            g, there = chain_origin(way, hop)
            block = target.at[line_place(g, t)]
            chain_hop(kind, way, hop, block)
            send(remote(block, block, core_send.at[kind - 1, g], core_recv.at[kind - 1, g], core), there)

    def line_settle(kind, target):
        for g in range(ep):
            block = target.at[line_place(g, 1 - t)]
            await_arrival(
                remote(block, block, core_send.at[kind - 1, g], core_recv.at[kind - 1, g], core), f != g
            )

    start = 0
    for ref in (query_ref, key_ref, value_ref, extra_ref, wo_ref):
        pltpu.make_async_copy(
            ref, attn_out.at[mine, pl.ds(start, ref.shape[1])], local_sem.at[0]
        ).start()
        start += ref.shape[1]
    pltpu.make_async_copy(attn_out.at[mine], attn_out.at[mine], local_sem.at[0]).wait()
    chain_begin(0, attn_out.at[mine], attn_out.at[mine])
    own_outer = pltpu.make_async_copy(outer_ref, outer_out.at[own_tokens], local_sem.at[2])
    own_outer.start()
    own_columns = (slice(None), pl.ds(pl.multiple_of(f * tokens, 128), tokens))
    own_routes = pltpu.make_async_copy(routes_ref, routes_out.at[own_columns], local_sem.at[3])
    own_routes.start()
    for d in range(1, ep):
        send(
            remote(
                routes_ref, routes_out.at[own_columns], z_send.at[4, d - 1], z_recv.at[4, d - 1], line[d - 1]
            )
        )
    for kind, ref in enumerate((gate_ref, up_ref, down_ref)):
        for e in range(local):
            target = expert_out.at[mine, pl.ds((kind * local + e) * hidden, hidden)]
            pltpu.make_async_copy(ref.at[f * local + e], target, local_sem.at[1]).start()
    spread(0, f)

    length = segment_ref.shape[1]
    seg_keys = segment_ref[...].astype(jnp.float32)
    seg_here = segment_ref[:, pl.ds(pl.multiple_of(c * tokens, 128), tokens)].astype(jnp.float32)
    seg_queries = jnp.broadcast_to(seg_here, (128, tokens)).T[:, :1]
    key_order = lax.broadcasted_iota(jnp.int32, (tokens, length), 1)
    query_order = lax.broadcasted_iota(jnp.int32, (tokens, length), 0) + c * tokens
    same = seg_keys == seg_queries
    seen = same & (key_order <= query_order)
    bias_s[...] = jnp.where(seen, 0.0, MASKED_SCORE)
    place = jnp.sum(jnp.where(same & (key_order < query_order), 1.0, 0.0), -1, keepdims=True)
    angle = place * freq_ref[...]
    lane = lax.broadcasted_iota(jnp.int32, (tokens, 128), 1)
    first_half = lax.rem(lane, HD) < HD // 2
    cosine = jnp.cos(angle)
    sine = jnp.where(first_half, -jnp.sin(angle), jnp.sin(angle))
    cos_out[...] = cosine
    sin_out[...] = sine
    inputs = input_ref[...].astype(jnp.float32)
    inverse = lax.rsqrt(jnp.mean(inputs * inputs, -1, keepdims=True) + EPSILON)

    pass_on(0, f)
    for hop in range(1, ep):
        for way in range(2):
            g, there = chain_origin(way, hop)
            chain_hop(0, way, hop, attn_out.at[shard_rows(g, c)])
            spread(0, g, there)
        if hop > 1:
            for way in range(2):
                pass_on(0, *chain_origin(way, hop - 1))
    for way in range(2):
        pass_on(0, *chain_origin(way, ep - 1))
    for d in range(1, ep):
        for kind, ref in enumerate((gate_ref, up_ref, down_ref)):
            for e in range(local):
                target = expert_out.at[mine, pl.ds((kind * local + e) * hidden, hidden)]
                remote(
                    ref.at[peer(d) * local + e], target, z_send.at[1, d - 1], z_recv.at[1, d - 1],
                    line[d - 1],
                ).start()
    pltpu.make_async_copy(expert_out.at[mine], expert_out.at[mine], local_sem.at[1]).wait()
    spread(1, f)
    settle(0)
    stores = [pltpu.make_async_copy(attn_out, attn_hbm, out_sem.at[0])]
    stores[0].start()

    def store(number, source, target):
        stores.append(pltpu.make_async_copy(source, target, out_sem.at[number]))
        stores[-1].start()

    gains = attn_out[:, qkv_width : qkv_width + 128].astype(jnp.float32).T
    normed1_out[...] = (inputs * inverse * gains[EXPERTS : EXPERTS + 1, :]).astype(low)
    store(1, normed1_out, normed1_hbm)

    def project(start):
        return jnp.dot(
            normed1_out[...], attn_out[:, start : start + 256], preferred_element_type=jnp.float32
        )

    def turned(tile):
        swapped = jnp.where(first_half, pltpu.roll(tile, 128 - HD // 2, 1), pltpu.roll(tile, HD // 2, 1))
        return tile * cos_out[...] + swapped * sin_out[...]

    here = pl.ds(pl.multiple_of(c * tokens, 16), tokens)
    for start in range(0, kv_width, 256):
        tile = project(width + start)
        for side in (0, 128):
            pair_out[here, start + side : start + side + 128] = turned(tile[:, side : side + 128]).astype(low)
    for start in range(0, kv_width, 256):
        pair_out[here, kv_width + start : kv_width + start + 256] = project(width + kv_width + start).astype(low)
    for k in (3, 1, 2):
        send(remote(pair_out.at[here], pair_out.at[here], key_send.at[k - 1], key_recv.at[k - 1], plane[k - 1]))
    for start in range(0, width, 256):
        tile = project(start)
        for side in (0, 128):
            query_out[:, start + side : start + side + 128] = turned(tile[:, side : side + 128]).astype(low)
    store(2, query_out, query_hbm)
    for h in range(heads):
        query_s[h] = query_out[:, h * HD : (h + 1) * HD]
    for k in range(1, 4):
        block = pair_out.at[pl.ds(pl.multiple_of((c ^ k) * tokens, 16), tokens)]
        remote(block, block, key_send.at[k - 1], key_recv.at[k - 1], plane[k - 1]).wait_recv()
    store(3, pair_out, pair_hbm)
    for g in range(key_heads):
        key_s[g] = pair_out[:, g * HD : (g + 1) * HD]
        value_s[g] = pair_out[:, kv_width + g * HD : kv_width + (g + 1) * HD]
    pass_on(1, f)
    for d in range(1, ep):
        z_arrival(1, d)
        spread(1, peer(ep - d))
    chain_begin(2, outer_ref.at[my_half], outer_out.at[line_place(f, t)])

    def attend(h, carry):
        g = lax.div(h, heads // key_heads)
        query = query_s[h] * jnp.asarray(HD**-0.5, low)
        scores = lax.dot_general(
            query, key_s[g], (((1,), (1,)), ((), ())), preferred_element_type=jnp.float32
        ) + bias_s[...]
        top = jnp.max(scores, -1, keepdims=True)
        weights = jnp.exp(scores - top)
        total = jnp.sum(weights, -1, keepdims=True)
        summed = jnp.dot(weights.astype(low), value_s[g], preferred_element_type=jnp.float32)
        mixed_s[h] = (summed / total).astype(low)
        log_out[h] = jnp.broadcast_to(top + jnp.log(total), (tokens, 128)).T[:1, :]
        return carry

    lax.fori_loop(0, heads, attend, 0)
    for h in range(heads):
        mixed_out[:, h * HD : (h + 1) * HD] = mixed_s[h]
    store(4, mixed_out, mixed_hbm)
    model = input_ref.shape[1]
    for start in range(0, model, 256):
        part_s[:, start : start + 256] = lax.dot_general(
            mixed_out[...], attn_out[start : start + 256, qkv_width + 128 :],
            (((1,), (1,)), ((), ())), preferred_element_type=jnp.float32,
        ).astype(low)
    exchange = remote(part_s, other_s, pair_send, pair_recv, core)
    send(exchange)
    pass_on(1, peer(ep - 1))
    line_hop(2, 1, outer_out)
    exchange.wait_recv()
    middle = input_ref[...].astype(jnp.float32) + (
        part_s[...].astype(jnp.float32) + other_s[...].astype(jnp.float32)
    )
    middle_out[...] = middle
    store(5, middle_out, middle_hbm)
    inverse = lax.rsqrt(jnp.mean(middle * middle, -1, keepdims=True) + EPSILON)
    gains = attn_out[:, qkv_width : qkv_width + 128].astype(jnp.float32).T
    normed2_s[...] = (middle * inverse * gains[EXPERTS + 1 : EXPERTS + 2, :]).astype(low)
    chain_begin(1, normed2_s.at[my_half], normed2_out.at[line_place(f, t)])
    own_normed2 = pltpu.make_async_copy(normed2_s, normed2_out.at[own_tokens], local_sem.at[4])
    own_normed2.start()
    for d in range(2, ep):
        pass_on(1, peer(ep - d))
    line_hop(1, 1, normed2_out)
    line_hop(2, 2, outer_out)
    line_hop(1, 2, normed2_out)
    line_hop(2, 3, outer_out)
    line_hop(1, 3, normed2_out)
    settle(1)
    line_settle(2, outer_out)
    line_settle(1, normed2_out)
    for d in range(1, ep):
        place = (slice(None), pl.ds(pl.multiple_of(peer(ep - d) * tokens, 128), tokens))
        remote(
            routes_out.at[place], routes_out.at[place], z_send.at[4, d - 1], z_recv.at[4, d - 1], core
        ).wait_recv()
        remote(
            expert_out.at[mine], expert_out.at[mine], z_send.at[1, d - 1], z_recv.at[1, d - 1], core
        ).wait_send()
    extra_out[...] = attn_out[:, qkv_width : qkv_width + 128]
    own_outer.wait()
    own_routes.wait()
    own_normed2.wait()
    for copy in stores:
        copy.wait()
    all_sent(sent)


def front(
    query, key, value, extra, wo, gate, up, down, outer, routes, inputs, segments, freq
):
    ep = lax.axis_size("fsdp")
    rows = query.shape[0]
    heads, key_heads = query.shape[1] // HD, key.shape[1] // HD
    width = sum(part.shape[1] for part in (query, key, value, extra, wo))
    total = rows * ep * lax.axis_size("ctx")
    local = gate.shape[0] // ep
    tokens, model = inputs.shape
    length = segments.shape[1]
    low = jnp.bfloat16
    dma = pltpu.SemaphoreType.DMA
    anywhere = pl.BlockSpec(memory_space=pl.ANY)
    vmem = pl.BlockSpec(memory_space=pltpu.VMEM)
    shape = jax.ShapeDtypeStruct
    kept = (
        ((total, width), low),
        ((tokens, model), low),
        ((tokens, heads * HD), low),
        ((length, 2 * key_heads * HD), low),
        ((tokens, heads * HD), low),
        ((tokens, model), jnp.float32),
    )
    return pl.pallas_call(
        front_kernel,
        out_shape=(
            shape((total, 3 * local * gate.shape[2]), low),
            shape((ep * tokens, model), low),
            shape((routes.shape[0], ep * tokens), routes.dtype),
            shape((ep * tokens, model), low),
        )
        + tuple(shape(*each) for each in kept)
        + (
            shape((heads, 1, tokens), jnp.float32),
            shape((tokens, 128), jnp.float32),
            shape((tokens, 128), jnp.float32),
            shape((total, 128), low),
        ),
        in_specs=[anywhere] * 10 + [vmem] * 3,
        out_specs=(anywhere,) * 10 + (vmem,) * 4,
        scratch_shapes=[pltpu.VMEM(*each) for each in kept]
        + [
            dma((len(kept),)),
            pltpu.VMEM((heads, tokens, HD), low),
            pltpu.VMEM((key_heads, length, HD), low),
            pltpu.VMEM((key_heads, length, HD), low),
            pltpu.VMEM((heads, tokens, HD), low),
            pltpu.VMEM((tokens, length), jnp.float32),
            pltpu.VMEM((tokens, model), low),
            pltpu.VMEM((tokens, model), low),
            pltpu.VMEM((tokens, model), low),
            dma((5,)),
            dma((5, ep - 1)),
            dma((5, ep - 1)),
            dma((2, ep, 2, 2)),
            dma((2, ep, 2, 2)),
            dma((2, ep, 2)),
            dma((2, ep, 2)),
            dma((2, ep)),
            dma((2, ep)),
            dma((3,)),
            dma((3,)),
            dma,
            dma,
            dma((3, 2, ep - 1)),
            dma((3, 2, ep - 1)),
        ],
        compiler_params=pltpu.CompilerParams(
            collective_id=1, has_side_effects=True, vmem_limit_bytes=60 * 1024 * 1024
        ),
        cost_estimate=lasting(165),
        name="front",
    )(query, key, value, extra, wo, gate, up, down, outer, routes, inputs, segments, freq)


def z_sum_scratch(ep, tokens, width, low):
    dma = pltpu.SemaphoreType.DMA
    return [
        pltpu.VMEM((ep, tokens // 2, width), low),
        pltpu.VMEM((ep - 1, tokens // 2, width), low),
        pltpu.VMEM((ep - 1, tokens // 2, width), low),
        dma((ep,)),
        dma((ep,)),
        dma((ep - 1,)),
        dma((ep - 1,)),
        dma,
        dma,
    ]


class ZSum:
    size = 9

    def __init__(self, part, scratch, sent):
        self.part, self.sent = part, sent
        (
            self.core_in, self.z_out, self.z_in, self.core_send, self.core_recv,
            self.z_send, self.z_recv, self.back_send, self.back_recv,
        ) = scratch
        self.ep, self.half = self.core_in.shape[0], self.core_in.shape[1]
        self.f, self.c, self.t = lax.axis_index("fsdp"), lax.axis_index("ctx"), lax.axis_index("tp")
        self.core = at_device(self.f, self.c, 1 - self.t)

    def peer(self, distance):
        return lax.rem(self.f + distance, self.ep)

    def place(self, fsdp, part):
        return pl.ds(pl.multiple_of(fsdp * 2 * self.half + part * self.half, 16), self.half)

    def rows(self, part):
        return pl.ds(pl.multiple_of(part * self.half, 16), self.half)

    def send(self, copy):
        copy.start()
        self.sent.append((None, copy))

    def to_core(self, d):
        self.send(
            remote(
                self.part.at[self.place(self.peer(d), 1 - self.t)], self.core_in.at[d],
                self.core_send.at[d], self.core_recv.at[d], self.core,
            )
        )

    def added(self, d):
        landing = self.core_in.at[d]
        remote(landing, landing, self.core_send.at[d], self.core_recv.at[d], self.core).wait_recv()
        mine = self.part[self.place(self.peer(d), self.t), :]
        return mine.astype(jnp.float32) + self.core_in[d].astype(jnp.float32)

    def to_z(self, d):
        self.z_out[d - 1] = self.added(d).astype(self.z_out.dtype)
        self.send(
            remote(
                self.z_out.at[d - 1], self.z_in.at[d - 1], self.z_send.at[d - 1], self.z_recv.at[d - 1],
                at_device(self.peer(d), self.c, self.t),
            )
        )

    def collect(self):
        total = self.added(0)
        for d in range(1, self.ep):
            landing = self.z_in.at[d - 1]
            remote(landing, landing, self.z_send.at[d - 1], self.z_recv.at[d - 1], self.core).wait_recv()
            total = total + self.z_in[d - 1].astype(jnp.float32)
        return total

    def share(self, out):
        mine = out.at[self.rows(self.t)]
        self.send(remote(mine, mine, self.back_send, self.back_recv, self.core))

    def finish(self, out):
        other = out.at[self.rows(1 - self.t)]
        remote(other, other, self.back_send, self.back_recv, self.core).wait_recv()


def pair_sum_scratch(ep, tokens, width, low):
    dma = pltpu.SemaphoreType.DMA
    return [
        pltpu.VMEM((ep, tokens // 2, width), low),
        pltpu.VMEM((4, tokens // 2, width), low),
        dma((ep,)),
        dma((ep,)),
        dma((4,)),
        dma((4,)),
        dma((2,)),
    ]


class PairSum:
    def __init__(self, part, mine, scratch, sent):
        self.part, self.mine, self.sent = part, mine, sent
        (
            self.own, self.landing, self.core_send, self.core_recv, self.send_sem, self.recv_sem, self.cross_sem
        ) = scratch
        self.ep, self.half = self.own.shape[0], self.own.shape[1]
        self.f, c, self.t = lax.axis_index("fsdp"), lax.axis_index("ctx"), lax.axis_index("tp")
        self.core = at_device(self.f, c, 1 - self.t)
        self.partner = self.f ^ 1
        self.inner = (self.f == 1) | (self.f == 2)
        self.others = [2 - (self.f & 2) + j for j in range(2)]
        self.devices = [at_device(g, c, self.t) for g in self.others]
        self.beside = at_device(self.partner, c, self.t)

    def place(self, g, part):
        return pl.ds(pl.multiple_of(g * 2 * self.half + part * self.half, 16), self.half)

    def send(self, copy, when=None):
        if when is None:
            copy.start()
        else:
            pl.when(when)(copy.start)
        self.sent.append((when, copy))

    def to_core(self):
        for g in range(self.ep):
            self.send(
                remote(
                    self.part.at[self.place(g, 1 - self.t)], self.own.at[g],
                    self.core_send.at[g], self.core_recv.at[g], self.core,
                )
            )

    def both_cores(self, g):
        block = self.own.at[g]
        remote(block, block, self.core_send.at[g], self.core_recv.at[g], self.core).wait_recv()
        return self.mine[g].astype(jnp.float32) + self.own[g].astype(jnp.float32)

    def begin(self):
        outer = jnp.logical_not(self.inner)
        for j, g in enumerate(self.others):
            self.own[g] = self.both_cores(g).astype(self.own.dtype)
            self.send(
                remote(
                    self.own.at[g], self.landing.at[1 + j], self.send_sem.at[1 + j], self.recv_sem.at[1 + j],
                    self.beside,
                ),
                outer,
            )
        self.own[self.partner] = self.both_cores(self.partner).astype(self.own.dtype)
        self.send(
            remote(
                self.own.at[self.partner], self.landing.at[0], self.send_sem.at[0], self.recv_sem.at[0], self.beside
            )
        )

    def cross(self):
        for j, g in enumerate(self.others):

            @pl.when(self.inner)
            def _():
                block = self.landing.at[1 + j]
                remote(block, block, self.send_sem.at[1 + j], self.recv_sem.at[1 + j], self.beside).wait_recv()
                added = self.own[g].astype(jnp.float32) + self.landing[1 + j].astype(jnp.float32)
                self.own[g] = added.astype(self.own.dtype)

            self.send(
                remote(
                    self.own.at[g], self.landing.at[3], self.cross_sem.at[j], self.recv_sem.at[3], self.devices[j]
                ),
                self.inner,
            )

    def collect(self):
        total = self.both_cores(self.f)
        for slot in (0, 3):
            block = self.landing.at[slot]
            remote(block, block, self.send_sem.at[slot], self.recv_sem.at[slot], self.beside).wait_recv()
            total = total + self.landing[slot].astype(jnp.float32)
        return total


def all_sent(sent):
    for when, copy in sent:
        if when is None:
            copy.wait_send()
        else:
            pl.when(when)(copy.wait_send)


def shard_sum_scratch(ep, rows, width, low):
    cut = first_columns(width)
    widths = [cut] if cut == width else [cut, width - cut]
    dma = pltpu.SemaphoreType.DMA
    scratch = []
    for part in widths:
        scratch += [
            pltpu.VMEM((ep, 2, rows, part), low),
            pltpu.VMEM((ep, rows, part), low),
            pltpu.VMEM((ep - 1, rows, part), low),
        ]
    return scratch + [
        dma((2, ep, 2)), dma((2, ep, 2)), dma((2, ep)), dma((2, ep)), dma((2, ep)), dma((2, ep))
    ]


def first_columns(width):
    return width if width == 128 else -(-width // 256) * 128


class ShardSum:
    def __init__(self, part, rows, width, scratch, sent):
        self.part, self.rows, self.sent = part, rows, sent
        cut = first_columns(width)
        self.columns = [pl.ds(0, cut)] + ([] if cut == width else [pl.ds(cut, width - cut)])
        self.ways = range(len(self.columns))
        (
            self.first_send, self.first_recv, self.second_send, self.second_recv, self.z_send, self.z_recv
        ) = scratch[-6:]
        self.first_in = [scratch[3 * way] for way in self.ways]
        self.second_in = [scratch[3 * way + 1] for way in self.ways]
        self.z_in = [scratch[3 * way + 2] for way in self.ways]
        self.ep = self.first_in[0].shape[0]
        self.f, self.c, self.t = lax.axis_index("fsdp"), lax.axis_index("ctx"), lax.axis_index("tp")
        self.neighbours = (at_device(self.f, self.c ^ 1, self.t), at_device(self.f, self.c ^ 2, self.t))
        self.order = list(range(1, self.ep)) + [0]

    def peer(self, distance):
        return lax.rem(self.f + distance, self.ep)

    def block(self, distance, ctx, way):
        start = (self.peer(distance) * 4 + ctx) * self.rows
        return pl.ds(pl.multiple_of(start, 16), self.rows), self.columns[way]

    def send(self, copy):
        copy.start()
        self.sent.append((None, copy))

    def first(self, d):
        for number in range(2):
            for way in self.ways:
                target = self.c ^ 3 if number == 0 else self.c ^ (1 << way)
                self.send(
                    remote(
                        self.part.at[self.block(d, target, way)], self.first_in[way].at[d, number],
                        self.first_send.at[way, d, number], self.first_recv.at[way, d, number],
                        self.neighbours[way],
                    )
                )

    def second(self, d):
        for way in self.ways:
            for number in range(2):
                landing = self.first_in[way].at[d, number]
                remote(
                    landing, landing, self.first_send.at[way, d, number],
                    self.first_recv.at[way, d, number], self.neighbours[way],
                ).wait_recv()
            term = self.part[self.block(d, self.c ^ (2 >> way), way)]
            added = term.astype(jnp.float32) + self.first_in[way][d, 0].astype(jnp.float32)
            self.first_in[way][d, 0] = added.astype(self.part.dtype)
            self.send(
                remote(
                    self.first_in[way].at[d, 0], self.second_in[way].at[d],
                    self.second_send.at[way, d], self.second_recv.at[way, d], self.neighbours[1 - way],
                )
            )

    def total(self, d, way):
        landing = self.second_in[way].at[d]
        remote(
            landing, landing, self.second_send.at[way, d], self.second_recv.at[way, d], self.neighbours[1 - way]
        ).wait_recv()
        term = self.part[self.block(d, self.c, way)]
        return (
            term.astype(jnp.float32)
            + self.first_in[way][d, 1].astype(jnp.float32)
            + self.second_in[way][d].astype(jnp.float32)
        )

    def to_z(self, d, out):
        for way in self.ways:
            total = self.total(d, way)
            if d == 0:
                out[:, self.columns[way]] = total
                continue
            self.first_in[way][d, 1] = total.astype(self.part.dtype)
            self.send(
                remote(
                    self.first_in[way].at[d, 1], self.z_in[way].at[d - 1],
                    self.z_send.at[way, d], self.z_recv.at[way, d], at_device(self.peer(d), self.c, self.t),
                )
            )

    def from_z(self, out):
        for way in self.ways:
            for d in range(1, self.ep):
                landing = self.z_in[way].at[d - 1]
                remote(
                    landing, landing, self.z_send.at[way, d], self.z_recv.at[way, d], self.neighbours[0]
                ).wait_recv()
                out[:, self.columns[way]] += self.z_in[way][d - 1].astype(jnp.float32)


def all_partners(ep):
    f, c, t = lax.axis_index("fsdp"), lax.axis_index("ctx"), lax.axis_index("tp")
    line = [at_device(lax.rem(f + d, ep), c, t) for d in range(1, ep)]
    return line + [at_device(f, c ^ 1, t), at_device(f, c ^ 2, t), at_device(f, c, 1 - t)]


class PlaneHalf:
    def __init__(self, part, rows, local, landings, send_sem, recv_sem, sent):
        self.part, self.rows, self.landings, self.sent = part, rows, landings, sent
        self.send_sem, self.recv_sem = send_sem, recv_sem
        self.local, self.cut = local, landings[0].shape[-1] // local
        self.ep = landings[0].shape[0]
        self.f, self.c, t = lax.axis_index("fsdp"), lax.axis_index("ctx"), lax.axis_index("tp")
        self.neighbours = (at_device(self.f, self.c ^ 1, t), at_device(self.f, self.c ^ 2, t))

    def block(self, distance, ctx, way, e):
        start = (lax.rem(self.f + distance, self.ep) * 4 + ctx) * self.rows
        columns = pl.ds((2 * e + way) * self.cut, self.cut)
        return pl.ds(pl.multiple_of(start, 16), self.rows), columns

    def landed(self, d, number, way):
        landing = self.landings[way].at[d, number]
        return remote(
            landing, landing, self.send_sem.at[way, d, number], self.recv_sem.at[way, d, number],
            self.neighbours[way],
        )

    def start(self, d, e):
        for number in range(2):
            for way in range(2):
                target = self.c ^ 3 if number == 0 else self.c ^ (1 << way)
                remote(
                    self.part.at[self.block(d, target, way, e)],
                    self.landings[way].at[d, number, :, pl.ds(e * self.cut, self.cut)],
                    self.send_sem.at[way, d, number], self.recv_sem.at[way, d, number], self.neighbours[way],
                ).start()

    def finish(self, d):
        for way in range(2):
            for number in range(2):
                copy = self.landed(d, number, way)
                copy.wait_recv()
                self.sent.append((None, copy))
                ctx = self.c ^ (2 >> way) if number == 0 else self.c
                for e in range(self.local):
                    at = slice(e * self.cut, (e + 1) * self.cut)
                    term = self.part[self.block(d, ctx, way, e)].astype(jnp.float32)
                    added = term + self.landings[way][d, number, :, at].astype(jnp.float32)
                    self.landings[way][d, number, :, at] = added.astype(self.part.dtype)


def experts_kernel(
    routes_ref, extra_ref, tokens_hbm, outer_hbm, weight_hbm,
    returned_ref, mixture_out, relay_out, own_out, gates_out,
    tokens_ref, outer_ref, weight_ref, in_sem,
    gates_s, gated_s, side_s, part_s, mixture_s, sums_s, first_x, first_y, plane_send, plane_recv, local_sem, *scratch,
):
    ep = lax.axis_size("fsdp")
    f = lax.axis_index("fsdp")
    low = jnp.bfloat16
    reach, model = tokens_ref.shape
    span = weight_ref.shape[1] // 3
    tokens = reach // ep
    rows = model // (4 * ep)
    local = EXPERTS // ep
    hidden = span // local
    sent = []
    back = ZSum(part_s, scratch, sent)
    plane = PlaneHalf(sums_s, rows, local, (first_x, first_y), plane_send, plane_recv, sent)
    pairs = [(tokens_hbm, tokens_ref), (outer_hbm, outer_ref)]
    for e in range(local):
        for kind in range(3):
            at = (slice(None), pl.ds(kind * span + e * hidden, hidden))
            pairs.insert(1 + 3 * e + kind + (e > 0 or kind > 1), (weight_hbm.at[at], weight_ref.at[at]))
    coming = fetch(pairs, in_sem)
    greet(all_partners(ep))

    lane = lax.broadcasted_iota(jnp.int32, (reach, 128), 1)
    uses = routes_ref.shape[0]
    turned = jnp.concatenate(
        [routes_ref[...].astype(jnp.float32), jnp.zeros((128 - uses, reach), jnp.float32)], 0
    ).T.astype(jnp.int32)
    chosen = turned[:, 0:1] == lane
    for k in range(1, uses):
        chosen = chosen | (turned[:, k : k + 1] == lane)
    coming[0].wait()
    logits = jnp.dot(tokens_ref[...], extra_ref[...], preferred_element_type=jnp.float32)
    logits = jnp.where(chosen, logits, MASKED_SCORE)
    lifted = jnp.where(chosen, jnp.exp(logits - jnp.max(logits, -1, keepdims=True)), 0.0)
    gates_s[...] = lifted / jnp.sum(lifted, -1, keepdims=True)
    own = pl.ds(pl.multiple_of(f * tokens, 16), tokens)
    gates_out[...] = gates_s[own, :]

    part_s[:, model:] = jnp.zeros((reach, 128), low)
    order = list(range(1, ep)) + [0]
    over = (((0,), (0,)), ((), ()))
    across = (((1,), (1,)), ((), ()))

    def act(e):
        at = slice(e * hidden, (e + 1) * hidden)
        at_up = slice(span + e * hidden, span + (e + 1) * hidden)
        at_down = slice(2 * span + e * hidden, 2 * span + (e + 1) * hidden)
        mine = lane == f * local + e
        gate = jnp.sum(jnp.where(mine, gates_s[...], 0.0), -1, keepdims=True)
        for copy in coming[1:5] if e == 0 else coming[2 + 3 * e : 5 + 3 * e]:
            copy.wait()
        former = jnp.dot(tokens_ref[...], weight_ref[:, at], preferred_element_type=jnp.float32)
        latter = jnp.dot(tokens_ref[...], weight_ref[:, at_up], preferred_element_type=jnp.float32)
        grad = jnp.dot(outer_ref[...], weight_ref[:, at_down], preferred_element_type=jnp.float32)
        logistic = 1.0 / (1.0 + jnp.exp(-former))
        active = former * logistic
        value = (active * latter).astype(low).astype(jnp.float32)
        gated_s[:, at] = (value * gate).astype(low)
        picked = jnp.sum(value * grad, -1, keepdims=True)
        dgate = jnp.where(mine & (gate > 0.0), picked, 0.0)
        high = dgate.astype(low).astype(jnp.float32)
        part_s[:, model:] += (high + pltpu.roll(dgate - high, EXPERTS, 1)).astype(low)
        grad = grad * gate
        side_s[:, at] = (grad * latter * logistic * (1.0 + former * (1.0 - logistic))).astype(low)
        side_s[:, at_up] = (grad * active).astype(low)

    def sums(e):
        for d in order:
            at = pl.ds(pl.multiple_of(lax.rem(f + d, ep) * 4 * rows, 128), 4 * rows)
            start = 3 * e * hidden
            for kind, (left, right) in enumerate(((tokens_ref, side_s), (tokens_ref, side_s), (outer_ref, gated_s))):
                column = (kind * span if kind < 2 else 0) + e * hidden
                sums_s[at, start + kind * hidden : start + (kind + 1) * hidden] = lax.dot_general(
                    left[:, at], right[:, column : column + hidden], over, preferred_element_type=jnp.float32
                ).astype(low)
            plane.start(d, e)

    def dn2(d):
        here = pl.ds(pl.multiple_of(back.peer(d) * tokens, 16), tokens)

        def tile(n, carry):
            at = pl.ds(pl.multiple_of(n * 256, 256), 256)
            part_s[here, at] = lax.dot_general(
                side_s[here, :], weight_ref[at, : 2 * span], across, preferred_element_type=jnp.float32
            ).astype(low)
            return carry

        lax.fori_loop(0, model // 256, tile, 0)
        back.to_core(d)

    def mixtures(n, carry):
        at = pl.ds(pl.multiple_of(n * 256, 256), 256)
        mixture_s[:, at] = lax.dot_general(
            gated_s[...], weight_ref[at, 2 * span :], across, preferred_element_type=jnp.float32
        ).astype(low)
        return carry

    act(0)
    sums(0)
    for e in range(1, local):
        act(e)
    sums(1)
    for step, d in enumerate(order):
        dn2(d)
        if step > 0:
            back.to_z(order[step - 1])
    for e in range(2, local):
        sums(e)
    lax.fori_loop(0, model // 256, mixtures, 0)
    mixture_copy = pltpu.make_async_copy(mixture_s, mixture_out, local_sem.at[2])
    mixture_copy.start()
    for d in order:
        plane.finish(d)
        for way in range(2):
            for number, out in enumerate((relay_out, own_out)):
                pltpu.make_async_copy(
                    plane.landings[way].at[d, number], out.at[way, d], local_sem.at[number]
                ).start()
    returned_ref[back.rows(back.t), :] = back.collect()
    back.share(returned_ref)
    mixture_copy.wait()
    back.finish(returned_ref)
    for number, out in enumerate((relay_out, own_out)):
        pltpu.make_async_copy(out, out, local_sem.at[number]).wait()
    all_sent(sent)


def run_experts(tokens_all, outer_all, routes_all, extra, weights, collective_id):
    ep = lax.axis_size("fsdp")
    reach, model = tokens_all.shape
    tokens, low = reach // ep, tokens_all.dtype
    rows = model // (4 * ep)
    full = weights.shape[1]
    span = full // 3
    dma = pltpu.SemaphoreType.DMA
    anywhere = pl.BlockSpec(memory_space=pl.ANY)
    vmem = pl.BlockSpec(memory_space=pltpu.VMEM)
    shape = jax.ShapeDtypeStruct
    return pl.pallas_call(
        experts_kernel,
        out_shape=(
            shape((tokens, model + 128), jnp.float32),
            shape((reach, model), low),
            shape((2, ep, rows, full // 2), low),
            shape((2, ep, rows, full // 2), low),
            shape((tokens, 128), jnp.float32),
        ),
        in_specs=[vmem] * 2 + [anywhere] * 3,
        out_specs=(vmem, anywhere, anywhere, anywhere, vmem),
        scratch_shapes=[
            pltpu.VMEM(tokens_all.shape, low),
            pltpu.VMEM(outer_all.shape, low),
            pltpu.VMEM(weights.shape, low),
            dma((2 + 3 * EXPERTS // ep,)),
            pltpu.VMEM((reach, 128), jnp.float32),
            pltpu.VMEM((reach, span), low),
            pltpu.VMEM((reach, 2 * span), low),
            pltpu.VMEM((reach, model + 128), low),
            pltpu.VMEM((reach, model), low),
            pltpu.VMEM(weights.shape, low),
            pltpu.VMEM((ep, 2, rows, full // 2), low),
            pltpu.VMEM((ep, 2, rows, full // 2), low),
            dma((2, ep, 2)),
            dma((2, ep, 2)),
            dma((3,)),
        ]
        + z_sum_scratch(ep, tokens, model + 128, low),
        compiler_params=pltpu.CompilerParams(
            collective_id=collective_id, has_side_effects=True, vmem_limit_bytes=63 * 1024 * 1024
        ),
        cost_estimate=lasting(90),
        name="experts",
    )(routes_all, extra, tokens_all, outer_all, weights)


def rear_kernel(
    gates_ref, log_ref, cos_ref, sin_ref, segment_ref, returned_hbm, middle_hbm, outer_hbm, extra_hbm,
    mixed_hbm, query_hbm, pair_hbm, input_hbm, normed1_hbm, mixture_ref, relay_ref, own_ref, attn_ref,
    input_grad, layer_out, qkv_out, wo_out, expert_out,
    returned_ref, middle_ref, outer_ref, extra_ref, mixed_ref, query_ref, pair_ref, input_ref, normed1_ref, in_sem,
    wo_s, qkv_s, query_s, grad_s, mixed_s, key_s, value_s, bias_s, query_grad_s, key_grad_s, value_grad_s,
    pair_s, landing_s, back_s, attn_grad_s, part_s, other_s, router_s, gains_s, mixture_s, own_s, second_s,
    local_sem, key_send, key_recv, pair_send, pair_recv, second_send, second_recv, swap_send, swap_recv, layer_send, layer_recv, *scratch,
):
    ep, rows = expert_out.shape[0], expert_out.shape[2]
    f, c, t = lax.axis_index("fsdp"), lax.axis_index("ctx"), lax.axis_index("tp")
    low = jnp.bfloat16
    tokens, model = input_ref.shape
    heads, key_heads = query_s.shape[0], key_s.shape[0]
    groups = heads // key_heads
    width, kv_width = heads * HD, key_heads * HD
    qkv_width = width + 2 * kv_width
    sent = []
    mixture = PairSum(mixture_ref, mixture_s, scratch[:7], sent)
    scratch = scratch[7:]
    size = len(shard_sum_scratch(ep, rows, 256, low))
    wo = ShardSum(wo_s, rows, width, scratch[:size], sent)
    qkv = ShardSum(qkv_s, rows, qkv_width + 128, scratch[size:], sent)
    partners = all_partners(ep)
    plane = [at_device(f, c ^ k, t) for k in range(1, 4)]
    core = partners[-1]

    coming = fetch(
        [
            (returned_hbm, returned_ref), (middle_hbm, middle_ref), (outer_hbm, outer_ref), (extra_hbm, extra_ref),
            (mixed_hbm, mixed_ref), (query_hbm, query_ref), (pair_hbm, pair_ref), (input_hbm, input_ref),
            (normed1_hbm, normed1_ref),
        ],
        in_sem,
    )
    copies = [
        pltpu.make_async_copy(attn_ref.at[:, pl.ds(qkv_width + 128, width)], wo_s, local_sem.at[0]),
        pltpu.make_async_copy(attn_ref.at[:, pl.ds(0, qkv_width + 128)], qkv_s, local_sem.at[1]),
    ]
    for copy in copies:
        copy.start()
    for g in range(ep):
        pltpu.make_async_copy(mixture_ref.at[mixture.place(g, t)], mixture_s.at[g], local_sem.at[2]).start()
    copies.append(pltpu.make_async_copy(own_ref, own_s, local_sem.at[3]))
    copies[2].start()
    greet(partners + plane[2:])
    order = wo.order
    mixture.to_core()
    seconds = {}

    def second(d):
        for way in range(2):
            copy = remote(
                relay_ref.at[way, d], second_s.at[way, d], second_send.at[way, d], second_recv.at[way, d],
                plane[1 - way],
            )
            copy.start()
            sent.append((None, copy))
            seconds[way, d] = copy

    def swap(d):
        for way in range(2):
            seconds[way, d].wait_recv()
        own_s[:, d] = (own_s[:, d].astype(jnp.float32) + second_s[:, d].astype(jnp.float32)).astype(low)
        if d == 0:
            copy = pltpu.make_async_copy(own_s.at[:, 0], expert_out.at[f], swap_send.at[0])
            copy.start()
            copies.append(copy)
        else:
            copy = remote(own_s.at[:, d], expert_out.at[f], swap_send.at[d], swap_recv.at[d], partners[d - 1])
            copy.start()
            sent.append((None, copy))

    second(1)

    small_lane = lax.broadcasted_iota(jnp.int32, (tokens, 128), 1)
    for copy in coming[:4]:
        copy.wait()
    gains = extra_ref[...].astype(jnp.float32).T
    gain_one, gain_two = gains[EXPERTS : EXPERTS + 1, :], gains[EXPERTS + 1 : EXPERTS + 2, :]
    tail = returned_ref[:, model:]
    picked = jnp.where(small_lane < EXPERTS, tail + pltpu.roll(tail, 128 - EXPERTS, 1), 0.0)
    gates = gates_ref[...]
    logit_grad = (gates * (picked - jnp.sum(gates * picked, -1, keepdims=True))).astype(low)
    second_grad = returned_ref[:, :model] + lax.dot_general(
        logit_grad, extra_ref[...], (((1,), (1,)), ((), ())), preferred_element_type=jnp.float32
    )
    middle = middle_ref[...]
    inverse = lax.rsqrt(jnp.mean(middle * middle, -1, keepdims=True) + EPSILON)
    scaled = second_grad * gain_two
    mean_term = jnp.mean(scaled * middle, -1, keepdims=True)
    gains_s[1:2, :] = jnp.sum(second_grad * middle * inverse, 0, keepdims=True)
    middle_grad = outer_ref[...].astype(jnp.float32) + (
        inverse * scaled - middle * (inverse * inverse * inverse) * mean_term
    )
    input_grad[...] = middle_grad
    attn_grad_s[...] = middle_grad.astype(low)

    pltpu.make_async_copy(mixture_s, mixture_s, local_sem.at[2]).wait()
    mixture.begin()
    second(2)
    copies[0].wait()
    for start in range(0, width, 256):
        tile = jnp.dot(
            attn_grad_s[...], wo_s[:, start : start + 256], preferred_element_type=jnp.float32
        ).astype(low)
        for side in range(0, 256, HD):
            grad_s[(start + side) // HD] = tile[:, side : side + HD]

    copies[2].wait()
    swap(1)
    second(3)
    length = segment_ref.shape[1]
    seg_keys = jnp.broadcast_to(segment_ref[...].astype(jnp.float32), (128, length)).T[:, :1]
    seg_queries = segment_ref[:, pl.ds(pl.multiple_of(c * tokens, 128), tokens)].astype(jnp.float32)
    key_order = lax.broadcasted_iota(jnp.int32, (length, tokens), 0)
    query_order = lax.broadcasted_iota(jnp.int32, (length, tokens), 1) + c * tokens
    bias_s[...] = jnp.where((seg_keys == seg_queries) & (key_order <= query_order), 0.0, MASKED_SCORE)
    for copy in coming[4:]:
        copy.wait()
    for h in range(heads):
        query_s[h] = query_ref[:, h * HD : (h + 1) * HD]
        mixed_s[h] = mixed_ref[:, h * HD : (h + 1) * HD]
    for g in range(key_heads):
        key_s[g] = pair_ref[:, g * HD : (g + 1) * HD]
        value_s[g] = pair_ref[:, kv_width + g * HD : kv_width + (g + 1) * HD]
    across = (((1,), (1,)), ((), ()))

    def attend_back(g, carry):
        key_grad = jnp.zeros((length, HD), jnp.float32)
        value_grad = jnp.zeros((length, HD), jnp.float32)
        for number in range(groups):
            h = g * groups + number
            query = query_s[h] * jnp.asarray(HD**-0.5, low)
            grad = grad_s[h]
            scores = lax.dot_general(key_s[g], query, across, preferred_element_type=jnp.float32) + bias_s[...]
            probs = jnp.exp(scores - log_ref[h])
            value_grad += jnp.dot(probs.astype(low), grad, preferred_element_type=jnp.float32)
            prob_grad = lax.dot_general(value_s[g], grad, across, preferred_element_type=jnp.float32)
            delta = jnp.sum((grad.astype(jnp.float32) * mixed_s[h].astype(jnp.float32)).T, 0, keepdims=True)
            score_grad = (probs * (prob_grad - delta)).astype(low)
            key_grad += jnp.dot(score_grad, query, preferred_element_type=jnp.float32)
            query_grad = lax.dot_general(
                key_s[g], score_grad, (((0,), (0,)), ((), ())), preferred_element_type=jnp.float32
            )
            query_grad_s[h] = query_grad.T * (HD**-0.5)
        key_grad_s[g] = key_grad.astype(low)
        value_grad_s[g] = value_grad.astype(low)
        return carry

    lax.fori_loop(0, key_heads // 2, attend_back, 0)
    swap(2)
    second(0)
    lax.fori_loop(key_heads // 2, key_heads, attend_back, 0)
    for g in range(key_heads):
        pair_s[:, g * HD : (g + 1) * HD] = key_grad_s[g]
        pair_s[:, kv_width + g * HD : kv_width + (g + 1) * HD] = value_grad_s[g]
    for k in (3, 1, 2):
        place = pl.ds(pl.multiple_of((c ^ k) * tokens, 16), tokens)
        copy = remote(pair_s.at[place], landing_s.at[k - 1], key_send.at[k - 1], key_recv.at[k - 1], plane[k - 1])
        copy.start()
        sent.append((None, copy))
    def wo_sums(n, carry):
        at = pl.ds(pl.multiple_of(n * 256, 256), 256)
        wo_s[at, :] = lax.dot_general(
            attn_grad_s[:, at], mixed_ref[...], (((0,), (0,)), ((), ())), preferred_element_type=jnp.float32
        ).astype(low)
        return carry

    lax.fori_loop(0, model // 256, wo_sums, 0)
    router_s[...] = lax.dot_general(
        (middle * inverse * gain_two).astype(low), logit_grad, (((0,), (0,)), ((), ())),
        preferred_element_type=jnp.float32,
    )

    swap(3)
    swap(0)
    mixture.cross()
    first_half = lax.rem(small_lane, HD) < HD // 2

    def turned_back(tile):
        swapped = jnp.where(first_half, pltpu.roll(tile, 128 - HD // 2, 1), pltpu.roll(tile, HD // 2, 1))
        return tile * cos_ref[...] - swapped * sin_ref[...]

    for start in range(0, width, 128):
        tile = jnp.concatenate([query_grad_s[start // HD], query_grad_s[start // HD + 1]], 1)
        back_s[:, start : start + 128] = turned_back(tile).astype(low)

    pair = pair_s[pl.ds(pl.multiple_of(c * tokens, 16), tokens), :].astype(jnp.float32)
    for k in (1, 2, 3):
        block = landing_s.at[k - 1]
        remote(block, block, key_send.at[k - 1], key_recv.at[k - 1], plane[k - 1]).wait_recv()
        pair = pair + landing_s[k - 1].astype(jnp.float32)
    for d in order:
        wo.first(d)
    for start in range(0, kv_width, 128):
        back_s[:, width + start : width + start + 128] = turned_back(pair[:, start : start + 128]).astype(low)
    back_s[:, width + kv_width :] = pair[:, kv_width:].astype(low)
    copies[1].wait()
    for start in range(0, model, 256):
        part_s[:, start : start + 256] = lax.dot_general(
            back_s[...], qkv_s[start : start + 256, :qkv_width], across, preferred_element_type=jnp.float32
        ).astype(low)
    exchange = remote(part_s, other_s, pair_send, pair_recv, core)
    exchange.start()
    sent.append((None, exchange))

    def qkv_sums(n, carry):
        at = pl.ds(pl.multiple_of(n * 256, 256), 256)
        qkv_s[at, :qkv_width] = lax.dot_general(
            normed1_ref[:, at], back_s[...], (((0,), (0,)), ((), ())), preferred_element_type=jnp.float32
        ).astype(low)
        return carry

    lax.fori_loop(0, model // 256, qkv_sums, 0)
    exchange.wait_recv()
    first_grad = part_s[...].astype(jnp.float32) + other_s[...].astype(jnp.float32)
    inputs = input_ref[...].astype(jnp.float32)
    inverse = lax.rsqrt(jnp.mean(inputs * inputs, -1, keepdims=True) + EPSILON)
    gains_s[0:1, :] = jnp.sum(first_grad * inputs * inverse, 0, keepdims=True)
    line = lax.broadcasted_iota(jnp.int32, (128, model), 0)
    turned = jnp.where(line == EXPERTS, gains_s[0:1, :], jnp.where(line == EXPERTS + 1, gains_s[1:2, :], 0.0)).T
    qkv_s[:, qkv_width:] = (router_s[...] + turned).astype(low)
    qkv.first(1)
    qkv.first(2)
    for d in wo.order:
        wo.second(d)
    scaled = first_grad * gain_one
    mean_term = jnp.mean(scaled * inputs, -1, keepdims=True)
    input_grad[...] += inverse * scaled - inputs * (inverse * inverse * inverse) * mean_term
    qkv.second(1)
    qkv.first(3)
    wo.to_z(1, wo_out)
    qkv.second(2)
    qkv.first(0)
    qkv.to_z(1, qkv_out)
    wo.to_z(2, wo_out)
    qkv.second(3)
    qkv.to_z(2, qkv_out)
    wo.to_z(3, wo_out)
    qkv.second(0)
    qkv.to_z(3, qkv_out)
    wo.to_z(0, wo_out)
    qkv.to_z(0, qkv_out)
    copies[3].wait()
    for d in range(1, ep):
        landing = expert_out.at[lax.rem(f + ep - d, ep)]
        remote(landing, landing, swap_send.at[d], swap_recv.at[d], core).wait_recv()
    wo.from_z(wo_out)
    half, other_half = (pl.ds(pl.multiple_of(part * (tokens // 2), 16), tokens // 2) for part in (t, 1 - t))
    layer_out[half, :] = (middle_ref[half, :] + mixture.collect()).astype(low)
    layer_copy = remote(layer_out.at[half], layer_out.at[half], layer_send, layer_recv, core)
    layer_copy.start()
    sent.append((None, layer_copy))
    qkv.from_z(qkv_out)
    remote(layer_out.at[other_half], layer_out.at[other_half], layer_send, layer_recv, core).wait_recv()
    all_sent(sent)


def rear(
    returned, gates, middle, inputs, outer, normed1, query, pair, mixed, log_total, cosine, sine, segments, extra,
    mixture, relay, own, attn, collective_id,
):
    ep = lax.axis_size("fsdp")
    tokens, model = inputs.shape
    rows = own.shape[2]
    heads, key_heads = query.shape[1] // HD, pair.shape[1] // (2 * HD)
    width, kv_width = heads * HD, key_heads * HD
    qkv_width = width + 2 * kv_width
    length = pair.shape[0]
    low = jnp.bfloat16
    dma = pltpu.SemaphoreType.DMA
    anywhere = pl.BlockSpec(memory_space=pl.ANY)
    vmem = pl.BlockSpec(memory_space=pltpu.VMEM)
    shape = jax.ShapeDtypeStruct
    room = pltpu.VMEM
    fetched = (returned, middle, outer, extra, mixed, query, pair, inputs, normed1)
    return pl.pallas_call(
        rear_kernel,
        out_shape=(
            shape((tokens, model), jnp.float32),
            shape((tokens, model), low),
            shape((rows, qkv_width + 128), jnp.float32),
            shape((rows, width), jnp.float32),
            shape((ep, 2, rows, own.shape[3]), low),
        ),
        in_specs=[vmem] * 5 + [anywhere] * 13,
        out_specs=(vmem,) * 4 + (anywhere,),
        scratch_shapes=[room(each.shape, each.dtype) for each in fetched]
        + [
            dma((len(fetched),)),
            room((model, width), low),
            room((model, qkv_width + 128), low),
            room((heads, tokens, HD), low),
            room((heads, tokens, HD), low),
            room((heads, tokens, HD), low),
            room((key_heads, length, HD), low),
            room((key_heads, length, HD), low),
            room((length, tokens), jnp.float32),
            room((heads, tokens, HD), jnp.float32),
            room((key_heads, length, HD), low),
            room((key_heads, length, HD), low),
            room((length, 2 * kv_width), low),
            room((3, tokens, 2 * kv_width), low),
            room((tokens, qkv_width), low),
            room((tokens, model), low),
            room((tokens, model), low),
            room((tokens, model), low),
            room((model, 128), jnp.float32),
            room((8, model), jnp.float32),
            room((ep, tokens // 2, model), low),
            room(own.shape, low),
            room(own.shape, low),
            dma((4,)),
            dma((3,)),
            dma((3,)),
            dma,
            dma,
            dma((2, ep)),
            dma((2, ep)),
            dma((ep,)),
            dma((ep,)),
            dma,
            dma,
        ]
        + pair_sum_scratch(ep, tokens, model, low)
        + shard_sum_scratch(ep, rows, width, low)
        + shard_sum_scratch(ep, rows, qkv_width + 128, low),
        compiler_params=pltpu.CompilerParams(
            collective_id=collective_id, has_side_effects=True, vmem_limit_bytes=63 * 1024 * 1024
        ),
        cost_estimate=lasting(170),
        name="rear",
    )(gates, log_total, cosine, sine, segments, *fetched, mixture, relay, own, attn)


def finish_kernel(
    expert_ref, qkv_ref, wo_ref, input_ref, layer_ref,
    query_out, key_out, value_out, output_out, router_out, gain_one_out, gain_two_out,
    gate_out, up_out, down_out, input_out, layer_out,
):
    local, _, hidden = gate_out.shape
    cut = expert_ref.shape[3] // local
    for e in range(local):
        at = slice(e * cut, (e + 1) * cut)
        both = jnp.concatenate([expert_ref[0, 0, :, at], expert_ref[0, 1, :, at]], 1).astype(jnp.float32)
        for kind, out in enumerate((gate_out, up_out, down_out)):
            out[e] = both[:, kind * hidden : (kind + 1) * hidden]
    input_out[...] = input_ref[...]
    layer_out[...] = layer_ref[...]

    @pl.when(pl.program_id(0) == 0)
    def _():
        width, kv_width = query_out.shape[1], key_out.shape[1]
        query_out[...] = qkv_ref[:, :width]
        key_out[...] = qkv_ref[:, width : width + kv_width]
        value_out[...] = qkv_ref[:, width + kv_width : width + 2 * kv_width]
        small = qkv_ref[:, width + 2 * kv_width :].T
        router_out[...] = small[:EXPERTS]
        gain_one_out[...] = small[EXPERTS : EXPERTS + 1]
        gain_two_out[...] = small[EXPERTS + 1 : EXPERTS + 2]
        output_out[...] = wo_ref[...]


def finish(experts, qkv, wo, input_grad, layer_output, kv_width, hidden):
    ep, _, rows, half = experts.shape
    width = wo.shape[1]
    local = 2 * half // (3 * hidden)
    tokens, model = input_grad.shape
    shape = jax.ShapeDtypeStruct

    def whole(*dims):
        return pl.BlockSpec(dims, lambda i: (0, 0))

    by_z = pl.BlockSpec((local, rows, hidden), lambda i: (i, 0, 0))
    by_rows = pl.BlockSpec((tokens // ep, model), lambda i: (i, 0))
    return pl.pallas_call(
        finish_kernel,
        grid=(ep,),
        out_shape=(
            shape((rows, width), jnp.float32),
            shape((rows, kv_width), jnp.float32),
            shape((rows, kv_width), jnp.float32),
            shape((rows, width), jnp.float32),
            shape((EXPERTS, rows), jnp.float32),
            shape((1, rows), jnp.float32),
            shape((1, rows), jnp.float32),
            shape((ep * local, rows, hidden), jnp.float32),
            shape((ep * local, rows, hidden), jnp.float32),
            shape((ep * local, rows, hidden), jnp.float32),
            shape((tokens, model), jnp.float32),
            shape((tokens, model), layer_output.dtype),
        ),
        in_specs=[
            pl.BlockSpec((1, 2, rows, half), lambda i: (i, 0, 0, 0)),
            whole(*qkv.shape),
            whole(*wo.shape),
            by_rows,
            by_rows,
        ],
        out_specs=(
            whole(rows, width),
            whole(rows, kv_width),
            whole(rows, kv_width),
            whole(rows, width),
            whole(EXPERTS, rows),
            whole(1, rows),
            whole(1, rows),
            by_z,
            by_z,
            by_z,
            by_rows,
            by_rows,
        ),
        compiler_params=pltpu.CompilerParams(vmem_limit_bytes=60 * 1024 * 1024),
        cost_estimate=lasting(6),
        name="finish",
    )(experts, qkv, wo, input_grad, layer_output)


def plain_shards(
    layer_input,
    segments,
    routes,
    norm_gain,
    query_weight,
    key_weight,
    value_weight,
    output_weight,
    ffn_gain,
    router_weight,
    gate_weight,
    up_weight,
    down_weight,
    cotangent,
):
    low = jnp.bfloat16
    both = ("fsdp", "ctx")
    ep = lax.axis_size("fsdp")
    tokens = layer_input.shape[0]
    seq_len = segments.shape[1]
    rows = query_weight.shape[0]
    width = query_weight.shape[1]
    kv_width = key_weight.shape[1]
    hidden_width = gate_weight.shape[2]
    local = EXPERTS // ep
    span = local * hidden_width

    qkv_width = width + 2 * kv_width
    extra = jnp.concatenate([router_weight, norm_gain[:, None], ffn_gain[:, None]], 1)
    extra = jnp.pad(extra, ((0, 0), (0, 128 - extra.shape[1])))
    attn_shard = jnp.concatenate([query_weight, key_weight, value_weight, extra, output_weight.T], 1)
    down_shard = down_weight.transpose(0, 2, 1)
    begin = lax.axis_index("ctx") * tokens
    segment_row = segments[0]
    query_doc = lax.dynamic_slice_in_dim(segment_row, begin, tokens)
    query_order = begin + jnp.arange(tokens, dtype=jnp.int32)
    scale = HD ** (-0.5)
    inputs = layer_input.astype(jnp.float32)
    key_groups = kv_width // HD
    groups = width // kv_width
    freq = 10000.0 ** (-2.0 * jnp.arange(HD // 2, dtype=jnp.float32) / HD)

    def unpack(attn_full):
        return (
            attn_full[:, :qkv_width],
            attn_full[:, qkv_width : qkv_width + EXPERTS],
            attn_full[:, qkv_width + EXPERTS],
            attn_full[:, qkv_width + EXPERTS + 1],
            attn_full[:, qkv_width + 128 :],
        )

    attn_full = lax.all_gather(attn_shard, both, axis=0, tiled=True)
    qkv_full, router_full, gain_one, gain_two, output_turned = unpack(attn_full)
    packed = jnp.concatenate([gate_weight, up_weight, down_shard], -1)
    expert_full = spread_experts(packed)
    expert_full = expert_full.reshape(D, local, 3, hidden_width).transpose(0, 2, 1, 3)
    expert_full = expert_full.reshape(D, 3 * span)
    outer_all = lax.all_gather(cotangent, "fsdp", axis=0, tiled=True)
    routes_all = lax.all_gather(routes, "fsdp", axis=0, tiled=True)
    place = lax.dynamic_slice_in_dim(document_place(segment_row), begin, tokens)
    angle = place.astype(jnp.float32)[:, None] * freq[None, :]
    cosine, sine = jnp.cos(angle), jnp.sin(angle)
    first_norm, first_inverse = normalize(inputs, gain_one)
    normed1 = first_norm.astype(low)
    projected = jnp.dot(normed1, qkv_full, preferred_element_type=jnp.float32)
    query = rotate(projected[:, :width], cosine, sine).astype(low)
    key = rotate(projected[:, width : width + kv_width], cosine, sine).astype(low)
    value = projected[:, width + kv_width :].astype(low)
    pair_all = lax.all_gather(jnp.concatenate([key, value], 1), "ctx", axis=0, tiled=True)
    heads = query.reshape(tokens, key_groups, groups, HD)
    key_heads = pair_all[:, :kv_width].reshape(seq_len, key_groups, HD)
    value_heads = pair_all[:, kv_width:].reshape(seq_len, key_groups, HD)
    scores = jnp.einsum("qkgd,nkd->qkgn", heads, key_heads, preferred_element_type=jnp.float32) * scale
    seen = (segment_row[None, :] == query_doc[:, None]) & (
        jnp.arange(seq_len, dtype=jnp.int32)[None, :] <= query_order[:, None]
    )
    scores = jnp.where(seen[:, None, None, :], scores, MASKED_SCORE)
    running = jnp.max(scores, -1)
    weights = jnp.exp(scores - running[..., None])
    summed = jnp.einsum(
        "qkgn,nkd->qkgd", weights.astype(low), value_heads, preferred_element_type=jnp.float32
    )
    totals = jnp.sum(weights, -1)
    log_total = running + jnp.log(totals)
    mixed_low = (summed / totals[..., None]).reshape(tokens, -1).astype(low)
    attention = lax.psum(
        times_transpose(mixed_low, output_turned).astype(low), "tp"
    ).astype(jnp.float32)
    middle = inputs + attention
    second_norm, second_inverse = normalize(middle, gain_two)
    normed2 = second_norm.astype(low)
    normed2_all = lax.all_gather(normed2, "fsdp", axis=0, tiled=True)
    gate_up = expert_full[:, : 2 * span]
    down_turned = expert_full[:, 2 * span :]
    key_all = pair_all[:, :kv_width]
    value_all = pair_all[:, kv_width:]
    grouped = query.reshape(tokens, key_groups, groups, HD)

    def block_scores(key_piece, offset):
        count = key_piece.shape[0]
        key_heads = key_piece.reshape(count, key_groups, HD)
        scores = (
            jnp.einsum("qkgd,nkd->qkgn", grouped, key_heads, preferred_element_type=jnp.float32)
            * scale
        )
        key_doc = lax.dynamic_slice_in_dim(segment_row, offset, count)
        key_order = offset + jnp.arange(count, dtype=jnp.int32)
        seen = (key_doc[None, :] == query_doc[:, None]) & (
            key_order[None, :] <= query_order[:, None]
        )
        return (scores, seen[:, None, None, :], key_heads)

    def masked_away(offset, count):
        last_doc = lax.dynamic_index_in_dim(segment_row, offset + count - 1, keepdims=False)
        return (offset > query_order[tokens - 1]) | (last_doc < query_doc[0])

    place_z = lax.axis_index("fsdp")
    logits_all = jnp.dot(normed2_all, router_full, preferred_element_type=jnp.float32)
    expert_ids = jnp.arange(EXPERTS, dtype=jnp.int32)
    chosen_all = jnp.any(routes_all[:, :, None] == expert_ids[None, None, :], 1)
    masked_logits = jnp.where(chosen_all, logits_all, MASKED_SCORE)
    top = jnp.max(masked_logits, -1, keepdims=True)
    lifted = jnp.where(chosen_all, jnp.exp(masked_logits - top), 0.0)
    gates_all = lifted / jnp.sum(lifted, -1, keepdims=True)
    gates_here = lax.dynamic_slice_in_dim(gates_all, place_z * local, local, 1)
    chosen_here = lax.dynamic_slice_in_dim(chosen_all, place_z * local, local, 1)
    chosen = lax.dynamic_slice_in_dim(chosen_all, place_z * tokens, tokens, 0)
    gates = lax.dynamic_slice_in_dim(gates_all, place_z * tokens, tokens, 0)

    reach = normed2_all.shape[0]
    both_sides = jnp.dot(normed2_all, gate_up, preferred_element_type=jnp.float32)
    former = both_sides[:, :span]
    latter = both_sides[:, span:]
    hidden_grad = jnp.dot(outer_all, down_turned, preferred_element_type=jnp.float32)
    gate_wide = jnp.concatenate(
        [jnp.broadcast_to(gates_here[:, e : e + 1], (reach, hidden_width)) for e in range(local)], 1
    )
    logistic = jax.nn.sigmoid(former)
    active = former * logistic
    hidden = (active * latter).astype(low).astype(jnp.float32)
    gated = (hidden * gate_wide).astype(low)
    parts = [slice(e * hidden_width, (e + 1) * hidden_width) for e in range(local)]
    dgates = jnp.stack([jnp.sum(hidden[:, part] * hidden_grad[:, part], -1) for part in parts], 1)
    scaled_grad = hidden_grad * gate_wide
    former_grad = (scaled_grad * latter * logistic * (1.0 + former * (1.0 - logistic))).astype(low)
    latter_grad = (scaled_grad * active).astype(low)
    side_grads = jnp.concatenate([former_grad, latter_grad], 1)
    mixture_low = times_transpose(gated, down_turned).astype(low)
    input_part = times_transpose(side_grads, gate_up)
    side_sums = contract_rows(normed2_all, side_grads)
    down_sums = contract_rows(outer_all, gated)
    dgates = jnp.where(chosen_here, dgates, 0.0)
    dgates_wide = lax.dynamic_update_slice_in_dim(
        jnp.zeros((reach, EXPERTS), jnp.float32), dgates, place_z * local, 1
    )
    dgates_high = dgates_wide.astype(low)
    dgates_rest = (dgates_wide - dgates_high.astype(jnp.float32)).astype(low)
    dgates_sent = jnp.concatenate([dgates_high, dgates_rest], 1)
    dgates_sent = jnp.pad(dgates_sent, ((0, 0), (0, 128 - 2 * EXPERTS)))
    back_part = jnp.concatenate([input_part.astype(low), dgates_sent], 1)
    returned = lax.psum_scatter(
        lax.psum(back_part, "tp"), "fsdp", scatter_dimension=0, tiled=True
    ).astype(jnp.float32)
    expert_sums = jnp.concatenate([side_sums, down_sums], 1).astype(low)
    expert_out = collect_experts(expert_sums, rows).reshape(ep, rows, 3, local, hidden_width)
    side_out = expert_out[:, :, :2].transpose(2, 0, 3, 1, 4).reshape(2, EXPERTS, rows, hidden_width)
    side_out = side_out.astype(jnp.float32)
    down_out = expert_out[:, :, 2].transpose(0, 2, 3, 1).reshape(EXPERTS, hidden_width, rows).astype(jnp.float32)

    outer_grad = cotangent.astype(jnp.float32)
    input_grad_part = returned[:, :D]
    picked = returned[:, D : D + EXPERTS] + returned[:, D + EXPERTS : D + 2 * EXPERTS]
    logit_grad = (gates * (picked - jnp.sum(gates * picked, -1, keepdims=True))).astype(low)
    router_sums = contract_rows(normed2, logit_grad)
    second_grad = input_grad_part + times_transpose(logit_grad, router_full)
    middle_back, gain_two_sums = norm_back(second_grad, middle, second_inverse, gain_two)
    middle_grad = outer_grad + middle_back
    attention_grad = middle_grad.astype(low)
    output_sums = contract_rows(attention_grad, mixed_low)
    mixed_grad = jnp.dot(attention_grad, output_turned, preferred_element_type=jnp.float32).astype(low)
    mixed_heads = mixed_grad.reshape(tokens, key_groups, groups, HD)
    delta = jnp.sum(mixed_heads.astype(jnp.float32) * mixed_low.reshape(mixed_heads.shape), -1)

    def back_two(number, state):
        offset = number * tokens
        key_piece = lax.dynamic_slice_in_dim(key_all, offset, tokens, 0)
        value_piece = lax.dynamic_slice_in_dim(value_all, offset, tokens, 0)

        def back_compute(inner):
            query_sum, pair_sum = inner
            scores, seen, key_heads = block_scores(key_piece, offset)
            probs = jnp.where(seen, jnp.exp(scores - log_total[..., None]), 0.0)
            value_heads = value_piece.reshape(tokens, key_groups, HD)
            prob_grad = jnp.einsum(
                "qkgd,nkd->qkgn", mixed_heads, value_heads, preferred_element_type=jnp.float32
            )
            score_grad = (probs * (prob_grad - delta[..., None])).astype(low)
            query_sum = (
                query_sum
                + jnp.einsum(
                    "qkgn,nkd->qkgd", score_grad, key_heads, preferred_element_type=jnp.float32
                )
                * scale
            )
            key_block = (
                jnp.einsum(
                    "qkgn,qkgd->nkd", score_grad, grouped, preferred_element_type=jnp.float32
                )
                * scale
            )
            value_block = jnp.einsum(
                "qkgn,qkgd->nkd", probs.astype(low), mixed_heads, preferred_element_type=jnp.float32
            )
            pair = jnp.concatenate([key_block.reshape(tokens, -1), value_block.reshape(tokens, -1)], 1)
            return (query_sum, lax.dynamic_update_slice_in_dim(pair_sum, pair, offset, 0))

        return lax.cond(masked_away(offset, tokens), lambda inner: inner, back_compute, state)

    back_state = (
        jnp.zeros((tokens, key_groups, groups, HD), jnp.float32),
        jnp.zeros((seq_len, 2 * kv_width), jnp.float32),
    )
    query_sum, pair_sum = lax.fori_loop(0, seq_len // tokens, back_two, back_state)
    pair_local = lax.psum_scatter(
        pair_sum.astype(low), "ctx", scatter_dimension=0, tiled=True
    ).astype(jnp.float32)
    query_back = rotate(query_sum.reshape(tokens, -1), cosine, -sine)
    key_back = rotate(pair_local[:, :kv_width], cosine, -sine)
    qkv_back = jnp.concatenate([query_back, key_back, pair_local[:, kv_width:]], 1).astype(low)
    qkv_sums = contract_rows(normed1, qkv_back)
    first_part = times_transpose(qkv_back, qkv_full)
    first_grad = lax.psum(first_part.astype(low), "tp").astype(jnp.float32)
    input_back, gain_one_sums = norm_back(first_grad, inputs, first_inverse, gain_one)
    input_grad = middle_grad + input_back
    small_sums = jnp.concatenate([router_sums, gain_one_sums[:, None], gain_two_sums[:, None]], 1)
    small_sums = jnp.pad(small_sums, ((0, 0), (0, 128 - small_sums.shape[1])))
    attn_sums = jnp.concatenate([qkv_sums.astype(low), small_sums.astype(low), output_sums.astype(low)], 1)
    attn_out = lax.psum_scatter(attn_sums, both, scatter_dimension=0, tiled=True).astype(jnp.float32)
    mixture = lax.psum_scatter(
        lax.psum(mixture_low, "tp"), "fsdp", scatter_dimension=0, tiled=True
    ).astype(jnp.float32)
    layer_output = (middle + mixture).astype(low)
    small_out = attn_out[:, qkv_width : qkv_width + 128]
    return (
        layer_output,
        input_grad,
        small_out[:, EXPERTS],
        attn_out[:, :width],
        attn_out[:, width : width + kv_width],
        attn_out[:, width + kv_width : qkv_width],
        attn_out[:, qkv_width + 128 :].T,
        small_out[:, EXPERTS + 1],
        small_out[:, :EXPERTS],
        side_out[0],
        side_out[1],
        down_out,
    )


def shards(
    layer_input,
    segments,
    routes,
    norm_gain,
    query_weight,
    key_weight,
    value_weight,
    output_weight,
    ffn_gain,
    router_weight,
    gate_weight,
    up_weight,
    down_weight,
    cotangent,
):
    extra = jnp.concatenate([router_weight, norm_gain[:, None], ffn_gain[:, None]], 1)
    extra = jnp.pad(extra, ((0, 0), (0, 128 - extra.shape[1])))
    freq = 10000.0 ** (-2.0 * np.arange(HD // 2) / HD)
    (
        expert_full, outer_all, routes_all, normed2_all,
        attn_full, normed1, query, pair_all, mixed, middle, log_total, cosine, sine, extra_all,
    ) = front(
        query_weight, key_weight, value_weight, extra, output_weight.T, gate_weight, up_weight,
        down_weight.transpose(0, 2, 1), cotangent, routes.T, layer_input, segments,
        np.tile(freq.astype(np.float32), 4)[None, :],
    )
    returned, mixture, relay, own, gates = run_experts(
        normed2_all, outer_all, routes_all, extra_all, expert_full, 2
    )
    input_grad, layer_output, qkv_out, wo_out, expert_out = rear(
        returned, gates, middle, layer_input, cotangent, normed1, query, pair_all, mixed, log_total, cosine, sine,
        segments, extra_all, mixture, relay, own, attn_full, 3,
    )
    (
        query_out, key_out, value_out, output_out, router_out, gain_one_out, gain_two_out,
        gate_out, up_out, down_out, input_grad, layer_output,
    ) = finish(expert_out, qkv_out, wo_out, input_grad, layer_output, key_weight.shape[1], gate_weight.shape[2])
    return (
        layer_output,
        input_grad,
        gain_one_out[0],
        query_out,
        key_out,
        value_out,
        output_out.T,
        gain_two_out[0],
        router_out.T,
        gate_out,
        up_out,
        down_out.transpose(0, 2, 1),
    )


def solution(mesh):
    in_specs = (
        P(("fsdp", "ctx"), None),
        P("fsdp", None),
        P(("fsdp", "ctx"), None),
        P(("fsdp", "ctx")),
        P(("fsdp", "ctx"), "tp"),
        P(("fsdp", "ctx"), "tp"),
        P(("fsdp", "ctx"), "tp"),
        P("tp", ("fsdp", "ctx")),
        P(("fsdp", "ctx")),
        P(("fsdp", "ctx"), None),
        P(None, ("fsdp", "ctx"), "tp"),
        P(None, ("fsdp", "ctx"), "tp"),
        P(None, "tp", ("fsdp", "ctx")),
        P(("fsdp", "ctx"), None),
    )
    out_specs = (
        P(("fsdp", "ctx"), None),
        P(("fsdp", "ctx"), None),
        P(("fsdp", "ctx")),
        P(("fsdp", "ctx"), "tp"),
        P(("fsdp", "ctx"), "tp"),
        P(("fsdp", "ctx"), "tp"),
        P("tp", ("fsdp", "ctx")),
        P(("fsdp", "ctx")),
        P(("fsdp", "ctx"), None),
        P(None, ("fsdp", "ctx"), "tp"),
        P(None, ("fsdp", "ctx"), "tp"),
        P(None, "tp", ("fsdp", "ctx")),
    )
    fits = mesh.shape["ctx"] == 4 and mesh.shape["fsdp"] == 4 and mesh.shape["tp"] == 2
    body = shards if fits else plain_shards
    return jax.shard_map(body, mesh=mesh, in_specs=in_specs, out_specs=out_specs, check_vma=False)
```

```python
import jax
import jax.numpy as jnp
import numpy as np
from jax import lax
from jax.experimental import pallas as pl
from jax.experimental.pallas import tpu as pltpu
from jax.sharding import PartitionSpec as P

MESH = pl.DeviceIdType.MESH

D = 1536
HD = 64
EXPERTS = 16


EPSILON = 1e-05
MASKED_SCORE = -1e30


def rotate(values, cosine, sine):
    rows = values.shape[0]
    shaped = values.reshape(rows, -1, HD)
    half = HD // 2
    cosine, sine = cosine[:, None, :], sine[:, None, :]
    former = shaped[..., :half]
    latter = shaped[..., half:]
    turned = jnp.concatenate([former * cosine - latter * sine, latter * cosine + former * sine], -1)
    return turned.reshape(rows, -1)


def normalize(values, gain):
    inverse = lax.rsqrt(jnp.mean(values * values, -1, keepdims=True) + EPSILON)
    return (values * inverse * gain.astype(jnp.float32), inverse)


def norm_back(grad, values, inverse, gain):
    scaled = grad * gain.astype(jnp.float32)
    gain_grad = jnp.sum(grad * values * inverse, 0)
    mean_term = jnp.mean(scaled * values, -1, keepdims=True)
    return (inverse * scaled - values * inverse**3 * mean_term, gain_grad)


def document_place(segment_row):
    length = segment_row.shape[0]
    order = jnp.arange(length, dtype=jnp.int32)
    fresh = jnp.concatenate([jnp.ones((1,), jnp.bool_), segment_row[1:] != segment_row[:-1]])
    starts = lax.cummax(jnp.where(fresh, order, 0), axis=0)
    return order - starts


def contract_rows(left, right):
    return lax.dot_general(
        left, right, (((0,), (0,)), ((), ())), preferred_element_type=jnp.float32
    )


def times_transpose(left, right):
    return lax.dot_general(
        left, right, (((1,), (1,)), ((), ())), preferred_element_type=jnp.float32
    )


def spread_experts(packed):
    ep = lax.axis_size("fsdp")
    local = packed.shape[0] // ep
    rows = packed.shape[1]
    swapped = lax.all_to_all(packed, "fsdp", 0, 0, tiled=True)
    swapped = swapped.reshape(ep, local, rows, -1).transpose(0, 2, 1, 3)
    swapped = swapped.reshape(ep, rows, -1)
    whole = lax.all_gather(swapped, "ctx", axis=1)
    return whole.reshape(ep * lax.axis_size("ctx") * rows, -1)


def collect_experts(sums, rows):
    ep, ring = lax.axis_size("fsdp"), lax.axis_size("ctx")
    turned = sums.reshape(ep, ring, rows, -1).transpose(1, 0, 2, 3).reshape(sums.shape)
    mine = lax.psum_scatter(turned, "ctx", scatter_dimension=0, tiled=True)
    return lax.all_to_all(mine, "fsdp", 0, 0, tiled=True)


def at_device(fsdp, ctx, tp):
    return {"fsdp": fsdp, "ctx": ctx, "tp": tp}


def fetch(pairs, sems):
    copies = [pltpu.make_async_copy(source, target, sems.at[i]) for i, (source, target) in enumerate(pairs)]
    for copy in copies:
        copy.start()
    return copies


def greet(partners):
    barrier = pltpu.get_barrier_semaphore()
    for device in partners:
        pl.semaphore_signal(barrier, inc=1, device_id=device, device_id_type=MESH)
    pl.semaphore_wait(barrier, len(partners))


def remote(source, target, send, recv, device):
    return pltpu.make_async_remote_copy(
        src_ref=source, dst_ref=target, send_sem=send, recv_sem=recv, device_id=device, device_id_type=MESH
    )


def lasting(us):
    return pl.CostEstimate(flops=0, bytes_accessed=us * 3690000, transcendentals=0)


def front_kernel(
    query_ref, key_ref, value_ref, extra_ref, wo_ref, gate_ref, up_ref, down_ref, outer_ref, routes_ref,
    input_ref, segment_ref, freq_ref,
    expert_out, outer_out, routes_out, normed2_out,
    attn_hbm, normed1_hbm, query_hbm, pair_hbm, mixed_hbm, middle_hbm, log_out, cos_out, sin_out, extra_out,
    attn_out, normed1_out, query_out, pair_out, mixed_out, middle_out, out_sem,
    query_s, key_s, value_s, mixed_s, bias_s, part_s, other_s, normed2_s,
    local_sem, z_send, z_recv, plane_send, plane_recv, relay_send, relay_recv, core_send, core_recv,
    key_send, key_recv, pair_send, pair_recv, chain_send, chain_recv,
):
    ep = z_send.shape[1] + 1
    f, c, t = lax.axis_index("fsdp"), lax.axis_index("ctx"), lax.axis_index("tp")
    low = jnp.bfloat16
    rows = query_ref.shape[0]
    local = gate_ref.shape[0] // ep
    hidden = gate_ref.shape[2]
    tokens = outer_ref.shape[0]
    half = tokens // 2
    heads = query_s.shape[0]
    key_heads = key_s.shape[0]
    width, kv_width = heads * HD, key_heads * HD
    qkv_width = width + 2 * kv_width
    outs = (attn_out, expert_out)
    cuts = [(out.shape[1] // 256) * 128 for out in outs]

    def peer(distance):
        return lax.rem(f + distance, ep)

    def shard_rows(fsdp, ctx):
        return pl.ds(pl.multiple_of((fsdp * 4 + ctx) * rows, 16), rows)

    def columns(kind, side):
        cut, full = cuts[kind], outs[kind].shape[1]
        return pl.ds(0, cut) if side == 0 else pl.ds(cut, full - cut)

    line = [at_device(peer(d), c, t) for d in range(1, ep)]
    plane = [at_device(f, c ^ k, t) for k in range(1, 4)]
    x_device, y_device = plane[0], plane[1]
    core = at_device(f, c, 1 - t)
    greet(line + plane + [core])

    mine = shard_rows(f, c)
    sent = []

    def send(copy, when=None):
        if when is None:
            copy.start()
        else:
            pl.when(when)(copy.start)
        sent.append((when, copy))

    def await_arrival(copy, when=None):
        if when is None:
            copy.wait_recv()
        else:
            pl.when(when)(copy.wait_recv)

    def z_arrival(kind, d):
        place = shard_rows(peer(ep - d), c)
        remote(
            outs[kind].at[place], outs[kind].at[place], z_send.at[kind, d - 1], z_recv.at[kind, d - 1], x_device
        ).wait_recv()

    def spread(kind, g, when=None):
        place = shard_rows(g, c)
        for step in range(2):
            for way, device in enumerate((x_device, y_device)):
                side = step ^ way
                block = outs[kind].at[place, columns(kind, side)]
                send(
                    remote(
                        block, block, plane_send.at[kind, g, way, side], plane_recv.at[kind, g, way, side], device
                    ),
                    when,
                )

    def pass_on(kind, g, when=None):
        for way, device in enumerate((y_device, x_device)):
            place = shard_rows(g, c ^ (1 << way))
            block = outs[kind].at[place, columns(kind, way)]
            await_arrival(
                remote(
                    block, block, plane_send.at[kind, g, way, way], plane_recv.at[kind, g, way, way], device
                ),
                when,
            )
            send(remote(block, block, relay_send.at[kind, g, way], relay_recv.at[kind, g, way], device), when)

    def settle(kind):
        for g in range(ep):
            for way, device in enumerate((x_device, y_device)):
                side = 1 - way
                block = outs[kind].at[shard_rows(g, c ^ (1 << way)), columns(kind, side)]
                remote(
                    block, block, plane_send.at[kind, g, way, side], plane_recv.at[kind, g, way, side], device
                ).wait_recv()
                block = outs[kind].at[shard_rows(g, c ^ 3), columns(kind, way)]
                remote(
                    block, block, relay_send.at[kind, g, way], relay_recv.at[kind, g, way], device
                ).wait_recv()

    nexts = (at_device(jnp.minimum(f + 1, ep - 1), c, t), at_device(jnp.maximum(f - 1, 0), c, t))
    more = (f < ep - 1, f > 0)

    def chain_origin(way, hop):
        if way == 0:
            return jnp.maximum(f - hop, 0), f >= hop
        return jnp.minimum(f + hop, ep - 1), f + hop < ep

    def chain_begin(kind, source, target):
        for way in range(2):
            send(
                remote(source, target, chain_send.at[kind, way, 0], chain_recv.at[kind, way, 0], nexts[way]),
                more[way],
            )

    def chain_hop(kind, way, hop, block):
        there = chain_origin(way, hop)[1]
        await_arrival(
            remote(
                block, block, chain_send.at[kind, way, hop - 1], chain_recv.at[kind, way, hop - 1], nexts[way]
            ),
            there,
        )
        if hop < ep - 1:
            send(
                remote(block, block, chain_send.at[kind, way, hop], chain_recv.at[kind, way, hop], nexts[way]),
                there & more[way],
            )

    def line_place(fsdp, part):
        return pl.ds(pl.multiple_of(fsdp * tokens + part * half, 16), half)

    own_tokens = pl.ds(pl.multiple_of(f * tokens, 16), tokens)
    my_half = pl.ds(pl.multiple_of(t * half, 16), half)

    def line_hop(kind, hop, target):
        for way in range(2):
            g, there = chain_origin(way, hop)
            block = target.at[line_place(g, t)]
            chain_hop(kind, way, hop, block)
            send(remote(block, block, core_send.at[kind - 1, g], core_recv.at[kind - 1, g], core), there)

    def line_settle(kind, target):
        for g in range(ep):
            block = target.at[line_place(g, 1 - t)]
            await_arrival(
                remote(block, block, core_send.at[kind - 1, g], core_recv.at[kind - 1, g], core), f != g
            )

    start = 0
    for ref in (query_ref, key_ref, value_ref, extra_ref, wo_ref):
        pltpu.make_async_copy(
            ref, attn_out.at[mine, pl.ds(start, ref.shape[1])], local_sem.at[0]
        ).start()
        start += ref.shape[1]
    pltpu.make_async_copy(attn_out.at[mine], attn_out.at[mine], local_sem.at[0]).wait()
    chain_begin(0, attn_out.at[mine], attn_out.at[mine])
    own_outer = pltpu.make_async_copy(outer_ref, outer_out.at[own_tokens], local_sem.at[2])
    own_outer.start()
    own_columns = (slice(None), pl.ds(pl.multiple_of(f * tokens, 128), tokens))
    own_routes = pltpu.make_async_copy(routes_ref, routes_out.at[own_columns], local_sem.at[3])
    own_routes.start()
    for d in range(1, ep):
        send(
            remote(
                routes_ref, routes_out.at[own_columns], z_send.at[4, d - 1], z_recv.at[4, d - 1], line[d - 1]
            )
        )
    for kind, ref in enumerate((gate_ref, up_ref, down_ref)):
        for e in range(local):
            target = expert_out.at[mine, pl.ds((kind * local + e) * hidden, hidden)]
            pltpu.make_async_copy(ref.at[f * local + e], target, local_sem.at[1]).start()
    spread(0, f)

    length = segment_ref.shape[1]
    seg_keys = segment_ref[...].astype(jnp.float32)
    seg_here = segment_ref[:, pl.ds(pl.multiple_of(c * tokens, 128), tokens)].astype(jnp.float32)
    seg_queries = jnp.broadcast_to(seg_here, (128, tokens)).T[:, :1]
    key_order = lax.broadcasted_iota(jnp.int32, (tokens, length), 1)
    query_order = lax.broadcasted_iota(jnp.int32, (tokens, length), 0) + c * tokens
    same = seg_keys == seg_queries
    seen = same & (key_order <= query_order)
    bias_s[...] = jnp.where(seen, 0.0, MASKED_SCORE)
    place = jnp.sum(jnp.where(same & (key_order < query_order), 1.0, 0.0), -1, keepdims=True)
    angle = place * freq_ref[...]
    lane = lax.broadcasted_iota(jnp.int32, (tokens, 128), 1)
    first_half = lax.rem(lane, HD) < HD // 2
    cosine = jnp.cos(angle)
    sine = jnp.where(first_half, -jnp.sin(angle), jnp.sin(angle))
    cos_out[...] = cosine
    sin_out[...] = sine
    inputs = input_ref[...].astype(jnp.float32)
    inverse = lax.rsqrt(jnp.mean(inputs * inputs, -1, keepdims=True) + EPSILON)

    pass_on(0, f)
    for hop in range(1, ep):
        for way in range(2):
            g, there = chain_origin(way, hop)
            chain_hop(0, way, hop, attn_out.at[shard_rows(g, c)])
            spread(0, g, there)
        if hop > 1:
            for way in range(2):
                pass_on(0, *chain_origin(way, hop - 1))
    for way in range(2):
        pass_on(0, *chain_origin(way, ep - 1))
    for d in range(1, ep):
        for kind, ref in enumerate((gate_ref, up_ref, down_ref)):
            for e in range(local):
                target = expert_out.at[mine, pl.ds((kind * local + e) * hidden, hidden)]
                remote(
                    ref.at[peer(d) * local + e], target, z_send.at[1, d - 1], z_recv.at[1, d - 1],
                    line[d - 1],
                ).start()
    pltpu.make_async_copy(expert_out.at[mine], expert_out.at[mine], local_sem.at[1]).wait()
    spread(1, f)
    settle(0)
    stores = [pltpu.make_async_copy(attn_out, attn_hbm, out_sem.at[0])]
    stores[0].start()

    def store(number, source, target):
        stores.append(pltpu.make_async_copy(source, target, out_sem.at[number]))
        stores[-1].start()

    gains = attn_out[:, qkv_width : qkv_width + 128].astype(jnp.float32).T
    normed1_out[...] = (inputs * inverse * gains[EXPERTS : EXPERTS + 1, :]).astype(low)
    store(1, normed1_out, normed1_hbm)

    def project(start):
        return jnp.dot(
            normed1_out[...], attn_out[:, start : start + 256], preferred_element_type=jnp.float32
        )

    def turned(tile):
        swapped = jnp.where(first_half, pltpu.roll(tile, 128 - HD // 2, 1), pltpu.roll(tile, HD // 2, 1))
        return tile * cos_out[...] + swapped * sin_out[...]

    here = pl.ds(pl.multiple_of(c * tokens, 16), tokens)
    for start in range(0, kv_width, 256):
        tile = project(width + start)
        for side in (0, 128):
            pair_out[here, start + side : start + side + 128] = turned(tile[:, side : side + 128]).astype(low)
    for start in range(0, kv_width, 256):
        pair_out[here, kv_width + start : kv_width + start + 256] = project(width + kv_width + start).astype(low)
    for k in (3, 1, 2):
        send(remote(pair_out.at[here], pair_out.at[here], key_send.at[k - 1], key_recv.at[k - 1], plane[k - 1]))
    for start in range(0, width, 256):
        tile = project(start)
        for side in (0, 128):
            query_out[:, start + side : start + side + 128] = turned(tile[:, side : side + 128]).astype(low)
    store(2, query_out, query_hbm)
    for h in range(heads):
        query_s[h] = query_out[:, h * HD : (h + 1) * HD]
    for k in range(1, 4):
        block = pair_out.at[pl.ds(pl.multiple_of((c ^ k) * tokens, 16), tokens)]
        remote(block, block, key_send.at[k - 1], key_recv.at[k - 1], plane[k - 1]).wait_recv()
    store(3, pair_out, pair_hbm)
    for g in range(key_heads):
        key_s[g] = pair_out[:, g * HD : (g + 1) * HD]
        value_s[g] = pair_out[:, kv_width + g * HD : kv_width + (g + 1) * HD]
    pass_on(1, f)
    for d in range(1, ep):
        z_arrival(1, d)
        spread(1, peer(ep - d))
    chain_begin(2, outer_ref.at[my_half], outer_out.at[line_place(f, t)])

    def attend(h, carry):
        g = lax.div(h, heads // key_heads)
        query = query_s[h] * jnp.asarray(HD**-0.5, low)
        scores = lax.dot_general(
            query, key_s[g], (((1,), (1,)), ((), ())), preferred_element_type=jnp.float32
        ) + bias_s[...]
        top = jnp.max(scores, -1, keepdims=True)
        weights = jnp.exp(scores - top)
        total = jnp.sum(weights, -1, keepdims=True)
        summed = jnp.dot(weights.astype(low), value_s[g], preferred_element_type=jnp.float32)
        mixed_s[h] = (summed / total).astype(low)
        log_out[h] = jnp.broadcast_to(top + jnp.log(total), (tokens, 128)).T[:1, :]
        return carry

    lax.fori_loop(0, heads, attend, 0)
    for h in range(heads):
        mixed_out[:, h * HD : (h + 1) * HD] = mixed_s[h]
    store(4, mixed_out, mixed_hbm)
    model = input_ref.shape[1]
    for start in range(0, model, 256):
        part_s[:, start : start + 256] = lax.dot_general(
            mixed_out[...], attn_out[start : start + 256, qkv_width + 128 :],
            (((1,), (1,)), ((), ())), preferred_element_type=jnp.float32,
        ).astype(low)
    exchange = remote(part_s, other_s, pair_send, pair_recv, core)
    send(exchange)
    pass_on(1, peer(ep - 1))
    line_hop(2, 1, outer_out)
    exchange.wait_recv()
    middle = input_ref[...].astype(jnp.float32) + (
        part_s[...].astype(jnp.float32) + other_s[...].astype(jnp.float32)
    )
    middle_out[...] = middle
    store(5, middle_out, middle_hbm)
    inverse = lax.rsqrt(jnp.mean(middle * middle, -1, keepdims=True) + EPSILON)
    gains = attn_out[:, qkv_width : qkv_width + 128].astype(jnp.float32).T
    normed2_s[...] = (middle * inverse * gains[EXPERTS + 1 : EXPERTS + 2, :]).astype(low)
    chain_begin(1, normed2_s.at[my_half], normed2_out.at[line_place(f, t)])
    own_normed2 = pltpu.make_async_copy(normed2_s, normed2_out.at[own_tokens], local_sem.at[4])
    own_normed2.start()
    for d in range(2, ep):
        pass_on(1, peer(ep - d))
    line_hop(1, 1, normed2_out)
    line_hop(2, 2, outer_out)
    line_hop(1, 2, normed2_out)
    line_hop(2, 3, outer_out)
    line_hop(1, 3, normed2_out)
    settle(1)
    line_settle(2, outer_out)
    line_settle(1, normed2_out)
    for d in range(1, ep):
        place = (slice(None), pl.ds(pl.multiple_of(peer(ep - d) * tokens, 128), tokens))
        remote(
            routes_out.at[place], routes_out.at[place], z_send.at[4, d - 1], z_recv.at[4, d - 1], core
        ).wait_recv()
        remote(
            expert_out.at[mine], expert_out.at[mine], z_send.at[1, d - 1], z_recv.at[1, d - 1], core
        ).wait_send()
    extra_out[...] = attn_out[:, qkv_width : qkv_width + 128]
    own_outer.wait()
    own_routes.wait()
    own_normed2.wait()
    for copy in stores:
        copy.wait()
    all_sent(sent)


def front(
    query, key, value, extra, wo, gate, up, down, outer, routes, inputs, segments, freq
):
    ep = lax.axis_size("fsdp")
    rows = query.shape[0]
    heads, key_heads = query.shape[1] // HD, key.shape[1] // HD
    width = sum(part.shape[1] for part in (query, key, value, extra, wo))
    total = rows * ep * lax.axis_size("ctx")
    local = gate.shape[0] // ep
    tokens, model = inputs.shape
    length = segments.shape[1]
    low = jnp.bfloat16
    dma = pltpu.SemaphoreType.DMA
    anywhere = pl.BlockSpec(memory_space=pl.ANY)
    vmem = pl.BlockSpec(memory_space=pltpu.VMEM)
    shape = jax.ShapeDtypeStruct
    kept = (
        ((total, width), low),
        ((tokens, model), low),
        ((tokens, heads * HD), low),
        ((length, 2 * key_heads * HD), low),
        ((tokens, heads * HD), low),
        ((tokens, model), jnp.float32),
    )
    return pl.pallas_call(
        front_kernel,
        out_shape=(
            shape((total, 3 * local * gate.shape[2]), low),
            shape((ep * tokens, model), low),
            shape((routes.shape[0], ep * tokens), routes.dtype),
            shape((ep * tokens, model), low),
        )
        + tuple(shape(*each) for each in kept)
        + (
            shape((heads, 1, tokens), jnp.float32),
            shape((tokens, 128), jnp.float32),
            shape((tokens, 128), jnp.float32),
            shape((total, 128), low),
        ),
        in_specs=[anywhere] * 10 + [vmem] * 3,
        out_specs=(anywhere,) * 10 + (vmem,) * 4,
        scratch_shapes=[pltpu.VMEM(*each) for each in kept]
        + [
            dma((len(kept),)),
            pltpu.VMEM((heads, tokens, HD), low),
            pltpu.VMEM((key_heads, length, HD), low),
            pltpu.VMEM((key_heads, length, HD), low),
            pltpu.VMEM((heads, tokens, HD), low),
            pltpu.VMEM((tokens, length), jnp.float32),
            pltpu.VMEM((tokens, model), low),
            pltpu.VMEM((tokens, model), low),
            pltpu.VMEM((tokens, model), low),
            dma((5,)),
            dma((5, ep - 1)),
            dma((5, ep - 1)),
            dma((2, ep, 2, 2)),
            dma((2, ep, 2, 2)),
            dma((2, ep, 2)),
            dma((2, ep, 2)),
            dma((2, ep)),
            dma((2, ep)),
            dma((3,)),
            dma((3,)),
            dma,
            dma,
            dma((3, 2, ep - 1)),
            dma((3, 2, ep - 1)),
        ],
        compiler_params=pltpu.CompilerParams(
            collective_id=1, has_side_effects=True, vmem_limit_bytes=60 * 1024 * 1024
        ),
        cost_estimate=lasting(165),
        name="front",
    )(query, key, value, extra, wo, gate, up, down, outer, routes, inputs, segments, freq)


def z_sum_scratch(ep, tokens, width, low):
    dma = pltpu.SemaphoreType.DMA
    return [
        pltpu.VMEM((ep, tokens // 2, width), low),
        pltpu.VMEM((ep - 1, tokens // 2, width), low),
        pltpu.VMEM((ep - 1, tokens // 2, width), low),
        dma((ep,)),
        dma((ep,)),
        dma((ep - 1,)),
        dma((ep - 1,)),
        dma,
        dma,
    ]


class ZSum:
    size = 9

    def __init__(self, part, scratch, sent):
        self.part, self.sent = part, sent
        (
            self.core_in, self.z_out, self.z_in, self.core_send, self.core_recv,
            self.z_send, self.z_recv, self.back_send, self.back_recv,
        ) = scratch
        self.ep, self.half = self.core_in.shape[0], self.core_in.shape[1]
        self.f, self.c, self.t = lax.axis_index("fsdp"), lax.axis_index("ctx"), lax.axis_index("tp")
        self.core = at_device(self.f, self.c, 1 - self.t)

    def peer(self, distance):
        return lax.rem(self.f + distance, self.ep)

    def place(self, fsdp, part):
        return pl.ds(pl.multiple_of(fsdp * 2 * self.half + part * self.half, 16), self.half)

    def rows(self, part):
        return pl.ds(pl.multiple_of(part * self.half, 16), self.half)

    def send(self, copy):
        copy.start()
        self.sent.append((None, copy))

    def to_core(self, d):
        self.send(
            remote(
                self.part.at[self.place(self.peer(d), 1 - self.t)], self.core_in.at[d],
                self.core_send.at[d], self.core_recv.at[d], self.core,
            )
        )

    def added(self, d):
        landing = self.core_in.at[d]
        remote(landing, landing, self.core_send.at[d], self.core_recv.at[d], self.core).wait_recv()
        mine = self.part[self.place(self.peer(d), self.t), :]
        return mine.astype(jnp.float32) + self.core_in[d].astype(jnp.float32)

    def to_z(self, d):
        self.z_out[d - 1] = self.added(d).astype(self.z_out.dtype)
        self.send(
            remote(
                self.z_out.at[d - 1], self.z_in.at[d - 1], self.z_send.at[d - 1], self.z_recv.at[d - 1],
                at_device(self.peer(d), self.c, self.t),
            )
        )

    def collect(self):
        total = self.added(0)
        for d in range(1, self.ep):
            landing = self.z_in.at[d - 1]
            remote(landing, landing, self.z_send.at[d - 1], self.z_recv.at[d - 1], self.core).wait_recv()
            total = total + self.z_in[d - 1].astype(jnp.float32)
        return total

    def share(self, out):
        mine = out.at[self.rows(self.t)]
        self.send(remote(mine, mine, self.back_send, self.back_recv, self.core))

    def finish(self, out):
        other = out.at[self.rows(1 - self.t)]
        remote(other, other, self.back_send, self.back_recv, self.core).wait_recv()


def pair_sum_scratch(ep, tokens, width, low):
    dma = pltpu.SemaphoreType.DMA
    return [
        pltpu.VMEM((ep, tokens // 2, width), low),
        pltpu.VMEM((4, tokens // 2, width), low),
        dma((ep,)),
        dma((ep,)),
        dma((4,)),
        dma((4,)),
        dma((2,)),
    ]


class PairSum:
    def __init__(self, part, mine, scratch, sent):
        self.part, self.mine, self.sent = part, mine, sent
        (
            self.own, self.landing, self.core_send, self.core_recv, self.send_sem, self.recv_sem, self.cross_sem
        ) = scratch
        self.ep, self.half = self.own.shape[0], self.own.shape[1]
        self.f, c, self.t = lax.axis_index("fsdp"), lax.axis_index("ctx"), lax.axis_index("tp")
        self.core = at_device(self.f, c, 1 - self.t)
        self.partner = self.f ^ 1
        self.inner = (self.f == 1) | (self.f == 2)
        self.others = [2 - (self.f & 2) + j for j in range(2)]
        self.devices = [at_device(g, c, self.t) for g in self.others]
        self.beside = at_device(self.partner, c, self.t)

    def place(self, g, part):
        return pl.ds(pl.multiple_of(g * 2 * self.half + part * self.half, 16), self.half)

    def send(self, copy, when=None):
        if when is None:
            copy.start()
        else:
            pl.when(when)(copy.start)
        self.sent.append((when, copy))

    def to_core(self):
        for g in range(self.ep):
            self.send(
                remote(
                    self.part.at[self.place(g, 1 - self.t)], self.own.at[g],
                    self.core_send.at[g], self.core_recv.at[g], self.core,
                )
            )

    def both_cores(self, g):
        block = self.own.at[g]
        remote(block, block, self.core_send.at[g], self.core_recv.at[g], self.core).wait_recv()
        return self.mine[g].astype(jnp.float32) + self.own[g].astype(jnp.float32)

    def begin(self):
        outer = jnp.logical_not(self.inner)
        for j, g in enumerate(self.others):
            self.own[g] = self.both_cores(g).astype(self.own.dtype)
            self.send(
                remote(
                    self.own.at[g], self.landing.at[1 + j], self.send_sem.at[1 + j], self.recv_sem.at[1 + j],
                    self.beside,
                ),
                outer,
            )
        self.own[self.partner] = self.both_cores(self.partner).astype(self.own.dtype)
        self.send(
            remote(
                self.own.at[self.partner], self.landing.at[0], self.send_sem.at[0], self.recv_sem.at[0], self.beside
            )
        )

    def cross(self):
        for j, g in enumerate(self.others):

            @pl.when(self.inner)
            def _():
                block = self.landing.at[1 + j]
                remote(block, block, self.send_sem.at[1 + j], self.recv_sem.at[1 + j], self.beside).wait_recv()
                added = self.own[g].astype(jnp.float32) + self.landing[1 + j].astype(jnp.float32)
                self.own[g] = added.astype(self.own.dtype)

            self.send(
                remote(
                    self.own.at[g], self.landing.at[3], self.cross_sem.at[j], self.recv_sem.at[3], self.devices[j]
                ),
                self.inner,
            )

    def collect(self):
        total = self.both_cores(self.f)
        for slot in (0, 3):
            block = self.landing.at[slot]
            remote(block, block, self.send_sem.at[slot], self.recv_sem.at[slot], self.beside).wait_recv()
            total = total + self.landing[slot].astype(jnp.float32)
        return total


def all_sent(sent):
    for when, copy in sent:
        if when is None:
            copy.wait_send()
        else:
            pl.when(when)(copy.wait_send)


def shard_sum_scratch(ep, rows, width, low):
    cut = first_columns(width)
    widths = [cut] if cut == width else [cut, width - cut]
    dma = pltpu.SemaphoreType.DMA
    scratch = []
    for part in widths:
        scratch += [
            pltpu.VMEM((ep, 2, rows, part), low),
            pltpu.VMEM((ep, rows, part), low),
            pltpu.VMEM((ep, rows, part), low),
        ]
    return scratch + [
        dma((2, ep, 2)), dma((2, ep, 2)), dma((2, ep)), dma((2, ep)), dma((2, ep)), dma((2, ep))
    ]


def first_columns(width):
    return width if width == 128 else -(-width // 256) * 128


class ShardSum:
    def __init__(self, part, rows, width, scratch, sent):
        self.part, self.rows, self.sent = part, rows, sent
        cut = first_columns(width)
        self.columns = [pl.ds(0, cut)] + ([] if cut == width else [pl.ds(cut, width - cut)])
        self.ways = range(len(self.columns))
        (
            self.first_send, self.first_recv, self.second_send, self.second_recv, self.z_send, self.z_recv
        ) = scratch[-6:]
        self.first_in = [scratch[3 * way] for way in self.ways]
        self.second_in = [scratch[3 * way + 1] for way in self.ways]
        self.z_in = [scratch[3 * way + 2] for way in self.ways]
        self.ep = self.first_in[0].shape[0]
        self.f, self.c, self.t = lax.axis_index("fsdp"), lax.axis_index("ctx"), lax.axis_index("tp")
        self.neighbours = (at_device(self.f, self.c ^ 1, self.t), at_device(self.f, self.c ^ 2, self.t))
        self.order = list(range(1, self.ep)) + [0]

    def peer(self, distance):
        return lax.rem(self.f + distance, self.ep)

    def block(self, distance, ctx, way):
        start = (self.peer(distance) * 4 + ctx) * self.rows
        return pl.ds(pl.multiple_of(start, 16), self.rows), self.columns[way]

    def send(self, copy):
        copy.start()
        self.sent.append((None, copy))

    def first(self, d):
        for number in range(2):
            for way in self.ways:
                target = self.c ^ 3 if number == 0 else self.c ^ (1 << way)
                self.send(
                    remote(
                        self.part.at[self.block(d, target, way)], self.first_in[way].at[d, number],
                        self.first_send.at[way, d, number], self.first_recv.at[way, d, number],
                        self.neighbours[way],
                    )
                )

    def second(self, d):
        for way in self.ways:
            for number in range(2):
                landing = self.first_in[way].at[d, number]
                remote(
                    landing, landing, self.first_send.at[way, d, number],
                    self.first_recv.at[way, d, number], self.neighbours[way],
                ).wait_recv()
            term = self.part[self.block(d, self.c ^ (2 >> way), way)]
            added = term.astype(jnp.float32) + self.first_in[way][d, 0].astype(jnp.float32)
            self.first_in[way][d, 0] = added.astype(self.part.dtype)
            self.send(
                remote(
                    self.first_in[way].at[d, 0], self.second_in[way].at[d],
                    self.second_send.at[way, d], self.second_recv.at[way, d], self.neighbours[1 - way],
                )
            )

    def total(self, d, way):
        landing = self.second_in[way].at[d]
        remote(
            landing, landing, self.second_send.at[way, d], self.second_recv.at[way, d], self.neighbours[1 - way]
        ).wait_recv()
        term = self.part[self.block(d, self.c, way)]
        return (
            term.astype(jnp.float32)
            + self.first_in[way][d, 1].astype(jnp.float32)
            + self.second_in[way][d].astype(jnp.float32)
        )

    def to_z(self, d, out):
        for way in self.ways:
            total = self.total(d, way)
            if d == 0:
                out[:, self.columns[way]] = total
                continue
            self.first_in[way][d, 1] = total.astype(self.part.dtype)
            self.send(
                remote(
                    self.first_in[way].at[d, 1], self.z_in[way].at[d - 1],
                    self.z_send.at[way, d], self.z_recv.at[way, d], at_device(self.peer(d), self.c, self.t),
                )
            )

    def from_z(self, out):
        for way in self.ways:
            for d in range(1, self.ep):
                landing = self.z_in[way].at[d - 1]
                remote(
                    landing, landing, self.z_send.at[way, d], self.z_recv.at[way, d], self.neighbours[0]
                ).wait_recv()
                out[:, self.columns[way]] += self.z_in[way][d - 1].astype(jnp.float32)

    def halves(self):
        others = [2 - (self.f & 2) + j for j in range(2)]
        return (self.f == 1) | (self.f == 2), list(enumerate(others, 1)), self.f ^ 1

    def distance(self, g):
        return lax.rem(g + self.ep - self.f, self.ep)

    def pair_begin(self, out):
        inner, others, partner = self.halves()
        beside = at_device(partner, self.c, self.t)
        for way in self.ways:
            for slot, g in others + [(0, partner)]:
                d = self.distance(g)
                self.first_in[way][d, 1] = self.total(d, way).astype(self.part.dtype)
                copy = remote(
                    self.first_in[way].at[d, 1], self.z_in[way].at[slot],
                    self.z_send.at[way, slot], self.z_recv.at[way, slot], beside,
                )
                when = None if slot == 0 else jnp.logical_not(inner)
                if when is None:
                    copy.start()
                else:
                    pl.when(when)(copy.start)
                self.sent.append((when, copy))
            out[:, self.columns[way]] = self.total(0, way)

    def pair_cross(self):
        inner, others, partner = self.halves()
        beside = at_device(partner, self.c, self.t)
        for way in self.ways:
            for slot, g in others:
                d = self.distance(g)

                @pl.when(inner)
                def _():
                    block = self.z_in[way].at[slot]
                    remote(block, block, self.z_send.at[way, slot], self.z_recv.at[way, slot], beside).wait_recv()
                    added = self.first_in[way][d, 1].astype(jnp.float32) + self.z_in[way][slot].astype(jnp.float32)
                    self.first_in[way][d, 1] = added.astype(self.part.dtype)

                copy = remote(
                    self.first_in[way].at[d, 1], self.z_in[way].at[3],
                    self.z_send.at[way, slot], self.z_recv.at[way, 3], at_device(g, self.c, self.t),
                )
                pl.when(inner)(copy.start)
                self.sent.append((inner, copy))

    def pair_collect(self, out):
        for way in self.ways:
            for slot in (0, 3):
                block = self.z_in[way].at[slot]
                remote(
                    block, block, self.z_send.at[way, slot], self.z_recv.at[way, slot], self.neighbours[0]
                ).wait_recv()
                out[:, self.columns[way]] += self.z_in[way][slot].astype(jnp.float32)


def all_partners(ep):
    f, c, t = lax.axis_index("fsdp"), lax.axis_index("ctx"), lax.axis_index("tp")
    line = [at_device(lax.rem(f + d, ep), c, t) for d in range(1, ep)]
    return line + [at_device(f, c ^ 1, t), at_device(f, c ^ 2, t), at_device(f, c, 1 - t)]


class PlaneHalf:
    def __init__(self, part, rows, local, landings, send_sem, recv_sem, sent):
        self.part, self.rows, self.landings, self.sent = part, rows, landings, sent
        self.send_sem, self.recv_sem = send_sem, recv_sem
        self.local, self.cut = local, landings[0].shape[-1] // local
        self.ep = landings[0].shape[0]
        self.f, self.c, t = lax.axis_index("fsdp"), lax.axis_index("ctx"), lax.axis_index("tp")
        self.neighbours = (at_device(self.f, self.c ^ 1, t), at_device(self.f, self.c ^ 2, t))

    def block(self, distance, ctx, way, e):
        start = (lax.rem(self.f + distance, self.ep) * 4 + ctx) * self.rows
        columns = pl.ds((2 * e + way) * self.cut, self.cut)
        return pl.ds(pl.multiple_of(start, 16), self.rows), columns

    def landed(self, d, number, way):
        landing = self.landings[way].at[d, number]
        return remote(
            landing, landing, self.send_sem.at[way, d, number], self.recv_sem.at[way, d, number],
            self.neighbours[way],
        )

    def start(self, d, e):
        for number in range(2):
            for way in range(2):
                target = self.c ^ 3 if number == 0 else self.c ^ (1 << way)
                remote(
                    self.part.at[self.block(d, target, way, e)],
                    self.landings[way].at[d, number, :, pl.ds(e * self.cut, self.cut)],
                    self.send_sem.at[way, d, number], self.recv_sem.at[way, d, number], self.neighbours[way],
                ).start()

    def finish(self, d):
        for way in range(2):
            for number in range(2):
                copy = self.landed(d, number, way)
                copy.wait_recv()
                self.sent.append((None, copy))
                ctx = self.c ^ (2 >> way) if number == 0 else self.c
                for e in range(self.local):
                    at = slice(e * self.cut, (e + 1) * self.cut)
                    term = self.part[self.block(d, ctx, way, e)].astype(jnp.float32)
                    added = term + self.landings[way][d, number, :, at].astype(jnp.float32)
                    self.landings[way][d, number, :, at] = added.astype(self.part.dtype)


def experts_kernel(
    routes_ref, extra_ref, tokens_hbm, outer_hbm, weight_hbm,
    returned_ref, mixture_out, relay_out, own_out, gates_out,
    tokens_ref, outer_ref, weight_ref, in_sem,
    gates_s, gated_s, side_s, part_s, mixture_s, sums_s, first_x, first_y, plane_send, plane_recv, local_sem, *scratch,
):
    ep = lax.axis_size("fsdp")
    f = lax.axis_index("fsdp")
    low = jnp.bfloat16
    reach, model = tokens_ref.shape
    span = weight_ref.shape[1] // 3
    tokens = reach // ep
    rows = model // (4 * ep)
    local = EXPERTS // ep
    hidden = span // local
    sent = []
    back = ZSum(part_s, scratch, sent)
    plane = PlaneHalf(sums_s, rows, local, (first_x, first_y), plane_send, plane_recv, sent)
    pairs = [(tokens_hbm, tokens_ref), (outer_hbm, outer_ref)]
    for e in range(local):
        for kind in range(3):
            at = (slice(None), pl.ds(kind * span + e * hidden, hidden))
            pairs.insert(1 + 3 * e + kind + (e > 0 or kind > 1), (weight_hbm.at[at], weight_ref.at[at]))
    coming = fetch(pairs, in_sem)
    greet(all_partners(ep))

    lane = lax.broadcasted_iota(jnp.int32, (reach, 128), 1)
    uses = routes_ref.shape[0]
    turned = jnp.concatenate(
        [routes_ref[...].astype(jnp.float32), jnp.zeros((128 - uses, reach), jnp.float32)], 0
    ).T.astype(jnp.int32)
    chosen = turned[:, 0:1] == lane
    for k in range(1, uses):
        chosen = chosen | (turned[:, k : k + 1] == lane)
    coming[0].wait()
    logits = jnp.dot(tokens_ref[...], extra_ref[...], preferred_element_type=jnp.float32)
    logits = jnp.where(chosen, logits, MASKED_SCORE)
    lifted = jnp.where(chosen, jnp.exp(logits - jnp.max(logits, -1, keepdims=True)), 0.0)
    gates_s[...] = lifted / jnp.sum(lifted, -1, keepdims=True)
    own = pl.ds(pl.multiple_of(f * tokens, 16), tokens)
    gates_out[...] = gates_s[own, :]

    part_s[:, model:] = jnp.zeros((reach, 128), low)
    order = list(range(1, ep)) + [0]
    over = (((0,), (0,)), ((), ()))
    across = (((1,), (1,)), ((), ()))

    def act(e):
        at = slice(e * hidden, (e + 1) * hidden)
        at_up = slice(span + e * hidden, span + (e + 1) * hidden)
        at_down = slice(2 * span + e * hidden, 2 * span + (e + 1) * hidden)
        mine = lane == f * local + e
        gate = jnp.sum(jnp.where(mine, gates_s[...], 0.0), -1, keepdims=True)
        for copy in coming[1:5] if e == 0 else coming[2 + 3 * e : 5 + 3 * e]:
            copy.wait()
        former = jnp.dot(tokens_ref[...], weight_ref[:, at], preferred_element_type=jnp.float32)
        latter = jnp.dot(tokens_ref[...], weight_ref[:, at_up], preferred_element_type=jnp.float32)
        grad = jnp.dot(outer_ref[...], weight_ref[:, at_down], preferred_element_type=jnp.float32)
        logistic = 1.0 / (1.0 + jnp.exp(-former))
        active = former * logistic
        value = (active * latter).astype(low).astype(jnp.float32)
        gated_s[:, at] = (value * gate).astype(low)
        picked = jnp.sum(value * grad, -1, keepdims=True)
        dgate = jnp.where(mine & (gate > 0.0), picked, 0.0)
        high = dgate.astype(low).astype(jnp.float32)
        part_s[:, model:] += (high + pltpu.roll(dgate - high, EXPERTS, 1)).astype(low)
        grad = grad * gate
        side_s[:, at] = (grad * latter * logistic * (1.0 + former * (1.0 - logistic))).astype(low)
        side_s[:, at_up] = (grad * active).astype(low)

    def sums(e):
        for d in order:
            at = pl.ds(pl.multiple_of(lax.rem(f + d, ep) * 4 * rows, 128), 4 * rows)
            start = 3 * e * hidden
            for kind, (left, right) in enumerate(((tokens_ref, side_s), (tokens_ref, side_s), (outer_ref, gated_s))):
                column = (kind * span if kind < 2 else 0) + e * hidden
                sums_s[at, start + kind * hidden : start + (kind + 1) * hidden] = lax.dot_general(
                    left[:, at], right[:, column : column + hidden], over, preferred_element_type=jnp.float32
                ).astype(low)
            plane.start(d, e)

    def dn2(d):
        here = pl.ds(pl.multiple_of(back.peer(d) * tokens, 16), tokens)

        def tile(n, carry):
            at = pl.ds(pl.multiple_of(n * 256, 256), 256)
            part_s[here, at] = lax.dot_general(
                side_s[here, :], weight_ref[at, : 2 * span], across, preferred_element_type=jnp.float32
            ).astype(low)
            return carry

        lax.fori_loop(0, model // 256, tile, 0)
        back.to_core(d)

    def mixtures(n, carry):
        at = pl.ds(pl.multiple_of(n * 256, 256), 256)
        mixture_s[:, at] = lax.dot_general(
            gated_s[...], weight_ref[at, 2 * span :], across, preferred_element_type=jnp.float32
        ).astype(low)
        return carry

    act(0)
    sums(0)
    for e in range(1, local):
        act(e)
    sums(1)
    for step, d in enumerate(order):
        dn2(d)
        if step > 0:
            back.to_z(order[step - 1])
    for e in range(2, local):
        sums(e)
    lax.fori_loop(0, model // 256, mixtures, 0)
    mixture_copy = pltpu.make_async_copy(mixture_s, mixture_out, local_sem.at[2])
    mixture_copy.start()
    returned_ref[back.rows(back.t), :] = back.collect()
    back.share(returned_ref)
    for d in order:
        plane.finish(d)
        for way in range(2):
            for number, out in enumerate((relay_out, own_out)):
                pltpu.make_async_copy(
                    plane.landings[way].at[d, number], out.at[way, d], local_sem.at[number]
                ).start()
    mixture_copy.wait()
    back.finish(returned_ref)
    for number, out in enumerate((relay_out, own_out)):
        pltpu.make_async_copy(out, out, local_sem.at[number]).wait()
    all_sent(sent)


def run_experts(tokens_all, outer_all, routes_all, extra, weights, collective_id):
    ep = lax.axis_size("fsdp")
    reach, model = tokens_all.shape
    tokens, low = reach // ep, tokens_all.dtype
    rows = model // (4 * ep)
    full = weights.shape[1]
    span = full // 3
    dma = pltpu.SemaphoreType.DMA
    anywhere = pl.BlockSpec(memory_space=pl.ANY)
    vmem = pl.BlockSpec(memory_space=pltpu.VMEM)
    shape = jax.ShapeDtypeStruct
    return pl.pallas_call(
        experts_kernel,
        out_shape=(
            shape((tokens, model + 128), jnp.float32),
            shape((reach, model), low),
            shape((2, ep, rows, full // 2), low),
            shape((2, ep, rows, full // 2), low),
            shape((tokens, 128), jnp.float32),
        ),
        in_specs=[vmem] * 2 + [anywhere] * 3,
        out_specs=(vmem, anywhere, anywhere, anywhere, vmem),
        scratch_shapes=[
            pltpu.VMEM(tokens_all.shape, low),
            pltpu.VMEM(outer_all.shape, low),
            pltpu.VMEM(weights.shape, low),
            dma((2 + 3 * EXPERTS // ep,)),
            pltpu.VMEM((reach, 128), jnp.float32),
            pltpu.VMEM((reach, span), low),
            pltpu.VMEM((reach, 2 * span), low),
            pltpu.VMEM((reach, model + 128), low),
            pltpu.VMEM((reach, model), low),
            pltpu.VMEM(weights.shape, low),
            pltpu.VMEM((ep, 2, rows, full // 2), low),
            pltpu.VMEM((ep, 2, rows, full // 2), low),
            dma((2, ep, 2)),
            dma((2, ep, 2)),
            dma((3,)),
        ]
        + z_sum_scratch(ep, tokens, model + 128, low),
        compiler_params=pltpu.CompilerParams(
            collective_id=collective_id, has_side_effects=True, vmem_limit_bytes=63 * 1024 * 1024
        ),
        cost_estimate=lasting(90),
        name="experts",
    )(routes_all, extra, tokens_all, outer_all, weights)


def rear_kernel(
    gates_ref, log_ref, cos_ref, sin_ref, segment_ref, returned_hbm, middle_hbm, outer_hbm, extra_hbm,
    mixed_hbm, query_hbm, pair_hbm, input_hbm, normed1_hbm, mixture_ref, relay_ref, own_ref, attn_ref,
    input_grad, layer_out, qkv_out, wo_out, expert_out,
    returned_ref, middle_ref, outer_ref, extra_ref, mixed_ref, query_ref, pair_ref, input_ref, normed1_ref, in_sem,
    wo_s, qkv_s, query_s, grad_s, mixed_s, key_s, value_s, bias_s, query_grad_s, key_grad_s, value_grad_s,
    pair_s, landing_s, back_s, attn_grad_s, part_s, other_s, router_s, gains_s, mixture_s, own_s, second_s,
    local_sem, key_send, key_recv, pair_send, pair_recv, second_send, second_recv, swap_send, swap_recv, layer_send, layer_recv, *scratch,
):
    ep, rows = expert_out.shape[0], expert_out.shape[2]
    f, c, t = lax.axis_index("fsdp"), lax.axis_index("ctx"), lax.axis_index("tp")
    low = jnp.bfloat16
    tokens, model = input_ref.shape
    heads, key_heads = query_s.shape[0], key_s.shape[0]
    groups = heads // key_heads
    width, kv_width = heads * HD, key_heads * HD
    qkv_width = width + 2 * kv_width
    sent = []
    mixture = PairSum(mixture_ref, mixture_s, scratch[:7], sent)
    scratch = scratch[7:]
    size = len(shard_sum_scratch(ep, rows, 256, low))
    wo = ShardSum(wo_s, rows, width, scratch[:size], sent)
    qkv = ShardSum(qkv_s, rows, qkv_width + 128, scratch[size:], sent)
    partners = all_partners(ep)
    plane = [at_device(f, c ^ k, t) for k in range(1, 4)]
    core = partners[-1]

    coming = fetch(
        [
            (returned_hbm, returned_ref), (middle_hbm, middle_ref), (outer_hbm, outer_ref), (extra_hbm, extra_ref),
            (mixed_hbm, mixed_ref), (query_hbm, query_ref), (pair_hbm, pair_ref), (input_hbm, input_ref),
            (normed1_hbm, normed1_ref),
        ],
        in_sem,
    )
    copies = [
        pltpu.make_async_copy(attn_ref.at[:, pl.ds(qkv_width + 128, width)], wo_s, local_sem.at[0]),
        pltpu.make_async_copy(attn_ref.at[:, pl.ds(0, qkv_width + 128)], qkv_s, local_sem.at[1]),
    ]
    for copy in copies:
        copy.start()
    for g in range(ep):
        pltpu.make_async_copy(mixture_ref.at[mixture.place(g, t)], mixture_s.at[g], local_sem.at[2]).start()
    copies.append(pltpu.make_async_copy(own_ref, own_s, local_sem.at[3]))
    copies[2].start()
    greet(partners + plane[2:])
    order = wo.order
    mixture.to_core()
    seconds = {}

    def second(d):
        for way in range(2):
            copy = remote(
                relay_ref.at[way, d], second_s.at[way, d], second_send.at[way, d], second_recv.at[way, d],
                plane[1 - way],
            )
            copy.start()
            sent.append((None, copy))
            seconds[way, d] = copy

    def swap(d):
        for way in range(2):
            seconds[way, d].wait_recv()
        own_s[:, d] = (own_s[:, d].astype(jnp.float32) + second_s[:, d].astype(jnp.float32)).astype(low)
        if d == 0:
            copy = pltpu.make_async_copy(own_s.at[:, 0], expert_out.at[f], swap_send.at[0])
            copy.start()
            copies.append(copy)
        else:
            copy = remote(own_s.at[:, d], expert_out.at[f], swap_send.at[d], swap_recv.at[d], partners[d - 1])
            copy.start()
            sent.append((None, copy))

    second(1)

    small_lane = lax.broadcasted_iota(jnp.int32, (tokens, 128), 1)
    for copy in coming[:4]:
        copy.wait()
    gains = extra_ref[...].astype(jnp.float32).T
    gain_one, gain_two = gains[EXPERTS : EXPERTS + 1, :], gains[EXPERTS + 1 : EXPERTS + 2, :]
    tail = returned_ref[:, model:]
    picked = jnp.where(small_lane < EXPERTS, tail + pltpu.roll(tail, 128 - EXPERTS, 1), 0.0)
    gates = gates_ref[...]
    logit_grad = (gates * (picked - jnp.sum(gates * picked, -1, keepdims=True))).astype(low)
    second_grad = returned_ref[:, :model] + lax.dot_general(
        logit_grad, extra_ref[...], (((1,), (1,)), ((), ())), preferred_element_type=jnp.float32
    )
    middle = middle_ref[...]
    inverse = lax.rsqrt(jnp.mean(middle * middle, -1, keepdims=True) + EPSILON)
    scaled = second_grad * gain_two
    mean_term = jnp.mean(scaled * middle, -1, keepdims=True)
    gains_s[1:2, :] = jnp.sum(second_grad * middle * inverse, 0, keepdims=True)
    middle_grad = outer_ref[...].astype(jnp.float32) + (
        inverse * scaled - middle * (inverse * inverse * inverse) * mean_term
    )
    input_grad[...] = middle_grad
    attn_grad_s[...] = middle_grad.astype(low)

    pltpu.make_async_copy(mixture_s, mixture_s, local_sem.at[2]).wait()
    mixture.begin()
    second(2)
    copies[0].wait()
    for start in range(0, width, 256):
        tile = jnp.dot(
            attn_grad_s[...], wo_s[:, start : start + 256], preferred_element_type=jnp.float32
        ).astype(low)
        for side in range(0, 256, HD):
            grad_s[(start + side) // HD] = tile[:, side : side + HD]

    copies[2].wait()
    swap(1)
    second(3)
    length = segment_ref.shape[1]
    seg_keys = jnp.broadcast_to(segment_ref[...].astype(jnp.float32), (128, length)).T[:, :1]
    seg_queries = segment_ref[:, pl.ds(pl.multiple_of(c * tokens, 128), tokens)].astype(jnp.float32)
    key_order = lax.broadcasted_iota(jnp.int32, (length, tokens), 0)
    query_order = lax.broadcasted_iota(jnp.int32, (length, tokens), 1) + c * tokens
    bias_s[...] = jnp.where((seg_keys == seg_queries) & (key_order <= query_order), 0.0, MASKED_SCORE)
    for copy in coming[4:]:
        copy.wait()
    for h in range(heads):
        query_s[h] = query_ref[:, h * HD : (h + 1) * HD]
        mixed_s[h] = mixed_ref[:, h * HD : (h + 1) * HD]
    for g in range(key_heads):
        key_s[g] = pair_ref[:, g * HD : (g + 1) * HD]
        value_s[g] = pair_ref[:, kv_width + g * HD : kv_width + (g + 1) * HD]
    across = (((1,), (1,)), ((), ()))

    def attend_back(g, carry):
        key_grad = jnp.zeros((length, HD), jnp.float32)
        value_grad = jnp.zeros((length, HD), jnp.float32)
        for number in range(groups):
            h = g * groups + number
            query = query_s[h] * jnp.asarray(HD**-0.5, low)
            grad = grad_s[h]
            scores = lax.dot_general(key_s[g], query, across, preferred_element_type=jnp.float32) + bias_s[...]
            probs = jnp.exp(scores - log_ref[h])
            value_grad += jnp.dot(probs.astype(low), grad, preferred_element_type=jnp.float32)
            prob_grad = lax.dot_general(value_s[g], grad, across, preferred_element_type=jnp.float32)
            delta = jnp.sum((grad.astype(jnp.float32) * mixed_s[h].astype(jnp.float32)).T, 0, keepdims=True)
            score_grad = (probs * (prob_grad - delta)).astype(low)
            key_grad += jnp.dot(score_grad, query, preferred_element_type=jnp.float32)
            query_grad = lax.dot_general(
                key_s[g], score_grad, (((0,), (0,)), ((), ())), preferred_element_type=jnp.float32
            )
            query_grad_s[h] = query_grad.T * (HD**-0.5)
        key_grad_s[g] = key_grad.astype(low)
        value_grad_s[g] = value_grad.astype(low)
        return carry

    lax.fori_loop(0, key_heads // 2, attend_back, 0)
    swap(2)
    second(0)
    lax.fori_loop(key_heads // 2, key_heads, attend_back, 0)
    for g in range(key_heads):
        pair_s[:, g * HD : (g + 1) * HD] = key_grad_s[g]
        pair_s[:, kv_width + g * HD : kv_width + (g + 1) * HD] = value_grad_s[g]
    for k in (3, 1, 2):
        place = pl.ds(pl.multiple_of((c ^ k) * tokens, 16), tokens)
        copy = remote(pair_s.at[place], landing_s.at[k - 1], key_send.at[k - 1], key_recv.at[k - 1], plane[k - 1])
        copy.start()
        sent.append((None, copy))
    def wo_sums(n, carry):
        at = pl.ds(pl.multiple_of(n * 256, 256), 256)
        wo_s[at, :] = lax.dot_general(
            attn_grad_s[:, at], mixed_ref[...], (((0,), (0,)), ((), ())), preferred_element_type=jnp.float32
        ).astype(low)
        return carry

    lax.fori_loop(0, model // 256, wo_sums, 0)
    router_s[...] = lax.dot_general(
        (middle * inverse * gain_two).astype(low), logit_grad, (((0,), (0,)), ((), ())),
        preferred_element_type=jnp.float32,
    )

    swap(3)
    swap(0)
    mixture.cross()
    first_half = lax.rem(small_lane, HD) < HD // 2

    def turned_back(tile):
        swapped = jnp.where(first_half, pltpu.roll(tile, 128 - HD // 2, 1), pltpu.roll(tile, HD // 2, 1))
        return tile * cos_ref[...] - swapped * sin_ref[...]

    for start in range(0, width, 128):
        tile = jnp.concatenate([query_grad_s[start // HD], query_grad_s[start // HD + 1]], 1)
        back_s[:, start : start + 128] = turned_back(tile).astype(low)

    pair = pair_s[pl.ds(pl.multiple_of(c * tokens, 16), tokens), :].astype(jnp.float32)
    for k in (1, 2, 3):
        block = landing_s.at[k - 1]
        remote(block, block, key_send.at[k - 1], key_recv.at[k - 1], plane[k - 1]).wait_recv()
        pair = pair + landing_s[k - 1].astype(jnp.float32)
    for d in order:
        wo.first(d)
    for start in range(0, kv_width, 128):
        back_s[:, width + start : width + start + 128] = turned_back(pair[:, start : start + 128]).astype(low)
    back_s[:, width + kv_width :] = pair[:, kv_width:].astype(low)
    copies[1].wait()
    for start in range(0, model, 256):
        part_s[:, start : start + 256] = lax.dot_general(
            back_s[...], qkv_s[start : start + 256, :qkv_width], across, preferred_element_type=jnp.float32
        ).astype(low)
    exchange = remote(part_s, other_s, pair_send, pair_recv, core)
    exchange.start()
    sent.append((None, exchange))

    def qkv_sums(n, carry):
        at = pl.ds(pl.multiple_of(n * 256, 256), 256)
        qkv_s[at, :qkv_width] = lax.dot_general(
            normed1_ref[:, at], back_s[...], (((0,), (0,)), ((), ())), preferred_element_type=jnp.float32
        ).astype(low)
        return carry

    lax.fori_loop(0, model // 256, qkv_sums, 0)
    exchange.wait_recv()
    first_grad = part_s[...].astype(jnp.float32) + other_s[...].astype(jnp.float32)
    inputs = input_ref[...].astype(jnp.float32)
    inverse = lax.rsqrt(jnp.mean(inputs * inputs, -1, keepdims=True) + EPSILON)
    gains_s[0:1, :] = jnp.sum(first_grad * inputs * inverse, 0, keepdims=True)
    line = lax.broadcasted_iota(jnp.int32, (128, model), 0)
    turned = jnp.where(line == EXPERTS, gains_s[0:1, :], jnp.where(line == EXPERTS + 1, gains_s[1:2, :], 0.0)).T
    qkv_s[:, qkv_width:] = (router_s[...] + turned).astype(low)
    qkv.first(1)
    qkv.first(2)
    for d in wo.order:
        wo.second(d)
    scaled = first_grad * gain_one
    mean_term = jnp.mean(scaled * inputs, -1, keepdims=True)
    input_grad[...] += inverse * scaled - inputs * (inverse * inverse * inverse) * mean_term
    qkv.second(1)
    qkv.first(3)
    wo.pair_begin(wo_out)
    qkv.second(2)
    qkv.first(0)
    qkv.second(3)
    wo.pair_cross()
    qkv.second(0)
    qkv.pair_begin(qkv_out)
    qkv.pair_cross()
    copies[3].wait()
    for d in range(1, ep):
        landing = expert_out.at[lax.rem(f + ep - d, ep)]
        remote(landing, landing, swap_send.at[d], swap_recv.at[d], core).wait_recv()
    wo.pair_collect(wo_out)
    half, other_half = (pl.ds(pl.multiple_of(part * (tokens // 2), 16), tokens // 2) for part in (t, 1 - t))
    layer_out[half, :] = (middle_ref[half, :] + mixture.collect()).astype(low)
    layer_copy = remote(layer_out.at[half], layer_out.at[half], layer_send, layer_recv, core)
    layer_copy.start()
    sent.append((None, layer_copy))
    qkv.pair_collect(qkv_out)
    remote(layer_out.at[other_half], layer_out.at[other_half], layer_send, layer_recv, core).wait_recv()
    all_sent(sent)


def rear(
    returned, gates, middle, inputs, outer, normed1, query, pair, mixed, log_total, cosine, sine, segments, extra,
    mixture, relay, own, attn, collective_id,
):
    ep = lax.axis_size("fsdp")
    tokens, model = inputs.shape
    rows = own.shape[2]
    heads, key_heads = query.shape[1] // HD, pair.shape[1] // (2 * HD)
    width, kv_width = heads * HD, key_heads * HD
    qkv_width = width + 2 * kv_width
    length = pair.shape[0]
    low = jnp.bfloat16
    dma = pltpu.SemaphoreType.DMA
    anywhere = pl.BlockSpec(memory_space=pl.ANY)
    vmem = pl.BlockSpec(memory_space=pltpu.VMEM)
    shape = jax.ShapeDtypeStruct
    room = pltpu.VMEM
    fetched = (returned, middle, outer, extra, mixed, query, pair, inputs, normed1)
    return pl.pallas_call(
        rear_kernel,
        out_shape=(
            shape((tokens, model), jnp.float32),
            shape((tokens, model), low),
            shape((rows, qkv_width + 128), jnp.float32),
            shape((rows, width), jnp.float32),
            shape((ep, 2, rows, own.shape[3]), low),
        ),
        in_specs=[vmem] * 5 + [anywhere] * 13,
        out_specs=(vmem,) * 4 + (anywhere,),
        scratch_shapes=[room(each.shape, each.dtype) for each in fetched]
        + [
            dma((len(fetched),)),
            room((model, width), low),
            room((model, qkv_width + 128), low),
            room((heads, tokens, HD), low),
            room((heads, tokens, HD), low),
            room((heads, tokens, HD), low),
            room((key_heads, length, HD), low),
            room((key_heads, length, HD), low),
            room((length, tokens), jnp.float32),
            room((heads, tokens, HD), jnp.float32),
            room((key_heads, length, HD), low),
            room((key_heads, length, HD), low),
            room((length, 2 * kv_width), low),
            room((3, tokens, 2 * kv_width), low),
            room((tokens, qkv_width), low),
            room((tokens, model), low),
            room((tokens, model), low),
            room((tokens, model), low),
            room((model, 128), jnp.float32),
            room((8, model), jnp.float32),
            room((ep, tokens // 2, model), low),
            room(own.shape, low),
            room(own.shape, low),
            dma((4,)),
            dma((3,)),
            dma((3,)),
            dma,
            dma,
            dma((2, ep)),
            dma((2, ep)),
            dma((ep,)),
            dma((ep,)),
            dma,
            dma,
        ]
        + pair_sum_scratch(ep, tokens, model, low)
        + shard_sum_scratch(ep, rows, width, low)
        + shard_sum_scratch(ep, rows, qkv_width + 128, low),
        compiler_params=pltpu.CompilerParams(
            collective_id=collective_id, has_side_effects=True, vmem_limit_bytes=63 * 1024 * 1024
        ),
        cost_estimate=lasting(170),
        name="rear",
    )(gates, log_total, cosine, sine, segments, *fetched, mixture, relay, own, attn)


def finish_kernel(
    expert_ref, qkv_ref, wo_ref, input_ref, layer_ref,
    query_out, key_out, value_out, output_out, router_out, gain_one_out, gain_two_out,
    gate_out, up_out, down_out, input_out, layer_out,
):
    local, _, hidden = gate_out.shape
    cut = expert_ref.shape[3] // local
    for e in range(local):
        at = slice(e * cut, (e + 1) * cut)
        both = jnp.concatenate([expert_ref[0, 0, :, at], expert_ref[0, 1, :, at]], 1).astype(jnp.float32)
        for kind, out in enumerate((gate_out, up_out, down_out)):
            out[e] = both[:, kind * hidden : (kind + 1) * hidden]
    input_out[...] = input_ref[...]
    layer_out[...] = layer_ref[...]

    @pl.when(pl.program_id(0) == 0)
    def _():
        width, kv_width = query_out.shape[1], key_out.shape[1]
        query_out[...] = qkv_ref[:, :width]
        key_out[...] = qkv_ref[:, width : width + kv_width]
        value_out[...] = qkv_ref[:, width + kv_width : width + 2 * kv_width]
        small = qkv_ref[:, width + 2 * kv_width :].T
        router_out[...] = small[:EXPERTS]
        gain_one_out[...] = small[EXPERTS : EXPERTS + 1]
        gain_two_out[...] = small[EXPERTS + 1 : EXPERTS + 2]
        output_out[...] = wo_ref[...]


def finish(experts, qkv, wo, input_grad, layer_output, kv_width, hidden):
    ep, _, rows, half = experts.shape
    width = wo.shape[1]
    local = 2 * half // (3 * hidden)
    tokens, model = input_grad.shape
    shape = jax.ShapeDtypeStruct

    def whole(*dims):
        return pl.BlockSpec(dims, lambda i: (0, 0))

    by_z = pl.BlockSpec((local, rows, hidden), lambda i: (i, 0, 0))
    by_rows = pl.BlockSpec((tokens // ep, model), lambda i: (i, 0))
    return pl.pallas_call(
        finish_kernel,
        grid=(ep,),
        out_shape=(
            shape((rows, width), jnp.float32),
            shape((rows, kv_width), jnp.float32),
            shape((rows, kv_width), jnp.float32),
            shape((rows, width), jnp.float32),
            shape((EXPERTS, rows), jnp.float32),
            shape((1, rows), jnp.float32),
            shape((1, rows), jnp.float32),
            shape((ep * local, rows, hidden), jnp.float32),
            shape((ep * local, rows, hidden), jnp.float32),
            shape((ep * local, rows, hidden), jnp.float32),
            shape((tokens, model), jnp.float32),
            shape((tokens, model), layer_output.dtype),
        ),
        in_specs=[
            pl.BlockSpec((1, 2, rows, half), lambda i: (i, 0, 0, 0)),
            whole(*qkv.shape),
            whole(*wo.shape),
            by_rows,
            by_rows,
        ],
        out_specs=(
            whole(rows, width),
            whole(rows, kv_width),
            whole(rows, kv_width),
            whole(rows, width),
            whole(EXPERTS, rows),
            whole(1, rows),
            whole(1, rows),
            by_z,
            by_z,
            by_z,
            by_rows,
            by_rows,
        ),
        compiler_params=pltpu.CompilerParams(vmem_limit_bytes=60 * 1024 * 1024),
        cost_estimate=lasting(6),
        name="finish",
    )(experts, qkv, wo, input_grad, layer_output)


def plain_shards(
    layer_input,
    segments,
    routes,
    norm_gain,
    query_weight,
    key_weight,
    value_weight,
    output_weight,
    ffn_gain,
    router_weight,
    gate_weight,
    up_weight,
    down_weight,
    cotangent,
):
    low = jnp.bfloat16
    both = ("fsdp", "ctx")
    ep = lax.axis_size("fsdp")
    tokens = layer_input.shape[0]
    seq_len = segments.shape[1]
    rows = query_weight.shape[0]
    width = query_weight.shape[1]
    kv_width = key_weight.shape[1]
    hidden_width = gate_weight.shape[2]
    local = EXPERTS // ep
    span = local * hidden_width

    qkv_width = width + 2 * kv_width
    extra = jnp.concatenate([router_weight, norm_gain[:, None], ffn_gain[:, None]], 1)
    extra = jnp.pad(extra, ((0, 0), (0, 128 - extra.shape[1])))
    attn_shard = jnp.concatenate([query_weight, key_weight, value_weight, extra, output_weight.T], 1)
    down_shard = down_weight.transpose(0, 2, 1)
    begin = lax.axis_index("ctx") * tokens
    segment_row = segments[0]
    query_doc = lax.dynamic_slice_in_dim(segment_row, begin, tokens)
    query_order = begin + jnp.arange(tokens, dtype=jnp.int32)
    scale = HD ** (-0.5)
    inputs = layer_input.astype(jnp.float32)
    key_groups = kv_width // HD
    groups = width // kv_width
    freq = 10000.0 ** (-2.0 * jnp.arange(HD // 2, dtype=jnp.float32) / HD)

    def unpack(attn_full):
        return (
            attn_full[:, :qkv_width],
            attn_full[:, qkv_width : qkv_width + EXPERTS],
            attn_full[:, qkv_width + EXPERTS],
            attn_full[:, qkv_width + EXPERTS + 1],
            attn_full[:, qkv_width + 128 :],
        )

    attn_full = lax.all_gather(attn_shard, both, axis=0, tiled=True)
    qkv_full, router_full, gain_one, gain_two, output_turned = unpack(attn_full)
    packed = jnp.concatenate([gate_weight, up_weight, down_shard], -1)
    expert_full = spread_experts(packed)
    expert_full = expert_full.reshape(D, local, 3, hidden_width).transpose(0, 2, 1, 3)
    expert_full = expert_full.reshape(D, 3 * span)
    outer_all = lax.all_gather(cotangent, "fsdp", axis=0, tiled=True)
    routes_all = lax.all_gather(routes, "fsdp", axis=0, tiled=True)
    place = lax.dynamic_slice_in_dim(document_place(segment_row), begin, tokens)
    angle = place.astype(jnp.float32)[:, None] * freq[None, :]
    cosine, sine = jnp.cos(angle), jnp.sin(angle)
    first_norm, first_inverse = normalize(inputs, gain_one)
    normed1 = first_norm.astype(low)
    projected = jnp.dot(normed1, qkv_full, preferred_element_type=jnp.float32)
    query = rotate(projected[:, :width], cosine, sine).astype(low)
    key = rotate(projected[:, width : width + kv_width], cosine, sine).astype(low)
    value = projected[:, width + kv_width :].astype(low)
    pair_all = lax.all_gather(jnp.concatenate([key, value], 1), "ctx", axis=0, tiled=True)
    heads = query.reshape(tokens, key_groups, groups, HD)
    key_heads = pair_all[:, :kv_width].reshape(seq_len, key_groups, HD)
    value_heads = pair_all[:, kv_width:].reshape(seq_len, key_groups, HD)
    scores = jnp.einsum("qkgd,nkd->qkgn", heads, key_heads, preferred_element_type=jnp.float32) * scale
    seen = (segment_row[None, :] == query_doc[:, None]) & (
        jnp.arange(seq_len, dtype=jnp.int32)[None, :] <= query_order[:, None]
    )
    scores = jnp.where(seen[:, None, None, :], scores, MASKED_SCORE)
    running = jnp.max(scores, -1)
    weights = jnp.exp(scores - running[..., None])
    summed = jnp.einsum(
        "qkgn,nkd->qkgd", weights.astype(low), value_heads, preferred_element_type=jnp.float32
    )
    totals = jnp.sum(weights, -1)
    log_total = running + jnp.log(totals)
    mixed_low = (summed / totals[..., None]).reshape(tokens, -1).astype(low)
    attention = lax.psum(
        times_transpose(mixed_low, output_turned).astype(low), "tp"
    ).astype(jnp.float32)
    middle = inputs + attention
    second_norm, second_inverse = normalize(middle, gain_two)
    normed2 = second_norm.astype(low)
    normed2_all = lax.all_gather(normed2, "fsdp", axis=0, tiled=True)
    gate_up = expert_full[:, : 2 * span]
    down_turned = expert_full[:, 2 * span :]
    key_all = pair_all[:, :kv_width]
    value_all = pair_all[:, kv_width:]
    grouped = query.reshape(tokens, key_groups, groups, HD)

    def block_scores(key_piece, offset):
        count = key_piece.shape[0]
        key_heads = key_piece.reshape(count, key_groups, HD)
        scores = (
            jnp.einsum("qkgd,nkd->qkgn", grouped, key_heads, preferred_element_type=jnp.float32)
            * scale
        )
        key_doc = lax.dynamic_slice_in_dim(segment_row, offset, count)
        key_order = offset + jnp.arange(count, dtype=jnp.int32)
        seen = (key_doc[None, :] == query_doc[:, None]) & (
            key_order[None, :] <= query_order[:, None]
        )
        return (scores, seen[:, None, None, :], key_heads)

    def masked_away(offset, count):
        last_doc = lax.dynamic_index_in_dim(segment_row, offset + count - 1, keepdims=False)
        return (offset > query_order[tokens - 1]) | (last_doc < query_doc[0])

    place_z = lax.axis_index("fsdp")
    logits_all = jnp.dot(normed2_all, router_full, preferred_element_type=jnp.float32)
    expert_ids = jnp.arange(EXPERTS, dtype=jnp.int32)
    chosen_all = jnp.any(routes_all[:, :, None] == expert_ids[None, None, :], 1)
    masked_logits = jnp.where(chosen_all, logits_all, MASKED_SCORE)
    top = jnp.max(masked_logits, -1, keepdims=True)
    lifted = jnp.where(chosen_all, jnp.exp(masked_logits - top), 0.0)
    gates_all = lifted / jnp.sum(lifted, -1, keepdims=True)
    gates_here = lax.dynamic_slice_in_dim(gates_all, place_z * local, local, 1)
    chosen_here = lax.dynamic_slice_in_dim(chosen_all, place_z * local, local, 1)
    chosen = lax.dynamic_slice_in_dim(chosen_all, place_z * tokens, tokens, 0)
    gates = lax.dynamic_slice_in_dim(gates_all, place_z * tokens, tokens, 0)

    reach = normed2_all.shape[0]
    both_sides = jnp.dot(normed2_all, gate_up, preferred_element_type=jnp.float32)
    former = both_sides[:, :span]
    latter = both_sides[:, span:]
    hidden_grad = jnp.dot(outer_all, down_turned, preferred_element_type=jnp.float32)
    gate_wide = jnp.concatenate(
        [jnp.broadcast_to(gates_here[:, e : e + 1], (reach, hidden_width)) for e in range(local)], 1
    )
    logistic = jax.nn.sigmoid(former)
    active = former * logistic
    hidden = (active * latter).astype(low).astype(jnp.float32)
    gated = (hidden * gate_wide).astype(low)
    parts = [slice(e * hidden_width, (e + 1) * hidden_width) for e in range(local)]
    dgates = jnp.stack([jnp.sum(hidden[:, part] * hidden_grad[:, part], -1) for part in parts], 1)
    scaled_grad = hidden_grad * gate_wide
    former_grad = (scaled_grad * latter * logistic * (1.0 + former * (1.0 - logistic))).astype(low)
    latter_grad = (scaled_grad * active).astype(low)
    side_grads = jnp.concatenate([former_grad, latter_grad], 1)
    mixture_low = times_transpose(gated, down_turned).astype(low)
    input_part = times_transpose(side_grads, gate_up)
    side_sums = contract_rows(normed2_all, side_grads)
    down_sums = contract_rows(outer_all, gated)
    dgates = jnp.where(chosen_here, dgates, 0.0)
    dgates_wide = lax.dynamic_update_slice_in_dim(
        jnp.zeros((reach, EXPERTS), jnp.float32), dgates, place_z * local, 1
    )
    dgates_high = dgates_wide.astype(low)
    dgates_rest = (dgates_wide - dgates_high.astype(jnp.float32)).astype(low)
    dgates_sent = jnp.concatenate([dgates_high, dgates_rest], 1)
    dgates_sent = jnp.pad(dgates_sent, ((0, 0), (0, 128 - 2 * EXPERTS)))
    back_part = jnp.concatenate([input_part.astype(low), dgates_sent], 1)
    returned = lax.psum_scatter(
        lax.psum(back_part, "tp"), "fsdp", scatter_dimension=0, tiled=True
    ).astype(jnp.float32)
    expert_sums = jnp.concatenate([side_sums, down_sums], 1).astype(low)
    expert_out = collect_experts(expert_sums, rows).reshape(ep, rows, 3, local, hidden_width)
    side_out = expert_out[:, :, :2].transpose(2, 0, 3, 1, 4).reshape(2, EXPERTS, rows, hidden_width)
    side_out = side_out.astype(jnp.float32)
    down_out = expert_out[:, :, 2].transpose(0, 2, 3, 1).reshape(EXPERTS, hidden_width, rows).astype(jnp.float32)

    outer_grad = cotangent.astype(jnp.float32)
    input_grad_part = returned[:, :D]
    picked = returned[:, D : D + EXPERTS] + returned[:, D + EXPERTS : D + 2 * EXPERTS]
    logit_grad = (gates * (picked - jnp.sum(gates * picked, -1, keepdims=True))).astype(low)
    router_sums = contract_rows(normed2, logit_grad)
    second_grad = input_grad_part + times_transpose(logit_grad, router_full)
    middle_back, gain_two_sums = norm_back(second_grad, middle, second_inverse, gain_two)
    middle_grad = outer_grad + middle_back
    attention_grad = middle_grad.astype(low)
    output_sums = contract_rows(attention_grad, mixed_low)
    mixed_grad = jnp.dot(attention_grad, output_turned, preferred_element_type=jnp.float32).astype(low)
    mixed_heads = mixed_grad.reshape(tokens, key_groups, groups, HD)
    delta = jnp.sum(mixed_heads.astype(jnp.float32) * mixed_low.reshape(mixed_heads.shape), -1)

    def back_two(number, state):
        offset = number * tokens
        key_piece = lax.dynamic_slice_in_dim(key_all, offset, tokens, 0)
        value_piece = lax.dynamic_slice_in_dim(value_all, offset, tokens, 0)

        def back_compute(inner):
            query_sum, pair_sum = inner
            scores, seen, key_heads = block_scores(key_piece, offset)
            probs = jnp.where(seen, jnp.exp(scores - log_total[..., None]), 0.0)
            value_heads = value_piece.reshape(tokens, key_groups, HD)
            prob_grad = jnp.einsum(
                "qkgd,nkd->qkgn", mixed_heads, value_heads, preferred_element_type=jnp.float32
            )
            score_grad = (probs * (prob_grad - delta[..., None])).astype(low)
            query_sum = (
                query_sum
                + jnp.einsum(
                    "qkgn,nkd->qkgd", score_grad, key_heads, preferred_element_type=jnp.float32
                )
                * scale
            )
            key_block = (
                jnp.einsum(
                    "qkgn,qkgd->nkd", score_grad, grouped, preferred_element_type=jnp.float32
                )
                * scale
            )
            value_block = jnp.einsum(
                "qkgn,qkgd->nkd", probs.astype(low), mixed_heads, preferred_element_type=jnp.float32
            )
            pair = jnp.concatenate([key_block.reshape(tokens, -1), value_block.reshape(tokens, -1)], 1)
            return (query_sum, lax.dynamic_update_slice_in_dim(pair_sum, pair, offset, 0))

        return lax.cond(masked_away(offset, tokens), lambda inner: inner, back_compute, state)

    back_state = (
        jnp.zeros((tokens, key_groups, groups, HD), jnp.float32),
        jnp.zeros((seq_len, 2 * kv_width), jnp.float32),
    )
    query_sum, pair_sum = lax.fori_loop(0, seq_len // tokens, back_two, back_state)
    pair_local = lax.psum_scatter(
        pair_sum.astype(low), "ctx", scatter_dimension=0, tiled=True
    ).astype(jnp.float32)
    query_back = rotate(query_sum.reshape(tokens, -1), cosine, -sine)
    key_back = rotate(pair_local[:, :kv_width], cosine, -sine)
    qkv_back = jnp.concatenate([query_back, key_back, pair_local[:, kv_width:]], 1).astype(low)
    qkv_sums = contract_rows(normed1, qkv_back)
    first_part = times_transpose(qkv_back, qkv_full)
    first_grad = lax.psum(first_part.astype(low), "tp").astype(jnp.float32)
    input_back, gain_one_sums = norm_back(first_grad, inputs, first_inverse, gain_one)
    input_grad = middle_grad + input_back
    small_sums = jnp.concatenate([router_sums, gain_one_sums[:, None], gain_two_sums[:, None]], 1)
    small_sums = jnp.pad(small_sums, ((0, 0), (0, 128 - small_sums.shape[1])))
    attn_sums = jnp.concatenate([qkv_sums.astype(low), small_sums.astype(low), output_sums.astype(low)], 1)
    attn_out = lax.psum_scatter(attn_sums, both, scatter_dimension=0, tiled=True).astype(jnp.float32)
    mixture = lax.psum_scatter(
        lax.psum(mixture_low, "tp"), "fsdp", scatter_dimension=0, tiled=True
    ).astype(jnp.float32)
    layer_output = (middle + mixture).astype(low)
    small_out = attn_out[:, qkv_width : qkv_width + 128]
    return (
        layer_output,
        input_grad,
        small_out[:, EXPERTS],
        attn_out[:, :width],
        attn_out[:, width : width + kv_width],
        attn_out[:, width + kv_width : qkv_width],
        attn_out[:, qkv_width + 128 :].T,
        small_out[:, EXPERTS + 1],
        small_out[:, :EXPERTS],
        side_out[0],
        side_out[1],
        down_out,
    )


def shards(
    layer_input,
    segments,
    routes,
    norm_gain,
    query_weight,
    key_weight,
    value_weight,
    output_weight,
    ffn_gain,
    router_weight,
    gate_weight,
    up_weight,
    down_weight,
    cotangent,
):
    extra = jnp.concatenate([router_weight, norm_gain[:, None], ffn_gain[:, None]], 1)
    extra = jnp.pad(extra, ((0, 0), (0, 128 - extra.shape[1])))
    freq = 10000.0 ** (-2.0 * np.arange(HD // 2) / HD)
    (
        expert_full, outer_all, routes_all, normed2_all,
        attn_full, normed1, query, pair_all, mixed, middle, log_total, cosine, sine, extra_all,
    ) = front(
        query_weight, key_weight, value_weight, extra, output_weight.T, gate_weight, up_weight,
        down_weight.transpose(0, 2, 1), cotangent, routes.T, layer_input, segments,
        np.tile(freq.astype(np.float32), 4)[None, :],
    )
    returned, mixture, relay, own, gates = run_experts(
        normed2_all, outer_all, routes_all, extra_all, expert_full, 2
    )
    input_grad, layer_output, qkv_out, wo_out, expert_out = rear(
        returned, gates, middle, layer_input, cotangent, normed1, query, pair_all, mixed, log_total, cosine, sine,
        segments, extra_all, mixture, relay, own, attn_full, 3,
    )
    (
        query_out, key_out, value_out, output_out, router_out, gain_one_out, gain_two_out,
        gate_out, up_out, down_out, input_grad, layer_output,
    ) = finish(expert_out, qkv_out, wo_out, input_grad, layer_output, key_weight.shape[1], gate_weight.shape[2])
    return (
        layer_output,
        input_grad,
        gain_one_out[0],
        query_out,
        key_out,
        value_out,
        output_out.T,
        gain_two_out[0],
        router_out.T,
        gate_out,
        up_out,
        down_out.transpose(0, 2, 1),
    )


def solution(mesh):
    in_specs = (
        P(("fsdp", "ctx"), None),
        P("fsdp", None),
        P(("fsdp", "ctx"), None),
        P(("fsdp", "ctx")),
        P(("fsdp", "ctx"), "tp"),
        P(("fsdp", "ctx"), "tp"),
        P(("fsdp", "ctx"), "tp"),
        P("tp", ("fsdp", "ctx")),
        P(("fsdp", "ctx")),
        P(("fsdp", "ctx"), None),
        P(None, ("fsdp", "ctx"), "tp"),
        P(None, ("fsdp", "ctx"), "tp"),
        P(None, "tp", ("fsdp", "ctx")),
        P(("fsdp", "ctx"), None),
    )
    out_specs = (
        P(("fsdp", "ctx"), None),
        P(("fsdp", "ctx"), None),
        P(("fsdp", "ctx")),
        P(("fsdp", "ctx"), "tp"),
        P(("fsdp", "ctx"), "tp"),
        P(("fsdp", "ctx"), "tp"),
        P("tp", ("fsdp", "ctx")),
        P(("fsdp", "ctx")),
        P(("fsdp", "ctx"), None),
        P(None, ("fsdp", "ctx"), "tp"),
        P(None, ("fsdp", "ctx"), "tp"),
        P(None, "tp", ("fsdp", "ctx")),
    )
    fits = mesh.shape["ctx"] == 4 and mesh.shape["fsdp"] == 4 and mesh.shape["tp"] == 2
    body = shards if fits else plain_shards
    return jax.shard_map(body, mesh=mesh, in_specs=in_specs, out_specs=out_specs, check_vma=False)
```

```python
import jax
import jax.numpy as jnp
import numpy as np
from jax import lax
from jax.experimental import pallas as pl
from jax.experimental.pallas import tpu as pltpu
from jax.sharding import PartitionSpec as P

MESH = pl.DeviceIdType.MESH

D = 1536
HD = 64
EXPERTS = 16


EPSILON = 1e-05
MASKED_SCORE = -1e30


def rotate(values, cosine, sine):
    rows = values.shape[0]
    shaped = values.reshape(rows, -1, HD)
    half = HD // 2
    cosine, sine = cosine[:, None, :], sine[:, None, :]
    former = shaped[..., :half]
    latter = shaped[..., half:]
    turned = jnp.concatenate([former * cosine - latter * sine, latter * cosine + former * sine], -1)
    return turned.reshape(rows, -1)


def normalize(values, gain):
    inverse = lax.rsqrt(jnp.mean(values * values, -1, keepdims=True) + EPSILON)
    return (values * inverse * gain.astype(jnp.float32), inverse)


def norm_back(grad, values, inverse, gain):
    scaled = grad * gain.astype(jnp.float32)
    gain_grad = jnp.sum(grad * values * inverse, 0)
    mean_term = jnp.mean(scaled * values, -1, keepdims=True)
    return (inverse * scaled - values * inverse**3 * mean_term, gain_grad)


def document_place(segment_row):
    length = segment_row.shape[0]
    order = jnp.arange(length, dtype=jnp.int32)
    fresh = jnp.concatenate([jnp.ones((1,), jnp.bool_), segment_row[1:] != segment_row[:-1]])
    starts = lax.cummax(jnp.where(fresh, order, 0), axis=0)
    return order - starts


def contract_rows(left, right):
    return lax.dot_general(
        left, right, (((0,), (0,)), ((), ())), preferred_element_type=jnp.float32
    )


def times_transpose(left, right):
    return lax.dot_general(
        left, right, (((1,), (1,)), ((), ())), preferred_element_type=jnp.float32
    )


def spread_experts(packed):
    ep = lax.axis_size("fsdp")
    local = packed.shape[0] // ep
    rows = packed.shape[1]
    swapped = lax.all_to_all(packed, "fsdp", 0, 0, tiled=True)
    swapped = swapped.reshape(ep, local, rows, -1).transpose(0, 2, 1, 3)
    swapped = swapped.reshape(ep, rows, -1)
    whole = lax.all_gather(swapped, "ctx", axis=1)
    return whole.reshape(ep * lax.axis_size("ctx") * rows, -1)


def collect_experts(sums, rows):
    ep, ring = lax.axis_size("fsdp"), lax.axis_size("ctx")
    turned = sums.reshape(ep, ring, rows, -1).transpose(1, 0, 2, 3).reshape(sums.shape)
    mine = lax.psum_scatter(turned, "ctx", scatter_dimension=0, tiled=True)
    return lax.all_to_all(mine, "fsdp", 0, 0, tiled=True)


def at_device(fsdp, ctx, tp):
    return {"fsdp": fsdp, "ctx": ctx, "tp": tp}


def fetch(pairs, sems):
    copies = [pltpu.make_async_copy(source, target, sems.at[i]) for i, (source, target) in enumerate(pairs)]
    for copy in copies:
        copy.start()
    return copies


def greet(partners):
    barrier = pltpu.get_barrier_semaphore()
    for device in partners:
        pl.semaphore_signal(barrier, inc=1, device_id=device, device_id_type=MESH)
    pl.semaphore_wait(barrier, len(partners))


def remote(source, target, send, recv, device):
    return pltpu.make_async_remote_copy(
        src_ref=source, dst_ref=target, send_sem=send, recv_sem=recv, device_id=device, device_id_type=MESH
    )


def lasting(us):
    return pl.CostEstimate(flops=0, bytes_accessed=us * 3690000, transcendentals=0)


def front_kernel(
    query_ref, key_ref, value_ref, wo_ref, gate_ref, up_ref, down_ref, outer_ref, routes_ref,
    input_ref, segment_ref, freq_ref, router_ref, gain_one_ref, gain_two_ref,
    expert_out, outer_out, routes_out, normed2_out,
    attn_hbm, normed1_hbm, query_hbm, pair_hbm, mixed_hbm, middle_hbm, log_out, cos_out, sin_out, extra_out,
    attn_out, normed1_out, query_out, pair_out, mixed_out, middle_out, out_sem,
    query_s, key_s, value_s, mixed_s, bias_s, part_s, other_s, normed2_s,
    local_sem, z_send, z_recv, plane_send, plane_recv, relay_send, relay_recv, core_send, core_recv,
    key_send, key_recv, pair_send, pair_recv, chain_send, chain_recv, own_sem,
):
    ep = z_send.shape[1] + 1
    f, c, t = lax.axis_index("fsdp"), lax.axis_index("ctx"), lax.axis_index("tp")
    low = jnp.bfloat16
    rows = query_ref.shape[0]
    local = gate_ref.shape[0] // ep
    hidden = gate_ref.shape[2]
    tokens = outer_ref.shape[0]
    half = tokens // 2
    heads = query_s.shape[0]
    key_heads = key_s.shape[0]
    width, kv_width = heads * HD, key_heads * HD
    qkv_width = width + 2 * kv_width
    outs = (attn_out, expert_out)
    cuts = [(out.shape[1] // 256) * 128 for out in outs]

    def peer(distance):
        return lax.rem(f + distance, ep)

    def shard_rows(fsdp, ctx):
        return pl.ds(pl.multiple_of((fsdp * 4 + ctx) * rows, 16), rows)

    def columns(kind, side):
        cut, full = cuts[kind], outs[kind].shape[1]
        return pl.ds(0, cut) if side == 0 else pl.ds(cut, full - cut)

    line = [at_device(peer(d), c, t) for d in range(1, ep)]
    plane = [at_device(f, c ^ k, t) for k in range(1, 4)]
    x_device, y_device = plane[0], plane[1]
    core = at_device(f, c, 1 - t)
    mine = shard_rows(f, c)
    own_attn = []
    for start, ref in (
        (0, query_ref), (width, key_ref), (width + kv_width, value_ref), (qkv_width + 128, wo_ref)
    ):
        target = attn_out.at[mine, pl.ds(start, ref.shape[1])]
        own_attn.append(pltpu.make_async_copy(ref, target, own_sem.at[len(own_attn)]))
        own_attn[-1].start()
    shown = jnp.concatenate([router_ref[...].astype(jnp.float32), jnp.zeros((128 - EXPERTS, rows), jnp.float32)], 0)
    row = lax.broadcasted_iota(jnp.int32, (128, rows), 0)
    shown = jnp.where(row == EXPERTS, gain_one_ref[...].astype(jnp.float32), shown)
    shown = jnp.where(row == EXPERTS + 1, gain_two_ref[...].astype(jnp.float32), shown)
    attn_out[mine, qkv_width : qkv_width + 128] = shown.T.astype(low)
    greet(line + plane + [core])
    sent = []

    def send(copy, when=None):
        if when is None:
            copy.start()
        else:
            pl.when(when)(copy.start)
        sent.append((when, copy))

    def await_arrival(copy, when=None):
        if when is None:
            copy.wait_recv()
        else:
            pl.when(when)(copy.wait_recv)

    def z_arrival(kind, d):
        place = shard_rows(peer(ep - d), c)
        remote(
            outs[kind].at[place], outs[kind].at[place], z_send.at[kind, d - 1], z_recv.at[kind, d - 1], x_device
        ).wait_recv()

    def spread(kind, g, when=None):
        place = shard_rows(g, c)
        for step in range(2):
            for way, device in enumerate((x_device, y_device)):
                side = step ^ way
                block = outs[kind].at[place, columns(kind, side)]
                send(
                    remote(
                        block, block, plane_send.at[kind, g, way, side], plane_recv.at[kind, g, way, side], device
                    ),
                    when,
                )

    def pass_on(kind, g, when=None):
        for way, device in enumerate((y_device, x_device)):
            place = shard_rows(g, c ^ (1 << way))
            block = outs[kind].at[place, columns(kind, way)]
            await_arrival(
                remote(
                    block, block, plane_send.at[kind, g, way, way], plane_recv.at[kind, g, way, way], device
                ),
                when,
            )
            send(remote(block, block, relay_send.at[kind, g, way], relay_recv.at[kind, g, way], device), when)

    def settle(kind):
        for g in range(ep):
            for way, device in enumerate((x_device, y_device)):
                side = 1 - way
                block = outs[kind].at[shard_rows(g, c ^ (1 << way)), columns(kind, side)]
                remote(
                    block, block, plane_send.at[kind, g, way, side], plane_recv.at[kind, g, way, side], device
                ).wait_recv()
                block = outs[kind].at[shard_rows(g, c ^ 3), columns(kind, way)]
                remote(
                    block, block, relay_send.at[kind, g, way], relay_recv.at[kind, g, way], device
                ).wait_recv()

    nexts = (at_device(jnp.minimum(f + 1, ep - 1), c, t), at_device(jnp.maximum(f - 1, 0), c, t))
    more = (f < ep - 1, f > 0)

    def chain_origin(way, hop):
        if way == 0:
            return jnp.maximum(f - hop, 0), f >= hop
        return jnp.minimum(f + hop, ep - 1), f + hop < ep

    def chain_begin(kind, source, target):
        for way in range(2):
            send(
                remote(source, target, chain_send.at[kind, way, 0], chain_recv.at[kind, way, 0], nexts[way]),
                more[way],
            )

    def chain_hop(kind, way, hop, block):
        there = chain_origin(way, hop)[1]
        await_arrival(
            remote(
                block, block, chain_send.at[kind, way, hop - 1], chain_recv.at[kind, way, hop - 1], nexts[way]
            ),
            there,
        )
        if hop < ep - 1:
            send(
                remote(block, block, chain_send.at[kind, way, hop], chain_recv.at[kind, way, hop], nexts[way]),
                there & more[way],
            )

    def line_place(fsdp, part):
        return pl.ds(pl.multiple_of(fsdp * tokens + part * half, 16), half)

    own_tokens = pl.ds(pl.multiple_of(f * tokens, 16), tokens)
    my_half = pl.ds(pl.multiple_of(t * half, 16), half)

    def line_hop(kind, hop, target):
        for way in range(2):
            g, there = chain_origin(way, hop)
            block = target.at[line_place(g, t)]
            chain_hop(kind, way, hop, block)
            send(remote(block, block, core_send.at[kind - 1, g], core_recv.at[kind - 1, g], core), there)

    def line_settle(kind, target):
        for g in range(ep):
            block = target.at[line_place(g, 1 - t)]
            await_arrival(
                remote(block, block, core_send.at[kind - 1, g], core_recv.at[kind - 1, g], core), f != g
            )

    for copy in own_attn:
        copy.wait()
    chain_begin(0, attn_out.at[mine], attn_out.at[mine])
    own_outer = pltpu.make_async_copy(outer_ref, outer_out.at[own_tokens], local_sem.at[2])
    own_outer.start()
    own_columns = (slice(None), pl.ds(pl.multiple_of(f * tokens, 128), tokens))
    own_routes = pltpu.make_async_copy(routes_ref, routes_out.at[own_columns], local_sem.at[3])
    own_routes.start()
    for d in range(1, ep):
        send(
            remote(
                routes_ref, routes_out.at[own_columns], z_send.at[4, d - 1], z_recv.at[4, d - 1], line[d - 1]
            )
        )
    for kind, ref in enumerate((gate_ref, up_ref, down_ref)):
        for e in range(local):
            target = expert_out.at[mine, pl.ds((kind * local + e) * hidden, hidden)]
            pltpu.make_async_copy(ref.at[f * local + e], target, local_sem.at[1]).start()
    spread(0, f)

    length = segment_ref.shape[1]
    seg_keys = segment_ref[...].astype(jnp.float32)
    seg_here = segment_ref[:, pl.ds(pl.multiple_of(c * tokens, 128), tokens)].astype(jnp.float32)
    seg_queries = jnp.broadcast_to(seg_here, (128, tokens)).T[:, :1]
    key_order = lax.broadcasted_iota(jnp.int32, (tokens, length), 1)
    query_order = lax.broadcasted_iota(jnp.int32, (tokens, length), 0) + c * tokens
    same = seg_keys == seg_queries
    seen = same & (key_order <= query_order)
    bias_s[...] = jnp.where(seen, 0.0, MASKED_SCORE)
    place = jnp.sum(jnp.where(same & (key_order < query_order), 1.0, 0.0), -1, keepdims=True)
    angle = place * freq_ref[...]
    lane = lax.broadcasted_iota(jnp.int32, (tokens, 128), 1)
    first_half = lax.rem(lane, HD) < HD // 2
    cosine = jnp.cos(angle)
    sine = jnp.where(first_half, -jnp.sin(angle), jnp.sin(angle))
    cos_out[...] = cosine
    sin_out[...] = sine
    inputs = input_ref[...].astype(jnp.float32)
    inverse = lax.rsqrt(jnp.mean(inputs * inputs, -1, keepdims=True) + EPSILON)

    pass_on(0, f)
    for hop in range(1, ep):
        for way in range(2):
            g, there = chain_origin(way, hop)
            chain_hop(0, way, hop, attn_out.at[shard_rows(g, c)])
            spread(0, g, there)
        if hop > 1:
            for way in range(2):
                pass_on(0, *chain_origin(way, hop - 1))
    for way in range(2):
        pass_on(0, *chain_origin(way, ep - 1))
    for d in range(1, ep):
        for kind, ref in enumerate((gate_ref, up_ref, down_ref)):
            for e in range(local):
                target = expert_out.at[mine, pl.ds((kind * local + e) * hidden, hidden)]
                remote(
                    ref.at[peer(d) * local + e], target, z_send.at[1, d - 1], z_recv.at[1, d - 1],
                    line[d - 1],
                ).start()
    pltpu.make_async_copy(expert_out.at[mine], expert_out.at[mine], local_sem.at[1]).wait()
    spread(1, f)
    settle(0)
    stores = [pltpu.make_async_copy(attn_out, attn_hbm, out_sem.at[0])]
    stores[0].start()

    def store(number, source, target):
        stores.append(pltpu.make_async_copy(source, target, out_sem.at[number]))
        stores[-1].start()

    gains = attn_out[:, qkv_width : qkv_width + 128].astype(jnp.float32).T
    normed1_out[...] = (inputs * inverse * gains[EXPERTS : EXPERTS + 1, :]).astype(low)
    store(1, normed1_out, normed1_hbm)

    def project(start):
        return jnp.dot(
            normed1_out[...], attn_out[:, start : start + 256], preferred_element_type=jnp.float32
        )

    def turned(tile):
        swapped = jnp.where(first_half, pltpu.roll(tile, 128 - HD // 2, 1), pltpu.roll(tile, HD // 2, 1))
        return tile * cos_out[...] + swapped * sin_out[...]

    here = pl.ds(pl.multiple_of(c * tokens, 16), tokens)
    for start in range(0, kv_width, 256):
        tile = project(width + start)
        for side in (0, 128):
            pair_out[here, start + side : start + side + 128] = turned(tile[:, side : side + 128]).astype(low)
    for start in range(0, kv_width, 256):
        pair_out[here, kv_width + start : kv_width + start + 256] = project(width + kv_width + start).astype(low)
    for k in (3, 1, 2):
        send(remote(pair_out.at[here], pair_out.at[here], key_send.at[k - 1], key_recv.at[k - 1], plane[k - 1]))
    for start in range(0, width, 256):
        tile = project(start)
        for side in (0, 128):
            query_out[:, start + side : start + side + 128] = turned(tile[:, side : side + 128]).astype(low)
    store(2, query_out, query_hbm)
    for h in range(heads):
        query_s[h] = query_out[:, h * HD : (h + 1) * HD]
    for k in range(1, 4):
        block = pair_out.at[pl.ds(pl.multiple_of((c ^ k) * tokens, 16), tokens)]
        remote(block, block, key_send.at[k - 1], key_recv.at[k - 1], plane[k - 1]).wait_recv()
    store(3, pair_out, pair_hbm)
    for g in range(key_heads):
        key_s[g] = pair_out[:, g * HD : (g + 1) * HD]
        value_s[g] = pair_out[:, kv_width + g * HD : kv_width + (g + 1) * HD]
    pass_on(1, f)
    for d in range(1, ep):
        z_arrival(1, d)
        spread(1, peer(ep - d))
    chain_begin(2, outer_ref.at[my_half], outer_out.at[line_place(f, t)])

    def attend(h, carry):
        g = lax.div(h, heads // key_heads)
        query = query_s[h] * jnp.asarray(HD**-0.5, low)
        scores = lax.dot_general(
            query, key_s[g], (((1,), (1,)), ((), ())), preferred_element_type=jnp.float32
        ) + bias_s[...]
        top = jnp.max(scores, -1, keepdims=True)
        weights = jnp.exp(scores - top)
        total = jnp.sum(weights, -1, keepdims=True)
        summed = jnp.dot(weights.astype(low), value_s[g], preferred_element_type=jnp.float32)
        mixed_s[h] = (summed / total).astype(low)
        log_out[h] = jnp.broadcast_to(top + jnp.log(total), (tokens, 128)).T[:1, :]
        return carry

    lax.fori_loop(0, heads, attend, 0)
    for h in range(heads):
        mixed_out[:, h * HD : (h + 1) * HD] = mixed_s[h]
    store(4, mixed_out, mixed_hbm)
    model = input_ref.shape[1]
    for start in range(0, model, 256):
        part_s[:, start : start + 256] = lax.dot_general(
            mixed_out[...], attn_out[start : start + 256, qkv_width + 128 :],
            (((1,), (1,)), ((), ())), preferred_element_type=jnp.float32,
        ).astype(low)
    exchange = remote(part_s, other_s, pair_send, pair_recv, core)
    send(exchange)
    pass_on(1, peer(ep - 1))
    line_hop(2, 1, outer_out)
    exchange.wait_recv()
    middle = input_ref[...].astype(jnp.float32) + (
        part_s[...].astype(jnp.float32) + other_s[...].astype(jnp.float32)
    )
    middle_out[...] = middle
    store(5, middle_out, middle_hbm)
    inverse = lax.rsqrt(jnp.mean(middle * middle, -1, keepdims=True) + EPSILON)
    gains = attn_out[:, qkv_width : qkv_width + 128].astype(jnp.float32).T
    normed2_s[...] = (middle * inverse * gains[EXPERTS + 1 : EXPERTS + 2, :]).astype(low)
    chain_begin(1, normed2_s.at[my_half], normed2_out.at[line_place(f, t)])
    own_normed2 = pltpu.make_async_copy(normed2_s, normed2_out.at[own_tokens], local_sem.at[4])
    own_normed2.start()
    for d in range(2, ep):
        pass_on(1, peer(ep - d))
    line_hop(1, 1, normed2_out)
    line_hop(2, 2, outer_out)
    line_hop(1, 2, normed2_out)
    line_hop(2, 3, outer_out)
    line_hop(1, 3, normed2_out)
    settle(1)
    line_settle(2, outer_out)
    line_settle(1, normed2_out)
    for d in range(1, ep):
        place = (slice(None), pl.ds(pl.multiple_of(peer(ep - d) * tokens, 128), tokens))
        remote(
            routes_out.at[place], routes_out.at[place], z_send.at[4, d - 1], z_recv.at[4, d - 1], core
        ).wait_recv()
        remote(
            expert_out.at[mine], expert_out.at[mine], z_send.at[1, d - 1], z_recv.at[1, d - 1], core
        ).wait_send()
    extra_out[...] = attn_out[:, qkv_width : qkv_width + 128]
    own_outer.wait()
    own_routes.wait()
    own_normed2.wait()
    for copy in stores:
        copy.wait()
    all_sent(sent)


def front(
    query, key, value, wo, gate, up, down, outer, routes, inputs, segments, freq, router, gain_one, gain_two
):
    ep = lax.axis_size("fsdp")
    rows = query.shape[0]
    heads, key_heads = query.shape[1] // HD, key.shape[1] // HD
    width = sum(part.shape[1] for part in (query, key, value, wo)) + 128
    total = rows * ep * lax.axis_size("ctx")
    local = gate.shape[0] // ep
    tokens, model = inputs.shape
    length = segments.shape[1]
    low = jnp.bfloat16
    dma = pltpu.SemaphoreType.DMA
    anywhere = pl.BlockSpec(memory_space=pl.ANY)
    vmem = pl.BlockSpec(memory_space=pltpu.VMEM)
    shape = jax.ShapeDtypeStruct
    kept = (
        ((total, width), low),
        ((tokens, model), low),
        ((tokens, heads * HD), low),
        ((length, 2 * key_heads * HD), low),
        ((tokens, heads * HD), low),
        ((tokens, model), jnp.float32),
    )
    return pl.pallas_call(
        front_kernel,
        out_shape=(
            shape((total, 3 * local * gate.shape[2]), low),
            shape((ep * tokens, model), low),
            shape((routes.shape[0], ep * tokens), routes.dtype),
            shape((ep * tokens, model), low),
        )
        + tuple(shape(*each) for each in kept)
        + (
            shape((heads, 1, tokens), jnp.float32),
            shape((tokens, 128), jnp.float32),
            shape((tokens, 128), jnp.float32),
            shape((total, 128), low),
        ),
        in_specs=[anywhere] * 9 + [vmem] * 6,
        out_specs=(anywhere,) * 10 + (vmem,) * 4,
        scratch_shapes=[pltpu.VMEM(*each) for each in kept]
        + [
            dma((len(kept),)),
            pltpu.VMEM((heads, tokens, HD), low),
            pltpu.VMEM((key_heads, length, HD), low),
            pltpu.VMEM((key_heads, length, HD), low),
            pltpu.VMEM((heads, tokens, HD), low),
            pltpu.VMEM((tokens, length), jnp.float32),
            pltpu.VMEM((tokens, model), low),
            pltpu.VMEM((tokens, model), low),
            pltpu.VMEM((tokens, model), low),
            dma((5,)),
            dma((5, ep - 1)),
            dma((5, ep - 1)),
            dma((2, ep, 2, 2)),
            dma((2, ep, 2, 2)),
            dma((2, ep, 2)),
            dma((2, ep, 2)),
            dma((2, ep)),
            dma((2, ep)),
            dma((3,)),
            dma((3,)),
            dma,
            dma,
            dma((3, 2, ep - 1)),
            dma((3, 2, ep - 1)),
            dma((4,)),
        ],
        compiler_params=pltpu.CompilerParams(
            collective_id=1, has_side_effects=True, vmem_limit_bytes=60 * 1024 * 1024
        ),
        cost_estimate=lasting(165),
        name="front",
    )(query, key, value, wo, gate, up, down, outer, routes, inputs, segments, freq, router, gain_one, gain_two)


def z_sum_scratch(ep, tokens, width, low):
    dma = pltpu.SemaphoreType.DMA
    return [
        pltpu.VMEM((ep, tokens // 2, width), low),
        pltpu.VMEM((ep - 1, tokens // 2, width), low),
        pltpu.VMEM((ep - 1, tokens // 2, width), low),
        dma((ep,)),
        dma((ep,)),
        dma((ep - 1,)),
        dma((ep - 1,)),
        dma,
        dma,
    ]


class ZSum:
    size = 9

    def __init__(self, part, scratch, sent):
        self.part, self.sent = part, sent
        (
            self.core_in, self.z_out, self.z_in, self.core_send, self.core_recv,
            self.z_send, self.z_recv, self.back_send, self.back_recv,
        ) = scratch
        self.ep, self.half = self.core_in.shape[0], self.core_in.shape[1]
        self.f, self.c, self.t = lax.axis_index("fsdp"), lax.axis_index("ctx"), lax.axis_index("tp")
        self.core = at_device(self.f, self.c, 1 - self.t)

    def peer(self, distance):
        return lax.rem(self.f + distance, self.ep)

    def place(self, fsdp, part):
        return pl.ds(pl.multiple_of(fsdp * 2 * self.half + part * self.half, 16), self.half)

    def rows(self, part):
        return pl.ds(pl.multiple_of(part * self.half, 16), self.half)

    def send(self, copy):
        copy.start()
        self.sent.append((None, copy))

    def to_core(self, d):
        self.send(
            remote(
                self.part.at[self.place(self.peer(d), 1 - self.t)], self.core_in.at[d],
                self.core_send.at[d], self.core_recv.at[d], self.core,
            )
        )

    def added(self, d):
        landing = self.core_in.at[d]
        remote(landing, landing, self.core_send.at[d], self.core_recv.at[d], self.core).wait_recv()
        mine = self.part[self.place(self.peer(d), self.t), :]
        return mine.astype(jnp.float32) + self.core_in[d].astype(jnp.float32)

    def to_z(self, d):
        self.z_out[d - 1] = self.added(d).astype(self.z_out.dtype)
        self.send(
            remote(
                self.z_out.at[d - 1], self.z_in.at[d - 1], self.z_send.at[d - 1], self.z_recv.at[d - 1],
                at_device(self.peer(d), self.c, self.t),
            )
        )

    def collect(self):
        total = self.added(0)
        for d in range(1, self.ep):
            landing = self.z_in.at[d - 1]
            remote(landing, landing, self.z_send.at[d - 1], self.z_recv.at[d - 1], self.core).wait_recv()
            total = total + self.z_in[d - 1].astype(jnp.float32)
        return total

    def share(self, out):
        mine = out.at[self.rows(self.t)]
        self.send(remote(mine, mine, self.back_send, self.back_recv, self.core))

    def finish(self, out):
        other = out.at[self.rows(1 - self.t)]
        remote(other, other, self.back_send, self.back_recv, self.core).wait_recv()


def pair_sum_scratch(ep, tokens, width, low):
    dma = pltpu.SemaphoreType.DMA
    return [
        pltpu.VMEM((ep, tokens // 2, width), low),
        pltpu.VMEM((4, tokens // 2, width), low),
        dma((ep,)),
        dma((ep,)),
        dma((4,)),
        dma((4,)),
        dma((2,)),
    ]


class PairSum:
    def __init__(self, part, mine, scratch, sent):
        self.part, self.mine, self.sent = part, mine, sent
        (
            self.own, self.landing, self.core_send, self.core_recv, self.send_sem, self.recv_sem, self.cross_sem
        ) = scratch
        self.ep, self.half = self.own.shape[0], self.own.shape[1]
        self.f, c, self.t = lax.axis_index("fsdp"), lax.axis_index("ctx"), lax.axis_index("tp")
        self.core = at_device(self.f, c, 1 - self.t)
        self.partner = self.f ^ 1
        self.inner = (self.f == 1) | (self.f == 2)
        self.others = [2 - (self.f & 2) + j for j in range(2)]
        self.devices = [at_device(g, c, self.t) for g in self.others]
        self.beside = at_device(self.partner, c, self.t)

    def place(self, g, part):
        return pl.ds(pl.multiple_of(g * 2 * self.half + part * self.half, 16), self.half)

    def send(self, copy, when=None):
        if when is None:
            copy.start()
        else:
            pl.when(when)(copy.start)
        self.sent.append((when, copy))

    def to_core(self):
        for g in range(self.ep):
            self.send(
                remote(
                    self.part.at[self.place(g, 1 - self.t)], self.own.at[g],
                    self.core_send.at[g], self.core_recv.at[g], self.core,
                )
            )

    def both_cores(self, g):
        block = self.own.at[g]
        remote(block, block, self.core_send.at[g], self.core_recv.at[g], self.core).wait_recv()
        return self.mine[g].astype(jnp.float32) + self.own[g].astype(jnp.float32)

    def begin(self):
        outer = jnp.logical_not(self.inner)
        for j, g in enumerate(self.others):
            self.own[g] = self.both_cores(g).astype(self.own.dtype)
            self.send(
                remote(
                    self.own.at[g], self.landing.at[1 + j], self.send_sem.at[1 + j], self.recv_sem.at[1 + j],
                    self.beside,
                ),
                outer,
            )
        self.own[self.partner] = self.both_cores(self.partner).astype(self.own.dtype)
        self.send(
            remote(
                self.own.at[self.partner], self.landing.at[0], self.send_sem.at[0], self.recv_sem.at[0], self.beside
            )
        )

    def cross(self):
        for j, g in enumerate(self.others):

            @pl.when(self.inner)
            def _():
                block = self.landing.at[1 + j]
                remote(block, block, self.send_sem.at[1 + j], self.recv_sem.at[1 + j], self.beside).wait_recv()
                added = self.own[g].astype(jnp.float32) + self.landing[1 + j].astype(jnp.float32)
                self.own[g] = added.astype(self.own.dtype)

            self.send(
                remote(
                    self.own.at[g], self.landing.at[3], self.cross_sem.at[j], self.recv_sem.at[3], self.devices[j]
                ),
                self.inner,
            )

    def collect(self):
        total = self.both_cores(self.f)
        for slot in (0, 3):
            block = self.landing.at[slot]
            remote(block, block, self.send_sem.at[slot], self.recv_sem.at[slot], self.beside).wait_recv()
            total = total + self.landing[slot].astype(jnp.float32)
        return total


def all_sent(sent):
    for when, copy in sent:
        if when is None:
            copy.wait_send()
        else:
            pl.when(when)(copy.wait_send)


def shard_sum_scratch(ep, rows, width, low):
    cut = first_columns(width)
    widths = [cut] if cut == width else [cut, width - cut]
    dma = pltpu.SemaphoreType.DMA
    scratch = []
    for part in widths:
        scratch += [
            pltpu.VMEM((ep, 2, rows, part), low),
            pltpu.VMEM((ep, rows, part), low),
            pltpu.VMEM((ep, rows, part), low),
        ]
    return scratch + [
        dma((2, ep, 2)), dma((2, ep, 2)), dma((2, ep)), dma((2, ep)), dma((2, ep)), dma((2, ep))
    ]


def first_columns(width):
    return width if width == 128 else -(-width // 256) * 128


class ShardSum:
    def __init__(self, part, rows, width, scratch, sent):
        self.part, self.rows, self.sent = part, rows, sent
        cut = first_columns(width)
        self.columns = [pl.ds(0, cut)] + ([] if cut == width else [pl.ds(cut, width - cut)])
        self.ways = range(len(self.columns))
        (
            self.first_send, self.first_recv, self.second_send, self.second_recv, self.z_send, self.z_recv
        ) = scratch[-6:]
        self.first_in = [scratch[3 * way] for way in self.ways]
        self.second_in = [scratch[3 * way + 1] for way in self.ways]
        self.z_in = [scratch[3 * way + 2] for way in self.ways]
        self.ep = self.first_in[0].shape[0]
        self.f, self.c, self.t = lax.axis_index("fsdp"), lax.axis_index("ctx"), lax.axis_index("tp")
        self.neighbours = (at_device(self.f, self.c ^ 1, self.t), at_device(self.f, self.c ^ 2, self.t))
        self.order = list(range(1, self.ep)) + [0]

    def peer(self, distance):
        return lax.rem(self.f + distance, self.ep)

    def block(self, distance, ctx, way):
        start = (self.peer(distance) * 4 + ctx) * self.rows
        return pl.ds(pl.multiple_of(start, 16), self.rows), self.columns[way]

    def send(self, copy):
        copy.start()
        self.sent.append((None, copy))

    def first(self, d):
        for number in range(2):
            for way in self.ways:
                target = self.c ^ 3 if number == 0 else self.c ^ (1 << way)
                self.send(
                    remote(
                        self.part.at[self.block(d, target, way)], self.first_in[way].at[d, number],
                        self.first_send.at[way, d, number], self.first_recv.at[way, d, number],
                        self.neighbours[way],
                    )
                )

    def second(self, d):
        for way in self.ways:
            for number in range(2):
                landing = self.first_in[way].at[d, number]
                remote(
                    landing, landing, self.first_send.at[way, d, number],
                    self.first_recv.at[way, d, number], self.neighbours[way],
                ).wait_recv()
            term = self.part[self.block(d, self.c ^ (2 >> way), way)]
            added = term.astype(jnp.float32) + self.first_in[way][d, 0].astype(jnp.float32)
            self.first_in[way][d, 0] = added.astype(self.part.dtype)
            self.send(
                remote(
                    self.first_in[way].at[d, 0], self.second_in[way].at[d],
                    self.second_send.at[way, d], self.second_recv.at[way, d], self.neighbours[1 - way],
                )
            )

    def total(self, d, way):
        landing = self.second_in[way].at[d]
        remote(
            landing, landing, self.second_send.at[way, d], self.second_recv.at[way, d], self.neighbours[1 - way]
        ).wait_recv()
        term = self.part[self.block(d, self.c, way)]
        return (
            term.astype(jnp.float32)
            + self.first_in[way][d, 1].astype(jnp.float32)
            + self.second_in[way][d].astype(jnp.float32)
        )

    def to_z(self, d, out):
        for way in self.ways:
            total = self.total(d, way)
            if d == 0:
                out[:, self.columns[way]] = total
                continue
            self.first_in[way][d, 1] = total.astype(self.part.dtype)
            self.send(
                remote(
                    self.first_in[way].at[d, 1], self.z_in[way].at[d - 1],
                    self.z_send.at[way, d], self.z_recv.at[way, d], at_device(self.peer(d), self.c, self.t),
                )
            )

    def from_z(self, out):
        for way in self.ways:
            for d in range(1, self.ep):
                landing = self.z_in[way].at[d - 1]
                remote(
                    landing, landing, self.z_send.at[way, d], self.z_recv.at[way, d], self.neighbours[0]
                ).wait_recv()
                out[:, self.columns[way]] += self.z_in[way][d - 1].astype(jnp.float32)

    def halves(self):
        others = [2 - (self.f & 2) + j for j in range(2)]
        return (self.f == 1) | (self.f == 2), list(enumerate(others, 1)), self.f ^ 1

    def distance(self, g):
        return lax.rem(g + self.ep - self.f, self.ep)

    def pair_begin(self, out):
        inner, others, partner = self.halves()
        beside = at_device(partner, self.c, self.t)
        for way in self.ways:
            for slot, g in others + [(0, partner)]:
                d = self.distance(g)
                self.first_in[way][d, 1] = self.total(d, way).astype(self.part.dtype)
                copy = remote(
                    self.first_in[way].at[d, 1], self.z_in[way].at[slot],
                    self.z_send.at[way, slot], self.z_recv.at[way, slot], beside,
                )
                when = None if slot == 0 else jnp.logical_not(inner)
                if when is None:
                    copy.start()
                else:
                    pl.when(when)(copy.start)
                self.sent.append((when, copy))
            out[:, self.columns[way]] = self.total(0, way)

    def pair_cross(self):
        inner, others, partner = self.halves()
        beside = at_device(partner, self.c, self.t)
        for way in self.ways:
            for slot, g in others:
                d = self.distance(g)

                @pl.when(inner)
                def _():
                    block = self.z_in[way].at[slot]
                    remote(block, block, self.z_send.at[way, slot], self.z_recv.at[way, slot], beside).wait_recv()
                    added = self.first_in[way][d, 1].astype(jnp.float32) + self.z_in[way][slot].astype(jnp.float32)
                    self.first_in[way][d, 1] = added.astype(self.part.dtype)

                copy = remote(
                    self.first_in[way].at[d, 1], self.z_in[way].at[3],
                    self.z_send.at[way, slot], self.z_recv.at[way, 3], at_device(g, self.c, self.t),
                )
                pl.when(inner)(copy.start)
                self.sent.append((inner, copy))

    def pair_collect(self, out):
        for way in self.ways:
            for slot in (0, 3):
                block = self.z_in[way].at[slot]
                remote(
                    block, block, self.z_send.at[way, slot], self.z_recv.at[way, slot], self.neighbours[0]
                ).wait_recv()
                out[:, self.columns[way]] += self.z_in[way][slot].astype(jnp.float32)


def all_partners(ep):
    f, c, t = lax.axis_index("fsdp"), lax.axis_index("ctx"), lax.axis_index("tp")
    line = [at_device(lax.rem(f + d, ep), c, t) for d in range(1, ep)]
    return line + [at_device(f, c ^ 1, t), at_device(f, c ^ 2, t), at_device(f, c, 1 - t)]


class PlaneHalf:
    def __init__(self, part, rows, local, landings, send_sem, recv_sem, sent):
        self.part, self.rows, self.landings, self.sent = part, rows, landings, sent
        self.send_sem, self.recv_sem = send_sem, recv_sem
        self.local, self.cut = local, landings[0].shape[-1] // local
        self.ep = landings[0].shape[0]
        self.f, self.c, t = lax.axis_index("fsdp"), lax.axis_index("ctx"), lax.axis_index("tp")
        self.neighbours = (at_device(self.f, self.c ^ 1, t), at_device(self.f, self.c ^ 2, t))

    def block(self, distance, ctx, way, e):
        start = (lax.rem(self.f + distance, self.ep) * 4 + ctx) * self.rows
        columns = pl.ds((2 * e + way) * self.cut, self.cut)
        return pl.ds(pl.multiple_of(start, 16), self.rows), columns

    def landed(self, d, number, way):
        landing = self.landings[way].at[d, number]
        return remote(
            landing, landing, self.send_sem.at[way, d, number], self.recv_sem.at[way, d, number],
            self.neighbours[way],
        )

    def start(self, d, e):
        for number in range(2):
            for way in range(2):
                target = self.c ^ 3 if number == 0 else self.c ^ (1 << way)
                remote(
                    self.part.at[self.block(d, target, way, e)],
                    self.landings[way].at[d, number, :, pl.ds(e * self.cut, self.cut)],
                    self.send_sem.at[way, d, number], self.recv_sem.at[way, d, number], self.neighbours[way],
                ).start()

    def finish(self, d):
        for way in range(2):
            for number in range(2):
                copy = self.landed(d, number, way)
                copy.wait_recv()
                self.sent.append((None, copy))
                ctx = self.c ^ (2 >> way) if number == 0 else self.c
                for e in range(self.local):
                    at = slice(e * self.cut, (e + 1) * self.cut)
                    term = self.part[self.block(d, ctx, way, e)].astype(jnp.float32)
                    added = term + self.landings[way][d, number, :, at].astype(jnp.float32)
                    self.landings[way][d, number, :, at] = added.astype(self.part.dtype)


def experts_kernel(
    routes_ref, extra_ref, tokens_hbm, outer_hbm, weight_hbm,
    returned_ref, mixture_out, relay_out, own_out, gates_out,
    tokens_ref, outer_ref, weight_ref, in_sem,
    gates_s, gated_s, side_s, part_s, mixture_s, sums_s, first_x, first_y, plane_send, plane_recv, local_sem, *scratch,
):
    ep = lax.axis_size("fsdp")
    f = lax.axis_index("fsdp")
    low = jnp.bfloat16
    reach, model = tokens_ref.shape
    span = weight_ref.shape[1] // 3
    tokens = reach // ep
    rows = model // (4 * ep)
    local = EXPERTS // ep
    hidden = span // local
    sent = []
    back = ZSum(part_s, scratch, sent)
    plane = PlaneHalf(sums_s, rows, local, (first_x, first_y), plane_send, plane_recv, sent)
    pairs = [(tokens_hbm, tokens_ref), (outer_hbm, outer_ref)]
    for e in range(local):
        for kind in range(3):
            at = (slice(None), pl.ds(kind * span + e * hidden, hidden))
            pairs.insert(1 + 3 * e + kind + (e > 0 or kind > 1), (weight_hbm.at[at], weight_ref.at[at]))
    coming = fetch(pairs, in_sem)
    greet(all_partners(ep))

    lane = lax.broadcasted_iota(jnp.int32, (reach, 128), 1)
    uses = routes_ref.shape[0]
    turned = jnp.concatenate(
        [routes_ref[...].astype(jnp.float32), jnp.zeros((128 - uses, reach), jnp.float32)], 0
    ).T.astype(jnp.int32)
    chosen = turned[:, 0:1] == lane
    for k in range(1, uses):
        chosen = chosen | (turned[:, k : k + 1] == lane)
    coming[0].wait()
    logits = jnp.dot(tokens_ref[...], extra_ref[...], preferred_element_type=jnp.float32)
    logits = jnp.where(chosen, logits, MASKED_SCORE)
    lifted = jnp.where(chosen, jnp.exp(logits - jnp.max(logits, -1, keepdims=True)), 0.0)
    gates_s[...] = lifted / jnp.sum(lifted, -1, keepdims=True)
    own = pl.ds(pl.multiple_of(f * tokens, 16), tokens)
    gates_out[...] = gates_s[own, :]

    part_s[:, model:] = jnp.zeros((reach, 128), low)
    order = list(range(1, ep)) + [0]
    over = (((0,), (0,)), ((), ()))
    across = (((1,), (1,)), ((), ()))

    def act(e):
        at = slice(e * hidden, (e + 1) * hidden)
        at_up = slice(span + e * hidden, span + (e + 1) * hidden)
        at_down = slice(2 * span + e * hidden, 2 * span + (e + 1) * hidden)
        mine = lane == f * local + e
        gate = jnp.sum(jnp.where(mine, gates_s[...], 0.0), -1, keepdims=True)
        for copy in coming[1:5] if e == 0 else coming[2 + 3 * e : 5 + 3 * e]:
            copy.wait()
        former = jnp.dot(tokens_ref[...], weight_ref[:, at], preferred_element_type=jnp.float32)
        latter = jnp.dot(tokens_ref[...], weight_ref[:, at_up], preferred_element_type=jnp.float32)
        grad = jnp.dot(outer_ref[...], weight_ref[:, at_down], preferred_element_type=jnp.float32)
        logistic = 1.0 / (1.0 + jnp.exp(-former))
        active = former * logistic
        value = (active * latter).astype(low).astype(jnp.float32)
        gated_s[:, at] = (value * gate).astype(low)
        picked = jnp.sum(value * grad, -1, keepdims=True)
        dgate = jnp.where(mine & (gate > 0.0), picked, 0.0)
        high = dgate.astype(low).astype(jnp.float32)
        part_s[:, model:] += (high + pltpu.roll(dgate - high, EXPERTS, 1)).astype(low)
        grad = grad * gate
        side_s[:, at] = (grad * latter * logistic * (1.0 + former * (1.0 - logistic))).astype(low)
        side_s[:, at_up] = (grad * active).astype(low)

    def sums(e):
        for d in order:
            at = pl.ds(pl.multiple_of(lax.rem(f + d, ep) * 4 * rows, 128), 4 * rows)
            start = 3 * e * hidden
            for kind, (left, right) in enumerate(((tokens_ref, side_s), (tokens_ref, side_s), (outer_ref, gated_s))):
                column = (kind * span if kind < 2 else 0) + e * hidden
                sums_s[at, start + kind * hidden : start + (kind + 1) * hidden] = lax.dot_general(
                    left[:, at], right[:, column : column + hidden], over, preferred_element_type=jnp.float32
                ).astype(low)
            plane.start(d, e)

    def dn2(d):
        here = pl.ds(pl.multiple_of(back.peer(d) * tokens, 16), tokens)

        def tile(n, carry):
            at = pl.ds(pl.multiple_of(n * 256, 256), 256)
            part_s[here, at] = lax.dot_general(
                side_s[here, :], weight_ref[at, : 2 * span], across, preferred_element_type=jnp.float32
            ).astype(low)
            return carry

        lax.fori_loop(0, model // 256, tile, 0)
        back.to_core(d)

    def mixtures(n, carry):
        at = pl.ds(pl.multiple_of(n * 256, 256), 256)
        mixture_s[:, at] = lax.dot_general(
            gated_s[...], weight_ref[at, 2 * span :], across, preferred_element_type=jnp.float32
        ).astype(low)
        return carry

    act(0)
    sums(0)
    for e in range(1, local):
        act(e)
    sums(1)
    for step, d in enumerate(order):
        dn2(d)
        if step > 0:
            back.to_z(order[step - 1])
    for e in range(2, local):
        sums(e)
    lax.fori_loop(0, model // 256, mixtures, 0)
    mixture_copy = pltpu.make_async_copy(mixture_s, mixture_out, local_sem.at[2])
    mixture_copy.start()
    returned_ref[back.rows(back.t), :] = back.collect()
    back.share(returned_ref)
    for d in order:
        plane.finish(d)
        for way in range(2):
            for number, out in enumerate((relay_out, own_out)):
                pltpu.make_async_copy(
                    plane.landings[way].at[d, number], out.at[way, d], local_sem.at[number]
                ).start()
    mixture_copy.wait()
    back.finish(returned_ref)
    for number, out in enumerate((relay_out, own_out)):
        pltpu.make_async_copy(out, out, local_sem.at[number]).wait()
    all_sent(sent)


def run_experts(tokens_all, outer_all, routes_all, extra, weights, collective_id):
    ep = lax.axis_size("fsdp")
    reach, model = tokens_all.shape
    tokens, low = reach // ep, tokens_all.dtype
    rows = model // (4 * ep)
    full = weights.shape[1]
    span = full // 3
    dma = pltpu.SemaphoreType.DMA
    anywhere = pl.BlockSpec(memory_space=pl.ANY)
    vmem = pl.BlockSpec(memory_space=pltpu.VMEM)
    shape = jax.ShapeDtypeStruct
    return pl.pallas_call(
        experts_kernel,
        out_shape=(
            shape((tokens, model + 128), jnp.float32),
            shape((reach, model), low),
            shape((2, ep, rows, full // 2), low),
            shape((2, ep, rows, full // 2), low),
            shape((tokens, 128), jnp.float32),
        ),
        in_specs=[vmem] * 2 + [anywhere] * 3,
        out_specs=(vmem, anywhere, anywhere, anywhere, vmem),
        scratch_shapes=[
            pltpu.VMEM(tokens_all.shape, low),
            pltpu.VMEM(outer_all.shape, low),
            pltpu.VMEM(weights.shape, low),
            dma((2 + 3 * EXPERTS // ep,)),
            pltpu.VMEM((reach, 128), jnp.float32),
            pltpu.VMEM((reach, span), low),
            pltpu.VMEM((reach, 2 * span), low),
            pltpu.VMEM((reach, model + 128), low),
            pltpu.VMEM((reach, model), low),
            pltpu.VMEM(weights.shape, low),
            pltpu.VMEM((ep, 2, rows, full // 2), low),
            pltpu.VMEM((ep, 2, rows, full // 2), low),
            dma((2, ep, 2)),
            dma((2, ep, 2)),
            dma((3,)),
        ]
        + z_sum_scratch(ep, tokens, model + 128, low),
        compiler_params=pltpu.CompilerParams(
            collective_id=collective_id, has_side_effects=True, vmem_limit_bytes=63 * 1024 * 1024
        ),
        cost_estimate=lasting(90),
        name="experts",
    )(routes_all, extra, tokens_all, outer_all, weights)


def rear_kernel(
    gates_ref, log_ref, cos_ref, sin_ref, segment_ref, returned_hbm, middle_hbm, outer_hbm, extra_hbm,
    mixed_hbm, query_hbm, pair_hbm, input_hbm, normed1_hbm, mixture_ref, relay_ref, own_ref, attn_ref,
    input_grad, layer_out, qkv_out, wo_out, expert_out,
    returned_ref, middle_ref, outer_ref, extra_ref, mixed_ref, query_ref, pair_ref, input_ref, normed1_ref, in_sem,
    wo_s, qkv_s, query_s, grad_s, mixed_s, key_s, value_s, bias_s, query_grad_s, key_grad_s, value_grad_s,
    pair_s, landing_s, back_s, attn_grad_s, part_s, other_s, router_s, gains_s, mixture_s, own_s, second_s,
    local_sem, key_send, key_recv, pair_send, pair_recv, second_send, second_recv, swap_send, swap_recv, layer_send, layer_recv, *scratch,
):
    ep, rows = expert_out.shape[0], expert_out.shape[2]
    f, c, t = lax.axis_index("fsdp"), lax.axis_index("ctx"), lax.axis_index("tp")
    low = jnp.bfloat16
    tokens, model = input_ref.shape
    heads, key_heads = query_s.shape[0], key_s.shape[0]
    groups = heads // key_heads
    width, kv_width = heads * HD, key_heads * HD
    qkv_width = width + 2 * kv_width
    sent = []
    mixture = PairSum(mixture_ref, mixture_s, scratch[:7], sent)
    scratch = scratch[7:]
    size = len(shard_sum_scratch(ep, rows, 256, low))
    wo = ShardSum(wo_s, rows, width, scratch[:size], sent)
    qkv = ShardSum(qkv_s, rows, qkv_width + 128, scratch[size:], sent)
    partners = all_partners(ep)
    plane = [at_device(f, c ^ k, t) for k in range(1, 4)]
    core = partners[-1]

    coming = fetch(
        [
            (returned_hbm, returned_ref), (middle_hbm, middle_ref), (outer_hbm, outer_ref), (extra_hbm, extra_ref),
            (mixed_hbm, mixed_ref), (query_hbm, query_ref), (pair_hbm, pair_ref), (input_hbm, input_ref),
            (normed1_hbm, normed1_ref),
        ],
        in_sem,
    )
    copies = [
        pltpu.make_async_copy(attn_ref.at[:, pl.ds(qkv_width + 128, width)], wo_s, local_sem.at[0]),
        pltpu.make_async_copy(attn_ref.at[:, pl.ds(0, qkv_width + 128)], qkv_s, local_sem.at[1]),
    ]
    for copy in copies:
        copy.start()
    for g in range(ep):
        pltpu.make_async_copy(mixture_ref.at[mixture.place(g, t)], mixture_s.at[g], local_sem.at[2]).start()
    copies.append(pltpu.make_async_copy(own_ref, own_s, local_sem.at[3]))
    copies[2].start()
    greet(partners + plane[2:])
    order = wo.order
    mixture.to_core()
    seconds = {}

    def second(d):
        for way in range(2):
            copy = remote(
                relay_ref.at[way, d], second_s.at[way, d], second_send.at[way, d], second_recv.at[way, d],
                plane[1 - way],
            )
            copy.start()
            sent.append((None, copy))
            seconds[way, d] = copy

    def swap(d):
        for way in range(2):
            seconds[way, d].wait_recv()
        own_s[:, d] = (own_s[:, d].astype(jnp.float32) + second_s[:, d].astype(jnp.float32)).astype(low)
        if d == 0:
            copy = pltpu.make_async_copy(own_s.at[:, 0], expert_out.at[f], swap_send.at[0])
            copy.start()
            copies.append(copy)
        else:
            copy = remote(own_s.at[:, d], expert_out.at[f], swap_send.at[d], swap_recv.at[d], partners[d - 1])
            copy.start()
            sent.append((None, copy))

    second(1)

    small_lane = lax.broadcasted_iota(jnp.int32, (tokens, 128), 1)
    for copy in coming[:4]:
        copy.wait()
    gains = extra_ref[...].astype(jnp.float32).T
    gain_one, gain_two = gains[EXPERTS : EXPERTS + 1, :], gains[EXPERTS + 1 : EXPERTS + 2, :]
    tail = returned_ref[:, model:]
    picked = jnp.where(small_lane < EXPERTS, tail + pltpu.roll(tail, 128 - EXPERTS, 1), 0.0)
    gates = gates_ref[...]
    logit_grad = (gates * (picked - jnp.sum(gates * picked, -1, keepdims=True))).astype(low)
    second_grad = returned_ref[:, :model] + lax.dot_general(
        logit_grad, extra_ref[...], (((1,), (1,)), ((), ())), preferred_element_type=jnp.float32
    )
    middle = middle_ref[...]
    inverse = lax.rsqrt(jnp.mean(middle * middle, -1, keepdims=True) + EPSILON)
    scaled = second_grad * gain_two
    mean_term = jnp.mean(scaled * middle, -1, keepdims=True)
    gains_s[1:2, :] = jnp.sum(second_grad * middle * inverse, 0, keepdims=True)
    middle_grad = outer_ref[...].astype(jnp.float32) + (
        inverse * scaled - middle * (inverse * inverse * inverse) * mean_term
    )
    input_grad[...] = middle_grad
    attn_grad_s[...] = middle_grad.astype(low)

    pltpu.make_async_copy(mixture_s, mixture_s, local_sem.at[2]).wait()
    mixture.begin()
    second(2)
    copies[0].wait()
    for start in range(0, width, 256):
        tile = jnp.dot(
            attn_grad_s[...], wo_s[:, start : start + 256], preferred_element_type=jnp.float32
        ).astype(low)
        for side in range(0, 256, HD):
            grad_s[(start + side) // HD] = tile[:, side : side + HD]

    copies[2].wait()
    swap(1)
    second(3)
    length = segment_ref.shape[1]
    seg_keys = jnp.broadcast_to(segment_ref[...].astype(jnp.float32), (128, length)).T[:, :1]
    seg_queries = segment_ref[:, pl.ds(pl.multiple_of(c * tokens, 128), tokens)].astype(jnp.float32)
    key_order = lax.broadcasted_iota(jnp.int32, (length, tokens), 0)
    query_order = lax.broadcasted_iota(jnp.int32, (length, tokens), 1) + c * tokens
    bias_s[...] = jnp.where((seg_keys == seg_queries) & (key_order <= query_order), 0.0, MASKED_SCORE)
    for copy in coming[4:]:
        copy.wait()
    for h in range(heads):
        query_s[h] = query_ref[:, h * HD : (h + 1) * HD]
        mixed_s[h] = mixed_ref[:, h * HD : (h + 1) * HD]
    for g in range(key_heads):
        key_s[g] = pair_ref[:, g * HD : (g + 1) * HD]
        value_s[g] = pair_ref[:, kv_width + g * HD : kv_width + (g + 1) * HD]
    across = (((1,), (1,)), ((), ()))

    def attend_back(g, carry):
        key_grad = jnp.zeros((length, HD), jnp.float32)
        value_grad = jnp.zeros((length, HD), jnp.float32)
        for number in range(groups):
            h = g * groups + number
            query = query_s[h] * jnp.asarray(HD**-0.5, low)
            grad = grad_s[h]
            scores = lax.dot_general(key_s[g], query, across, preferred_element_type=jnp.float32) + bias_s[...]
            probs = jnp.exp(scores - log_ref[h])
            value_grad += jnp.dot(probs.astype(low), grad, preferred_element_type=jnp.float32)
            prob_grad = lax.dot_general(value_s[g], grad, across, preferred_element_type=jnp.float32)
            delta = jnp.sum((grad.astype(jnp.float32) * mixed_s[h].astype(jnp.float32)).T, 0, keepdims=True)
            score_grad = (probs * (prob_grad - delta)).astype(low)
            key_grad += jnp.dot(score_grad, query, preferred_element_type=jnp.float32)
            query_grad = lax.dot_general(
                key_s[g], score_grad, (((0,), (0,)), ((), ())), preferred_element_type=jnp.float32
            )
            query_grad_s[h] = query_grad.T * (HD**-0.5)
        key_grad_s[g] = key_grad.astype(low)
        value_grad_s[g] = value_grad.astype(low)
        return carry

    lax.fori_loop(0, key_heads // 2, attend_back, 0)
    swap(2)
    second(0)
    lax.fori_loop(key_heads // 2, key_heads, attend_back, 0)
    for g in range(key_heads):
        pair_s[:, g * HD : (g + 1) * HD] = key_grad_s[g]
        pair_s[:, kv_width + g * HD : kv_width + (g + 1) * HD] = value_grad_s[g]
    for k in (3, 1, 2):
        place = pl.ds(pl.multiple_of((c ^ k) * tokens, 16), tokens)
        copy = remote(pair_s.at[place], landing_s.at[k - 1], key_send.at[k - 1], key_recv.at[k - 1], plane[k - 1])
        copy.start()
        sent.append((None, copy))
    swap(3)
    swap(0)
    mixture.cross()

    def wo_sums(n, carry):
        at = pl.ds(pl.multiple_of(n * 256, 256), 256)
        wo_s[at, :] = lax.dot_general(
            attn_grad_s[:, at], mixed_ref[...], (((0,), (0,)), ((), ())), preferred_element_type=jnp.float32
        ).astype(low)
        return carry

    lax.fori_loop(0, model // 256, wo_sums, 0)
    router_s[...] = lax.dot_general(
        (middle * inverse * gain_two).astype(low), logit_grad, (((0,), (0,)), ((), ())),
        preferred_element_type=jnp.float32,
    )

    first_half = lax.rem(small_lane, HD) < HD // 2

    def turned_back(tile):
        swapped = jnp.where(first_half, pltpu.roll(tile, 128 - HD // 2, 1), pltpu.roll(tile, HD // 2, 1))
        return tile * cos_ref[...] - swapped * sin_ref[...]

    for start in range(0, width, 128):
        tile = jnp.concatenate([query_grad_s[start // HD], query_grad_s[start // HD + 1]], 1)
        back_s[:, start : start + 128] = turned_back(tile).astype(low)

    pair = pair_s[pl.ds(pl.multiple_of(c * tokens, 16), tokens), :].astype(jnp.float32)
    for k in (1, 2, 3):
        block = landing_s.at[k - 1]
        remote(block, block, key_send.at[k - 1], key_recv.at[k - 1], plane[k - 1]).wait_recv()
        pair = pair + landing_s[k - 1].astype(jnp.float32)
    for d in order:
        wo.first(d)
    for start in range(0, kv_width, 128):
        back_s[:, width + start : width + start + 128] = turned_back(pair[:, start : start + 128]).astype(low)
    back_s[:, width + kv_width :] = pair[:, kv_width:].astype(low)
    copies[1].wait()
    for start in range(0, model, 256):
        part_s[:, start : start + 256] = lax.dot_general(
            back_s[...], qkv_s[start : start + 256, :qkv_width], across, preferred_element_type=jnp.float32
        ).astype(low)
    exchange = remote(part_s, other_s, pair_send, pair_recv, core)
    exchange.start()
    sent.append((None, exchange))

    def qkv_sums(n, carry):
        at = pl.ds(pl.multiple_of(n * 256, 256), 256)
        qkv_s[at, :qkv_width] = lax.dot_general(
            normed1_ref[:, at], back_s[...], (((0,), (0,)), ((), ())), preferred_element_type=jnp.float32
        ).astype(low)
        return carry

    lax.fori_loop(0, model // 256, qkv_sums, 0)
    exchange.wait_recv()
    first_grad = part_s[...].astype(jnp.float32) + other_s[...].astype(jnp.float32)
    inputs = input_ref[...].astype(jnp.float32)
    inverse = lax.rsqrt(jnp.mean(inputs * inputs, -1, keepdims=True) + EPSILON)
    gains_s[0:1, :] = jnp.sum(first_grad * inputs * inverse, 0, keepdims=True)
    line = lax.broadcasted_iota(jnp.int32, (128, model), 0)
    turned = jnp.where(line == EXPERTS, gains_s[0:1, :], jnp.where(line == EXPERTS + 1, gains_s[1:2, :], 0.0)).T
    qkv_s[:, qkv_width:] = (router_s[...] + turned).astype(low)
    qkv.first(1)
    qkv.first(2)
    for d in wo.order:
        wo.second(d)
    scaled = first_grad * gain_one
    mean_term = jnp.mean(scaled * inputs, -1, keepdims=True)
    input_grad[...] += inverse * scaled - inputs * (inverse * inverse * inverse) * mean_term
    qkv.second(1)
    qkv.first(3)
    wo.pair_begin(wo_out)
    qkv.second(2)
    qkv.first(0)
    qkv.second(3)
    wo.pair_cross()
    qkv.second(0)
    qkv.pair_begin(qkv_out)
    qkv.pair_cross()
    copies[3].wait()
    for d in range(1, ep):
        landing = expert_out.at[lax.rem(f + ep - d, ep)]
        remote(landing, landing, swap_send.at[d], swap_recv.at[d], core).wait_recv()
    wo.pair_collect(wo_out)
    half, other_half = (pl.ds(pl.multiple_of(part * (tokens // 2), 16), tokens // 2) for part in (t, 1 - t))
    layer_out[half, :] = (middle_ref[half, :] + mixture.collect()).astype(low)
    layer_copy = remote(layer_out.at[half], layer_out.at[half], layer_send, layer_recv, core)
    layer_copy.start()
    sent.append((None, layer_copy))
    qkv.pair_collect(qkv_out)
    remote(layer_out.at[other_half], layer_out.at[other_half], layer_send, layer_recv, core).wait_recv()
    all_sent(sent)


def rear(
    returned, gates, middle, inputs, outer, normed1, query, pair, mixed, log_total, cosine, sine, segments, extra,
    mixture, relay, own, attn, collective_id,
):
    ep = lax.axis_size("fsdp")
    tokens, model = inputs.shape
    rows = own.shape[2]
    heads, key_heads = query.shape[1] // HD, pair.shape[1] // (2 * HD)
    width, kv_width = heads * HD, key_heads * HD
    qkv_width = width + 2 * kv_width
    length = pair.shape[0]
    low = jnp.bfloat16
    dma = pltpu.SemaphoreType.DMA
    anywhere = pl.BlockSpec(memory_space=pl.ANY)
    vmem = pl.BlockSpec(memory_space=pltpu.VMEM)
    shape = jax.ShapeDtypeStruct
    room = pltpu.VMEM
    fetched = (returned, middle, outer, extra, mixed, query, pair, inputs, normed1)
    return pl.pallas_call(
        rear_kernel,
        out_shape=(
            shape((tokens, model), jnp.float32),
            shape((tokens, model), low),
            shape((rows, qkv_width + 128), jnp.float32),
            shape((rows, width), jnp.float32),
            shape((ep, 2, rows, own.shape[3]), low),
        ),
        in_specs=[vmem] * 5 + [anywhere] * 13,
        out_specs=(vmem,) * 4 + (anywhere,),
        scratch_shapes=[room(each.shape, each.dtype) for each in fetched]
        + [
            dma((len(fetched),)),
            room((model, width), low),
            room((model, qkv_width + 128), low),
            room((heads, tokens, HD), low),
            room((heads, tokens, HD), low),
            room((heads, tokens, HD), low),
            room((key_heads, length, HD), low),
            room((key_heads, length, HD), low),
            room((length, tokens), jnp.float32),
            room((heads, tokens, HD), jnp.float32),
            room((key_heads, length, HD), low),
            room((key_heads, length, HD), low),
            room((length, 2 * kv_width), low),
            room((3, tokens, 2 * kv_width), low),
            room((tokens, qkv_width), low),
            room((tokens, model), low),
            room((tokens, model), low),
            room((tokens, model), low),
            room((model, 128), jnp.float32),
            room((8, model), jnp.float32),
            room((ep, tokens // 2, model), low),
            room(own.shape, low),
            room(own.shape, low),
            dma((4,)),
            dma((3,)),
            dma((3,)),
            dma,
            dma,
            dma((2, ep)),
            dma((2, ep)),
            dma((ep,)),
            dma((ep,)),
            dma,
            dma,
        ]
        + pair_sum_scratch(ep, tokens, model, low)
        + shard_sum_scratch(ep, rows, width, low)
        + shard_sum_scratch(ep, rows, qkv_width + 128, low),
        compiler_params=pltpu.CompilerParams(
            collective_id=collective_id, has_side_effects=True, vmem_limit_bytes=63 * 1024 * 1024
        ),
        cost_estimate=lasting(170),
        name="rear",
    )(gates, log_total, cosine, sine, segments, *fetched, mixture, relay, own, attn)


def finish_kernel(
    expert_ref, qkv_ref, wo_ref, input_ref, layer_ref,
    query_out, key_out, value_out, output_out, router_out, gain_one_out, gain_two_out,
    gate_out, up_out, down_out, input_out, layer_out,
):
    local, _, hidden = gate_out.shape
    cut = expert_ref.shape[3] // local
    for e in range(local):
        at = slice(e * cut, (e + 1) * cut)
        both = jnp.concatenate([expert_ref[0, 0, :, at], expert_ref[0, 1, :, at]], 1).astype(jnp.float32)
        for kind, out in enumerate((gate_out, up_out, down_out)):
            out[e] = both[:, kind * hidden : (kind + 1) * hidden]
    input_out[...] = input_ref[...]
    layer_out[...] = layer_ref[...]

    @pl.when(pl.program_id(0) == 0)
    def _():
        width, kv_width = query_out.shape[1], key_out.shape[1]
        query_out[...] = qkv_ref[:, :width]
        key_out[...] = qkv_ref[:, width : width + kv_width]
        value_out[...] = qkv_ref[:, width + kv_width : width + 2 * kv_width]
        small = qkv_ref[:, width + 2 * kv_width :].T
        router_out[...] = small[:EXPERTS]
        gain_one_out[...] = small[EXPERTS : EXPERTS + 1]
        gain_two_out[...] = small[EXPERTS + 1 : EXPERTS + 2]
        output_out[...] = wo_ref[...]


def finish(experts, qkv, wo, input_grad, layer_output, kv_width, hidden):
    ep, _, rows, half = experts.shape
    width = wo.shape[1]
    local = 2 * half // (3 * hidden)
    tokens, model = input_grad.shape
    shape = jax.ShapeDtypeStruct

    def whole(*dims):
        return pl.BlockSpec(dims, lambda i: (0, 0))

    by_z = pl.BlockSpec((local, rows, hidden), lambda i: (i, 0, 0))
    by_rows = pl.BlockSpec((tokens // ep, model), lambda i: (i, 0))
    return pl.pallas_call(
        finish_kernel,
        grid=(ep,),
        out_shape=(
            shape((rows, width), jnp.float32),
            shape((rows, kv_width), jnp.float32),
            shape((rows, kv_width), jnp.float32),
            shape((rows, width), jnp.float32),
            shape((EXPERTS, rows), jnp.float32),
            shape((1, rows), jnp.float32),
            shape((1, rows), jnp.float32),
            shape((ep * local, rows, hidden), jnp.float32),
            shape((ep * local, rows, hidden), jnp.float32),
            shape((ep * local, rows, hidden), jnp.float32),
            shape((tokens, model), jnp.float32),
            shape((tokens, model), layer_output.dtype),
        ),
        in_specs=[
            pl.BlockSpec((1, 2, rows, half), lambda i: (i, 0, 0, 0)),
            whole(*qkv.shape),
            whole(*wo.shape),
            by_rows,
            by_rows,
        ],
        out_specs=(
            whole(rows, width),
            whole(rows, kv_width),
            whole(rows, kv_width),
            whole(rows, width),
            whole(EXPERTS, rows),
            whole(1, rows),
            whole(1, rows),
            by_z,
            by_z,
            by_z,
            by_rows,
            by_rows,
        ),
        compiler_params=pltpu.CompilerParams(vmem_limit_bytes=60 * 1024 * 1024),
        cost_estimate=lasting(6),
        name="finish",
    )(experts, qkv, wo, input_grad, layer_output)


def plain_shards(
    layer_input,
    segments,
    routes,
    norm_gain,
    query_weight,
    key_weight,
    value_weight,
    output_weight,
    ffn_gain,
    router_weight,
    gate_weight,
    up_weight,
    down_weight,
    cotangent,
):
    low = jnp.bfloat16
    both = ("fsdp", "ctx")
    ep = lax.axis_size("fsdp")
    tokens = layer_input.shape[0]
    seq_len = segments.shape[1]
    rows = query_weight.shape[0]
    width = query_weight.shape[1]
    kv_width = key_weight.shape[1]
    hidden_width = gate_weight.shape[2]
    local = EXPERTS // ep
    span = local * hidden_width

    qkv_width = width + 2 * kv_width
    extra = jnp.concatenate([router_weight, norm_gain[:, None], ffn_gain[:, None]], 1)
    extra = jnp.pad(extra, ((0, 0), (0, 128 - extra.shape[1])))
    attn_shard = jnp.concatenate([query_weight, key_weight, value_weight, extra, output_weight.T], 1)
    down_shard = down_weight.transpose(0, 2, 1)
    begin = lax.axis_index("ctx") * tokens
    segment_row = segments[0]
    query_doc = lax.dynamic_slice_in_dim(segment_row, begin, tokens)
    query_order = begin + jnp.arange(tokens, dtype=jnp.int32)
    scale = HD ** (-0.5)
    inputs = layer_input.astype(jnp.float32)
    key_groups = kv_width // HD
    groups = width // kv_width
    freq = 10000.0 ** (-2.0 * jnp.arange(HD // 2, dtype=jnp.float32) / HD)

    def unpack(attn_full):
        return (
            attn_full[:, :qkv_width],
            attn_full[:, qkv_width : qkv_width + EXPERTS],
            attn_full[:, qkv_width + EXPERTS],
            attn_full[:, qkv_width + EXPERTS + 1],
            attn_full[:, qkv_width + 128 :],
        )

    attn_full = lax.all_gather(attn_shard, both, axis=0, tiled=True)
    qkv_full, router_full, gain_one, gain_two, output_turned = unpack(attn_full)
    packed = jnp.concatenate([gate_weight, up_weight, down_shard], -1)
    expert_full = spread_experts(packed)
    expert_full = expert_full.reshape(D, local, 3, hidden_width).transpose(0, 2, 1, 3)
    expert_full = expert_full.reshape(D, 3 * span)
    outer_all = lax.all_gather(cotangent, "fsdp", axis=0, tiled=True)
    routes_all = lax.all_gather(routes, "fsdp", axis=0, tiled=True)
    place = lax.dynamic_slice_in_dim(document_place(segment_row), begin, tokens)
    angle = place.astype(jnp.float32)[:, None] * freq[None, :]
    cosine, sine = jnp.cos(angle), jnp.sin(angle)
    first_norm, first_inverse = normalize(inputs, gain_one)
    normed1 = first_norm.astype(low)
    projected = jnp.dot(normed1, qkv_full, preferred_element_type=jnp.float32)
    query = rotate(projected[:, :width], cosine, sine).astype(low)
    key = rotate(projected[:, width : width + kv_width], cosine, sine).astype(low)
    value = projected[:, width + kv_width :].astype(low)
    pair_all = lax.all_gather(jnp.concatenate([key, value], 1), "ctx", axis=0, tiled=True)
    heads = query.reshape(tokens, key_groups, groups, HD)
    key_heads = pair_all[:, :kv_width].reshape(seq_len, key_groups, HD)
    value_heads = pair_all[:, kv_width:].reshape(seq_len, key_groups, HD)
    scores = jnp.einsum("qkgd,nkd->qkgn", heads, key_heads, preferred_element_type=jnp.float32) * scale
    seen = (segment_row[None, :] == query_doc[:, None]) & (
        jnp.arange(seq_len, dtype=jnp.int32)[None, :] <= query_order[:, None]
    )
    scores = jnp.where(seen[:, None, None, :], scores, MASKED_SCORE)
    running = jnp.max(scores, -1)
    weights = jnp.exp(scores - running[..., None])
    summed = jnp.einsum(
        "qkgn,nkd->qkgd", weights.astype(low), value_heads, preferred_element_type=jnp.float32
    )
    totals = jnp.sum(weights, -1)
    log_total = running + jnp.log(totals)
    mixed_low = (summed / totals[..., None]).reshape(tokens, -1).astype(low)
    attention = lax.psum(
        times_transpose(mixed_low, output_turned).astype(low), "tp"
    ).astype(jnp.float32)
    middle = inputs + attention
    second_norm, second_inverse = normalize(middle, gain_two)
    normed2 = second_norm.astype(low)
    normed2_all = lax.all_gather(normed2, "fsdp", axis=0, tiled=True)
    gate_up = expert_full[:, : 2 * span]
    down_turned = expert_full[:, 2 * span :]
    key_all = pair_all[:, :kv_width]
    value_all = pair_all[:, kv_width:]
    grouped = query.reshape(tokens, key_groups, groups, HD)

    def block_scores(key_piece, offset):
        count = key_piece.shape[0]
        key_heads = key_piece.reshape(count, key_groups, HD)
        scores = (
            jnp.einsum("qkgd,nkd->qkgn", grouped, key_heads, preferred_element_type=jnp.float32)
            * scale
        )
        key_doc = lax.dynamic_slice_in_dim(segment_row, offset, count)
        key_order = offset + jnp.arange(count, dtype=jnp.int32)
        seen = (key_doc[None, :] == query_doc[:, None]) & (
            key_order[None, :] <= query_order[:, None]
        )
        return (scores, seen[:, None, None, :], key_heads)

    def masked_away(offset, count):
        last_doc = lax.dynamic_index_in_dim(segment_row, offset + count - 1, keepdims=False)
        return (offset > query_order[tokens - 1]) | (last_doc < query_doc[0])

    place_z = lax.axis_index("fsdp")
    logits_all = jnp.dot(normed2_all, router_full, preferred_element_type=jnp.float32)
    expert_ids = jnp.arange(EXPERTS, dtype=jnp.int32)
    chosen_all = jnp.any(routes_all[:, :, None] == expert_ids[None, None, :], 1)
    masked_logits = jnp.where(chosen_all, logits_all, MASKED_SCORE)
    top = jnp.max(masked_logits, -1, keepdims=True)
    lifted = jnp.where(chosen_all, jnp.exp(masked_logits - top), 0.0)
    gates_all = lifted / jnp.sum(lifted, -1, keepdims=True)
    gates_here = lax.dynamic_slice_in_dim(gates_all, place_z * local, local, 1)
    chosen_here = lax.dynamic_slice_in_dim(chosen_all, place_z * local, local, 1)
    chosen = lax.dynamic_slice_in_dim(chosen_all, place_z * tokens, tokens, 0)
    gates = lax.dynamic_slice_in_dim(gates_all, place_z * tokens, tokens, 0)

    reach = normed2_all.shape[0]
    both_sides = jnp.dot(normed2_all, gate_up, preferred_element_type=jnp.float32)
    former = both_sides[:, :span]
    latter = both_sides[:, span:]
    hidden_grad = jnp.dot(outer_all, down_turned, preferred_element_type=jnp.float32)
    gate_wide = jnp.concatenate(
        [jnp.broadcast_to(gates_here[:, e : e + 1], (reach, hidden_width)) for e in range(local)], 1
    )
    logistic = jax.nn.sigmoid(former)
    active = former * logistic
    hidden = (active * latter).astype(low).astype(jnp.float32)
    gated = (hidden * gate_wide).astype(low)
    parts = [slice(e * hidden_width, (e + 1) * hidden_width) for e in range(local)]
    dgates = jnp.stack([jnp.sum(hidden[:, part] * hidden_grad[:, part], -1) for part in parts], 1)
    scaled_grad = hidden_grad * gate_wide
    former_grad = (scaled_grad * latter * logistic * (1.0 + former * (1.0 - logistic))).astype(low)
    latter_grad = (scaled_grad * active).astype(low)
    side_grads = jnp.concatenate([former_grad, latter_grad], 1)
    mixture_low = times_transpose(gated, down_turned).astype(low)
    input_part = times_transpose(side_grads, gate_up)
    side_sums = contract_rows(normed2_all, side_grads)
    down_sums = contract_rows(outer_all, gated)
    dgates = jnp.where(chosen_here, dgates, 0.0)
    dgates_wide = lax.dynamic_update_slice_in_dim(
        jnp.zeros((reach, EXPERTS), jnp.float32), dgates, place_z * local, 1
    )
    dgates_high = dgates_wide.astype(low)
    dgates_rest = (dgates_wide - dgates_high.astype(jnp.float32)).astype(low)
    dgates_sent = jnp.concatenate([dgates_high, dgates_rest], 1)
    dgates_sent = jnp.pad(dgates_sent, ((0, 0), (0, 128 - 2 * EXPERTS)))
    back_part = jnp.concatenate([input_part.astype(low), dgates_sent], 1)
    returned = lax.psum_scatter(
        lax.psum(back_part, "tp"), "fsdp", scatter_dimension=0, tiled=True
    ).astype(jnp.float32)
    expert_sums = jnp.concatenate([side_sums, down_sums], 1).astype(low)
    expert_out = collect_experts(expert_sums, rows).reshape(ep, rows, 3, local, hidden_width)
    side_out = expert_out[:, :, :2].transpose(2, 0, 3, 1, 4).reshape(2, EXPERTS, rows, hidden_width)
    side_out = side_out.astype(jnp.float32)
    down_out = expert_out[:, :, 2].transpose(0, 2, 3, 1).reshape(EXPERTS, hidden_width, rows).astype(jnp.float32)

    outer_grad = cotangent.astype(jnp.float32)
    input_grad_part = returned[:, :D]
    picked = returned[:, D : D + EXPERTS] + returned[:, D + EXPERTS : D + 2 * EXPERTS]
    logit_grad = (gates * (picked - jnp.sum(gates * picked, -1, keepdims=True))).astype(low)
    router_sums = contract_rows(normed2, logit_grad)
    second_grad = input_grad_part + times_transpose(logit_grad, router_full)
    middle_back, gain_two_sums = norm_back(second_grad, middle, second_inverse, gain_two)
    middle_grad = outer_grad + middle_back
    attention_grad = middle_grad.astype(low)
    output_sums = contract_rows(attention_grad, mixed_low)
    mixed_grad = jnp.dot(attention_grad, output_turned, preferred_element_type=jnp.float32).astype(low)
    mixed_heads = mixed_grad.reshape(tokens, key_groups, groups, HD)
    delta = jnp.sum(mixed_heads.astype(jnp.float32) * mixed_low.reshape(mixed_heads.shape), -1)

    def back_two(number, state):
        offset = number * tokens
        key_piece = lax.dynamic_slice_in_dim(key_all, offset, tokens, 0)
        value_piece = lax.dynamic_slice_in_dim(value_all, offset, tokens, 0)

        def back_compute(inner):
            query_sum, pair_sum = inner
            scores, seen, key_heads = block_scores(key_piece, offset)
            probs = jnp.where(seen, jnp.exp(scores - log_total[..., None]), 0.0)
            value_heads = value_piece.reshape(tokens, key_groups, HD)
            prob_grad = jnp.einsum(
                "qkgd,nkd->qkgn", mixed_heads, value_heads, preferred_element_type=jnp.float32
            )
            score_grad = (probs * (prob_grad - delta[..., None])).astype(low)
            query_sum = (
                query_sum
                + jnp.einsum(
                    "qkgn,nkd->qkgd", score_grad, key_heads, preferred_element_type=jnp.float32
                )
                * scale
            )
            key_block = (
                jnp.einsum(
                    "qkgn,qkgd->nkd", score_grad, grouped, preferred_element_type=jnp.float32
                )
                * scale
            )
            value_block = jnp.einsum(
                "qkgn,qkgd->nkd", probs.astype(low), mixed_heads, preferred_element_type=jnp.float32
            )
            pair = jnp.concatenate([key_block.reshape(tokens, -1), value_block.reshape(tokens, -1)], 1)
            return (query_sum, lax.dynamic_update_slice_in_dim(pair_sum, pair, offset, 0))

        return lax.cond(masked_away(offset, tokens), lambda inner: inner, back_compute, state)

    back_state = (
        jnp.zeros((tokens, key_groups, groups, HD), jnp.float32),
        jnp.zeros((seq_len, 2 * kv_width), jnp.float32),
    )
    query_sum, pair_sum = lax.fori_loop(0, seq_len // tokens, back_two, back_state)
    pair_local = lax.psum_scatter(
        pair_sum.astype(low), "ctx", scatter_dimension=0, tiled=True
    ).astype(jnp.float32)
    query_back = rotate(query_sum.reshape(tokens, -1), cosine, -sine)
    key_back = rotate(pair_local[:, :kv_width], cosine, -sine)
    qkv_back = jnp.concatenate([query_back, key_back, pair_local[:, kv_width:]], 1).astype(low)
    qkv_sums = contract_rows(normed1, qkv_back)
    first_part = times_transpose(qkv_back, qkv_full)
    first_grad = lax.psum(first_part.astype(low), "tp").astype(jnp.float32)
    input_back, gain_one_sums = norm_back(first_grad, inputs, first_inverse, gain_one)
    input_grad = middle_grad + input_back
    small_sums = jnp.concatenate([router_sums, gain_one_sums[:, None], gain_two_sums[:, None]], 1)
    small_sums = jnp.pad(small_sums, ((0, 0), (0, 128 - small_sums.shape[1])))
    attn_sums = jnp.concatenate([qkv_sums.astype(low), small_sums.astype(low), output_sums.astype(low)], 1)
    attn_out = lax.psum_scatter(attn_sums, both, scatter_dimension=0, tiled=True).astype(jnp.float32)
    mixture = lax.psum_scatter(
        lax.psum(mixture_low, "tp"), "fsdp", scatter_dimension=0, tiled=True
    ).astype(jnp.float32)
    layer_output = (middle + mixture).astype(low)
    small_out = attn_out[:, qkv_width : qkv_width + 128]
    return (
        layer_output,
        input_grad,
        small_out[:, EXPERTS],
        attn_out[:, :width],
        attn_out[:, width : width + kv_width],
        attn_out[:, width + kv_width : qkv_width],
        attn_out[:, qkv_width + 128 :].T,
        small_out[:, EXPERTS + 1],
        small_out[:, :EXPERTS],
        side_out[0],
        side_out[1],
        down_out,
    )


def shards(
    layer_input,
    segments,
    routes,
    norm_gain,
    query_weight,
    key_weight,
    value_weight,
    output_weight,
    ffn_gain,
    router_weight,
    gate_weight,
    up_weight,
    down_weight,
    cotangent,
):
    freq = 10000.0 ** (-2.0 * np.arange(HD // 2) / HD)
    (
        expert_full, outer_all, routes_all, normed2_all,
        attn_full, normed1, query, pair_all, mixed, middle, log_total, cosine, sine, extra_all,
    ) = front(
        query_weight, key_weight, value_weight, output_weight.T, gate_weight, up_weight,
        down_weight.transpose(0, 2, 1), cotangent, routes.T, layer_input, segments,
        np.tile(freq.astype(np.float32), 4)[None, :], router_weight.T, norm_gain[None, :], ffn_gain[None, :],
    )
    returned, mixture, relay, own, gates = run_experts(
        normed2_all, outer_all, routes_all, extra_all, expert_full, 2
    )
    input_grad, layer_output, qkv_out, wo_out, expert_out = rear(
        returned, gates, middle, layer_input, cotangent, normed1, query, pair_all, mixed, log_total, cosine, sine,
        segments, extra_all, mixture, relay, own, attn_full, 3,
    )
    (
        query_out, key_out, value_out, output_out, router_out, gain_one_out, gain_two_out,
        gate_out, up_out, down_out, input_grad, layer_output,
    ) = finish(expert_out, qkv_out, wo_out, input_grad, layer_output, key_weight.shape[1], gate_weight.shape[2])
    return (
        layer_output,
        input_grad,
        gain_one_out[0],
        query_out,
        key_out,
        value_out,
        output_out.T,
        gain_two_out[0],
        router_out.T,
        gate_out,
        up_out,
        down_out.transpose(0, 2, 1),
    )


def solution(mesh):
    in_specs = (
        P(("fsdp", "ctx"), None),
        P("fsdp", None),
        P(("fsdp", "ctx"), None),
        P(("fsdp", "ctx")),
        P(("fsdp", "ctx"), "tp"),
        P(("fsdp", "ctx"), "tp"),
        P(("fsdp", "ctx"), "tp"),
        P("tp", ("fsdp", "ctx")),
        P(("fsdp", "ctx")),
        P(("fsdp", "ctx"), None),
        P(None, ("fsdp", "ctx"), "tp"),
        P(None, ("fsdp", "ctx"), "tp"),
        P(None, "tp", ("fsdp", "ctx")),
        P(("fsdp", "ctx"), None),
    )
    out_specs = (
        P(("fsdp", "ctx"), None),
        P(("fsdp", "ctx"), None),
        P(("fsdp", "ctx")),
        P(("fsdp", "ctx"), "tp"),
        P(("fsdp", "ctx"), "tp"),
        P(("fsdp", "ctx"), "tp"),
        P("tp", ("fsdp", "ctx")),
        P(("fsdp", "ctx")),
        P(("fsdp", "ctx"), None),
        P(None, ("fsdp", "ctx"), "tp"),
        P(None, ("fsdp", "ctx"), "tp"),
        P(None, "tp", ("fsdp", "ctx")),
    )
    fits = mesh.shape["ctx"] == 4 and mesh.shape["fsdp"] == 4 and mesh.shape["tp"] == 2
    body = shards if fits else plain_shards
    return jax.shard_map(body, mesh=mesh, in_specs=in_specs, out_specs=out_specs, check_vma=False)
```
